32 devices in a mesh: groups: 2 (over x), tp: 4 (over y, core), seq: 4 (over z).
Axes of the slice: x: 2, y: 2, z: 4, core: 2. Of those that a mesh axis runs over, the one named last changes fastest.
Arguments:
- hidden_in: bfloat16 [6144, 4608], P(('groups', 'seq', 'tp')), parts along dimension 0, may hold values from -6 to 6
- pre_gain: float32 [4608], replicated, may hold values from 0.1 to 1.9
- post_gain: float32 [4608], replicated, may hold values from 0.1 to 1.9
- w_query: bfloat16 [4608, 1024], P(None, 'tp')
- w_key: bfloat16 [4608, 512], P(None, 'tp')
- w_value: bfloat16 [4608, 512], P(None, 'tp'), may hold values from -0.09375 to 0.09375
- w_out: bfloat16 [1024, 4608], P('tp'), may hold values from -0.1875 to 0.1875
- block_of: int32 [8], replicated, may hold values from 0 to 7, each once
Outputs:
- hidden_out: bfloat16 [6144, 4608], P(('groups', 'seq', 'tp')), parts along dimension 0
The draws below stay inside these ranges and needn't reach their ends.
There are 2 independent parts, one for each index of `groups`. The reference program is written for one: setup_inputs(seed, part) draws one part's arguments, and reference() takes and returns one part's arrays. A program takes and returns all parts, laid end to end along the dimension named above; an argument that names none is the same for every part. Nothing has to cross between parts.
Inputs may be any that keep to these rules, and one draw needn't show every extreme that they name: block_of is a permutation: storage block b (rows b * 384 onward) holds the prompt's positions from block_of[b] * 384 onward.
All inputs are finite; a program needn't handle non-finite values.
Results may differ from the reference program's by a relative error of at most 0.012.
Values may be sent and summed in bfloat16 or wider, within the bound.
No kernel may reach another device: no remote copies, remote signals or barrier semaphores. Data moves between devices by JAX's collectives and lax.ppermute only.
A program may use at most 64 MiB of HBM per device.

```python
import jax
import jax.numpy as jnp
from jax import lax

D = 4608
HD = 128
ATT_SCALAR = 144
KV_HEADS = 4
HEADS = 8
SEQ = 3072
BLOCK_ROWS = 384
BLOCKS = 8
N_TP = 4


def shared_directions(key):
    return jnp.clip(jax.random.normal(key, (D, KV_HEADS * HD), jnp.float32), -5.0, 5.0)


def draw_w_key(key, part):
    directions = shared_directions(key)
    return (directions * D ** (-0.5)).astype(jnp.bfloat16)


def draw_w_query(key, part):
    key = jax.random.fold_in(key, 7)
    own_part = jnp.clip(jax.random.normal(key, (D, HEADS * HD), jnp.float32), -5.0, 5.0)
    return (own_part * D ** (-0.5)).astype(jnp.bfloat16)


def levels(key, extent, split, least, high):
    loudness, own = 1.0, jax.random.fold_in(key, 6)
    for axis_at, blocks in split:
        draws = jnp.exp(jax.random.uniform(jax.random.fold_in(own, axis_at), (blocks,), jnp.float32, least / len(split), high / len(split)))
        loudness = loudness * jnp.repeat(draws, extent[axis_at] // blocks).reshape([-1 if axis == axis_at else 1 for axis in range(len(extent))])
    return loudness


def gaussian(key, shape, deviation, limit, shards=(), held_as=jnp.bfloat16):
    gain = levels(key, shape, shards, -0.22, 0.18) if shards else 1.0
    drawn = jax.random.normal(key, shape, jnp.float32) * deviation * gain
    return jnp.minimum(jnp.maximum(drawn, -limit), limit).astype(held_as)


def setup_inputs(seed: int = 0, part: int = 0) -> dict:
    key_list = jax.random.split(jax.random.key(seed), 9)
    part_splits = jax.random.split(jax.random.fold_in(key_list[8], part), 9)
    return {
        "hidden_in": gaussian(part_splits[0], (SEQ, D), 1.0, 6.0, ((0, 16),)),
        "pre_gain": jnp.clip(1.0 + 0.18 * jax.random.normal(key_list[1], (D,), jnp.float32), 0.1, 1.9),
        "post_gain": jnp.clip(1.0 + 0.18 * jax.random.normal(key_list[2], (D,), jnp.float32), 0.1, 1.9),
        "w_query": draw_w_query(jax.random.fold_in(key_list[8], 71), part),
        "w_key": draw_w_key(jax.random.fold_in(key_list[8], 71), part),
        "w_value": gaussian(key_list[5], (D, KV_HEADS * HD), D ** -0.5, 0.09375, ((1, 4),)),
        "w_out": gaussian(key_list[6], (HEADS * HD, D), (HEADS * HD) ** -0.5, 0.1875, ((0, 4),)),
        "block_of": jax.random.permutation(key_list[7], BLOCKS).astype(jnp.int32),
    }


def normalize(row_values, gain_vector):
    features = row_values.astype(jnp.float32)
    return features * lax.rsqrt(lax.optimization_barrier(jnp.mean(features * features, axis=-1, keepdims=True)) + 1e-06) * gain_vector.astype(jnp.float32)

def rotate_pairs(features, positions):
    half_dim = HD // 2
    frequency = jnp.power(jnp.float32(10000.0), -jnp.arange(half_dim, dtype=jnp.float32) * (2.0 / HD))
    angles = positions.astype(jnp.float32)[:, None] * frequency[None, :]
    cosine = jnp.cos(angles)[:, None, :]
    sine_part = jnp.sin(angles)[:, None, :]
    first_half = features[..., :half_dim]
    second_half = features[..., half_dim:]
    return jnp.concatenate([first_half * cosine - second_half * sine_part, second_half * cosine + first_half * sine_part], axis=-1)

def attend_block(operands, keys_all, values_all, key_positions):
    queries_blk, query_positions = operands
    scores = jnp.einsum('qgjd,kgd->gjqk', queries_blk.astype(jnp.float32), keys_all)
    visible = key_positions[None, :] <= query_positions[:, None]
    peak = lax.optimization_barrier(jnp.max(jnp.where(visible, scores, -jnp.inf), axis=3, keepdims=True))
    exponent = jnp.where(visible, jnp.exp(scores - peak), 0.0)
    denominator = lax.optimization_barrier(jnp.sum(exponent, axis=3))
    weights = lax.optimization_barrier(exponent.astype(jnp.bfloat16)).astype(jnp.float32)
    summed = jnp.einsum('gjqk,kgd->qgjd', weights, values_all)
    return (summed / jnp.transpose(denominator, (2, 0, 1))[..., None]).astype(jnp.bfloat16)

def reference(hidden_in, pre_gain, post_gain, w_query, w_key, w_value, w_out, block_of):
    row_index = jnp.arange(SEQ, dtype=jnp.int32)
    positions = block_of[row_index // BLOCK_ROWS] * BLOCK_ROWS + row_index % BLOCK_ROWS
    normed = normalize(hidden_in, pre_gain).astype(jnp.bfloat16)
    queries = jnp.dot(normed, w_query, preferred_element_type=jnp.float32).reshape(SEQ, HEADS, HD)
    queries = (rotate_pairs(queries, positions) * ATT_SCALAR ** (-0.5)).astype(jnp.bfloat16)
    keys_all = jnp.dot(normed, w_key, preferred_element_type=jnp.float32).reshape(SEQ, KV_HEADS, HD)
    keys_all = rotate_pairs(keys_all, positions).astype(jnp.bfloat16).astype(jnp.float32)
    values_all = jnp.dot(normed, w_value, preferred_element_type=jnp.float32).astype(jnp.bfloat16)
    values_all = values_all.astype(jnp.float32).reshape(SEQ, KV_HEADS, HD)
    queries_blocks = queries.reshape(BLOCKS, BLOCK_ROWS, KV_HEADS, 2, HD)
    position_blocks = positions.reshape(BLOCKS, BLOCK_ROWS)
    attended = lax.map(lambda operands: attend_block(operands, keys_all, values_all, positions), (queries_blocks, position_blocks))
    attended = attended.reshape(SEQ, HEADS * HD)
    group_cols = HEADS * HD // N_TP
    projected = jnp.zeros((SEQ, D), jnp.float32)
    for group in range(N_TP):
        partial_sum = jnp.dot(attended[:, group * group_cols:(group + 1) * group_cols], w_out[group * group_cols:(group + 1) * group_cols], preferred_element_type=jnp.float32)
        projected = projected + lax.optimization_barrier(partial_sum.astype(jnp.bfloat16)).astype(jnp.float32)
    return (hidden_in.astype(jnp.float32) + normalize(projected, post_gain)).astype(jnp.bfloat16)
```

```python
import functools
import math

import jax
import jax.numpy as jnp
from jax import lax
from jax.experimental import pallas as pl
from jax.experimental.pallas import tpu as pltpu
from jax.sharding import PartitionSpec as P

HD = 128
ATT_SCALAR = 144
EPS = 1e-6
VMEM = 56 * 1024 * 1024
B_CHUNKS = 2


def params(**more):
    return pltpu.CompilerParams(vmem_limit_bytes=VMEM, **more)


def qkv_kernel(parts, heads, *refs):
    x_refs = refs[:parts]
    gain, wq, wk, wv, cosine, sine, q_out, kv_out, acc, squares = refs[parts:]
    step, steps = pl.program_id(0), pl.num_programs(0)
    rows = x_refs[0].shape[0]
    width = x_refs[0].shape[1]

    @pl.when(step == 0)
    def _():
        acc[...] = jnp.zeros_like(acc)
        squares[...] = jnp.zeros_like(squares)

    weights = jnp.concatenate([wq[...], wk[...], wv[...]], axis=1)
    for part, x_ref in enumerate(x_refs):
        span = pl.ds(part * rows, rows)
        x = x_ref[...].astype(jnp.float32)
        square = x * x
        folded = square[:, :128]
        for lane in range(128, width, 128):
            folded = folded + square[:, lane : lane + 128]
        squares[span, :] += folded
        scaled = (x * gain[...]).astype(jnp.bfloat16)
        acc[span, :] += jnp.dot(scaled, weights, preferred_element_type=jnp.float32)

    @pl.when(step == steps - 1)
    def _():
        total = jnp.sum(squares[...], axis=1, keepdims=True)
        scale = lax.rsqrt(total / (width * steps) + EPS)
        cos, sin = cosine[...], sine[...]

        def rotated(at):
            y = acc[:, at * HD : (at + 1) * HD] * scale
            return y * cos + pltpu.roll(y, HD // 2, 1) * sin

        factor = ATT_SCALAR ** (-0.5) * math.log2(math.e)
        for head in range(heads):
            q_out[:, head * HD : (head + 1) * HD] = (rotated(head) * factor).astype(jnp.bfloat16)
        kv_out[:, :HD] = rotated(heads).astype(jnp.bfloat16)
        kv_out[:, HD:] = (acc[:, (heads + 1) * HD :] * scale).astype(jnp.bfloat16)


def qkv(xs, gain, wq, wk, wv, cosine, sine):
    parts, (rows, width) = len(xs), xs[0].shape
    total = parts * rows
    heads = wq.shape[1] // HD
    columns = wq.shape[1] + 2 * HD
    depth = width // 4
    by_depth = lambda n: pl.BlockSpec((depth, n), lambda k: (k, 0))
    whole = lambda n: pl.BlockSpec((total, n), lambda k: (0, 0))
    return pl.pallas_call(
        functools.partial(qkv_kernel, parts, heads),
        grid=(width // depth,),
        in_specs=[pl.BlockSpec((rows, depth), lambda k: (0, k))] * parts
        + [pl.BlockSpec((1, depth), lambda k: (0, k))]
        + [by_depth(wq.shape[1]), by_depth(HD), by_depth(HD), whole(HD), whole(HD)],
        out_specs=[whole(wq.shape[1]), whole(2 * HD)],
        out_shape=[
            jax.ShapeDtypeStruct((total, wq.shape[1]), jnp.bfloat16),
            jax.ShapeDtypeStruct((total, 2 * HD), jnp.bfloat16),
        ],
        scratch_shapes=[
            pltpu.VMEM((total, columns), jnp.float32),
            pltpu.VMEM((total, 128), jnp.float32),
        ],
        compiler_params=params(),
        cost_estimate=pl.CostEstimate(
            flops=2 * total * width * columns,
            bytes_accessed=2 * width * (total + columns),
            transcendentals=0,
        ),
        name="norm_qkv",
    )(*xs, gain.reshape(1, -1), wq, wk, wv, cosine, sine)


def attention_kernel(kv_parts, heads, tile, starts, *refs):
    (q_ref,) = refs[:1]
    kv_refs = refs[1 : 1 + kv_parts]
    out, kv, peak, acc, arrived = refs[1 + kv_parts :]
    q_blocks, rows, _ = q_ref.shape
    slots = kv.shape[0]
    each = slots // kv_parts
    copies = [
        pltpu.make_async_copy(part, kv.at[pl.ds(at * each, each)], arrived.at[at])
        for at, part in enumerate(kv_refs)
    ]
    for copy in copies:
        copy.start()
    for copy in copies:
        copy.wait()
    ones = jnp.ones((rows, HD), jnp.bfloat16)

    def attend(block, slot, diagonal):
        keys = kv[slot, :, :HD]
        values = jnp.concatenate([kv[slot, :, HD:], ones], axis=1)
        for first in range(0, rows, tile):
            for head in range(heads):
                span = pl.ds(first, tile)
                q = q_ref[block, span, head * HD : (head + 1) * HD]
                scores = lax.dot_general(
                    q, keys, (((1,), (1,)), ((), ())), preferred_element_type=jnp.float32
                )
                if diagonal:
                    row = first + lax.broadcasted_iota(jnp.int32, scores.shape, 0)
                    column = lax.broadcasted_iota(jnp.int32, scores.shape, 1)
                    scores = jnp.where(column <= row, scores, -1e30)
                top = jnp.broadcast_to(jnp.max(scores, axis=1, keepdims=True), (tile, HD))
                if not diagonal:
                    before = peak[block, head, span, :]
                    top = jnp.maximum(before, top)
                wide = jnp.concatenate([top] * (rows // HD), axis=1)
                weights = jnp.exp2(scores - wide).astype(jnp.bfloat16)
                summed = jnp.dot(weights, values, preferred_element_type=jnp.float32)
                if not diagonal:
                    fade = jnp.exp2(before - top)
                    fade = jnp.concatenate([fade, fade], axis=1)
                    summed = summed + acc[block, head, span, :] * fade
                acc[block, head, span, :] = summed
                peak[block, head, span, :] = top

    def per_block(block, carry):
        q_start = starts[block]

        def same(slot, carry):
            @pl.when(starts[q_blocks + slot] == q_start)
            def _():
                attend(block, slot, True)

            return carry

        def earlier(slot, carry):
            @pl.when(starts[q_blocks + slot] < q_start)
            def _():
                attend(block, slot, False)

            return carry

        lax.fori_loop(0, slots, same, 0)
        lax.fori_loop(0, slots, earlier, 0)
        for head in range(heads):
            result = acc[block, head]
            out[block, :, head * HD : (head + 1) * HD] = (
                result[:, :HD] / result[:, HD:]
            ).astype(jnp.bfloat16)
        return carry

    lax.fori_loop(0, q_blocks, per_block, 0)


def attention(q, kv_parts, q_starts, kv_starts):
    blocks, rows, columns = q.shape
    heads = columns // HD
    slots = sum(part.shape[0] for part in kv_parts)
    return pl.pallas_call(
        functools.partial(attention_kernel, len(kv_parts), heads, 128),
        in_specs=[pl.BlockSpec(memory_space=pltpu.SMEM), pl.BlockSpec(memory_space=pltpu.VMEM)]
        + [pl.BlockSpec(memory_space=pl.ANY)] * len(kv_parts),
        out_specs=pl.BlockSpec(memory_space=pltpu.VMEM),
        out_shape=jax.ShapeDtypeStruct(q.shape, jnp.bfloat16),
        scratch_shapes=[
            pltpu.VMEM((slots, rows, 2 * HD), jnp.bfloat16),
            pltpu.VMEM((blocks, heads, rows, HD), jnp.float32),
            pltpu.VMEM((blocks, heads, rows, 2 * HD), jnp.float32),
            pltpu.SemaphoreType.DMA((len(kv_parts),)),
        ],
        compiler_params=params(),
        cost_estimate=pl.CostEstimate(
            flops=4 * q.size * slots * rows,
            bytes_accessed=4 * q.size + 4 * slots * rows * HD,
            transcendentals=blocks * heads * slots * rows * rows,
        ),
        name="attention",
    )(jnp.concatenate([q_starts, kv_starts]), q, *kv_parts)


def output_kernel(places, chunks, at, *refs):
    attended = refs[:4]
    pieces = refs[4 : 4 + len(places)]
    hidden, gain, out, weights, projected, arrived = refs[4 + len(places) :]
    width = hidden.shape[1]
    step = width // chunks

    def copies(chunk):
        lanes = pl.ds(chunk * step, step)
        return [
            pltpu.make_async_copy(
                piece.at[:, lanes],
                weights.at[pl.ds(pl.multiple_of(at[index], 16), places[index]), lanes],
                arrived.at[chunk, index],
            )
            for index, piece in enumerate(pieces)
        ]

    for chunk in range(chunks):
        for copy in copies(chunk):
            copy.start()
    left = jnp.concatenate([part[...] for part in attended], axis=1)
    square = jnp.zeros((hidden.shape[0], 128), jnp.float32)
    for chunk in range(chunks):
        for copy in copies(chunk):
            copy.wait()
        lanes = pl.ds(chunk * step, step)
        part = jnp.dot(left, weights[:, lanes], preferred_element_type=jnp.float32)
        projected[:, lanes] = part
        for lane in range(0, step, 128):
            piece = part[:, lane : lane + 128]
            square = square + piece * piece
    mean = jnp.sum(square, axis=1, keepdims=True) / width
    scale = lax.rsqrt(mean + EPS)
    for chunk in range(chunks):
        lanes = pl.ds(chunk * step, step)
        normed = projected[:, lanes] * scale * gain[:, lanes]
        out[:, lanes] = (hidden[:, lanes].astype(jnp.float32) + normed).astype(jnp.bfloat16)


def output(attended, pieces, places, hidden, gain):
    rows, width = hidden.shape
    depth = sum(piece.shape[0] for piece in pieces)
    chunks = 6
    vmem = pl.BlockSpec(memory_space=pltpu.VMEM)
    return pl.pallas_call(
        functools.partial(output_kernel, [piece.shape[0] for piece in pieces], chunks),
        in_specs=[pl.BlockSpec(memory_space=pltpu.SMEM)]
        + [vmem] * 4
        + [pl.BlockSpec(memory_space=pl.ANY)] * len(pieces)
        + [vmem, vmem],
        out_specs=vmem,
        out_shape=jax.ShapeDtypeStruct(hidden.shape, jnp.bfloat16),
        scratch_shapes=[
            pltpu.VMEM((depth, width), jnp.bfloat16),
            pltpu.VMEM((rows, width), jnp.float32),
            pltpu.SemaphoreType.DMA((chunks, len(pieces))),
        ],
        compiler_params=params(),
        cost_estimate=pl.CostEstimate(
            flops=2 * rows * width * depth,
            bytes_accessed=2 * width * (depth + 2 * rows),
            transcendentals=0,
        ),
        name="output_norm",
    )(places, *attended, *pieces, hidden, gain.reshape(1, -1))


def rotary_tables(positions):
    half = HD // 2
    frequency = jnp.power(
        jnp.float32(10000.0), -jnp.arange(half, dtype=jnp.float32) * (2.0 / HD)
    )
    angles = positions.astype(jnp.float32)[:, None] * frequency[None, :]
    cos, sin = jnp.cos(angles), jnp.sin(angles)
    return jnp.concatenate([cos, cos], axis=1), jnp.concatenate([-sin, sin], axis=1)


def lookup(block_of, index):
    ids = jnp.arange(block_of.shape[0], dtype=jnp.int32)
    return jnp.sum(jnp.where(index[..., None] == ids, block_of, 0), axis=-1)


def flipped(array, axis, bit):
    size = lax.axis_size(axis)
    return lax.ppermute(array, axis, [(i, i ^ bit) for i in range(size)])


def shifted(array, axis, by):
    size = lax.axis_size(axis)
    return lax.ppermute(array, axis, [(i, (i + by) % size) for i in range(size)])


def after(array, *others):
    return lax.optimization_barrier((array, *others))[0]


def two_chips(hidden, pre_gain, post_gain, wq, wk, wv, w_out, block_of):
    rows = hidden.shape[0]
    block_rows = 2 * rows
    seq_count, group_count = lax.axis_size("seq"), lax.axis_size("groups")
    seq, tp, group = lax.axis_index("seq"), lax.axis_index("tp"), lax.axis_index("groups")
    chip = tp // 2
    core = tp % 2

    def in_order(mine, other):
        return jnp.where(core == 0, mine, other), jnp.where(core == 0, other, mine)

    lines = (seq - jnp.arange(seq_count, dtype=jnp.int32)) % seq_count
    near_starts = lookup(block_of, 2 * lines + chip) * block_rows
    far_starts = lookup(block_of, 2 * lines + 1 - chip) * block_rows
    offsets = jnp.arange(block_rows, dtype=jnp.int32)
    positions = jnp.concatenate([near_starts[0] + offsets, far_starts[0] + offsets])
    cosine, sine = rotary_tables(positions)

    size = rows // B_CHUNKS
    far = []
    for at in range(B_CHUNKS):
        far.append(flipped(hidden[at * size : (at + 1) * size], "tp", 2))
    partner = flipped(hidden, "tp", 1)

    def project(mine, other, which):
        xs = in_order(mine, other)
        return qkv(xs, pre_gain, wq, wk, wv, cosine[which], sine[which])

    q_near, kv_near = project(hidden, partner, slice(0, block_rows))
    near_parts = [kv_near] + [shifted(kv_near, "seq", by) for by in range(1, seq_count)]

    half = w_out.shape[0] // group_count
    sent = lax.dynamic_slice_in_dim(w_out, group * half, half, axis=0)
    sent = after(sent, *far)
    w_far = [flipped(sent, "tp", 2)]
    w_far += [shifted(w_far[0], "groups", by) for by in range(1, group_count)]
    w_partner = flipped(w_out, "tp", 1)
    w_cross = [flipped(piece, "tp", 1) for piece in w_far]

    far_mine = jnp.concatenate(far, axis=0)
    far_other = jnp.concatenate([flipped(piece, "tp", 1) for piece in far], axis=0)
    q_far, kv_far = project(far_mine, far_other, slice(block_rows, 2 * block_rows))
    far_parts = [kv_far] + [shifted(kv_far, "seq", by) for by in range(1, seq_count)]

    attended = attention(
        jnp.stack([q_near, q_far]),
        [part[None] for part in near_parts + far_parts],
        jnp.stack([near_starts[0], far_starts[0]]),
        jnp.concatenate([near_starts, far_starts]),
    )
    near = attended[0].reshape(2, rows, -1)
    away = attended[1].reshape(2, rows, -1)
    pick = lambda pair, which: jnp.where(which == 0, pair[0], pair[1])
    gathered = [
        pick(near, core),
        flipped(pick(near, 1 - core), "tp", 1),
        flipped(pick(away, core), "tp", 2),
        flipped(pick(away, 1 - core), "tp", 3),
    ]
    depth = w_out.shape[0]
    order = [(group - by) % group_count * half for by in range(group_count)]
    places = [0, depth] + [2 * depth + at for at in order] + [3 * depth + at for at in order]
    places = jnp.stack([jnp.asarray(at, jnp.int32) for at in places])
    return output(gathered, [w_out, w_partner] + w_far + w_cross, places, hidden, post_gain)


def any_count(hidden, pre_gain, post_gain, wq, wk, wv, w_out, block_of):
    normed_rows = lax.all_gather(hidden, "tp", axis=0, tiled=True)
    seq_rows = normed_rows.shape[0]
    block_rows = seq_rows // 2
    own = 2 * lax.axis_index("seq") + jnp.arange(2, dtype=jnp.int32)
    q_starts = lookup(block_of, own) * block_rows
    offsets = jnp.arange(block_rows, dtype=jnp.int32)
    cosine, sine = rotary_tables((q_starts[:, None] + offsets).reshape(-1))
    q, kv = qkv([normed_rows], pre_gain, wq, wk, wv, cosine, sine)
    kv = lax.all_gather(kv, "seq", axis=0, tiled=True).reshape(-1, block_rows, kv.shape[1])
    attended = attention(
        q.reshape(2, block_rows, -1), [kv], q_starts, block_of * block_rows
    ).reshape(seq_rows, -1)
    partial = jnp.dot(attended, w_out, preferred_element_type=jnp.float32)
    summed = lax.psum_scatter(
        partial.astype(jnp.bfloat16), "tp", scatter_dimension=0, tiled=True
    ).astype(jnp.float32)
    mean = jnp.mean(summed * summed, axis=-1, keepdims=True)
    normed = summed * lax.rsqrt(mean + EPS) * post_gain
    return (hidden.astype(jnp.float32) + normed).astype(jnp.bfloat16)


def solution(mesh):
    return jax.shard_map(
        two_chips if mesh.shape["tp"] == 4 else any_count,
        mesh=mesh,
        in_specs=(
            P(("groups", "seq", "tp"), None),
            P(),
            P(),
            P(None, "tp"),
            P(None, "tp"),
            P(None, "tp"),
            P("tp", None),
            P(),
        ),
        out_specs=P(("groups", "seq", "tp"), None),
        check_vma=False,
    )
```

```python
import functools
import math

import jax
import jax.numpy as jnp
from jax import lax
from jax.experimental import pallas as pl
from jax.experimental.pallas import tpu as pltpu
from jax.sharding import PartitionSpec as P

HD = 128
ATT_SCALAR = 144
EPS = 1e-6
MIB = 1024 * 1024
HIDDEN = -1e30

ANY = pl.BlockSpec(memory_space=pl.ANY)
VMEM = pl.BlockSpec(memory_space=pltpu.VMEM)
SMEM = pl.BlockSpec(memory_space=pltpu.SMEM)


def params(mib):
    return pltpu.CompilerParams(vmem_limit_bytes=mib * MIB)


def norm_kernel(hidden, gain, out):
    x = hidden[...].astype(jnp.float32)
    square = x * x
    folded = square[:, :128]
    for lane in range(128, x.shape[1], 128):
        folded = folded + square[:, lane : lane + 128]
    mean = jnp.sum(folded, axis=1, keepdims=True) / x.shape[1]
    out[...] = (x * lax.rsqrt(mean + EPS) * gain[...]).astype(jnp.bfloat16)


def norm(hidden, gain, first, rows):
    width = hidden.shape[1]
    step = math.gcd(math.gcd(first, rows), 64) if first else math.gcd(rows, 64)
    return pl.pallas_call(
        norm_kernel,
        grid=(rows // step,),
        in_specs=[
            pl.BlockSpec((step, width), lambda i: (first // step + i, 0)),
            pl.BlockSpec((1, width), lambda i: (0, 0)),
        ],
        out_specs=pl.BlockSpec((step, width), lambda i: (i, 0)),
        out_shape=jax.ShapeDtypeStruct((rows, width), jnp.bfloat16),
        compiler_params=params(12),
        cost_estimate=pl.CostEstimate(
            flops=6 * rows * width, bytes_accessed=4 * rows * width, transcendentals=0
        ),
        name="norm_rows",
    )(hidden, gain.reshape(1, -1))


def qkv_kernel(parts, heads, *refs):
    parts_refs = refs[:parts]
    weights, cosine, sine, q_out, kv_out, rows, arrived = refs[parts:]
    copies, first = [], 0
    for at, part in enumerate(parts_refs):
        span = pl.ds(first, part.shape[0])
        copies.append(pltpu.make_async_copy(part, rows.at[span], arrived.at[at]))
        first += part.shape[0]
    for copy in copies:
        copy.start()
    for copy in copies:
        copy.wait()
    product = jnp.dot(rows[...], weights[...], preferred_element_type=jnp.float32)
    cos, sin = cosine[...], sine[...]

    def rotated(at):
        y = product[:, at * HD : (at + 1) * HD]
        return y * cos + pltpu.roll(y, HD // 2, 1) * sin

    factor = ATT_SCALAR ** (-0.5) * math.log2(math.e)
    for head in range(heads):
        q_out[head] = (rotated(head) * factor).astype(jnp.bfloat16)
    kv_out[:, :HD] = rotated(heads).astype(jnp.bfloat16)
    kv_out[:, HD:] = product[:, (heads + 1) * HD :].astype(jnp.bfloat16)


def qkv(parts, weights, cosine, sine):
    total = sum(part.shape[0] for part in parts)
    width, columns = weights.shape
    heads = columns // HD - 2
    return pl.pallas_call(
        functools.partial(qkv_kernel, len(parts), heads),
        in_specs=[ANY] * len(parts) + [VMEM] * 3,
        out_specs=[VMEM, VMEM],
        out_shape=[
            jax.ShapeDtypeStruct((heads, total, HD), jnp.bfloat16),
            jax.ShapeDtypeStruct((total, 2 * HD), jnp.bfloat16),
        ],
        scratch_shapes=[
            pltpu.VMEM((total, width), jnp.bfloat16),
            pltpu.SemaphoreType.DMA((len(parts),)),
        ],
        compiler_params=params(24),
        cost_estimate=pl.CostEstimate(
            flops=2 * total * width * columns,
            bytes_accessed=2 * width * (total + columns),
            transcendentals=0,
        ),
        name="qkv",
    )(*parts, weights, cosine, sine)


class Step:
    def __init__(self, q, group, slots, same=None, merged=False):
        self.q, self.group, self.slots = q, group, slots
        self.same, self.merged = same, merged


def attention_kernel(plan, fresh, final, sizes, *refs):
    q_count, group_parts = sizes
    refs = list(refs)
    take = lambda n: [refs.pop(0) for _ in range(n)]
    q_starts, k_starts = take(2)
    q_refs = take(q_count)
    q_places = take(q_count)
    k_places = take(len(group_parts))
    kv_parts = [take(n) for n in group_parts]
    old = {q: take(2) for q in range(q_count) if q not in fresh}
    outs = take(len(final)) if final else None
    new = [take(2) for _ in range(q_count)]
    kvs = take(len(group_parts))
    (arrived,) = refs
    copies, at = [], 0
    for parts, kv in zip(kv_parts, kvs):
        for slot, part in enumerate(parts):
            each = kv.shape[0] // len(parts)
            copies.append(
                pltpu.make_async_copy(part, kv.at[pl.ds(slot * each, each)], arrived.at[at])
            )
            at += 1
    for copy in copies:
        copy.start()
    for q, (peak, acc) in old.items():
        new[q][0][...] = peak[...]
        new[q][1][...] = acc[...]
    for copy in copies:
        copy.wait()
    offsets, total = [], 0
    for parts, kv in zip(kv_parts, kvs):
        offsets.append(total)
        total += kv.shape[0]

    def attend(q, keys_values, begin, visible=None, bias=None):
        q_ref, (peak, acc) = q_refs[q], new[q]
        heads, rows, _ = q_ref.shape
        keys, values = keys_values[:, :HD], keys_values[:, HD:]
        values = jnp.concatenate([values, jnp.ones_like(values)], axis=1)
        count = keys.shape[0]
        tile = min(rows, 128)
        for first in range(0, rows, tile):
            q_tile = q_ref[:, first : first + tile, :].reshape(heads * tile, HD)
            scores = lax.dot_general(
                q_tile, keys, (((1,), (1,)), ((), ())), preferred_element_type=jnp.float32
            )
            if visible is not None:
                seen = visible(first, tile)
                seen = jnp.concatenate([seen] * heads, axis=0)
                scores = jnp.where(seen, scores, HIDDEN)
            if bias is not None:
                scores = scores + bias
            top = jnp.max(scores, axis=1, keepdims=True)
            top = jnp.broadcast_to(top, (heads * tile, HD))
            span = pl.ds(first * heads, heads * tile)
            if not begin:
                before = peak[span, :]
                top = jnp.maximum(before, top)
            wide = jnp.concatenate([top] * (count // HD), axis=1)
            weights = jnp.exp2(scores - wide).astype(jnp.bfloat16)
            summed = jnp.dot(weights, values, preferred_element_type=jnp.float32)
            if not begin:
                fade = jnp.exp2(before - top)
                summed = summed + acc[span, :] * jnp.concatenate([fade, fade], axis=1)
            acc[span, :] = summed
            peak[span, :] = top

    begun = set(range(q_count)) - set(fresh)
    for step in plan:
        q, group, kv = step.q, step.group, kvs[step.group]
        base = offsets[group]
        if step.same is not None:
            q_place, k_place = q_places[q], k_places[group]
            visible = lambda first, tile: k_place[...] <= q_place[first : first + tile, :]
            attend(q, kv[step.same], q not in begun, visible=visible)
            begun.add(q)
        start = q_starts[q]
        slots = step.slots
        if not slots:
            continue
        if step.merged:
            count = kv.shape[1]
            shown = [k_starts[base + slot] < start for slot in slots]
            anything = functools.reduce(jnp.logical_or, shown)

            @pl.when(anything)
            def _():
                bias = [
                    jnp.where(see, 0.0, HIDDEN) * jnp.ones((1, count), jnp.float32)
                    for see in shown
                ]
                keys_values = kv[slots[0] : slots[-1] + 1].reshape(len(slots) * count, 2 * HD)
                attend(q, keys_values, False, bias=jnp.concatenate(bias, axis=1))

        else:

            def one(slot, carry):
                @pl.when(k_starts[base + slot] < start)
                def _():
                    attend(q, kv[slot], False)

                return carry

            lax.fori_loop(slots[0], slots[-1] + 1, one, 0)

    if final:
        for out, spans in zip(outs, final):
            put = 0
            for q, first, rows in spans:
                acc = new[q][1]
                heads, q_rows, _ = q_refs[q].shape
                tile = min(q_rows, 128)
                for head in range(heads):
                    for at in range(first, first + rows, min(tile, rows)):
                        size = min(tile, rows)
                        from_row = at // tile * tile * heads + head * tile + at % tile
                        part = acc[from_row : from_row + size, :]
                        out[
                            put + at - first : put + at - first + size,
                            head * HD : (head + 1) * HD,
                        ] = (part[:, :HD] / part[:, HD:]).astype(jnp.bfloat16)
                put += rows


def attention(plan, qs, q_starts, q_places, groups, k_starts, k_places, state, final=None):
    fresh = [at for at, held in enumerate(state) if held is None]
    held = [array for pair in state if pair is not None for array in pair]
    shapes = []
    for q in qs:
        heads, rows, _ = q.shape
        shapes += [(heads * rows, HD), (heads * rows, 2 * HD)]
    states = [jax.ShapeDtypeStruct(shape, jnp.float32) for shape in shapes]
    if final:
        width = qs[0].shape[0] * HD
        out_shape = [
            jax.ShapeDtypeStruct((sum(rows for _, _, rows in spans), width), jnp.bfloat16)
            for spans in final
        ]
        scratch = [pltpu.VMEM(shape, jnp.float32) for shape in shapes]
    else:
        out_shape, scratch = states, []
    buffers = [
        pltpu.VMEM((sum(p.shape[0] for p in parts),) + parts[0].shape[1:], jnp.bfloat16)
        for parts in groups
    ]
    parts = [part for parts in groups for part in parts]
    work = 0
    for step in plan:
        slots = len(step.slots) + (step.same is not None)
        work += qs[step.q].size // HD * groups[step.group][0].shape[1] * slots
    sizes = (len(qs), [len(parts) for parts in groups])
    results = pl.pallas_call(
        functools.partial(attention_kernel, plan, fresh, final, sizes),
        in_specs=[SMEM] * 2
        + [VMEM] * (2 * len(qs) + len(groups))
        + [ANY] * len(parts)
        + [VMEM] * len(held),
        out_specs=[VMEM] * len(out_shape),
        out_shape=out_shape,
        scratch_shapes=scratch + buffers + [pltpu.SemaphoreType.DMA((len(parts),))],
        compiler_params=params(20),
        cost_estimate=pl.CostEstimate(
            flops=4 * work * HD, bytes_accessed=2 * work // HD, transcendentals=work
        ),
        name="attention",
    )(q_starts, k_starts, *qs, *q_places, *k_places, *parts, *held)
    if final:
        return results
    return [tuple(results[2 * at : 2 * at + 2]) for at in range(len(qs))]


def output_kernel(pieces, chunks, at, *refs):
    attended = refs[:4]
    weights = refs[4 : 4 + len(pieces)]
    hidden, gain, out, projected = refs[4 + len(pieces) :]
    width = hidden.shape[1]
    step = width // chunks
    lefts = []
    for index, (part, piece) in enumerate(zip(pieces, weights)):
        depth = piece.shape[0]
        if depth == attended[part].shape[1]:
            lefts.append(attended[part][...])
        else:
            lefts.append(attended[part][:, pl.ds(pl.multiple_of(at[index], HD), depth)])
    square = jnp.zeros((hidden.shape[0], 128), jnp.float32)
    for chunk in range(chunks):
        lanes = slice(chunk * step, chunk * step + step)
        total = jnp.dot(lefts[0], weights[0][:, lanes], preferred_element_type=jnp.float32)
        for left, piece in zip(lefts[1:], weights[1:]):
            total = total + jnp.dot(left, piece[:, lanes], preferred_element_type=jnp.float32)
        projected[:, lanes] = total
        for lane in range(0, step, 128):
            piece = total[:, lane : lane + 128]
            square = square + piece * piece
    mean = jnp.sum(square, axis=1, keepdims=True) / width
    scale = lax.rsqrt(mean + EPS)
    for chunk in range(chunks):
        lanes = slice(chunk * step, chunk * step + step)
        normed = projected[:, lanes] * scale * gain[:, lanes]
        out[:, lanes] = (hidden[:, lanes].astype(jnp.float32) + normed).astype(jnp.bfloat16)


def output(attended, pieces, weights, places, hidden, gain):
    rows, width = hidden.shape
    depth = sum(piece.shape[0] for piece in weights)
    return pl.pallas_call(
        functools.partial(output_kernel, pieces, 6),
        in_specs=[SMEM] + [VMEM] * (4 + len(weights) + 2),
        out_specs=VMEM,
        out_shape=jax.ShapeDtypeStruct(hidden.shape, jnp.bfloat16),
        scratch_shapes=[pltpu.VMEM((rows, width), jnp.float32)],
        compiler_params=params(26),
        cost_estimate=pl.CostEstimate(
            flops=2 * rows * width * depth,
            bytes_accessed=2 * width * (depth + 2 * rows),
            transcendentals=0,
        ),
        name="output_norm",
    )(places, *attended, *weights, hidden, gain.reshape(1, -1))


def rotary_tables(positions):
    half = HD // 2
    frequency = jnp.power(
        jnp.float32(10000.0), -jnp.arange(half, dtype=jnp.float32) * (2.0 / HD)
    )
    angles = positions.astype(jnp.float32)[:, None] * frequency[None, :]
    cos, sin = jnp.cos(angles), jnp.sin(angles)
    return jnp.concatenate([cos, cos], axis=1), jnp.concatenate([-sin, sin], axis=1)


def lookup(block_of, index):
    ids = jnp.arange(block_of.shape[0], dtype=jnp.int32)
    return jnp.sum(jnp.where(index[..., None] == ids, block_of, 0), axis=-1)


def flipped(array, axis, bit):
    size = lax.axis_size(axis)
    return lax.ppermute(array, axis, [(i, i ^ bit) for i in range(size)])


def shifted(array, axis, by):
    size = lax.axis_size(axis)
    return lax.ppermute(array, axis, [(i, (i + by) % size) for i in range(size)])


def after(array, *others):
    return lax.optimization_barrier((array, *others))[0]


def two_chips(hidden, pre_gain, post_gain, wq, wk, wv, w_out, block_of):
    rows = hidden.shape[0]
    block_rows = 2 * rows
    cuts = [rows * 2 // 3, rows - rows * 2 // 3]
    lines, group_count = lax.axis_size("seq"), lax.axis_size("groups")
    seq, tp, group = lax.axis_index("seq"), lax.axis_index("tp"), lax.axis_index("groups")
    chip, core = tp // 2, tp % 2

    line = (seq - jnp.arange(lines, dtype=jnp.int32)) % lines
    near_starts = lookup(block_of, 2 * line + chip) * block_rows
    far_starts = lookup(block_of, 2 * line + 1 - chip) * block_rows
    place = []
    for first, size in zip((0, cuts[0]), cuts):
        run = first + jnp.arange(size, dtype=jnp.int32)
        place += [core * rows + run, (1 - core) * rows + run]
    place = jnp.concatenate(place)
    cosine, sine = rotary_tables(
        jnp.concatenate([near_starts[0] + place, far_starts[0] + place])
    )
    first, last = 2 * cuts[0], block_rows

    own = [norm(hidden, pre_gain, 0, cuts[0]), norm(hidden, pre_gain, cuts[0], cuts[1])]
    away = [flipped(chunk, "tp", 2) for chunk in own]
    partner = [flipped(chunk, "tp", 1) for chunk in own]
    weights = jnp.concatenate([wq, wk, wv], axis=1)

    q_near, kv_near = qkv(
        [own[0], partner[0], own[1], partner[1]],
        weights,
        cosine[:block_rows],
        sine[:block_rows],
    )
    near = [kv_near] + [shifted(kv_near, "seq", by) for by in range(1, lines)]
    near = [part[None] for part in near]
    column, row = place[:, None], place[None, :]
    head, tail = slice(0, first), slice(first, last)
    others = list(range(1, lines))
    (near_state,) = attention(
        [Step(0, 0, others, same=0)],
        [q_near],
        near_starts[:1],
        [column],
        [near],
        near_starts,
        [row],
        [None],
    )

    def project(chunk, span):
        other = flipped(chunk, "tp", 1)
        at = slice(block_rows + span.start, block_rows + span.stop)
        return qkv([chunk, other], weights, cosine[at], sine[at])

    away[0] = after(away[0], *near_state)
    q_head, kv_head = project(away[0], head)
    far_head = [kv_head] + [shifted(kv_head, "seq", by) for by in range(1, lines)]
    far_head = [part[None] for part in far_head]

    half = w_out.shape[0] // group_count
    sent = lax.dynamic_slice_in_dim(w_out, group * half, half, axis=0)
    sent = after(sent, kv_head)
    w_far = [flipped(sent, "tp", 2)]
    w_far += [shifted(w_far[0], "groups", by) for by in range(1, group_count)]
    w_partner = flipped(after(w_out, kv_near), "tp", 1)
    w_cross = [flipped(piece, "tp", 1) for piece in w_far]

    away[1] = after(away[1], kv_head)
    q_tail, kv_tail = project(away[1], tail)
    far_tail = [kv_tail] + [shifted(kv_tail, "seq", by) for by in range(1, lines)]
    far_tail = [part[None] for part in far_tail]

    q_starts = jnp.stack([near_starts[0], far_starts[0], far_starts[0]])
    qs = [q_near, q_head, q_tail]
    q_places = [column, column[head], column[tail]]
    everyone = list(range(lines))
    state = attention(
        [
            Step(1, 1, others, same=0),
            Step(2, 2, [], same=0),
            Step(0, 1, everyone),
            Step(1, 0, everyone),
            Step(2, 0, everyone),
            Step(2, 1, others, same=0),
        ],
        qs,
        q_starts,
        q_places,
        [near, far_head, far_tail[:1]],
        jnp.concatenate([near_starts, far_starts, far_starts[:1]]),
        [row, row[:, head], row[:, tail]],
        [near_state, None, None],
    )
    to = lambda half: [(0, half * cuts[0], cuts[0]), (0, first + half * cuts[1], cuts[1])]
    over = lambda half: [(1, half * cuts[0], cuts[0]), (2, half * cuts[1], cuts[1])]
    mine, partners, same, cross = attention(
        [
            Step(1, 0, others, same=0, merged=True),
            Step(2, 0, others, merged=True),
            Step(0, 0, everyone, merged=True),
        ],
        qs,
        q_starts,
        q_places,
        [far_tail],
        far_starts,
        [row[:, tail]],
        state,
        final=[to(0), to(1), over(0), over(1)],
    )
    gathered = [
        mine,
        flipped(partners, "tp", 1),
        flipped(same, "tp", 2),
        flipped(cross, "tp", 3),
    ]
    order = [(group - by) % group_count * half for by in range(group_count)]
    places = jnp.stack([jnp.asarray(at, jnp.int32) for at in [0, 0] + order + order])
    pieces = [0, 1] + [2] * group_count + [3] * group_count
    return output(
        gathered, pieces, [w_out, w_partner] + w_far + w_cross, places, hidden, post_gain
    )


def any_count(hidden, pre_gain, post_gain, wq, wk, wv, w_out, block_of):
    normed = norm(hidden, pre_gain, 0, hidden.shape[0])
    normed = lax.all_gather(normed, "tp", axis=0, tiled=True)
    seq_rows = normed.shape[0]
    block_rows = seq_rows // 2
    lines = lax.axis_size("seq")
    place = jnp.arange(block_rows, dtype=jnp.int32)
    line = (lax.axis_index("seq") - jnp.arange(lines, dtype=jnp.int32)) % lines
    block = (2 * line[:, None] + jnp.arange(2, dtype=jnp.int32)).reshape(-1)
    starts = lookup(block_of, block) * block_rows
    cosine, sine = rotary_tables((starts[:2, None] + place).reshape(-1))
    weights = jnp.concatenate([wq, wk, wv], axis=1)
    qs, keys_values = [], []
    for at in range(2):
        span = slice(at * block_rows, (at + 1) * block_rows)
        q, kv = qkv([normed[span]], weights, cosine[span], sine[span])
        qs.append(q)
        keys_values.append(kv)
    kv = lax.all_gather(jnp.stack(keys_values), "seq")[line].reshape(-1, block_rows, 2 * HD)
    rest = list(range(2, 2 * lines))
    attended = attention(
        [
            Step(0, 0, [1], same=0),
            Step(1, 0, [0], same=1),
            Step(0, 0, rest),
            Step(1, 0, rest),
        ],
        qs,
        starts[:2],
        [place[:, None]] * 2,
        [[kv]],
        starts,
        [place[None, :]],
        [None, None],
        final=[[(0, 0, block_rows), (1, 0, block_rows)]],
    )[0]
    partial = jnp.dot(attended, w_out, preferred_element_type=jnp.float32)
    summed = lax.psum_scatter(
        partial.astype(jnp.bfloat16), "tp", scatter_dimension=0, tiled=True
    ).astype(jnp.float32)
    mean = jnp.mean(summed * summed, axis=-1, keepdims=True)
    projected = summed * lax.rsqrt(mean + EPS) * post_gain
    return (hidden.astype(jnp.float32) + projected).astype(jnp.bfloat16)


def solution(mesh):
    return jax.shard_map(
        two_chips if mesh.shape["tp"] == 4 else any_count,
        mesh=mesh,
        in_specs=(
            P(("groups", "seq", "tp"), None),
            P(),
            P(),
            P(None, "tp"),
            P(None, "tp"),
            P(None, "tp"),
            P("tp", None),
            P(),
        ),
        out_specs=P(("groups", "seq", "tp"), None),
        check_vma=False,
    )
```

```python
import functools
import math

import jax
import jax.numpy as jnp
from jax import lax
from jax.experimental import pallas as pl
from jax.experimental.pallas import tpu as pltpu
from jax.sharding import PartitionSpec as P

HD = 128
ATT_SCALAR = 144
EPS = 1e-6
MIB = 1024 * 1024
HIDDEN = -1e30
NEVER = 1 << 30
COST = pl.CostEstimate(flops=1, bytes_accessed=1, transcendentals=0)

ANY = pl.BlockSpec(memory_space=pl.ANY)
VMEM = pl.BlockSpec(memory_space=pltpu.VMEM)
SMEM = pl.BlockSpec(memory_space=pltpu.SMEM)


def params(mib):
    return pltpu.CompilerParams(vmem_limit_bytes=mib * MIB)


def norm_kernel(hidden, gain, out):
    x = hidden[...].astype(jnp.float32)
    square = x * x
    folded = square[:, :128]
    for lane in range(128, x.shape[1], 128):
        folded = folded + square[:, lane : lane + 128]
    mean = jnp.sum(folded, axis=1, keepdims=True) / x.shape[1]
    out[...] = (x * lax.rsqrt(mean + EPS) * gain[...]).astype(jnp.bfloat16)


def norm(hidden, gain, first, rows):
    width = hidden.shape[1]
    step = math.gcd(math.gcd(first, rows), 64) if first else math.gcd(rows, 64)
    return pl.pallas_call(
        norm_kernel,
        grid=(rows // step,),
        in_specs=[
            pl.BlockSpec((step, width), lambda i: (first // step + i, 0)),
            pl.BlockSpec((1, width), lambda i: (0, 0)),
        ],
        out_specs=pl.BlockSpec((step, width), lambda i: (i, 0)),
        out_shape=jax.ShapeDtypeStruct((rows, width), jnp.bfloat16),
        compiler_params=params(12),
        cost_estimate=COST,
        name="norm_rows",
    )(hidden, gain.reshape(1, -1))


def qkv_kernel(parts, heads, *refs):
    parts_refs = refs[:parts]
    w_query, w_kv, cosine, sine, q_out, kv_out, rows, arrived = refs[parts:]
    copies, first = [], 0
    for at, part in enumerate(parts_refs):
        span = pl.ds(first, part.shape[0])
        copies.append(pltpu.make_async_copy(part, rows.at[span], arrived.at[at]))
        first += part.shape[0]
    for copy in copies:
        copy.start()
    for copy in copies:
        copy.wait()
    cos, sin = cosine[...], sine[...]
    product = jnp.dot(rows[...], w_kv[...], preferred_element_type=jnp.float32)

    def rotated(at):
        y = product[:, at * HD : (at + 1) * HD]
        return y * cos + pltpu.roll(y, HD // 2, 1) * sin

    factor = ATT_SCALAR ** (-0.5) * math.log2(math.e)
    kv_out[:, :HD] = rotated(0).astype(jnp.bfloat16)
    kv_out[:, HD:] = product[:, HD:].astype(jnp.bfloat16)
    product = jnp.dot(rows[...], w_query[...], preferred_element_type=jnp.float32)
    for head in range(heads):
        q_out[head] = (rotated(head) * factor).astype(jnp.bfloat16)


def qkv(parts, w_query, w_kv, cosine, sine):
    total = sum(part.shape[0] for part in parts)
    width, columns = w_query.shape
    heads = columns // HD
    return pl.pallas_call(
        functools.partial(qkv_kernel, len(parts), heads),
        in_specs=[ANY] * len(parts) + [VMEM] * 4,
        out_specs=[VMEM, VMEM],
        out_shape=[
            jax.ShapeDtypeStruct((heads, total, HD), jnp.bfloat16),
            jax.ShapeDtypeStruct((total, 2 * HD), jnp.bfloat16),
        ],
        scratch_shapes=[
            pltpu.VMEM((total, width), jnp.bfloat16),
            pltpu.SemaphoreType.DMA((len(parts),)),
        ],
        compiler_params=params(24),
        cost_estimate=COST,
        name="qkv",
    )(*parts, w_query, w_kv, cosine, sine)


class Step:
    def __init__(self, q, group, slots, same=None, merged=False):
        self.q, self.group, self.slots = q, group, slots
        self.same, self.merged = same, merged


def attention_kernel(plan, fresh, final, sizes, *refs):
    q_count, group_parts = sizes
    refs = list(refs)
    take = lambda n: [refs.pop(0) for _ in range(n)]
    q_starts, k_starts = take(2)
    q_refs = take(q_count)
    q_places = take(q_count)
    k_places = take(len(group_parts))
    kv_parts = [take(n) for n in group_parts]
    old = {q: take(2) for q in range(q_count) if q not in fresh}
    outs = take(len(final)) if final else None
    new = [take(2) for _ in range(q_count)]
    kvs = take(len(group_parts))
    (arrived,) = refs
    copies, at = [], 0
    for parts, kv in zip(kv_parts, kvs):
        for slot, part in enumerate(parts):
            each = kv.shape[0] // len(parts)
            copies.append(
                pltpu.make_async_copy(part, kv.at[pl.ds(slot * each, each)], arrived.at[at])
            )
            at += 1
    for copy in copies:
        copy.start()
    for q, (peak, acc) in old.items():
        new[q][0][...] = peak[...]
        new[q][1][...] = acc[...]
    for copy in copies:
        copy.wait()
    offsets, total = [], 0
    for parts, kv in zip(kv_parts, kvs):
        offsets.append(total)
        total += kv.shape[0]

    def attend(q, keys_values, begin, visible=None, bias=None):
        q_ref, (peak, acc) = q_refs[q], new[q]
        heads, rows, _ = q_ref.shape
        keys, values = keys_values[:, :HD], keys_values[:, HD:]
        values = jnp.concatenate([values, jnp.ones_like(values)], axis=1)
        count = keys.shape[0]
        tile = min(rows, 128)
        for first in range(0, rows, tile):
            q_tile = q_ref[:, first : first + tile, :].reshape(heads * tile, HD)
            scores = lax.dot_general(
                q_tile, keys, (((1,), (1,)), ((), ())), preferred_element_type=jnp.float32
            )
            if visible is not None:
                seen = visible(first, tile)
                seen = jnp.concatenate([seen] * heads, axis=0)
                scores = jnp.where(seen, scores, HIDDEN)
            if bias is not None:
                scores = scores + bias
            top = jnp.max(scores, axis=1, keepdims=True)
            top = jnp.broadcast_to(top, (heads * tile, HD))
            span = pl.ds(first * heads, heads * tile)
            if not begin:
                before = peak[span, :]
                top = jnp.maximum(before, top)
            wide = jnp.concatenate([top] * (count // HD), axis=1)
            weights = jnp.exp2(scores - wide).astype(jnp.bfloat16)
            summed = jnp.dot(weights, values, preferred_element_type=jnp.float32)
            if not begin:
                fade = jnp.exp2(before - top)
                summed = summed + acc[span, :] * jnp.concatenate([fade, fade], axis=1)
            acc[span, :] = summed
            peak[span, :] = top

    begun = set(range(q_count)) - set(fresh)
    for step in plan:
        q, group, kv = step.q, step.group, kvs[step.group]
        base = offsets[group]
        if step.same is not None:
            q_place, k_place = q_places[q], k_places[group]
            visible = lambda first, tile: k_place[...] <= q_place[first : first + tile, :]
            attend(q, kv[step.same], q not in begun, visible=visible)
            begun.add(q)
        start = q_starts[q]
        slots = step.slots
        if not slots:
            continue
        if step.merged:
            count = kv.shape[1]
            shown = [k_starts[base + slot] < start for slot in slots]
            anything = functools.reduce(jnp.logical_or, shown)

            @pl.when(anything)
            def _():
                bias = [
                    jnp.where(see, 0.0, HIDDEN) * jnp.ones((1, count), jnp.float32)
                    for see in shown
                ]
                keys_values = kv[slots[0] : slots[-1] + 1].reshape(len(slots) * count, 2 * HD)
                attend(q, keys_values, False, bias=jnp.concatenate(bias, axis=1))

        else:

            def one(slot, carry):
                @pl.when(k_starts[base + slot] < start)
                def _():
                    attend(q, kv[slot], False)

                return carry

            lax.fori_loop(slots[0], slots[-1] + 1, one, 0)

    if final:
        for out, spans in zip(outs, final):
            put = 0
            for q, first, rows in spans:
                acc = new[q][1]
                heads, q_rows, _ = q_refs[q].shape
                tile = min(q_rows, 128)
                for head in range(heads):
                    for at in range(first, first + rows, min(tile, rows)):
                        size = min(tile, rows)
                        from_row = at // tile * tile * heads + head * tile + at % tile
                        part = acc[from_row : from_row + size, :]
                        out[
                            put + at - first : put + at - first + size,
                            head * HD : (head + 1) * HD,
                        ] = (part[:, :HD] / part[:, HD:]).astype(jnp.bfloat16)
                put += rows


def attention(plan, qs, q_starts, q_places, groups, k_starts, k_places, state, final=None):
    fresh = [at for at, held in enumerate(state) if held is None]
    held = [array for pair in state if pair is not None for array in pair]
    shapes = []
    for q in qs:
        heads, rows, _ = q.shape
        shapes += [(heads * rows, HD), (heads * rows, 2 * HD)]
    states = [jax.ShapeDtypeStruct(shape, jnp.float32) for shape in shapes]
    if final:
        width = qs[0].shape[0] * HD
        out_shape = [
            jax.ShapeDtypeStruct((sum(rows for _, _, rows in spans), width), jnp.bfloat16)
            for spans in final
        ]
        scratch = [pltpu.VMEM(shape, jnp.float32) for shape in shapes]
    else:
        out_shape, scratch = states, []
    buffers = [
        pltpu.VMEM((sum(p.shape[0] for p in parts),) + parts[0].shape[1:], jnp.bfloat16)
        for parts in groups
    ]
    parts = [part for parts in groups for part in parts]
    sizes = (len(qs), [len(parts) for parts in groups])
    results = pl.pallas_call(
        functools.partial(attention_kernel, plan, fresh, final, sizes),
        in_specs=[SMEM] * 2
        + [VMEM] * (2 * len(qs) + len(groups))
        + [ANY] * len(parts)
        + [VMEM] * len(held),
        out_specs=[VMEM] * len(out_shape),
        out_shape=out_shape,
        scratch_shapes=scratch + buffers + [pltpu.SemaphoreType.DMA((len(parts),))],
        compiler_params=params(20),
        cost_estimate=COST,
        name="attention",
    )(q_starts, k_starts, *qs, *q_places, *k_places, *parts, *held)
    if final:
        return results
    return [tuple(results[2 * at : 2 * at + 2]) for at in range(len(qs))]


def near_kernel(chunks, *refs):
    lefts, pieces = refs[:2], refs[2:4]
    out, weights, arrived = refs[4:]
    step = out.shape[1] // chunks
    depth = pieces[0].shape[0]

    def copies(chunk):
        lanes = pl.ds(chunk * step, step)
        return [
            pltpu.make_async_copy(
                piece.at[:, lanes],
                weights.at[pl.ds(at * depth, depth), lanes],
                arrived.at[chunk, at],
            )
            for at, piece in enumerate(pieces)
        ]

    for chunk in range(chunks):
        for copy in copies(chunk):
            copy.start()
    left = jnp.concatenate([part[...] for part in lefts], axis=1)
    for chunk in range(chunks):
        for copy in copies(chunk):
            copy.wait()
        lanes = slice(chunk * step, chunk * step + step)
        out[:, lanes] = jnp.dot(left, weights[:, lanes], preferred_element_type=jnp.float32)


def output_near(lefts, pieces):
    rows, width = lefts[0].shape[0], pieces[0].shape[1]
    depth = sum(piece.shape[0] for piece in pieces)
    chunks = 6
    return pl.pallas_call(
        functools.partial(near_kernel, chunks),
        in_specs=[VMEM] * 2 + [ANY] * 2,
        out_specs=VMEM,
        out_shape=jax.ShapeDtypeStruct((rows, width), jnp.float32),
        scratch_shapes=[
            pltpu.VMEM((depth, width), jnp.bfloat16),
            pltpu.SemaphoreType.DMA((chunks, 2)),
        ],
        compiler_params=params(16),
        cost_estimate=COST,
        name="output_near",
    )(*lefts, *pieces)


def output_kernel(runs, depth, chunks, at, *refs):
    count = len({piece for piece, _, _, _ in runs})
    lefts, pieces = refs[:2], refs[2 : 2 + count]
    near, hidden, gain, out, weights, projected, staged, arrived, left_sem = refs[2 + count :]
    width = hidden.shape[1]
    step = width // chunks

    def copies(chunk):
        lanes = pl.ds(chunk * step, step)
        return [
            pltpu.make_async_copy(
                pieces[piece].at[pl.ds(first, rows), lanes],
                weights.at[pl.ds(pl.multiple_of(head * depth + at[index], 16), rows), lanes],
                arrived.at[chunk, index],
            )
            for index, (piece, first, rows, head) in enumerate(runs)
        ]

    for chunk in range(chunks):
        for copy in copies(chunk):
            copy.start()
    left = jnp.concatenate([part[...] for part in lefts], axis=1)
    square = jnp.zeros((hidden.shape[0], 128), jnp.float32)
    for chunk in range(chunks):
        for copy in copies(chunk):
            copy.wait()
        lanes = slice(chunk * step, chunk * step + step)
        total = near[:, lanes] + jnp.dot(
            left, weights[:, lanes], preferred_element_type=jnp.float32
        )
        projected[:, lanes] = total
        for lane in range(0, step, 128):
            part = total[:, lane : lane + 128]
            square = square + part * part
    mean = jnp.sum(square, axis=1, keepdims=True) / width
    scale = lax.rsqrt(mean + EPS)
    stores = []
    for chunk in range(chunks):
        lanes = slice(chunk * step, chunk * step + step)
        normed = projected[:, lanes] * scale * gain[:, lanes]
        staged[:, lanes] = (hidden[:, lanes].astype(jnp.float32) + normed).astype(jnp.bfloat16)
        lanes = pl.ds(chunk * step, step)
        stores.append(
            pltpu.make_async_copy(staged.at[:, lanes], out.at[:, lanes], left_sem.at[chunk])
        )
        stores[-1].start()
    for store in stores:
        store.wait()


def output(lefts, pieces, runs, places, near, hidden, gain):
    rows, width = hidden.shape
    depth = lefts[0].shape[1]
    chunks = 6
    return pl.pallas_call(
        functools.partial(output_kernel, runs, depth, chunks),
        in_specs=[SMEM] + [VMEM] * 2 + [ANY] * len(pieces) + [VMEM] * 3,
        out_specs=ANY,
        out_shape=jax.ShapeDtypeStruct(hidden.shape, jnp.bfloat16),
        scratch_shapes=[
            pltpu.VMEM((2 * depth, width), jnp.bfloat16),
            pltpu.VMEM((rows, width), jnp.float32),
            pltpu.VMEM((rows, width), jnp.bfloat16),
            pltpu.SemaphoreType.DMA((chunks, len(runs))),
            pltpu.SemaphoreType.DMA((chunks,)),
        ],
        compiler_params=params(24),
        cost_estimate=COST,
        name="output_norm",
    )(places, *lefts, *pieces, near, hidden, gain.reshape(1, -1))


def rotary_tables(positions):
    half = HD // 2
    frequency = jnp.power(
        jnp.float32(10000.0), -jnp.arange(half, dtype=jnp.float32) * (2.0 / HD)
    )
    angles = positions.astype(jnp.float32)[:, None] * frequency[None, :]
    cos, sin = jnp.cos(angles), jnp.sin(angles)
    return jnp.concatenate([cos, cos], axis=1), jnp.concatenate([-sin, sin], axis=1)


def lookup(block_of, index):
    ids = jnp.arange(block_of.shape[0], dtype=jnp.int32)
    return jnp.sum(jnp.where(index[..., None] == ids, block_of, 0), axis=-1)


def flipped(array, axis, bit):
    size = lax.axis_size(axis)
    return lax.ppermute(array, axis, [(i, i ^ bit) for i in range(size)])


def shifted(array, axis, by):
    size = lax.axis_size(axis)
    return lax.ppermute(array, axis, [(i, (i + by) % size) for i in range(size)])


def after(array, *others):
    return lax.optimization_barrier((array, *others))[0]


def along_line(array):
    up = lax.ppermute(array, "seq", [(0, 1), (1, 2), (2, 3)])
    down = lax.ppermute(array, "seq", [(1, 0), (2, 1), (3, 2)])
    across = lax.ppermute(array, "seq", [(0, 2), (1, 3), (2, 0), (3, 1)])
    passed = lax.ppermute(across, "seq", [(1, 0), (2, 3)])
    return [part[None] for part in (array, up, down, across, passed)]


def four_by_four(hidden, pre_gain, post_gain, wq, wk, wv, w_out, block_of):
    rows = hidden.shape[0]
    block_rows = 2 * rows
    cuts = [rows // 3 * 2, rows // 3]
    seq, tp, group = lax.axis_index("seq"), lax.axis_index("tp"), lax.axis_index("groups")
    chip, core = tp // 2, tp % 2

    depth = w_out.shape[0]
    part = depth // 4
    sent = lax.dynamic_slice_in_dim(w_out, (group * 2 + seq % 2) * part, part, axis=0)
    pair = lambda array: lax.ppermute(array, "seq", [(0, 1), (1, 0), (2, 3), (3, 2)])
    w_first = flipped(sent, "tp", 2)
    w_group, w_pair = shifted(w_first, "groups", 1), pair(w_first)
    w_partner = flipped(w_out, "tp", 1)
    place = [(group, seq), (1 - group, seq), (group, seq + 1), (1 - group, seq + 1)]
    places = [(at * 2 + line % 2) * part for at, line in place]
    places = jnp.stack(places[:3] * 2 + places[3:] * 2).astype(jnp.int32)
    runs = [(head, at * part, part, head) for head in range(2) for at in range(3)]
    runs += [(2, 0, part, 0), (3, 0, part, 1)]

    third = rows // 3
    own = [
        norm(hidden, pre_gain, at * third, third)
        for at in range(3)
    ]
    away = [flipped(chunk, "tp", 2) for chunk in (after(own[0], w_first), own[1], own[2])]
    partner = [flipped(chunk, "tp", 1) for chunk in own]
    w_kv = jnp.concatenate([wk, wv], axis=1)

    line = jnp.stack([seq, seq - 1, seq + 1, (seq + 2) % 4, 3 - seq])
    valid = (line >= 0) & (line < 4) & (jnp.arange(5) < jnp.where((seq == 1) | (seq == 2), 4, 5))
    place_of = lambda side: lookup(block_of, 2 * line + side) * block_rows
    near_starts = jnp.where(valid, place_of(chip), NEVER)
    far_starts = jnp.where(valid, place_of(1 - chip), NEVER)
    place = []
    for first, size in zip((0, cuts[0]), cuts):
        run = first + jnp.arange(size, dtype=jnp.int32)
        place += [core * rows + run, (1 - core) * rows + run]
    place = jnp.concatenate(place)
    cosine, sine = rotary_tables(
        jnp.concatenate([near_starts[0] + place, far_starts[0] + place])
    )
    first, last = 2 * cuts[0], block_rows
    column, row = place[:, None], place[None, :]
    head, tail = slice(0, first), slice(first, last)
    others, everyone = list(range(1, 5)), list(range(5))

    def project(parts, span):
        return qkv(parts, wq, w_kv, cosine[span], sine[span])

    q_near, kv_near = project(
        [after(own[0], w_partner), own[1], *partner[:2], own[2], partner[2]],
        slice(0, block_rows),
    )
    near = along_line(after(kv_near, w_group, w_pair, away[0]))
    w_last = shifted(after(w_pair, *near[1:4]), "groups", 1)

    (near_state,) = attention(
        [Step(0, 0, others, same=0)],
        [q_near],
        near_starts[:1],
        [column],
        [near],
        near_starts,
        [row],
        [None],
    )

    far_span = lambda span: slice(block_rows + span.start, block_rows + span.stop)
    away[1] = after(away[1], *near_state)
    heads = away[:2] + [flipped(chunk, "tp", 1) for chunk in away[:2]]
    q_head, kv_head = project(heads, far_span(head))
    far_head = along_line(kv_head)
    w_far = jnp.concatenate([w_first, w_group, w_pair], axis=0)
    w_cross = flipped(w_far, "tp", 1)
    q_head = after(q_head, w_cross)
    (head_state,) = attention(
        [Step(0, 1, [], same=0), Step(0, 0, everyone)],
        [q_head],
        far_starts[:1],
        [column[head]],
        [near, far_head[:1]],
        jnp.concatenate([near_starts, far_starts[:1]]),
        [row, row[:, head]],
        [None],
    )

    away[2] = after(away[2], *head_state, *far_head[1:4], w_last)
    w_last_cross = flipped(w_last, "tp", 1)
    q_tail, kv_tail = project([away[2], flipped(away[2], "tp", 1)], far_span(tail))
    far_tail = along_line(kv_tail)

    q_starts = jnp.stack([near_starts[0], far_starts[0], far_starts[0]])
    qs = [q_near, q_head, q_tail]
    q_places = [column, column[head], column[tail]]
    state = attention(
        [
            Step(2, 2, [], same=0),
            Step(2, 0, everyone),
            Step(2, 1, others, same=0),
            Step(0, 1, everyone),
            Step(1, 1, others),
        ],
        qs,
        q_starts,
        q_places,
        [near, far_head, far_tail[:1]],
        jnp.concatenate([near_starts, far_starts, far_starts[:1]]),
        [row, row[:, head], row[:, tail]],
        [near_state, head_state, None],
    )
    to = lambda half: [(0, half * cuts[0], cuts[0]), (0, first + half * cuts[1], cuts[1])]
    over = lambda half: [(1, half * cuts[0], cuts[0]), (2, half * cuts[1], cuts[1])]
    mine, partners, same, cross = attention(
        [
            Step(1, 0, others, same=0, merged=True),
            Step(2, 0, others, merged=True),
            Step(0, 0, everyone, merged=True),
        ],
        qs,
        q_starts,
        q_places,
        [far_tail],
        far_starts,
        [row[:, tail]],
        state,
        final=[to(0), to(1), over(0), over(1)],
    )
    cross = flipped(cross, "tp", 3)
    same = flipped(same, "tp", 2)
    near_sum = output_near([mine, flipped(partners, "tp", 1)], [w_out, w_partner])
    return output(
        [same, cross],
        [w_far, w_cross, w_last, w_last_cross],
        runs,
        places,
        near_sum,
        hidden,
        post_gain,
    )


def any_count(hidden, pre_gain, post_gain, wq, wk, wv, w_out, block_of):
    normed = norm(hidden, pre_gain, 0, hidden.shape[0])
    normed = lax.all_gather(normed, "tp", axis=0, tiled=True)
    seq_rows = normed.shape[0]
    block_rows = seq_rows // 2
    lines = lax.axis_size("seq")
    place = jnp.arange(block_rows, dtype=jnp.int32)
    line = (lax.axis_index("seq") - jnp.arange(lines, dtype=jnp.int32)) % lines
    block = (2 * line[:, None] + jnp.arange(2, dtype=jnp.int32)).reshape(-1)
    starts = lookup(block_of, block) * block_rows
    cosine, sine = rotary_tables((starts[:2, None] + place).reshape(-1))
    w_kv = jnp.concatenate([wk, wv], axis=1)
    qs, keys_values = [], []
    for at in range(2):
        span = slice(at * block_rows, (at + 1) * block_rows)
        q, kv = qkv([normed[span]], wq, w_kv, cosine[span], sine[span])
        qs.append(q)
        keys_values.append(kv)
    kv = lax.all_gather(jnp.stack(keys_values), "seq")[line].reshape(-1, block_rows, 2 * HD)
    rest = list(range(2, 2 * lines))
    attended = attention(
        [
            Step(0, 0, [1], same=0),
            Step(1, 0, [0], same=1),
            Step(0, 0, rest),
            Step(1, 0, rest),
        ],
        qs,
        starts[:2],
        [place[:, None]] * 2,
        [[kv]],
        starts,
        [place[None, :]],
        [None, None],
        final=[[(0, 0, block_rows), (1, 0, block_rows)]],
    )[0]
    partial = jnp.dot(attended, w_out, preferred_element_type=jnp.float32)
    summed = lax.psum_scatter(
        partial.astype(jnp.bfloat16), "tp", scatter_dimension=0, tiled=True
    ).astype(jnp.float32)
    mean = jnp.mean(summed * summed, axis=-1, keepdims=True)
    projected = summed * lax.rsqrt(mean + EPS) * post_gain
    return (hidden.astype(jnp.float32) + projected).astype(jnp.bfloat16)


def solution(mesh):
    return jax.shard_map(
        four_by_four if tuple(mesh.shape[name] for name in ("groups", "tp", "seq")) == (2, 4, 4) else any_count,
        mesh=mesh,
        in_specs=(
            P(("groups", "seq", "tp"), None),
            P(),
            P(),
            P(None, "tp"),
            P(None, "tp"),
            P(None, "tp"),
            P("tp", None),
            P(),
        ),
        out_specs=P(("groups", "seq", "tp"), None),
        check_vma=False,
    )
```

```python
import functools
import math

import jax
import jax.numpy as jnp
from jax import lax
from jax.experimental import pallas as pl
from jax.experimental.pallas import tpu as pltpu
from jax.sharding import PartitionSpec as P

HD = 128
ATT_SCALAR = 144
EPS = 1e-6
MIB = 1024 * 1024
HIDDEN = -1e30
COST = pl.CostEstimate(flops=1, bytes_accessed=1, transcendentals=0)

ANY = pl.BlockSpec(memory_space=pl.ANY)
HBM = pl.BlockSpec(memory_space=pltpu.HBM)
VMEM = pl.BlockSpec(memory_space=pltpu.VMEM)
SMEM = pl.BlockSpec(memory_space=pltpu.SMEM)


class Came:
    def __init__(self, array):
        self.array, self.shape = array, array.shape


def call(kernel, name, mib, in_specs, out_shape, scratch, *args, out=HBM):
    in_specs, pinned = list(in_specs), []
    for at, arg in enumerate(args):
        if isinstance(arg, Came):
            arg, in_specs[at] = arg.array, ANY
        elif in_specs[at] is not SMEM:
            arg = pltpu.with_memory_space_constraint(arg, in_specs[at].memory_space)
        pinned.append(arg)
    return pl.pallas_call(
        kernel,
        in_specs=in_specs,
        out_specs=[out] * len(out_shape),
        out_shape=[out.memory_space(shape, dtype) for shape, dtype in out_shape],
        scratch_shapes=scratch,
        compiler_params=pltpu.CompilerParams(vmem_limit_bytes=mib * MIB),
        cost_estimate=COST,
        name=name,
    )(*pinned)


class Copies:
    def __init__(self, semaphores):
        self.semaphores, self.used = semaphores, 0

    def start(self, source, target):
        copy = pltpu.make_async_copy(source, target, self.semaphores.at[self.used])
        self.used += 1
        copy.start()
        return copy


def norm_kernel(cuts, pieces, table, hidden, gain, w_out, *refs):
    whole, parts = refs[0], refs[1 : 1 + len(cuts)]
    w_piece, rows, staged, semaphores = refs[1 + len(cuts) :]
    copies = Copies(semaphores)
    count, width = hidden.shape
    step = count // pieces
    spans = [pl.ds(at * step, step) for at in range(pieces)]
    ins = [copies.start(hidden.at[span], rows.at[span]) for span in spans]
    size = w_piece.shape[0]
    first = pl.multiple_of(table[1] * size, size)
    outs = [copies.start(w_out.at[pl.ds(first, size)], w_piece)]
    scale = gain[...]
    for at, span in enumerate(spans):
        ins[at].wait()
        x = rows[span, :].astype(jnp.float32)
        square = x * x
        folded = square[:, :128]
        for lane in range(128, width, 128):
            folded = folded + square[:, lane : lane + 128]
        mean = jnp.sum(folded, axis=1, keepdims=True) / width
        staged[span, :] = (x * lax.rsqrt(mean + EPS) * scale).astype(jnp.bfloat16)
        outs.append(copies.start(staged.at[span], whole.at[span]))
        begin = 0
        for cut, part in zip(cuts, parts):
            if begin <= at * step < begin + cut:
                inside = pl.ds(at * step - begin, step)
                outs.append(copies.start(staged.at[span], part.at[inside]))
            begin += cut
    for copy in outs:
        copy.wait()


def norm(table, hidden, gain, w_out, cuts, share, pieces=3):
    rows, width = hidden.shape
    bf16 = jnp.bfloat16
    out_shape = [((rows, width), bf16)] + [((cut, width), bf16) for cut in cuts]
    return call(
        functools.partial(norm_kernel, cuts, pieces),
        "norm_rows",
        12,
        [SMEM, HBM, VMEM, HBM],
        out_shape + [((share, width), bf16)],
        [
            pltpu.VMEM((rows, width), bf16),
            pltpu.VMEM((rows, width), bf16),
            pltpu.SemaphoreType.DMA((1 + 3 * pieces,)),
        ],
        table,
        hidden,
        gain.reshape(1, -1),
        w_out,
    )


def qkv_kernel(runs, first, chunks, *refs):
    parts = refs[: len(runs)]
    wq, wk, wv, trig, q_out, kv_out = refs[len(runs) : len(runs) + 6]
    rows, weights, angles, q, kv, semaphores = refs[len(runs) + 6 :]
    copies = Copies(semaphores)
    total, width = rows.shape
    depth = width // chunks
    queries = wq.shape[1]
    waits = []
    for chunk in range(chunks):
        lanes = pl.ds(chunk * depth, depth)
        here, put = [], 0
        for part, (begin, count) in zip(parts, runs):
            source = part.at[pl.ds(begin, count), lanes]
            here.append(copies.start(source, rows.at[pl.ds(put, count), lanes]))
            put += count
        column = 0
        for weight in (wq, wk, wv):
            target = weights.at[lanes, pl.ds(column, weight.shape[1])]
            here.append(copies.start(weight.at[lanes], target))
            column += weight.shape[1]
        waits.append(here)
    waits[-1].append(copies.start(trig.at[pl.ds(first, total)], angles))
    product = None
    for chunk in range(chunks):
        for copy in waits[chunk]:
            copy.wait()
        lanes = slice(chunk * depth, (chunk + 1) * depth)
        term = jnp.dot(rows[:, lanes], weights[lanes, :], preferred_element_type=jnp.float32)
        product = term if product is None else product + term
    cos, sin = angles[:, :HD], angles[:, HD:]

    def rotated(at):
        y = product[:, at : at + HD]
        return y * cos + pltpu.roll(y, HD // 2, 1) * sin

    factor = ATT_SCALAR ** (-0.5) * math.log2(math.e)
    kv[:, :HD] = rotated(queries).astype(jnp.bfloat16)
    kv[:, HD:] = product[:, queries + HD :].astype(jnp.bfloat16)
    outs = [copies.start(kv, kv_out)]
    for head in range(queries // HD):
        q[head] = (rotated(head * HD) * factor).astype(jnp.bfloat16)
    outs.append(copies.start(q, q_out))
    for copy in outs:
        copy.wait()


def qkv(parts, weights, trig, first, chunks=4):
    total = sum(count for _, _, count in parts)
    width, queries = weights[0].shape
    bf16 = jnp.bfloat16
    heads = queries // HD
    runs = [(begin, count) for _, begin, count in parts]
    return call(
        functools.partial(qkv_kernel, runs, first, chunks),
        "qkv",
        24,
        [HBM] * (len(parts) + 4),
        [((heads, total, HD), bf16), ((total, 2 * HD), bf16)],
        [
            pltpu.VMEM((total, width), bf16),
            pltpu.VMEM((width, queries + 2 * HD), bf16),
            pltpu.VMEM((total, 2 * HD), jnp.float32),
            pltpu.VMEM((heads, total, HD), bf16),
            pltpu.VMEM((total, 2 * HD), bf16),
            pltpu.SemaphoreType.DMA((chunks * (len(parts) + 3) + 3,)),
        ],
        *[array for array, _, _ in parts],
        *weights,
        trig,
    )


class Step:
    def __init__(self, q, group, slots, same=None, merged=False):
        self.q, self.group, self.slots = q, group, slots
        self.same, self.merged = same, merged


class Chunk:
    def __init__(self, at, runs, share):
        self.at, self.runs, self.share = at, runs, share

    def places(self, core, axis, first, size):
        shape = (size, 1) if axis == 0 else (1, size)
        index = first + lax.broadcasted_iota(jnp.int32, shape, axis)
        result, begin = index, 0
        for which, offset, rows in self.runs:
            base = (core if which == 0 else 1 - core) * self.share + offset - begin
            inside = (index >= begin) & (index < begin + rows)
            result = jnp.where(inside, index + base, result)
            begin += rows
        return result


def attention_kernel(plan, q_chunks, k_chunks, group_parts, fresh, final, table, *refs):
    refs = list(refs)
    take = lambda n: [refs.pop(0) for _ in range(n)]
    count = len(q_chunks)
    q_refs = take(count)
    kv_parts = [take(n) for n in group_parts]
    old = {q: take(2) for q in range(count) if q not in fresh}
    outs = take(len(final) if final else 2 * count)
    qs, kvs = take(count), take(len(group_parts))
    if final:
        states, staged = [take(2) for _ in range(count)], take(len(final))
    else:
        states = [outs[2 * q : 2 * q + 2] for q in range(count)]
    (semaphores,) = refs
    copies = Copies(semaphores)
    core = table[0]
    waits = {}
    for at, (source, target) in enumerate(zip(q_refs, qs)):
        waits["q", at] = [copies.start(source, target)]
    for group, (parts, kv) in enumerate(zip(kv_parts, kvs)):
        each = kv.shape[0] // len(parts)
        waits["kv", group] = [
            copies.start(part, kv.at[pl.ds(slot * each, each)])
            for slot, part in enumerate(parts)
        ]
    def ready(*key):
        for copy in waits.pop(key, []):
            copy.wait()

    def attend(q, keys_values, begin, visible=None, bias=None):
        q_ref, (peak, acc) = qs[q], states[q]
        heads, rows, _ = q_ref.shape
        keys, values = keys_values[:, :HD], keys_values[:, HD:]
        values = jnp.concatenate([values, jnp.ones_like(values)], axis=1)
        count = keys.shape[0]
        tile = min(rows, 128)
        for first in range(0, rows, tile):
            q_tile = q_ref[:, first : first + tile, :].reshape(heads * tile, HD)
            scores = lax.dot_general(
                q_tile, keys, (((1,), (1,)), ((), ())), preferred_element_type=jnp.float32
            )
            if visible is not None:
                seen = jnp.concatenate([visible(first, tile)] * heads, axis=0)
                scores = jnp.where(seen, scores, HIDDEN)
            if bias is not None:
                scores = scores + bias
            top = jnp.max(scores, axis=1, keepdims=True)
            top = jnp.broadcast_to(top, (heads * tile, HD))
            span = pl.ds(first * heads, heads * tile)
            if not begin:
                before = peak[span, :]
                top = jnp.maximum(before, top)
            wide = jnp.concatenate([top] * (count // HD), axis=1)
            weights = jnp.exp2(scores - wide).astype(jnp.bfloat16)
            summed = jnp.dot(weights, values, preferred_element_type=jnp.float32)
            if not begin:
                fade = jnp.exp2(before - top)
                summed = summed + acc[span, :] * jnp.concatenate([fade, fade], axis=1)
            acc[span, :] = summed
            peak[span, :] = top

    begun = set(range(count)) - set(fresh)
    for q, held in old.items():
        for source, target in zip(held, states[q]):
            target[...] = source[...]
    for step in plan:
        q, group, kv = step.q, step.group, kvs[step.group]
        q_chunk, k_chunk = q_chunks[q], k_chunks[group]
        ready("q", q)
        ready("kv", group)
        if step.same is not None:
            keys_at = k_chunk.places(core, 1, 0, kv.shape[1])
            visible = lambda first, tile: keys_at <= q_chunk.places(core, 0, first, tile)
            attend(q, kv[step.same], q not in begun, visible=visible)
            begun.add(q)
        start = table[q_chunk.at]
        slots = step.slots
        if not slots:
            continue
        if step.merged:
            shown = [table[k_chunk.at + slot] < start for slot in slots]

            @pl.when(functools.reduce(jnp.logical_or, shown))
            def _():
                rows = kv.shape[1]
                bias = [
                    jnp.where(see, 0.0, HIDDEN) * jnp.ones((1, rows), jnp.float32)
                    for see in shown
                ]
                keys_values = kv[slots[0] : slots[-1] + 1].reshape(len(slots) * rows, 2 * HD)
                attend(q, keys_values, False, bias=jnp.concatenate(bias, axis=1))

        else:

            def one(slot, carry):
                @pl.when(table[k_chunk.at + slot] < start)
                def _():
                    attend(q, kv[slot], False)

                return carry

            lax.fori_loop(slots[0], slots[-1] + 1, one, 0)

    stores = []
    if final:
        for out, stage, spans in zip(outs, staged, final):
            put = 0
            for q, first, rows in spans:
                acc = states[q][1]
                heads, q_rows, _ = qs[q].shape
                tile = min(q_rows, 128)
                size = min(tile, rows)
                for head in range(heads):
                    for at in range(first, first + rows, size):
                        begin = at // tile * tile * heads + head * tile + at % tile
                        part = acc[begin : begin + size, :]
                        to = put + at - first
                        stage[to : to + size, head * HD : (head + 1) * HD] = (
                            part[:, :HD] / part[:, HD:]
                        ).astype(jnp.bfloat16)
                put += rows
            stores.append(copies.start(stage, out))
    for copy in stores:
        copy.wait()


def attention(plan, table, qs, q_chunks, groups, k_chunks, state, final=None):
    fresh = [at for at, held in enumerate(state) if held is None]
    held = [array for pair in state if pair is not None for array in pair]
    shapes = []
    for q in qs:
        heads, rows, _ = q.shape
        shapes += [(heads * rows, HD), (heads * rows, 2 * HD)]
    if final:
        width = qs[0].shape[0] * HD
        sums = [sum(rows for _, _, rows in spans) for spans in final]
        out_shape = [((rows, width), jnp.bfloat16) for rows in sums]
    else:
        out_shape = [(shape, jnp.float32) for shape in shapes]
    scratch = [pltpu.VMEM(q.shape, jnp.bfloat16) for q in qs]
    for parts in groups:
        slots = sum(part.shape[0] for part in parts)
        scratch.append(pltpu.VMEM((slots,) + parts[0].shape[1:], jnp.bfloat16))
    if final:
        scratch += [pltpu.VMEM(shape, jnp.float32) for shape in shapes]
        scratch += [pltpu.VMEM(shape, dtype) for shape, dtype in out_shape]
    parts = [part for parts in groups for part in parts]
    inputs = [*qs, *parts]
    sizes = [len(parts) for parts in groups]
    results = call(
        functools.partial(attention_kernel, plan, q_chunks, k_chunks, sizes, fresh, final),
        "attention",
        20,
        [SMEM] + [HBM] * len(inputs) + [VMEM] * len(held),
        out_shape,
        scratch + [pltpu.SemaphoreType.DMA((len(inputs) + len(out_shape),))],
        table,
        *inputs,
        *held,
        out=HBM if final else VMEM,
    )
    if final:
        return results
    return [tuple(results[2 * at : 2 * at + 2]) for at in range(len(qs))]


def fetch(copies, lefts, left, pieces, weights, chunks):
    columns = lefts[0].shape[1]
    depth, width = pieces[0].shape
    step = width // chunks
    first = [
        copies.start(part, left.at[:, pl.ds(at * columns, columns)])
        for at, part in enumerate(lefts)
    ]
    waits = []
    for chunk in range(chunks):
        lanes = pl.ds(chunk * step, step)
        waits.append(
            [
                copies.start(piece.at[:, lanes], weights.at[pl.ds(at * depth, depth), lanes])
                for at, piece in enumerate(pieces)
            ]
        )
    waits[0] += first
    return waits


def near_kernel(chunks, *refs):
    lefts, pieces = refs[:2], refs[2:4]
    out, left, weights, semaphores = refs[4:]
    copies = Copies(semaphores)
    waits = fetch(copies, lefts, left, pieces, weights, chunks)
    step = out.shape[1] // chunks
    for chunk in range(chunks):
        for copy in waits[chunk]:
            copy.wait()
        lanes = pl.ds(chunk * step, step)
        out[:, lanes] = jnp.dot(
            left[...], weights[:, lanes], preferred_element_type=jnp.float32
        ).astype(jnp.bfloat16)


def output_near(lefts, pieces, chunks=6):
    (rows, columns), (depth, width) = lefts[0].shape, pieces[0].shape
    bf16 = jnp.bfloat16
    return call(
        functools.partial(near_kernel, chunks),
        "output_near",
        16,
        [HBM] * 4,
        [((rows, width), bf16)],
        [
            pltpu.VMEM((rows, 2 * columns), bf16),
            pltpu.VMEM((2 * depth, width), bf16),
            pltpu.SemaphoreType.DMA((2 + 2 * chunks,)),
        ],
        *lefts,
        *pieces,
        out=VMEM,
    )[0]


def output_kernel(chunks, *refs):
    lefts, pieces = refs[:2], refs[2:4]
    hidden, near, gain, out, left, weights, held, projected, semaphores = refs[4:]
    copies = Copies(semaphores)
    waits = fetch(copies, lefts, left, pieces, weights, chunks)
    width = hidden.shape[1]
    step = width // chunks
    late = copies.start(hidden, held)
    square = jnp.zeros((hidden.shape[0], 128), jnp.float32)
    for chunk in range(chunks):
        for copy in waits[chunk]:
            copy.wait()
        lanes = pl.ds(chunk * step, step)
        total = near[:, lanes].astype(jnp.float32) + jnp.dot(
            left[...], weights[:, lanes], preferred_element_type=jnp.float32
        )
        projected[:, lanes] = total
        for lane in range(0, step, 128):
            part = total[:, lane : lane + 128]
            square = square + part * part
    mean = jnp.sum(square, axis=1, keepdims=True) / width
    scale = lax.rsqrt(mean + EPS)
    late.wait()
    stores = []
    for chunk in range(chunks):
        lanes = pl.ds(chunk * step, step)
        normed = projected[:, lanes] * scale * gain[:, lanes]
        held[:, lanes] = (held[:, lanes].astype(jnp.float32) + normed).astype(jnp.bfloat16)
        stores.append(copies.start(held.at[:, lanes], out.at[:, lanes]))
    for store in stores:
        store.wait()


def output(lefts, pieces, near, hidden, gain, chunks=6):
    rows, width = hidden.shape
    columns, depth = lefts[0].shape[1], pieces[0].shape[0]
    bf16 = jnp.bfloat16
    return call(
        functools.partial(output_kernel, chunks),
        "output_norm",
        24,
        [HBM] * 5 + [VMEM] * 2,
        [((rows, width), bf16)],
        [
            pltpu.VMEM((rows, 2 * columns), bf16),
            pltpu.VMEM((2 * depth, width), bf16),
            pltpu.VMEM((rows, width), bf16),
            pltpu.VMEM((rows, width), jnp.float32),
            pltpu.SemaphoreType.DMA((3 + 3 * chunks,)),
        ],
        *lefts,
        *pieces,
        hidden,
        near,
        gain,
    )[0]


def rotary_table(positions):
    half = HD // 2
    frequency = jnp.power(
        jnp.float32(10000.0), -jnp.arange(half, dtype=jnp.float32) * (2.0 / HD)
    )
    angles = positions.astype(jnp.float32)[:, None] * frequency[None, :]
    cos, sin = jnp.cos(angles), jnp.sin(angles)
    return jnp.concatenate([cos, cos, -sin, sin], axis=1)


def lookup(block_of, index):
    ids = jnp.arange(block_of.shape[0], dtype=jnp.int32)
    return jnp.sum(jnp.where(index[..., None] == ids, block_of, 0), axis=-1)


def flipped(array, axis, bit):
    size = lax.axis_size(axis)
    return lax.ppermute(array, axis, [(i, i ^ bit) for i in range(size)])


def along_line(array):
    size = lax.axis_size("seq")
    parts = [array[None]]
    for by in range(1, size):
        part = lax.ppermute(array, "seq", [(i, (i + by) % size) for i in range(size)])
        parts.append(Came(part[None]))
    return parts


def after(array, *others):
    return lax.optimization_barrier((array, *others))[0]


def two_chips(hidden, pre_gain, post_gain, wq, wk, wv, w_out, block_of):
    rows = hidden.shape[0]
    block_rows = 2 * rows
    cuts = [rows // 3 * 2, rows // 3]
    lines, groups = lax.axis_size("seq"), lax.axis_size("groups")
    seq, tp, group = lax.axis_index("seq"), lax.axis_index("tp"), lax.axis_index("groups")
    chip, core = tp // 2, tp % 2

    line = (seq - jnp.arange(lines, dtype=jnp.int32)) % lines
    near_starts = lookup(block_of, 2 * line + chip) * block_rows
    far_starts = lookup(block_of, 2 * line + 1 - chip) * block_rows
    scalars = jnp.stack([core, group * lines + seq]).astype(jnp.int32)
    table = jnp.concatenate([scalars, near_starts, far_starts])
    near_at, far_at = 2, 2 + lines

    share = w_out.shape[0] // (groups * lines)
    own, own_head, own_tail, w_piece = norm(table, hidden, pre_gain, w_out, cuts, share)
    partner = flipped(own, "tp", 1)
    w_piece = flipped(w_piece, "tp", 2)
    head, tail = flipped(own_head, "tp", 2), flipped(own_tail, "tp", 2)
    w_partner = flipped(w_out, "tp", 1)
    w_far = lax.all_gather(after(w_piece, partner), ("groups", "seq"), axis=0, tiled=True)

    run = [jnp.arange(size, dtype=jnp.int32) for size in cuts]
    place = [core * rows + run[0], (1 - core) * rows + run[0]]
    place += [core * rows + cuts[0] + run[1], (1 - core) * rows + cuts[0] + run[1]]
    place = jnp.concatenate(place)
    trig = rotary_table(jnp.concatenate([near_starts[0] + place, far_starts[0] + place]))
    weights = [wq, wk, wv]
    head_runs = [(0, 0, cuts[0]), (1, 0, cuts[0])]
    tail_runs = [(0, cuts[0], cuts[1]), (1, cuts[0], cuts[1])]
    near_chunk = Chunk(near_at, head_runs + tail_runs, rows)
    head_chunk, tail_chunk = Chunk(far_at, head_runs, rows), Chunk(far_at, tail_runs, rows)
    others, everyone = list(range(1, lines)), list(range(lines))

    q_near, kv_near = qkv(
        [
            (own, 0, cuts[0]),
            (Came(partner), 0, cuts[0]),
            (own, cuts[0], cuts[1]),
            (Came(partner), cuts[0], cuts[1]),
        ],
        weights,
        trig,
        0,
    )
    near = along_line(kv_near)
    (near_state,) = attention(
        [Step(0, 0, others, same=0)], table, [q_near], [near_chunk], [near], [near_chunk], [None]
    )

    head = after(head, *near_state, w_partner)
    q_head, kv_head = qkv(
        [(Came(head), 0, cuts[0]), (Came(flipped(head, "tp", 1)), 0, cuts[0])],
        weights,
        trig,
        block_rows,
    )
    far_head = along_line(kv_head)
    (head_state,) = attention(
        [Step(0, 1, [], same=0), Step(0, 0, everyone)],
        table,
        [q_head],
        [head_chunk],
        [near, far_head[:1]],
        [near_chunk, head_chunk],
        [None],
    )

    tail = after(tail, *head_state, *[part.array for part in far_head[1:]])
    q_tail, kv_tail = qkv(
        [(Came(tail), 0, cuts[1]), (Came(flipped(tail, "tp", 1)), 0, cuts[1])],
        weights,
        trig,
        block_rows + 2 * cuts[0],
    )
    far_tail = along_line(kv_tail)
    qs, q_chunks = [q_near, q_head, q_tail], [near_chunk, head_chunk, tail_chunk]
    state = attention(
        [
            Step(2, 2, [], same=0),
            Step(2, 0, everyone),
            Step(2, 1, others, same=0),
            Step(0, 1, everyone),
            Step(1, 1, others),
        ],
        table,
        qs,
        q_chunks,
        [near, far_head, far_tail[:1]],
        [near_chunk, head_chunk, tail_chunk],
        [near_state, head_state, None],
    )
    first = 2 * cuts[0]
    to = lambda half: [(0, half * cuts[0], cuts[0]), (0, first + half * cuts[1], cuts[1])]
    over = lambda half: [(1, half * cuts[0], cuts[0]), (2, half * cuts[1], cuts[1])]
    mine, partners, same, cross = attention(
        [
            Step(1, 0, others, same=0, merged=True),
            Step(2, 0, others, merged=True),
            Step(0, 0, everyone, merged=True),
        ],
        table,
        qs,
        q_chunks,
        [far_tail],
        [tail_chunk],
        state,
        final=[to(0), to(1), over(0), over(1)],
    )
    cross, same = flipped(cross, "tp", 3), flipped(same, "tp", 2)
    near_sum = output_near([mine, Came(flipped(partners, "tp", 1))], [w_out, Came(w_partner)])
    w_cross = flipped(after(w_far, mine), "tp", 1)
    return output(
        [Came(same), Came(cross)],
        [Came(w_far), Came(w_cross)],
        near_sum,
        hidden,
        post_gain.reshape(1, -1),
    )


def any_count(hidden, pre_gain, post_gain, wq, wk, wv, w_out, block_of):
    rows = hidden.shape[0]
    lines = lax.axis_size("seq")
    line = (lax.axis_index("seq") - jnp.arange(lines, dtype=jnp.int32)) % lines
    block = (2 * line[:, None] + jnp.arange(2, dtype=jnp.int32)).reshape(-1)
    block_rows = rows * lax.axis_size("tp") // 2
    starts = lookup(block_of, block) * block_rows
    table = jnp.concatenate([jnp.zeros(2, jnp.int32), starts])
    normed = norm(table, hidden, pre_gain, w_out, [], 16, 1)[0]
    normed = lax.all_gather(normed, "tp", axis=0, tiled=True)
    place = jnp.arange(block_rows, dtype=jnp.int32)
    trig = rotary_table((starts[:2, None] + place).reshape(-1))
    qs, keys_values = [], []
    for at in range(2):
        first = at * block_rows
        q, kv = qkv([(normed, first, block_rows)], [wq, wk, wv], trig, first)
        qs.append(q)
        keys_values.append(kv)
    kv = lax.all_gather(jnp.stack(keys_values), "seq")[line].reshape(-1, block_rows, 2 * HD)
    rest = list(range(2, 2 * lines))
    runs = [(0, 0, block_rows)]
    attended = attention(
        [Step(0, 0, [1], same=0), Step(1, 0, [0], same=1), Step(0, 0, rest), Step(1, 0, rest)],
        table,
        qs,
        [Chunk(2, runs, 0), Chunk(3, runs, 0)],
        [[kv]],
        [Chunk(2, runs, 0)],
        [None, None],
        final=[[(0, 0, block_rows), (1, 0, block_rows)]],
    )[0]
    partial = jnp.dot(attended, w_out, preferred_element_type=jnp.float32)
    summed = lax.psum_scatter(
        partial.astype(jnp.bfloat16), "tp", scatter_dimension=0, tiled=True
    ).astype(jnp.float32)
    mean = jnp.mean(summed * summed, axis=-1, keepdims=True)
    projected = summed * lax.rsqrt(mean + EPS) * post_gain
    return (hidden.astype(jnp.float32) + projected).astype(jnp.bfloat16)


def solution(mesh):
    return jax.shard_map(
        two_chips if mesh.shape["tp"] == 4 else any_count,
        mesh=mesh,
        in_specs=(
            P(("groups", "seq", "tp"), None),
            P(),
            P(),
            P(None, "tp"),
            P(None, "tp"),
            P(None, "tp"),
            P("tp", None),
            P(),
        ),
        out_specs=P(("groups", "seq", "tp"), None),
        check_vma=False,
    )
```

```python
import functools
import math

import jax
import jax.numpy as jnp
from jax import lax
from jax.experimental import pallas as pl
from jax.experimental.pallas import tpu as pltpu
from jax.sharding import PartitionSpec as P

HD = 128
ATT_SCALAR = 144
EPS = 1e-6
MIB = 1024 * 1024
HIDDEN = -1e30
COST = pl.CostEstimate(flops=1, bytes_accessed=1, transcendentals=0)

ANY = pl.BlockSpec(memory_space=pl.ANY)
HBM = pl.BlockSpec(memory_space=pltpu.HBM)
VMEM = pl.BlockSpec(memory_space=pltpu.VMEM)
SMEM = pl.BlockSpec(memory_space=pltpu.SMEM)


class Came:
    def __init__(self, array):
        self.array, self.shape = array, array.shape


def call(kernel, name, mib, in_specs, outs, scratch, *args, aliases=None):
    in_specs, pinned = list(in_specs), []
    for at, arg in enumerate(args):
        if isinstance(arg, Came):
            arg, in_specs[at] = arg.array, ANY
        elif in_specs[at] is not SMEM:
            arg = pltpu.with_memory_space_constraint(arg, in_specs[at].memory_space)
        pinned.append(arg)
    return pl.pallas_call(
        kernel,
        in_specs=in_specs,
        out_specs=[spec for _, _, spec in outs],
        out_shape=[spec.memory_space(shape, dtype) for shape, dtype, spec in outs],
        scratch_shapes=scratch,
        input_output_aliases=aliases or {},
        compiler_params=pltpu.CompilerParams(vmem_limit_bytes=mib * MIB),
        cost_estimate=COST,
        name=name,
    )(*pinned)


class Copies:
    def __init__(self, semaphores):
        self.semaphores, self.used = semaphores, 0

    def start(self, source, target):
        copy = pltpu.make_async_copy(source, target, self.semaphores.at[self.used])
        self.used += 1
        copy.start()
        return copy


def norm_kernel(cuts, pieces, table, hidden, gain, w_out, *refs):
    parts = refs[: len(cuts)]
    w_piece, rows, staged, bounced, semaphores = refs[len(cuts) :]
    copies = Copies(semaphores)
    count, width = hidden.shape
    step = count // pieces
    spans = [pl.ds(at * step, step) for at in range(pieces)]
    ins = [copies.start(hidden.at[span], rows.at[span]) for span in spans]
    size = w_piece.shape[0]
    first = pl.multiple_of(table[1] * size, size)
    piece = copies.start(w_out.at[pl.ds(first, size)], bounced)
    outs = []
    scale = gain[...]
    for at, span in enumerate(spans):
        ins[at].wait()
        x = rows[span, :].astype(jnp.float32)
        square = x * x
        folded = square[:, :128]
        for lane in range(128, width, 128):
            folded = folded + square[:, lane : lane + 128]
        mean = jnp.sum(folded, axis=1, keepdims=True) / width
        staged[span, :] = (x * lax.rsqrt(mean + EPS) * scale).astype(jnp.bfloat16)
        begin = 0
        for cut, part in zip(cuts, parts):
            if begin <= at * step < begin + cut:
                inside = pl.ds(at * step - begin, step)
                outs.append(copies.start(staged.at[span], part.at[inside]))
            begin += cut
    piece.wait()
    outs.append(copies.start(bounced, w_piece))
    for copy in outs:
        copy.wait()


def norm(table, hidden, gain, w_out, cuts, share, pieces=3):
    rows, width = hidden.shape
    bf16 = jnp.bfloat16
    outs = [((cut, width), bf16, HBM) for cut in cuts]
    return call(
        functools.partial(norm_kernel, cuts, pieces),
        "norm_rows",
        12,
        [SMEM, HBM, VMEM, HBM],
        outs + [((share, width), bf16, HBM)],
        [
            pltpu.VMEM((rows, width), bf16),
            pltpu.VMEM((rows, width), bf16),
            pltpu.VMEM((share, width), bf16),
            pltpu.SemaphoreType.DMA((2 + 2 * pieces,)),
        ],
        table,
        hidden,
        gain.reshape(1, -1),
        w_out,
    )


def hold_kernel(wq, wk, wv, out, semaphores):
    copies, column, waits = Copies(semaphores), 0, []
    for weight in (wq, wk, wv):
        count = weight.shape[1]
        waits.append(copies.start(weight, out.at[:, pl.ds(column, count)]))
        column += count
    for copy in waits:
        copy.wait()


def hold(wq, wk, wv):
    shape = (wq.shape[0], wq.shape[1] + wk.shape[1] + wv.shape[1])
    return call(
        hold_kernel,
        "hold_weights",
        1,
        [HBM] * 3,
        [(shape, wq.dtype, VMEM)],
        [pltpu.SemaphoreType.DMA((3,))],
        wq,
        wk,
        wv,
    )[0]


def qkv_kernel(runs, first, weights, trig, *refs):
    parts = refs[: len(runs)]
    q, kv, rows, angles, semaphores = refs[len(runs) :]
    copies, put, waits = Copies(semaphores), 0, []
    for part, (begin, count) in zip(parts, runs):
        target = rows.at[pl.ds(put, count)]
        waits.append(copies.start(part.at[pl.ds(begin, count)], target))
        put += count
    waits.append(copies.start(trig.at[pl.ds(first, put)], angles))
    for copy in waits:
        copy.wait()
    product = jnp.dot(rows[...], weights[...], preferred_element_type=jnp.float32)
    cos, sin = angles[:, :HD], angles[:, HD:]
    queries = weights.shape[1] - 2 * HD

    def rotated(at):
        y = product[:, at : at + HD]
        return y * cos + pltpu.roll(y, HD // 2, 1) * sin

    factor = ATT_SCALAR ** (-0.5) * math.log2(math.e)
    kv[:, :HD] = rotated(queries).astype(jnp.bfloat16)
    kv[:, HD:] = product[:, queries + HD :].astype(jnp.bfloat16)
    for head in range(queries // HD):
        q[head] = (rotated(head * HD) * factor).astype(jnp.bfloat16)


def qkv(parts, weights, trig, first):
    total = sum(count for _, _, count in parts)
    width, columns = weights.shape
    heads = columns // HD - 2
    runs = [(begin, count) for _, begin, count in parts]
    return call(
        functools.partial(qkv_kernel, runs, first),
        "qkv",
        12,
        [VMEM] + [HBM] * (len(parts) + 1),
        [((heads, total, HD), jnp.bfloat16, VMEM), ((total, 2 * HD), jnp.bfloat16, VMEM)],
        [
            pltpu.VMEM((total, width), jnp.bfloat16),
            pltpu.VMEM((total, 2 * HD), jnp.float32),
            pltpu.SemaphoreType.DMA((len(parts) + 1,)),
        ],
        weights,
        trig,
        *[array for array, _, _ in parts],
    )


class Step:
    def __init__(self, q, group, slots, same=None, merged=False):
        self.q, self.group, self.slots = q, group, slots
        self.same, self.merged = same, merged


class Chunk:
    def __init__(self, at, runs, share):
        self.at, self.runs, self.share = at, runs, share

    def places(self, core, axis, first, size):
        shape = (size, 1) if axis == 0 else (1, size)
        index = first + lax.broadcasted_iota(jnp.int32, shape, axis)
        result, begin = index, 0
        for which, offset, rows in self.runs:
            base = (core if which == 0 else 1 - core) * self.share + offset - begin
            inside = (index >= begin) & (index < begin + rows)
            result = jnp.where(inside, index + base, result)
            begin += rows
        return result


def attention_kernel(plan, q_chunks, k_chunks, group_parts, fresh, final, table, *refs):
    refs = list(refs)
    take = lambda n: [refs.pop(0) for _ in range(n)]
    count = len(q_chunks)
    qs = take(count)
    kv_parts = [take(n) for n in group_parts]
    take(2 * (count - len(fresh)))
    outs = take(len(final))
    states = [take(2) for _ in range(count)]
    kvs, staged = take(len(group_parts)), take(len(final))
    (semaphores,) = refs
    copies = Copies(semaphores)
    core = table[0]
    waits = {}
    for group, (parts, kv) in enumerate(zip(kv_parts, kvs)):
        each = kv.shape[0] // len(parts)
        waits[group] = [
            copies.start(part, kv.at[pl.ds(slot * each, each)])
            for slot, part in enumerate(parts)
        ]

    def ready(group):
        for copy in waits.pop(group, []):
            copy.wait()

    def attend(q, keys_values, begin, visible=None, bias=None):
        q_ref, (peak, acc) = qs[q], states[q]
        heads, rows, _ = q_ref.shape
        keys, values = keys_values[:, :HD], keys_values[:, HD:]
        values = jnp.concatenate([values, jnp.ones_like(values)], axis=1)
        count = keys.shape[0]
        tile = min(rows, 128)
        for first in range(0, rows, tile):
            q_tile = q_ref[:, first : first + tile, :].reshape(heads * tile, HD)
            scores = lax.dot_general(
                q_tile, keys, (((1,), (1,)), ((), ())), preferred_element_type=jnp.float32
            )
            if visible is not None:
                seen = jnp.concatenate([visible(first, tile)] * heads, axis=0)
                scores = jnp.where(seen, scores, HIDDEN)
            if bias is not None:
                scores = scores + bias
            top = jnp.max(scores, axis=1, keepdims=True)
            top = jnp.broadcast_to(top, (heads * tile, HD))
            span = pl.ds(first * heads, heads * tile)
            if not begin:
                before = peak[span, :]
                top = jnp.maximum(before, top)
            wide = jnp.concatenate([top] * (count // HD), axis=1)
            weights = jnp.exp2(scores - wide).astype(jnp.bfloat16)
            summed = jnp.dot(weights, values, preferred_element_type=jnp.float32)
            if not begin:
                fade = jnp.exp2(before - top)
                summed = summed + acc[span, :] * jnp.concatenate([fade, fade], axis=1)
            acc[span, :] = summed
            peak[span, :] = top

    begun = set(range(count)) - set(fresh)
    for step in plan:
        q, group, kv = step.q, step.group, kvs[step.group]
        q_chunk, k_chunk = q_chunks[q], k_chunks[group]
        if step.same is not None:
            keys_at = k_chunk.places(core, 1, 0, kv.shape[1])
            visible = lambda first, tile: keys_at <= q_chunk.places(core, 0, first, tile)
            own = kv_parts[group][0]
            attend(q, own[step.same], q not in begun, visible=visible)
            begun.add(q)
        start = table[q_chunk.at]
        slots = step.slots
        if not slots:
            continue
        ready(group)
        if step.merged:
            shown = [table[k_chunk.at + slot] < start for slot in slots]

            @pl.when(functools.reduce(jnp.logical_or, shown))
            def _():
                rows = kv.shape[1]
                bias = [
                    jnp.where(see, 0.0, HIDDEN) * jnp.ones((1, rows), jnp.float32)
                    for see in shown
                ]
                keys_values = kv[slots[0] : slots[-1] + 1].reshape(len(slots) * rows, 2 * HD)
                attend(q, keys_values, False, bias=jnp.concatenate(bias, axis=1))

        else:

            def one(slot, carry):
                @pl.when(table[k_chunk.at + slot] < start)
                def _():
                    attend(q, kv[slot], False)

                return carry

            lax.fori_loop(slots[0], slots[-1] + 1, one, 0)

    for group in list(waits):
        ready(group)
    stores = []
    for out, stage, spans in zip(outs, staged, final):
        put = 0
        for q, first, rows in spans:
            acc = states[q][1]
            heads, q_rows, _ = qs[q].shape
            tile = min(q_rows, 128)
            size = min(tile, rows)
            for head in range(heads):
                for at in range(first, first + rows, size):
                    begin = at // tile * tile * heads + head * tile + at % tile
                    part = acc[begin : begin + size, :]
                    to = put + at - first
                    stage[to : to + size, head * HD : (head + 1) * HD] = (
                        part[:, :HD] / part[:, HD:]
                    ).astype(jnp.bfloat16)
            put += rows
        stores.append(copies.start(stage, out))
    for copy in stores:
        copy.wait()


def attention(plan, table, qs, q_chunks, groups, k_chunks, state, final=()):
    fresh = [at for at, held in enumerate(state) if held is None]
    shapes = []
    for q in qs:
        heads, rows, _ = q.shape
        shapes += [(heads * rows, HD), (heads * rows, 2 * HD)]
    width = qs[0].shape[0] * HD
    sums = [sum(rows for _, _, rows in spans) for spans in final]
    outs = [((rows, width), jnp.bfloat16, HBM) for rows in sums]
    scratch = []
    for parts in groups:
        slots = sum(part.shape[0] for part in parts)
        scratch.append(pltpu.VMEM((slots,) + parts[0].shape[1:], jnp.bfloat16))
    scratch += [pltpu.VMEM((rows, width), jnp.bfloat16) for rows in sums]
    parts = [part for parts in groups for part in parts]
    sizes = [len(parts) for parts in groups]
    inputs, aliases = [table, *qs, *parts], {}
    for at, pair in enumerate(state):
        for half, array in enumerate(pair or ()):
            aliases[len(inputs)] = len(outs) + 2 * at + half
            inputs.append(array)
    results = call(
        functools.partial(attention_kernel, plan, q_chunks, k_chunks, sizes, fresh, final),
        "attention",
        20,
        [SMEM] + [VMEM] * (len(inputs) - 1),
        outs + [(shape, jnp.float32, VMEM) for shape in shapes],
        scratch + [pltpu.SemaphoreType.DMA((len(parts) + len(outs),))],
        *inputs,
        aliases=aliases,
    )
    if final:
        return results[: len(final)]
    return [tuple(results[2 * at : 2 * at + 2]) for at in range(len(qs))]


def fetch(copies, lefts, left, pieces, rows, weights, chunks):
    columns = lefts[0].shape[1]
    step = weights.shape[1] // chunks
    first = [
        copies.start(part, left.at[:, pl.ds(at * columns, columns)])
        for at, part in enumerate(lefts)
    ]
    waits = []
    for chunk in range(chunks):
        lanes = pl.ds(chunk * step, step)
        waits.append(
            [
                copies.start(piece.at[:, lanes], weights.at[pl.ds(row, piece.shape[0]), lanes])
                for row, piece in zip(rows, pieces)
            ]
        )
    waits[0] += first
    return waits


def near_kernel(chunks, *refs):
    lefts, pieces = refs[:2], refs[2:4]
    out, left, weights, semaphores = refs[4:]
    copies = Copies(semaphores)
    rows = [0, pieces[0].shape[0]]
    waits = fetch(copies, lefts, left, pieces, rows, weights, chunks)
    step = out.shape[1] // chunks
    for chunk in range(chunks):
        for copy in waits[chunk]:
            copy.wait()
        lanes = pl.ds(chunk * step, step)
        out[:, lanes] = jnp.dot(
            left[...], weights[:, lanes], preferred_element_type=jnp.float32
        ).astype(jnp.bfloat16)


def output_near(lefts, pieces, chunks=6):
    (rows, columns), (depth, width) = lefts[0].shape, pieces[0].shape
    bf16 = jnp.bfloat16
    return call(
        functools.partial(near_kernel, chunks),
        "output_near",
        16,
        [HBM] * 4,
        [((rows, width), bf16, VMEM)],
        [
            pltpu.VMEM((rows, 2 * columns), bf16),
            pltpu.VMEM((2 * depth, width), bf16),
            pltpu.SemaphoreType.DMA((2 + 2 * chunks,)),
        ],
        *lefts,
        *pieces,
    )[0]


def output_kernel(count, at, chunks, table, *refs):
    lefts, pieces = refs[:2], refs[2 : 2 + count]
    hidden, near, gain, out, left, weights, held, projected, semaphores = refs[2 + count :]
    copies = Copies(semaphores)
    depth = left.shape[1] // 2
    size = pieces[0].shape[0]
    each = depth // size
    rows = [
        pl.multiple_of(index // each * depth + table[at + index % each] * size, size)
        for index in range(count)
    ]
    waits = fetch(copies, lefts, left, pieces, rows, weights, chunks)
    width = hidden.shape[1]
    step = width // chunks
    late = copies.start(hidden, held)
    square = jnp.zeros((hidden.shape[0], 128), jnp.float32)
    for chunk in range(chunks):
        for copy in waits[chunk]:
            copy.wait()
        lanes = pl.ds(chunk * step, step)
        total = near[:, lanes].astype(jnp.float32) + jnp.dot(
            left[...], weights[:, lanes], preferred_element_type=jnp.float32
        )
        projected[:, lanes] = total
        for lane in range(0, step, 128):
            part = total[:, lane : lane + 128]
            square = square + part * part
    mean = jnp.sum(square, axis=1, keepdims=True) / width
    scale = lax.rsqrt(mean + EPS)
    late.wait()
    stores = []
    for chunk in range(chunks):
        lanes = pl.ds(chunk * step, step)
        normed = projected[:, lanes] * scale * gain[:, lanes]
        held[:, lanes] = (held[:, lanes].astype(jnp.float32) + normed).astype(jnp.bfloat16)
        stores.append(copies.start(held.at[:, lanes], out.at[:, lanes]))
    for store in stores:
        store.wait()


def output(table, at, lefts, pieces, near, hidden, gain, chunks=6):
    rows, width = hidden.shape
    columns = lefts[0].shape[1]
    bf16 = jnp.bfloat16
    return call(
        functools.partial(output_kernel, len(pieces), at, chunks),
        "output_norm",
        24,
        [SMEM] + [HBM] * (2 + len(pieces) + 1) + [VMEM] * 2,
        [((rows, width), bf16, HBM)],
        [
            pltpu.VMEM((rows, 2 * columns), bf16),
            pltpu.VMEM((2 * columns, width), bf16),
            pltpu.VMEM((rows, width), bf16),
            pltpu.VMEM((rows, width), jnp.float32),
            pltpu.SemaphoreType.DMA((3 + (len(pieces) + 1) * chunks,)),
        ],
        table,
        *lefts,
        *pieces,
        hidden,
        near,
        gain,
    )[0]


def rotary_table(positions):
    half = HD // 2
    frequency = jnp.power(
        jnp.float32(10000.0), -jnp.arange(half, dtype=jnp.float32) * (2.0 / HD)
    )
    angles = positions.astype(jnp.float32)[:, None] * frequency[None, :]
    cos, sin = jnp.cos(angles), jnp.sin(angles)
    return jnp.concatenate([cos, cos, -sin, sin], axis=1)


def lookup(block_of, index):
    ids = jnp.arange(block_of.shape[0], dtype=jnp.int32)
    return jnp.sum(jnp.where(index[..., None] == ids, block_of, 0), axis=-1)


def flipped(array, axis, bit):
    size = lax.axis_size(axis)
    return lax.ppermute(array, axis, [(i, i ^ bit) for i in range(size)])


def along_line(array):
    size = lax.axis_size("seq")
    parts = [array[None]]
    for by in range(1, size):
        part = lax.ppermute(array, "seq", [(i, (i + by) % size) for i in range(size)])
        parts.append(Came(part[None]))
    return parts


def came(parts):
    return [part.array for part in parts if isinstance(part, Came)]


def after(array, *others):
    return lax.optimization_barrier((array, *others))[0]


def two_chips(hidden, pre_gain, post_gain, wq, wk, wv, w_out, block_of):
    rows = hidden.shape[0]
    block_rows = 2 * rows
    cuts = [rows // 3 * 2, rows // 3]
    lines, groups = lax.axis_size("seq"), lax.axis_size("groups")
    seq, tp, group = lax.axis_index("seq"), lax.axis_index("tp"), lax.axis_index("groups")
    chip, core = tp // 2, tp % 2

    line = (seq - jnp.arange(lines, dtype=jnp.int32)) % lines
    near_starts = lookup(block_of, 2 * line + chip) * block_rows
    far_starts = lookup(block_of, 2 * line + 1 - chip) * block_rows
    mine, beside = seq % 2, 1 - seq % 2
    quarters = [(group, mine), (1 - group, mine), (group, beside), (1 - group, beside)]
    quarters = [2 * a + b for a, b in quarters]
    scalars = jnp.stack([core, *quarters]).astype(jnp.int32)
    table = jnp.concatenate([scalars, near_starts, far_starts])
    quarter_at, near_at, far_at = 1, 5, 5 + lines

    share = w_out.shape[0] // 4
    own_head, own_tail, w_quarter = norm(table, hidden, pre_gain, w_out, cuts, share)
    w_quarter = flipped(w_quarter, "tp", 2)
    head, tail = flipped(after(own_head, w_quarter), "tp", 2), flipped(own_tail, "tp", 2)
    partner_head, partner_tail = flipped(own_head, "tp", 1), flipped(own_tail, "tp", 1)
    w_partner = flipped(w_out, "tp", 1)
    weights = hold(wq, wk, wv)

    run = [jnp.arange(size, dtype=jnp.int32) for size in cuts]
    place = [core * rows + run[0], (1 - core) * rows + run[0]]
    place += [core * rows + cuts[0] + run[1], (1 - core) * rows + cuts[0] + run[1]]
    place = jnp.concatenate(place)
    trig = rotary_table(jnp.concatenate([near_starts[0] + place, far_starts[0] + place]))
    head_runs = [(0, 0, cuts[0]), (1, 0, cuts[0])]
    tail_runs = [(0, cuts[0], cuts[1]), (1, cuts[0], cuts[1])]
    near_chunk = Chunk(near_at, head_runs + tail_runs, rows)
    head_chunk, tail_chunk = Chunk(far_at, head_runs, rows), Chunk(far_at, tail_runs, rows)
    others, everyone = list(range(1, lines)), list(range(lines))

    q_near, kv_near = qkv(
        [
            (own_head, 0, cuts[0]),
            (Came(partner_head), 0, cuts[0]),
            (own_tail, 0, cuts[1]),
            (Came(after(partner_tail, w_partner)), 0, cuts[1]),
        ],
        weights,
        trig,
        0,
    )
    near = along_line(kv_near)
    swap = lambda array: flipped(array, "groups", 1)
    w_other = swap(w_quarter)
    w_beside = lax.ppermute(
        after(w_quarter, *came(near)), "seq", [(i, i ^ 1) for i in range(lines)]
    )
    w_last = swap(w_beside)
    cross_early = [flipped(piece, "tp", 1) for piece in (w_quarter, w_other)]
    cross_beside = flipped(w_beside, "tp", 1)
    q_near = after(q_near, w_other)
    (near_state,) = attention(
        [Step(0, 0, others, same=0)], table, [q_near], [near_chunk], [near], [near_chunk], [None]
    )

    sizes = [cuts[0] * 3 // 8, cuts[0] * 3 // 8, cuts[0] // 4]
    pieces = list(zip((0, sizes[0], sizes[0] + sizes[1]), sizes))
    head = after(head, *near_state)
    q_head, kv_head = qkv(
        [(Came(head), 0, cuts[0])]
        + [
            (Came(flipped(head[at : at + size], "tp", 1)), 0, size)
            for at, size in pieces
        ],
        weights,
        trig,
        block_rows,
    )
    far_head = along_line(kv_head)
    q_head = after(q_head, w_beside)
    (head_state,) = attention(
        [Step(0, 1, [], same=0), Step(0, 0, everyone)],
        table,
        [q_head],
        [head_chunk],
        [near, far_head[:1]],
        [near_chunk, head_chunk],
        [None],
    )

    tail = after(tail, *head_state, *came(far_head))
    q_tail, kv_tail = qkv(
        [(Came(tail), 0, cuts[1]), (Came(flipped(tail, "tp", 1)), 0, cuts[1])],
        weights,
        trig,
        block_rows + 2 * cuts[0],
    )
    far_tail = along_line(kv_tail)
    q_tail = after(q_tail, cross_beside, *cross_early)
    qs, q_chunks = [q_near, q_head, q_tail], [near_chunk, head_chunk, tail_chunk]
    state = attention(
        [
            Step(2, 2, [], same=0),
            Step(2, 0, everyone),
            Step(2, 1, others, same=0),
            Step(0, 1, everyone),
            Step(1, 1, others),
        ],
        table,
        qs,
        q_chunks,
        [near, far_head, far_tail[:1]],
        [near_chunk, head_chunk, tail_chunk],
        [near_state, head_state, None],
    )
    first = 2 * cuts[0]
    to = lambda half: [(0, half * cuts[0], cuts[0]), (0, first + half * cuts[1], cuts[1])]
    over = lambda half: [(1, half * cuts[0], cuts[0]), (2, half * cuts[1], cuts[1])]
    mine, partners, same, cross = attention(
        [
            Step(1, 0, others, same=0, merged=True),
            Step(2, 0, others, merged=True),
            Step(0, 0, everyone, merged=True),
        ],
        table,
        qs,
        q_chunks,
        [far_tail],
        [tail_chunk],
        state,
        final=[to(0), to(1), over(0), over(1)],
    )
    cross, same = flipped(cross, "tp", 3), flipped(same, "tp", 2)
    near_sum = output_near([mine, Came(flipped(partners, "tp", 1))], [w_out, Came(w_partner)])
    w_last = after(w_last, mine)
    quarters = [w_quarter, w_other, w_beside, w_last]
    quarters += [*cross_early, cross_beside, flipped(w_last, "tp", 1)]
    return output(
        table,
        quarter_at,
        [Came(same), Came(cross)],
        [Came(piece) for piece in quarters],
        near_sum,
        hidden,
        post_gain.reshape(1, -1),
    )


def any_count(hidden, pre_gain, post_gain, wq, wk, wv, w_out, block_of):
    rows = hidden.shape[0]
    lines = lax.axis_size("seq")
    line = (lax.axis_index("seq") - jnp.arange(lines, dtype=jnp.int32)) % lines
    block = (2 * line[:, None] + jnp.arange(2, dtype=jnp.int32)).reshape(-1)
    block_rows = rows * lax.axis_size("tp") // 2
    starts = lookup(block_of, block) * block_rows
    table = jnp.concatenate([jnp.zeros(2, jnp.int32), starts])
    normed = norm(table, hidden, pre_gain, w_out, [rows], 16, 1)[0]
    normed = lax.all_gather(normed, "tp", axis=0, tiled=True)
    place = jnp.arange(block_rows, dtype=jnp.int32)
    trig = rotary_table((starts[:2, None] + place).reshape(-1))
    weights = hold(wq, wk, wv)
    qs, keys_values = [], []
    for at in range(2):
        first = at * block_rows
        q, kv = qkv([(normed, first, block_rows)], weights, trig, first)
        qs.append(q)
        keys_values.append(kv)
    kv = lax.all_gather(jnp.stack(keys_values), "seq")[line].reshape(-1, block_rows, 2 * HD)
    rest = list(range(2, 2 * lines))
    runs = [(0, 0, block_rows)]
    attended = attention(
        [Step(0, 0, [1], same=0), Step(1, 0, [0], same=1), Step(0, 0, rest), Step(1, 0, rest)],
        table,
        qs,
        [Chunk(2, runs, 0), Chunk(3, runs, 0)],
        [[kv]],
        [Chunk(2, runs, 0)],
        [None, None],
        final=[[(0, 0, block_rows), (1, 0, block_rows)]],
    )[0]
    partial = jnp.dot(attended, w_out, preferred_element_type=jnp.float32)
    summed = lax.psum_scatter(
        partial.astype(jnp.bfloat16), "tp", scatter_dimension=0, tiled=True
    ).astype(jnp.float32)
    mean = jnp.mean(summed * summed, axis=-1, keepdims=True)
    projected = summed * lax.rsqrt(mean + EPS) * post_gain
    return (hidden.astype(jnp.float32) + projected).astype(jnp.bfloat16)


def solution(mesh):
    return jax.shard_map(
        two_chips if mesh.shape["tp"] == 4 else any_count,
        mesh=mesh,
        in_specs=(
            P(("groups", "seq", "tp"), None),
            P(),
            P(),
            P(None, "tp"),
            P(None, "tp"),
            P(None, "tp"),
            P("tp", None),
            P(),
        ),
        out_specs=P(("groups", "seq", "tp"), None),
        check_vma=False,
    )
```

```python
import functools
import math

import jax
import jax.numpy as jnp
from jax import lax
from jax.experimental import pallas as pl
from jax.experimental.pallas import tpu as pltpu
from jax.sharding import PartitionSpec as P

HD = 128
ATT_SCALAR = 144
EPS = 1e-6
MIB = 1024 * 1024
HIDDEN = -1e30
COST = pl.CostEstimate(flops=1, bytes_accessed=1, transcendentals=0)

ANY = pl.BlockSpec(memory_space=pl.ANY)
HBM = pl.BlockSpec(memory_space=pltpu.HBM)
VMEM = pl.BlockSpec(memory_space=pltpu.VMEM)
SMEM = pl.BlockSpec(memory_space=pltpu.SMEM)


class Came:
    def __init__(self, array):
        self.array, self.shape = array, array.shape


def call(kernel, name, mib, in_specs, outs, scratch, *args, aliases=None):
    in_specs, pinned = list(in_specs), []
    for at, arg in enumerate(args):
        if isinstance(arg, Came):
            arg, in_specs[at] = arg.array, ANY
        elif in_specs[at] is not SMEM:
            arg = pltpu.with_memory_space_constraint(arg, in_specs[at].memory_space)
        pinned.append(arg)
    return pl.pallas_call(
        kernel,
        in_specs=in_specs,
        out_specs=[spec for _, _, spec in outs],
        out_shape=[spec.memory_space(shape, dtype) for shape, dtype, spec in outs],
        scratch_shapes=scratch,
        input_output_aliases=aliases or {},
        compiler_params=pltpu.CompilerParams(vmem_limit_bytes=mib * MIB),
        cost_estimate=COST,
        name=name,
    )(*pinned)


class Copies:
    def __init__(self, semaphores):
        self.semaphores, self.used = semaphores, 0

    def start(self, source, target):
        copy = pltpu.make_async_copy(source, target, self.semaphores.at[self.used])
        self.used += 1
        copy.start()
        return copy


def norm_kernel(cuts, pieces, hidden, gain, *refs):
    parts, (rows, staged, semaphores) = refs[: len(cuts)], refs[len(cuts) :]
    copies = Copies(semaphores)
    count, width = hidden.shape
    step = count // pieces
    spans = [pl.ds(at * step, step) for at in range(pieces)]
    ins = [copies.start(hidden.at[span], rows.at[span]) for span in spans]
    scale = gain[...].reshape(1, width)
    outs = []
    for at, span in enumerate(spans):
        ins[at].wait()
        x = rows[span, :].astype(jnp.float32)
        square = x * x
        folded = square[:, :128]
        for lane in range(128, width, 128):
            folded = folded + square[:, lane : lane + 128]
        mean = jnp.sum(folded, axis=1, keepdims=True) / width
        staged[span, :] = (x * lax.rsqrt(mean + EPS) * scale).astype(jnp.bfloat16)
        begin = 0
        for cut, part in zip(cuts, parts):
            if begin <= at * step < begin + cut:
                inside = pl.ds(at * step - begin, step)
                outs.append(copies.start(staged.at[span], part.at[inside]))
            begin += cut
    for copy in outs:
        copy.wait()


def norm(hidden, gain, cuts, pieces=3):
    rows, width = hidden.shape
    bf16 = jnp.bfloat16
    return call(
        functools.partial(norm_kernel, cuts, pieces),
        "norm_rows",
        12,
        [HBM, VMEM],
        [((cut, width), bf16, HBM) for cut in cuts],
        [
            pltpu.VMEM((rows, width), bf16),
            pltpu.VMEM((rows, width), bf16),
            pltpu.SemaphoreType.DMA((2 * pieces,)),
        ],
        hidden,
        gain,
    )


def hold_kernel(wq, wk, wv, out, semaphores):
    copies, column, waits = Copies(semaphores), 0, []
    for weight in (wq, wk, wv):
        count = weight.shape[1]
        waits.append(copies.start(weight, out.at[:, pl.ds(column, count)]))
        column += count
    for copy in waits:
        copy.wait()


def hold(wq, wk, wv):
    shape = (wq.shape[0], wq.shape[1] + wk.shape[1] + wv.shape[1])
    return call(
        hold_kernel,
        "hold_weights",
        1,
        [HBM] * 3,
        [(shape, wq.dtype, VMEM)],
        [pltpu.SemaphoreType.DMA((3,))],
        wq,
        wk,
        wv,
    )[0]


def qkv_kernel(runs, first, weights, trig, *refs):
    parts = refs[: len(runs)]
    q, kv, rows, angles, semaphores = refs[len(runs) :]
    copies, put, waits = Copies(semaphores), 0, []
    for part, (begin, count) in zip(parts, runs):
        target = rows.at[pl.ds(put, count)]
        waits.append(copies.start(part.at[pl.ds(begin, count)], target))
        put += count
    waits.append(copies.start(trig.at[pl.ds(first, put)], angles))
    for copy in waits:
        copy.wait()
    product = jnp.dot(rows[...], weights[...], preferred_element_type=jnp.float32)
    cos, sin = angles[:, :HD], angles[:, HD:]
    queries = weights.shape[1] - 2 * HD

    def rotated(at):
        y = product[:, at : at + HD]
        return y * cos + pltpu.roll(y, HD // 2, 1) * sin

    factor = ATT_SCALAR ** (-0.5) * math.log2(math.e)
    kv[:, :HD] = rotated(queries).astype(jnp.bfloat16)
    kv[:, HD:] = product[:, queries + HD :].astype(jnp.bfloat16)
    for head in range(queries // HD):
        q[head] = (rotated(head * HD) * factor).astype(jnp.bfloat16)


def qkv(parts, weights, trig, first):
    total = sum(count for _, _, count in parts)
    width, columns = weights.shape
    heads = columns // HD - 2
    runs = [(begin, count) for _, begin, count in parts]
    return call(
        functools.partial(qkv_kernel, runs, first),
        "qkv",
        12,
        [VMEM] + [HBM] * (len(parts) + 1),
        [((heads, total, HD), jnp.bfloat16, VMEM), ((total, 2 * HD), jnp.bfloat16, VMEM)],
        [
            pltpu.VMEM((total, width), jnp.bfloat16),
            pltpu.VMEM((total, 2 * HD), jnp.float32),
            pltpu.SemaphoreType.DMA((len(parts) + 1,)),
        ],
        weights,
        trig,
        *[array for array, _, _ in parts],
    )


class Step:
    def __init__(self, q, group, slots, same=None, merged=False):
        self.q, self.group, self.slots = q, group, slots
        self.same, self.merged = same, merged


class Chunk:
    def __init__(self, at, runs, share):
        self.at, self.runs, self.share = at, runs, share

    def places(self, core, axis, first, size):
        shape = (size, 1) if axis == 0 else (1, size)
        index = first + lax.broadcasted_iota(jnp.int32, shape, axis)
        result, begin = index, 0
        for which, offset, rows in self.runs:
            base = (core if which == 0 else 1 - core) * self.share + offset - begin
            inside = (index >= begin) & (index < begin + rows)
            result = jnp.where(inside, index + base, result)
            begin += rows
        return result


def attention_kernel(plan, q_chunks, k_chunks, group_parts, fresh, final, table, *refs):
    refs = list(refs)
    take = lambda n: [refs.pop(0) for _ in range(n)]
    count = len(q_chunks)
    qs = take(count)
    kv_parts = [take(n) for n in group_parts]
    take(2 * (count - len(fresh)))
    outs = take(len(final))
    states = [take(2) for _ in range(count)]
    kvs, staged = take(len(group_parts)), take(len(final))
    (semaphores,) = refs
    copies = Copies(semaphores)
    core = table[0]
    waits = {}
    for group, (parts, kv) in enumerate(zip(kv_parts, kvs)):
        each = kv.shape[0] // len(parts)
        waits[group] = [
            copies.start(part, kv.at[pl.ds(slot * each, each)])
            for slot, part in enumerate(parts)
        ]

    def ready(group):
        for copy in waits.pop(group, []):
            copy.wait()

    def attend(q, keys_values, begin, visible=None, bias=None):
        q_ref, (peak, acc) = qs[q], states[q]
        heads, rows, _ = q_ref.shape
        keys, values = keys_values[:, :HD], keys_values[:, HD:]
        values = jnp.concatenate([values, jnp.ones_like(values)], axis=1)
        count = keys.shape[0]
        tile = min(rows, 128)
        for first in range(0, rows, tile):
            q_tile = q_ref[:, first : first + tile, :].reshape(heads * tile, HD)
            scores = lax.dot_general(
                q_tile, keys, (((1,), (1,)), ((), ())), preferred_element_type=jnp.float32
            )
            if visible is not None:
                seen = jnp.concatenate([visible(first, tile)] * heads, axis=0)
                scores = jnp.where(seen, scores, HIDDEN)
            if bias is not None:
                scores = scores + bias
            top = jnp.max(scores, axis=1, keepdims=True)
            top = jnp.broadcast_to(top, (heads * tile, HD))
            span = pl.ds(first * heads, heads * tile)
            if not begin:
                before = peak[span, :]
                top = jnp.maximum(before, top)
            wide = jnp.concatenate([top] * (count // HD), axis=1)
            weights = jnp.exp2(scores - wide).astype(jnp.bfloat16)
            summed = jnp.dot(weights, values, preferred_element_type=jnp.float32)
            if not begin:
                fade = jnp.exp2(before - top)
                summed = summed + acc[span, :] * jnp.concatenate([fade, fade], axis=1)
            acc[span, :] = summed
            peak[span, :] = top

    begun = set(range(count)) - set(fresh)
    for step in plan:
        q, group, kv = step.q, step.group, kvs[step.group]
        q_chunk, k_chunk = q_chunks[q], k_chunks[group]
        if step.same is not None:
            keys_at = k_chunk.places(core, 1, 0, kv.shape[1])
            visible = lambda first, tile: keys_at <= q_chunk.places(core, 0, first, tile)
            own = kv_parts[group][0]
            attend(q, own[step.same], q not in begun, visible=visible)
            begun.add(q)
        start = table[q_chunk.at]
        slots = step.slots
        if not slots:
            continue
        ready(group)
        if step.merged:
            shown = [table[k_chunk.at + slot] < start for slot in slots]

            @pl.when(functools.reduce(jnp.logical_or, shown))
            def _():
                rows = kv.shape[1]
                bias = [
                    jnp.where(see, 0.0, HIDDEN) * jnp.ones((1, rows), jnp.float32)
                    for see in shown
                ]
                keys_values = kv[slots[0] : slots[-1] + 1].reshape(len(slots) * rows, 2 * HD)
                attend(q, keys_values, False, bias=jnp.concatenate(bias, axis=1))

        else:

            def one(slot, carry):
                @pl.when(table[k_chunk.at + slot] < start)
                def _():
                    attend(q, kv[slot], False)

                return carry

            lax.fori_loop(slots[0], slots[-1] + 1, one, 0)

    for group in list(waits):
        ready(group)
    stores = []
    for out, stage, spans in zip(outs, staged, final):
        put = 0
        for q, first, rows in spans:
            acc = states[q][1]
            heads, q_rows, _ = qs[q].shape
            tile = min(q_rows, 128)
            size = min(tile, rows)
            for head in range(heads):
                for at in range(first, first + rows, size):
                    begin = at // tile * tile * heads + head * tile + at % tile
                    part = acc[begin : begin + size, :]
                    to = put + at - first
                    stage[to : to + size, head * HD : (head + 1) * HD] = (
                        part[:, :HD] / part[:, HD:]
                    ).astype(jnp.bfloat16)
            put += rows
        stores.append(copies.start(stage, out))
    for copy in stores:
        copy.wait()


def attention(plan, table, qs, q_chunks, groups, k_chunks, state, final=()):
    fresh = [at for at, held in enumerate(state) if held is None]
    shapes = []
    for q in qs:
        heads, rows, _ = q.shape
        shapes += [(heads * rows, HD), (heads * rows, 2 * HD)]
    width = qs[0].shape[0] * HD
    sums = [sum(rows for _, _, rows in spans) for spans in final]
    outs = [((rows, width), jnp.bfloat16, HBM) for rows in sums]
    scratch = []
    for parts in groups:
        slots = sum(part.shape[0] for part in parts)
        scratch.append(pltpu.VMEM((slots,) + parts[0].shape[1:], jnp.bfloat16))
    scratch += [pltpu.VMEM((rows, width), jnp.bfloat16) for rows in sums]
    parts = [part for parts in groups for part in parts]
    sizes = [len(parts) for parts in groups]
    inputs, aliases = [table, *qs, *parts], {}
    for at, pair in enumerate(state):
        for half, array in enumerate(pair or ()):
            aliases[len(inputs)] = len(outs) + 2 * at + half
            inputs.append(array)
    results = call(
        functools.partial(attention_kernel, plan, q_chunks, k_chunks, sizes, fresh, final),
        "attention",
        20,
        [SMEM] + [VMEM] * (len(inputs) - 1),
        outs + [(shape, jnp.float32, VMEM) for shape in shapes],
        scratch + [pltpu.SemaphoreType.DMA((len(parts) + len(outs),))],
        *inputs,
        aliases=aliases,
    )
    if final:
        return results[: len(final)]
    return [tuple(results[2 * at : 2 * at + 2]) for at in range(len(qs))]


def cut_kernel(pieces, at, table, weights, *refs):
    outs, (held, semaphores) = refs[:pieces], refs[pieces:]
    copies = Copies(semaphores)
    size = outs[0].shape[0]
    half = size * pieces
    first = pl.multiple_of(table[at] * half, half)
    ins = [
        copies.start(
            weights.at[pl.ds(first + piece * size, size)], held.at[pl.ds(piece * size, size)]
        )
        for piece in range(pieces)
    ]
    stores = []
    for piece in range(pieces):
        ins[piece].wait()
        stores.append(copies.start(held.at[pl.ds(piece * size, size)], outs[piece]))
    for copy in stores:
        copy.wait()


def cut(table, at, weights, pieces):
    depth, width = weights.shape
    size = depth // 2 // pieces
    return call(
        functools.partial(cut_kernel, pieces, at),
        "cut_weights",
        4,
        [SMEM, HBM],
        [((size, width), weights.dtype, HBM)] * pieces,
        [
            pltpu.VMEM((depth // 2, width), weights.dtype),
            pltpu.SemaphoreType.DMA((2 * pieces,)),
        ],
        table,
        weights,
    )


def near_kernel(chunks, left_hbm, weights_hbm, out, left, weights, semaphores):
    copies = Copies(semaphores)
    step = out.shape[1] // chunks
    first = copies.start(left_hbm, left)
    lanes = [pl.ds(chunk * step, step) for chunk in range(chunks)]
    waits = [copies.start(weights_hbm.at[:, at], weights.at[:, at]) for at in lanes]
    first.wait()
    for at, copy in zip(lanes, waits):
        copy.wait()
        out[:, at] = jnp.dot(left[...], weights[:, at], preferred_element_type=jnp.float32)


def output_near(left, weights, chunks=6):
    (rows, columns), width = left.shape, weights.shape[1]
    return call(
        functools.partial(near_kernel, chunks),
        "output_near",
        12,
        [HBM] * 2,
        [((rows, width), jnp.float32, VMEM)],
        [
            pltpu.VMEM(left.shape, left.dtype),
            pltpu.VMEM(weights.shape, weights.dtype),
            pltpu.SemaphoreType.DMA((1 + chunks,)),
        ],
        left,
        weights,
    )[0]


def send_kernel(at, chunks, table, left_hbm, near, *refs):
    count = len(refs) - 5
    pieces, (out, weights, left, staged, semaphores) = refs[:count], refs[count:]
    copies = Copies(semaphores)
    depth, width = weights.shape
    size = pieces[0].shape[0]
    step = width // chunks
    first = copies.start(left_hbm, left)
    lanes = [pl.ds(chunk * step, step) for chunk in range(chunks)]
    waits = []
    for span in lanes:
        here = []
        for index, piece in enumerate(pieces):
            half = table[at] if index < count // 2 else 1 - table[at]
            row = half * (depth // 2) + index % (count // 2) * size
            target = weights.at[pl.ds(pl.multiple_of(row, size), size), span]
            here.append(copies.start(piece.at[:, span], target))
        waits.append(here)
    first.wait()
    half = left.shape[0] // 2
    stores = []
    for span, here in zip(lanes, waits):
        for copy in here:
            copy.wait()
        staged[:, span] = (
            near[half:, span]
            + jnp.dot(left[half:, :], weights[:, span], preferred_element_type=jnp.float32)
        ).astype(jnp.bfloat16)
        stores.append(copies.start(staged.at[:, span], out.at[:, span]))
    for copy in stores:
        copy.wait()


def output_send(table, at, left, near, pieces, chunks=6):
    (rows, width), columns = near.shape, left.shape[1]
    half, bf16 = (rows // 2, width), jnp.bfloat16
    return call(
        functools.partial(send_kernel, at, chunks),
        "output_send",
        16,
        [SMEM, HBM, VMEM] + [HBM] * len(pieces),
        [(half, bf16, HBM), ((columns, width), bf16, VMEM)],
        [
            pltpu.VMEM(left.shape, bf16),
            pltpu.VMEM(half, bf16),
            pltpu.SemaphoreType.DMA((1 + (len(pieces) + 1) * chunks,)),
        ],
        table,
        left,
        near,
        *pieces,
    )


def keep_kernel(chunks, left_hbm, near, weights, out, left, semaphores):
    Copies(semaphores).start(left_hbm, left).wait()
    half, step = left.shape[0] // 2, out.shape[1] // chunks
    for chunk in range(chunks):
        span = pl.ds(chunk * step, step)
        out[:, span] = near[:half, span] + jnp.dot(
            left[:half, :], weights[:, span], preferred_element_type=jnp.float32
        )


def output_keep(left, near, weights, chunks=6):
    rows, width = near.shape
    return call(
        functools.partial(keep_kernel, chunks),
        "output_keep",
        4,
        [HBM, VMEM, VMEM],
        [((rows // 2, width), jnp.float32, VMEM)],
        [pltpu.VMEM(left.shape, jnp.bfloat16), pltpu.SemaphoreType.DMA((1,))],
        left,
        near,
        weights,
    )[0]


def final_kernel(chunks, received, hidden, kept, gain, out, other, held, semaphores):
    copies = Copies(semaphores)
    width = hidden.shape[1]
    step = width // chunks
    lanes = [pl.ds(chunk * step, step) for chunk in range(chunks)]
    waits = [copies.start(received.at[:, span], other.at[:, span]) for span in lanes]
    late = copies.start(hidden, held)
    square = jnp.zeros((hidden.shape[0], 128), jnp.float32)
    for span, copy in zip(lanes, waits):
        copy.wait()
        total = kept[:, span] + other[:, span].astype(jnp.float32)
        for lane in range(0, step, 128):
            part = total[:, lane : lane + 128]
            square = square + part * part
    mean = jnp.sum(square, axis=1, keepdims=True) / width
    scale = lax.rsqrt(mean + EPS)
    late.wait()
    gains = gain[...].reshape(1, width)
    stores = []
    for chunk, span in enumerate(lanes):
        total = kept[:, span] + other[:, span].astype(jnp.float32)
        normed = total * scale * gains[:, chunk * step : (chunk + 1) * step]
        held[:, span] = (held[:, span].astype(jnp.float32) + normed).astype(jnp.bfloat16)
        stores.append(copies.start(held.at[:, span], out.at[:, span]))
    for store in stores:
        store.wait()


def output(received, kept, hidden, gain, chunks=6):
    rows, width = hidden.shape
    bf16 = jnp.bfloat16
    return call(
        functools.partial(final_kernel, chunks),
        "output_norm",
        12,
        [HBM, HBM, VMEM, VMEM],
        [((rows, width), bf16, HBM)],
        [
            pltpu.VMEM((rows, width), bf16),
            pltpu.VMEM((rows, width), bf16),
            pltpu.SemaphoreType.DMA((1 + 2 * chunks,)),
        ],
        received,
        hidden,
        kept,
        gain,
    )[0]


def rotary_table(positions):
    half = HD // 2
    frequency = jnp.power(
        jnp.float32(10000.0), -jnp.arange(half, dtype=jnp.float32) * (2.0 / HD)
    )
    angles = positions.astype(jnp.float32)[:, None] * frequency[None, :]
    cos, sin = jnp.cos(angles), jnp.sin(angles)
    return jnp.concatenate([cos, cos, -sin, sin], axis=1)


def lookup(block_of, index):
    ids = jnp.arange(block_of.shape[0], dtype=jnp.int32)
    return jnp.sum(jnp.where(index[..., None] == ids, block_of, 0), axis=-1)


def flipped(array, axis, bit):
    size = lax.axis_size(axis)
    return lax.ppermute(array, axis, [(i, i ^ bit) for i in range(size)])


def along_line(array):
    size = lax.axis_size("seq")
    parts = [array[None]]
    for by in range(1, size):
        part = lax.ppermute(array, "seq", [(i, (i + by) % size) for i in range(size)])
        parts.append(Came(part[None]))
    return parts


def came(parts):
    return [part.array for part in parts if isinstance(part, Came)]


def after(array, *others):
    return lax.optimization_barrier((array, *others))[0]


def two_chips(hidden, pre_gain, post_gain, wq, wk, wv, w_out, block_of):
    rows = hidden.shape[0]
    block_rows = 2 * rows
    cuts = [rows // 3 * 2, rows // 3]
    lines, groups = lax.axis_size("seq"), lax.axis_size("groups")
    seq, tp, group = lax.axis_index("seq"), lax.axis_index("tp"), lax.axis_index("groups")
    chip, core = tp // 2, tp % 2

    line = (seq - jnp.arange(lines, dtype=jnp.int32)) % lines
    near_starts = lookup(block_of, 2 * line + chip) * block_rows
    far_starts = lookup(block_of, 2 * line + 1 - chip) * block_rows
    table = jnp.concatenate([jnp.stack([core, group]).astype(jnp.int32), near_starts, far_starts])
    group_at, near_at, far_at = 1, 2, 2 + lines

    own_head, own_tail = norm(hidden, pre_gain, cuts)
    head, tail = flipped(own_head, "tp", 2), flipped(own_tail, "tp", 2)
    partner_head, partner_tail = flipped(own_head, "tp", 1), flipped(own_tail, "tp", 1)
    weights = hold(wq, wk, wv)

    run = [jnp.arange(size, dtype=jnp.int32) for size in cuts]
    place = [core * rows + run[0], (1 - core) * rows + run[0]]
    place += [core * rows + cuts[0] + run[1], (1 - core) * rows + cuts[0] + run[1]]
    place = jnp.concatenate(place)
    trig = rotary_table(jnp.concatenate([near_starts[0] + place, far_starts[0] + place]))
    head_runs = [(0, 0, cuts[0]), (1, 0, cuts[0])]
    tail_runs = [(0, cuts[0], cuts[1]), (1, cuts[0], cuts[1])]
    near_chunk = Chunk(near_at, head_runs + tail_runs, rows)
    head_chunk, tail_chunk = Chunk(far_at, head_runs, rows), Chunk(far_at, tail_runs, rows)
    others, everyone = list(range(1, lines)), list(range(lines))

    q_near, kv_near = qkv(
        [
            (own_head, 0, cuts[0]),
            (Came(partner_head), 0, cuts[0]),
            (own_tail, 0, cuts[1]),
            (Came(partner_tail), 0, cuts[1]),
        ],
        weights,
        trig,
        0,
    )
    near = along_line(kv_near)
    w_cut = cut(table, group_at, after(w_out, kv_near), 4)
    q_near = after(q_near, *w_cut)
    (near_state,) = attention(
        [Step(0, 0, others, same=0)], table, [q_near], [near_chunk], [near], [near_chunk], [None]
    )

    sizes = [cuts[0] * 3 // 8, cuts[0] * 3 // 8, cuts[0] // 4]
    pieces = list(zip((0, sizes[0], sizes[0] + sizes[1]), sizes))
    head = after(head, *near_state)
    q_head, kv_head = qkv(
        [(Came(head), 0, cuts[0])]
        + [
            (Came(flipped(head[at : at + size], "tp", 1)), 0, size)
            for at, size in pieces
        ],
        weights,
        trig,
        block_rows,
    )
    far_head = along_line(kv_head)
    (head_state,) = attention(
        [Step(0, 1, [], same=0), Step(0, 0, everyone)],
        table,
        [q_head],
        [head_chunk],
        [near, far_head[:1]],
        [near_chunk, head_chunk],
        [None],
    )

    tail = after(tail, *head_state, *came(far_head))
    q_tail, kv_tail = qkv(
        [(Came(tail), 0, cuts[1]), (Came(flipped(tail, "tp", 1)), 0, cuts[1])],
        weights,
        trig,
        block_rows + 2 * cuts[0],
    )
    far_tail = along_line(kv_tail)

    w_far = [flipped(after(w_cut[0], head), "tp", 2), flipped(after(w_cut[1], tail), "tp", 2)]
    swap = lambda array: flipped(array, "groups", 1)
    w_far[0] = after(w_far[0], kv_tail)
    w_far.append(flipped(after(w_cut[2], w_far[0]), "tp", 2))
    w_other = [swap(w_far[0])]
    qs, q_chunks = [q_near, q_head, q_tail], [near_chunk, head_chunk, tail_chunk]
    state = attention(
        [
            Step(2, 2, [], same=0),
            Step(2, 0, everyone),
            Step(2, 1, others, same=0),
            Step(0, 1, everyone),
            Step(1, 1, others),
        ],
        table,
        qs,
        q_chunks,
        [near, far_head, far_tail[:1]],
        [near_chunk, head_chunk, tail_chunk],
        [near_state, head_state, None],
    )
    w_far[1] = after(w_far[1], *state[0], *came(far_tail))
    w_far.append(flipped(after(w_cut[3], w_far[1]), "tp", 2))
    w_other.append(swap(w_far[1]))
    state[0] = tuple(after(array, w_other[0]) for array in state[0])
    first = 2 * cuts[0]
    to = lambda half: [(0, half * cuts[0], cuts[0]), (0, first + half * cuts[1], cuts[1])]
    over = lambda half: [(1, half * cuts[0], cuts[0]), (2, half * cuts[1], cuts[1])]
    attended, away = attention(
        [
            Step(1, 0, others, same=0, merged=True),
            Step(2, 0, others, merged=True),
            Step(0, 0, everyone, merged=True),
        ],
        table,
        qs,
        q_chunks,
        [far_tail],
        [tail_chunk],
        state,
        final=[to(0) + to(1), over(0) + over(1)],
    )
    away = flipped(away, "tp", 2)
    near_sum = output_near(after(attended, w_other[1]), w_out)
    w_other += [swap(after(w_far[2], attended)), swap(after(w_far[3], near_sum))]
    pieces = [Came(piece) for piece in w_far + w_other]
    sent, w_laid = output_send(table, group_at, Came(away), near_sum, pieces)
    received = flipped(sent, "tp", 1)
    kept = output_keep(Came(away), near_sum, w_laid)
    return output(Came(received), kept, hidden, post_gain)


def any_count(hidden, pre_gain, post_gain, wq, wk, wv, w_out, block_of):
    rows = hidden.shape[0]
    lines = lax.axis_size("seq")
    line = (lax.axis_index("seq") - jnp.arange(lines, dtype=jnp.int32)) % lines
    block = (2 * line[:, None] + jnp.arange(2, dtype=jnp.int32)).reshape(-1)
    block_rows = rows * lax.axis_size("tp") // 2
    starts = lookup(block_of, block) * block_rows
    table = jnp.concatenate([jnp.zeros(2, jnp.int32), starts])
    normed = norm(hidden, pre_gain, [rows], 1)[0]
    normed = lax.all_gather(normed, "tp", axis=0, tiled=True)
    place = jnp.arange(block_rows, dtype=jnp.int32)
    trig = rotary_table((starts[:2, None] + place).reshape(-1))
    weights = hold(wq, wk, wv)
    qs, keys_values = [], []
    for at in range(2):
        first = at * block_rows
        q, kv = qkv([(normed, first, block_rows)], weights, trig, first)
        qs.append(q)
        keys_values.append(kv)
    kv = lax.all_gather(jnp.stack(keys_values), "seq")[line].reshape(-1, block_rows, 2 * HD)
    rest = list(range(2, 2 * lines))
    runs = [(0, 0, block_rows)]
    attended = attention(
        [Step(0, 0, [1], same=0), Step(1, 0, [0], same=1), Step(0, 0, rest), Step(1, 0, rest)],
        table,
        qs,
        [Chunk(2, runs, 0), Chunk(3, runs, 0)],
        [[kv]],
        [Chunk(2, runs, 0)],
        [None, None],
        final=[[(0, 0, block_rows), (1, 0, block_rows)]],
    )[0]
    partial = jnp.dot(attended, w_out, preferred_element_type=jnp.float32)
    summed = lax.psum_scatter(
        partial.astype(jnp.bfloat16), "tp", scatter_dimension=0, tiled=True
    ).astype(jnp.float32)
    mean = jnp.mean(summed * summed, axis=-1, keepdims=True)
    projected = summed * lax.rsqrt(mean + EPS) * post_gain
    return (hidden.astype(jnp.float32) + projected).astype(jnp.bfloat16)


def solution(mesh):
    return jax.shard_map(
        two_chips if mesh.shape["tp"] == 4 else any_count,
        mesh=mesh,
        in_specs=(
            P(("groups", "seq", "tp"), None),
            P(),
            P(),
            P(None, "tp"),
            P(None, "tp"),
            P(None, "tp"),
            P("tp", None),
            P(),
        ),
        out_specs=P(("groups", "seq", "tp"), None),
        check_vma=False,
    )
```

```python
import functools
import math

import jax
import jax.numpy as jnp
from jax import lax
from jax.experimental import pallas as pl
from jax.experimental.pallas import tpu as pltpu
from jax.sharding import PartitionSpec as P

HD = 128
ATT_SCALAR = 144
EPS = 1e-6
MIB = 1024 * 1024
HIDDEN = -1e30
COST = pl.CostEstimate(flops=1, bytes_accessed=1, transcendentals=0)

ANY = pl.BlockSpec(memory_space=pl.ANY)
HBM = pl.BlockSpec(memory_space=pltpu.HBM)
VMEM = pl.BlockSpec(memory_space=pltpu.VMEM)
SMEM = pl.BlockSpec(memory_space=pltpu.SMEM)


class Came:
    def __init__(self, array):
        self.array, self.shape = array, array.shape


def call(kernel, name, mib, in_specs, outs, scratch, *args, aliases=None):
    in_specs, pinned = list(in_specs), []
    for at, arg in enumerate(args):
        if isinstance(arg, Came):
            arg, in_specs[at] = arg.array, ANY
        elif in_specs[at] is not SMEM:
            arg = pltpu.with_memory_space_constraint(arg, in_specs[at].memory_space)
        pinned.append(arg)
    return pl.pallas_call(
        kernel,
        in_specs=in_specs,
        out_specs=[spec for _, _, spec in outs],
        out_shape=[spec.memory_space(shape, dtype) for shape, dtype, spec in outs],
        scratch_shapes=scratch,
        input_output_aliases=aliases or {},
        compiler_params=pltpu.CompilerParams(vmem_limit_bytes=mib * MIB),
        cost_estimate=COST,
        name=name,
    )(*pinned)


class Copies:
    def __init__(self, semaphores):
        self.semaphores, self.used = semaphores, 0

    def start(self, source, target):
        copy = pltpu.make_async_copy(source, target, self.semaphores.at[self.used])
        self.used += 1
        copy.start()
        return copy


def norm_kernel(cuts, pieces, hidden, gain, *refs):
    parts, (rows, staged, semaphores) = refs[: len(cuts)], refs[len(cuts) :]
    copies = Copies(semaphores)
    count, width = hidden.shape
    step = count // pieces
    spans = [pl.ds(at * step, step) for at in range(pieces)]
    ins = [copies.start(hidden.at[span], rows.at[span]) for span in spans]
    scale = gain[...].reshape(1, width)
    outs = []
    for at, span in enumerate(spans):
        ins[at].wait()
        x = rows[span, :].astype(jnp.float32)
        square = x * x
        folded = square[:, :128]
        for lane in range(128, width, 128):
            folded = folded + square[:, lane : lane + 128]
        mean = jnp.sum(folded, axis=1, keepdims=True) / width
        staged[span, :] = (x * lax.rsqrt(mean + EPS) * scale).astype(jnp.bfloat16)
        begin = 0
        for cut, part in zip(cuts, parts):
            if begin <= at * step < begin + cut:
                inside = pl.ds(at * step - begin, step)
                outs.append(copies.start(staged.at[span], part.at[inside]))
            begin += cut
    for copy in outs:
        copy.wait()


def norm(hidden, gain, cuts, pieces=3):
    rows, width = hidden.shape
    bf16 = jnp.bfloat16
    return call(
        functools.partial(norm_kernel, cuts, pieces),
        "norm_rows",
        12,
        [HBM, VMEM],
        [((cut, width), bf16, HBM) for cut in cuts],
        [
            pltpu.VMEM((rows, width), bf16),
            pltpu.VMEM((rows, width), bf16),
            pltpu.SemaphoreType.DMA((2 * pieces,)),
        ],
        hidden,
        gain,
    )


def rotate_into(product, angles, q, kv):
    cos, sin = angles[:, :HD], angles[:, HD:]
    queries = product.shape[1] - 2 * HD

    def rotated(at):
        y = product[:, at : at + HD]
        return y * cos + pltpu.roll(y, HD // 2, 1) * sin

    factor = ATT_SCALAR ** (-0.5) * math.log2(math.e)
    kv[:, :HD] = rotated(queries).astype(jnp.bfloat16)
    kv[:, HD:] = product[:, queries + HD :].astype(jnp.bfloat16)
    for head in range(queries // HD):
        q[head] = (rotated(head * HD) * factor).astype(jnp.bfloat16)


def first_qkv_kernel(count, first, chunks, trig, wq, wk, wv, *refs):
    parts = refs[:count]
    q, kv, weights, rows, angles, semaphores = refs[count:]
    copies, put, waits = Copies(semaphores), 0, []
    for part in parts:
        waits.append(copies.start(part, rows.at[pl.ds(put, part.shape[0])]))
        put += part.shape[0]
    depth = weights.shape[0] // chunks
    later = []
    for chunk in range(chunks):
        span, column, here = pl.ds(chunk * depth, depth), 0, []
        for weight in (wq, wk, wv):
            target = weights.at[span, pl.ds(column, weight.shape[1])]
            here.append(copies.start(weight.at[span], target))
            column += weight.shape[1]
        later.append(here)
    late = copies.start(trig.at[pl.ds(first, put)], angles)
    for copy in waits:
        copy.wait()
    product = None
    for chunk, here in enumerate(later):
        for copy in here:
            copy.wait()
        span = pl.ds(chunk * depth, depth)
        term = jnp.dot(rows[:, span], weights[span, :], preferred_element_type=jnp.float32)
        product = term if product is None else product + term
    late.wait()
    rotate_into(product, angles, q, kv)


def qkv_kernel(count, first, trig, weights, *refs):
    parts = refs[:count]
    q, kv, rows, angles, semaphores = refs[count:]
    copies, put, waits = Copies(semaphores), 0, []
    for part in parts:
        waits.append(copies.start(part, rows.at[pl.ds(put, part.shape[0])]))
        put += part.shape[0]
    waits.append(copies.start(trig.at[pl.ds(first, put)], angles))
    for copy in waits:
        copy.wait()
    product = jnp.dot(rows[...], weights[...], preferred_element_type=jnp.float32)
    rotate_into(product, angles, q, kv)


def qkv(parts, weights, trig, first, chunks=4):
    total, width = sum(part.shape[0] for part in parts), parts[0].shape[1]
    loads = isinstance(weights, tuple)
    if loads:
        kernel = functools.partial(first_qkv_kernel, len(parts), first, chunks)
        given, columns = weights, sum(weight.shape[1] for weight in weights)
    else:
        kernel = functools.partial(qkv_kernel, len(parts), first)
        given, columns = (weights,), weights.shape[1]
    heads, bf16 = columns // HD - 2, jnp.bfloat16
    outs = [((heads, total, HD), bf16, VMEM), ((total, 2 * HD), bf16, VMEM)]
    return call(
        kernel,
        "qkv",
        14,
        [HBM] + [HBM if loads else VMEM] * len(given) + [HBM] * len(parts),
        outs + [((width, columns), bf16, VMEM)] * loads,
        [
            pltpu.VMEM((total, width), bf16),
            pltpu.VMEM((total, 2 * HD), jnp.float32),
            pltpu.SemaphoreType.DMA((len(parts) + 1 + 3 * chunks * loads,)),
        ],
        trig,
        *given,
        *parts,
    )


class Step:
    def __init__(self, q, group, slots, same=None, merged=False):
        self.q, self.group, self.slots = q, group, slots
        self.same, self.merged = same, merged


class Chunk:
    def __init__(self, at, runs, share):
        self.at, self.runs, self.share = at, runs, share

    def places(self, core, axis, first, size):
        shape = (size, 1) if axis == 0 else (1, size)
        index = first + lax.broadcasted_iota(jnp.int32, shape, axis)
        result, begin = index, 0
        for which, offset, rows in self.runs:
            base = (core if which == 0 else 1 - core) * self.share + offset - begin
            inside = (index >= begin) & (index < begin + rows)
            result = jnp.where(inside, index + base, result)
            begin += rows
        return result


def attention_kernel(plan, q_chunks, k_chunks, group_parts, fresh, final, table, *refs):
    refs = list(refs)
    take = lambda n: [refs.pop(0) for _ in range(n)]
    count = len(q_chunks)
    qs = take(count)
    kv_parts = [take(n) for n in group_parts]
    take(2 * (count - len(fresh)))
    outs = take(len(final))
    states = [take(2) for _ in range(count)]
    kvs, staged = take(len(group_parts)), take(len(final))
    (semaphores,) = refs
    copies = Copies(semaphores)
    core = table[0]
    waits = {}
    for group, (parts, kv) in enumerate(zip(kv_parts, kvs)):
        each = kv.shape[0] // len(parts)
        waits[group] = [
            copies.start(part, kv.at[pl.ds(slot * each, each)])
            for slot, part in enumerate(parts)
        ]

    def ready(group):
        for copy in waits.pop(group, []):
            copy.wait()

    def attend(q, keys_values, begin, visible=None, bias=None):
        q_ref, (peak, acc) = qs[q], states[q]
        heads, rows, _ = q_ref.shape
        keys, values = keys_values[:, :HD], keys_values[:, HD:]
        values = jnp.concatenate([values, jnp.ones_like(values)], axis=1)
        count = keys.shape[0]
        tile = min(rows, 128)
        for first in range(0, rows, tile):
            q_tile = q_ref[:, first : first + tile, :].reshape(heads * tile, HD)
            scores = lax.dot_general(
                q_tile, keys, (((1,), (1,)), ((), ())), preferred_element_type=jnp.float32
            )
            if visible is not None:
                seen = jnp.concatenate([visible(first, tile)] * heads, axis=0)
                scores = jnp.where(seen, scores, HIDDEN)
            if bias is not None:
                scores = scores + bias
            top = jnp.max(scores, axis=1, keepdims=True)
            top = jnp.broadcast_to(top, (heads * tile, HD))
            span = pl.ds(first * heads, heads * tile)
            if not begin:
                before = peak[span, :]
                top = jnp.maximum(before, top)
            wide = jnp.concatenate([top] * (count // HD), axis=1)
            weights = jnp.exp2(scores - wide).astype(jnp.bfloat16)
            summed = jnp.dot(weights, values, preferred_element_type=jnp.float32)
            if not begin:
                fade = jnp.exp2(before - top)
                summed = summed + acc[span, :] * jnp.concatenate([fade, fade], axis=1)
            acc[span, :] = summed
            peak[span, :] = top

    begun = set(range(count)) - set(fresh)
    for step in plan:
        q, group, kv = step.q, step.group, kvs[step.group]
        q_chunk, k_chunk = q_chunks[q], k_chunks[group]
        if step.same is not None:
            keys_at = k_chunk.places(core, 1, 0, kv.shape[1])
            visible = lambda first, tile: keys_at <= q_chunk.places(core, 0, first, tile)
            own = kv_parts[group][0]
            attend(q, own[step.same], q not in begun, visible=visible)
            begun.add(q)
        start = table[q_chunk.at]
        slots = step.slots
        if not slots:
            continue
        ready(group)
        if step.merged:
            shown = [table[k_chunk.at + slot] < start for slot in slots]

            @pl.when(functools.reduce(jnp.logical_or, shown))
            def _():
                rows = kv.shape[1]
                bias = [
                    jnp.where(see, 0.0, HIDDEN) * jnp.ones((1, rows), jnp.float32)
                    for see in shown
                ]
                keys_values = kv[slots[0] : slots[-1] + 1].reshape(len(slots) * rows, 2 * HD)
                attend(q, keys_values, False, bias=jnp.concatenate(bias, axis=1))

        else:

            def one(slot, carry):
                @pl.when(table[k_chunk.at + slot] < start)
                def _():
                    attend(q, kv[slot], False)

                return carry

            lax.fori_loop(slots[0], slots[-1] + 1, one, 0)

    for group in list(waits):
        ready(group)
    stores = []
    for out, stage, spans in zip(outs, staged, final):
        put = 0
        for q, first, rows in spans:
            acc = states[q][1]
            heads, q_rows, _ = qs[q].shape
            tile = min(q_rows, 128)
            size = min(tile, rows)
            for head in range(heads):
                for at in range(first, first + rows, size):
                    begin = at // tile * tile * heads + head * tile + at % tile
                    part = acc[begin : begin + size, :]
                    to = put + at - first
                    stage[to : to + size, head * HD : (head + 1) * HD] = (
                        part[:, :HD] / part[:, HD:]
                    ).astype(jnp.bfloat16)
            put += rows
        stores.append(copies.start(stage, out))
    for copy in stores:
        copy.wait()


def attention(plan, table, qs, q_chunks, groups, k_chunks, state, final=()):
    fresh = [at for at, held in enumerate(state) if held is None]
    shapes = []
    for q in qs:
        heads, rows, _ = q.shape
        shapes += [(heads * rows, HD), (heads * rows, 2 * HD)]
    width = qs[0].shape[0] * HD
    sums = [sum(rows for _, _, rows in spans) for spans in final]
    outs = [((rows, width), jnp.bfloat16, HBM) for rows in sums]
    scratch = []
    for parts in groups:
        slots = sum(part.shape[0] for part in parts)
        scratch.append(pltpu.VMEM((slots,) + parts[0].shape[1:], jnp.bfloat16))
    scratch += [pltpu.VMEM((rows, width), jnp.bfloat16) for rows in sums]
    parts = [part for parts in groups for part in parts]
    sizes = [len(parts) for parts in groups]
    inputs, aliases = [table, *qs, *parts], {}
    for at, pair in enumerate(state):
        for half, array in enumerate(pair or ()):
            aliases[len(inputs)] = len(outs) + 2 * at + half
            inputs.append(array)
    results = call(
        functools.partial(attention_kernel, plan, q_chunks, k_chunks, sizes, fresh, final),
        "attention",
        20,
        [SMEM] + [VMEM] * (len(inputs) - 1),
        outs + [(shape, jnp.float32, VMEM) for shape in shapes],
        scratch + [pltpu.SemaphoreType.DMA((len(parts) + len(outs),))],
        *inputs,
        aliases=aliases,
    )
    if final:
        return results[: len(final)]
    return [tuple(results[2 * at : 2 * at + 2]) for at in range(len(qs))]


def cut_kernel(pieces, at, table, weights, *refs):
    outs, (held, semaphores) = refs[:pieces], refs[pieces:]
    copies = Copies(semaphores)
    size = outs[0].shape[0]
    half = size * pieces
    first = pl.multiple_of(table[at] * half, half)
    ins = [
        copies.start(
            weights.at[pl.ds(first + piece * size, size)], held.at[pl.ds(piece * size, size)]
        )
        for piece in range(pieces)
    ]
    stores = []
    for piece in range(pieces):
        ins[piece].wait()
        stores.append(copies.start(held.at[pl.ds(piece * size, size)], outs[piece]))
    for copy in stores:
        copy.wait()


def cut(table, at, weights, pieces):
    depth, width = weights.shape
    size = depth // 2 // pieces
    return call(
        functools.partial(cut_kernel, pieces, at),
        "cut_weights",
        4,
        [SMEM, HBM],
        [((size, width), weights.dtype, HBM)] * pieces,
        [
            pltpu.VMEM((depth // 2, width), weights.dtype),
            pltpu.SemaphoreType.DMA((2 * pieces,)),
        ],
        table,
        weights,
    )


def near_kernel(chunks, left_hbm, weights_hbm, out, left, weights, semaphores):
    copies = Copies(semaphores)
    step = out.shape[1] // chunks
    first = copies.start(left_hbm, left)
    lanes = [pl.ds(chunk * step, step) for chunk in range(chunks)]
    waits = [copies.start(weights_hbm.at[:, at], weights.at[:, at]) for at in lanes]
    first.wait()
    for at, copy in zip(lanes, waits):
        copy.wait()
        out[:, at] = jnp.dot(left[...], weights[:, at], preferred_element_type=jnp.float32)


def output_near(left, weights, chunks=6):
    (rows, columns), width = left.shape, weights.shape[1]
    return call(
        functools.partial(near_kernel, chunks),
        "output_near",
        12,
        [HBM] * 2,
        [((rows, width), jnp.float32, VMEM)],
        [
            pltpu.VMEM(left.shape, left.dtype),
            pltpu.VMEM(weights.shape, weights.dtype),
            pltpu.SemaphoreType.DMA((1 + chunks,)),
        ],
        left,
        weights,
    )[0]


def send_kernel(at, chunks, table, left_hbm, near, *refs):
    count = len(refs) - 5
    pieces, (out, weights, left, staged, semaphores) = refs[:count], refs[count:]
    copies = Copies(semaphores)
    depth, width = weights.shape
    size = pieces[0].shape[0]
    step = width // chunks
    first = copies.start(left_hbm, left)
    lanes = [pl.ds(chunk * step, step) for chunk in range(chunks)]
    waits = []
    for span in lanes:
        here = []
        for index, piece in enumerate(pieces):
            half = table[at] if index < count // 2 else 1 - table[at]
            row = half * (depth // 2) + index % (count // 2) * size
            target = weights.at[pl.ds(pl.multiple_of(row, size), size), span]
            here.append(copies.start(piece.at[:, span], target))
        waits.append(here)
    first.wait()
    half = left.shape[0] // 2
    stores = []
    for span, here in zip(lanes, waits):
        for copy in here:
            copy.wait()
        staged[:, span] = (
            near[half:, span]
            + jnp.dot(left[half:, :], weights[:, span], preferred_element_type=jnp.float32)
        ).astype(jnp.bfloat16)
        stores.append(copies.start(staged.at[:, span], out.at[:, span]))
    for copy in stores:
        copy.wait()


def output_send(table, at, left, near, pieces, chunks=6):
    (rows, width), columns = near.shape, left.shape[1]
    half, bf16 = (rows // 2, width), jnp.bfloat16
    return call(
        functools.partial(send_kernel, at, chunks),
        "output_send",
        16,
        [SMEM, HBM, VMEM] + [HBM] * len(pieces),
        [(half, bf16, HBM), ((columns, width), bf16, VMEM)],
        [
            pltpu.VMEM(left.shape, bf16),
            pltpu.VMEM(half, bf16),
            pltpu.SemaphoreType.DMA((1 + (len(pieces) + 1) * chunks,)),
        ],
        table,
        left,
        near,
        *pieces,
    )


def keep_kernel(chunks, left_hbm, near, weights, out, left, semaphores):
    Copies(semaphores).start(left_hbm, left).wait()
    half, step = left.shape[0] // 2, out.shape[1] // chunks
    for chunk in range(chunks):
        span = pl.ds(chunk * step, step)
        out[:, span] = near[:half, span] + jnp.dot(
            left[:half, :], weights[:, span], preferred_element_type=jnp.float32
        )


def output_keep(left, near, weights, chunks=6):
    rows, width = near.shape
    return call(
        functools.partial(keep_kernel, chunks),
        "output_keep",
        4,
        [HBM, VMEM, VMEM],
        [((rows // 2, width), jnp.float32, VMEM)],
        [pltpu.VMEM(left.shape, jnp.bfloat16), pltpu.SemaphoreType.DMA((1,))],
        left,
        near,
        weights,
    )[0]


def final_kernel(chunks, received, hidden, kept, gain, out, other, held, semaphores):
    copies = Copies(semaphores)
    width = hidden.shape[1]
    step = width // chunks
    lanes = [pl.ds(chunk * step, step) for chunk in range(chunks)]
    waits = [copies.start(received.at[:, span], other.at[:, span]) for span in lanes]
    late = copies.start(hidden, held)
    square = jnp.zeros((hidden.shape[0], 128), jnp.float32)
    for span, copy in zip(lanes, waits):
        copy.wait()
        total = kept[:, span] + other[:, span].astype(jnp.float32)
        for lane in range(0, step, 128):
            part = total[:, lane : lane + 128]
            square = square + part * part
    mean = jnp.sum(square, axis=1, keepdims=True) / width
    scale = lax.rsqrt(mean + EPS)
    late.wait()
    gains = gain[...].reshape(1, width)
    stores = []
    for chunk, span in enumerate(lanes):
        total = kept[:, span] + other[:, span].astype(jnp.float32)
        normed = total * scale * gains[:, chunk * step : (chunk + 1) * step]
        held[:, span] = (held[:, span].astype(jnp.float32) + normed).astype(jnp.bfloat16)
        stores.append(copies.start(held.at[:, span], out.at[:, span]))
    for store in stores:
        store.wait()


def output(received, kept, hidden, gain, chunks=6):
    rows, width = hidden.shape
    bf16 = jnp.bfloat16
    return call(
        functools.partial(final_kernel, chunks),
        "output_norm",
        12,
        [HBM, HBM, VMEM, VMEM],
        [((rows, width), bf16, HBM)],
        [
            pltpu.VMEM((rows, width), bf16),
            pltpu.VMEM((rows, width), bf16),
            pltpu.SemaphoreType.DMA((1 + 2 * chunks,)),
        ],
        received,
        hidden,
        kept,
        gain,
    )[0]


def rotary_table(positions):
    half = HD // 2
    frequency = jnp.power(
        jnp.float32(10000.0), -jnp.arange(half, dtype=jnp.float32) * (2.0 / HD)
    )
    angles = positions.astype(jnp.float32)[:, None] * frequency[None, :]
    cos, sin = jnp.cos(angles), jnp.sin(angles)
    return jnp.concatenate([cos, cos, -sin, sin], axis=1)


def lookup(block_of, index):
    ids = jnp.arange(block_of.shape[0], dtype=jnp.int32)
    return jnp.sum(jnp.where(index[..., None] == ids, block_of, 0), axis=-1)


def flipped(array, axis, bit):
    size = lax.axis_size(axis)
    return lax.ppermute(array, axis, [(i, i ^ bit) for i in range(size)])


def along_line(array):
    size = lax.axis_size("seq")
    parts = [array[None]]
    for by in range(1, size):
        part = lax.ppermute(array, "seq", [(i, (i + by) % size) for i in range(size)])
        parts.append(Came(part[None]))
    return parts


def came(parts):
    return [part.array for part in parts if isinstance(part, Came)]


def after(array, *others):
    return lax.optimization_barrier((array, *others))[0]


def two_chips(hidden, pre_gain, post_gain, wq, wk, wv, w_out, block_of):
    rows = hidden.shape[0]
    block_rows = 2 * rows
    lines, tp = lax.axis_size("seq"), lax.axis_index("tp")
    seq, group = lax.axis_index("seq"), lax.axis_index("groups")
    chip, core = tp // 2, tp % 2

    line = (seq - jnp.arange(lines, dtype=jnp.int32)) % lines
    near_starts = lookup(block_of, 2 * line + chip) * block_rows
    far_starts = lookup(block_of, 2 * line + 1 - chip) * block_rows
    table = jnp.concatenate([jnp.stack([core, group]).astype(jnp.int32), near_starts, far_starts])
    group_at, near_at, far_at = 1, 2, 2 + lines
    run = jnp.arange(rows, dtype=jnp.int32)
    place = jnp.concatenate([core * rows + run, (1 - core) * rows + run])
    trig = rotary_table(jnp.concatenate([near_starts[0] + place, far_starts[0] + place]))
    runs = [(0, 0, rows), (1, 0, rows)]
    near_chunk, far_chunk = Chunk(near_at, runs, rows), Chunk(far_at, runs, rows)
    others, everyone = list(range(1, lines)), list(range(lines))

    own = norm(hidden, pre_gain, [rows])[0]
    away = flipped(own, "tp", 2)
    partner = flipped(own, "tp", 1)

    q_near, kv_near, weights = qkv([own, Came(partner)], (wq, wk, wv), trig, 0)
    near = along_line(kv_near)
    w_cut = cut(table, group_at, after(w_out, kv_near), 4)
    q_near = after(q_near, *w_cut)
    (near_state,) = attention(
        [Step(0, 0, others, same=0)], table, [q_near], [near_chunk], [near], [near_chunk], [None]
    )

    away = after(away, *near_state)
    q_far, kv_far = qkv([Came(away), Came(flipped(away, "tp", 1))], weights, trig, block_rows)
    far = along_line(kv_far)

    fetched = lambda piece, *others: flipped(after(piece, *others), "tp", 2)
    swap = lambda array: flipped(array, "groups", 1)
    w_far = [fetched(piece, away) for piece in w_cut[:2]]
    w_far[0] = after(w_far[0], kv_far)
    w_far.append(fetched(w_cut[2], w_far[0]))
    w_other = [swap(w_far[0])]

    (far_state,) = attention(
        [Step(0, 1, [], same=0), Step(0, 0, everyone)],
        table,
        [after(q_far, w_other[0])],
        [far_chunk],
        [near, far[:1]],
        [near_chunk, far_chunk],
        [None],
    )
    w_far[1:] = [after(piece, came(far)[0]) for piece in w_far[1:]]
    w_far.append(fetched(w_cut[3], w_far[1]))
    w_other += [swap(piece) for piece in w_far[1:3]]
    attended, gone = attention(
        [Step(1, 0, others), Step(0, 0, everyone)],
        table,
        [q_near, q_far],
        [near_chunk, far_chunk],
        [far],
        [far_chunk],
        [near_state, far_state],
        final=[[(0, 0, block_rows)], [(1, 0, block_rows)]],
    )
    gone = flipped(gone, "tp", 2)
    near_sum = output_near(attended, w_out)
    w_other.append(swap(after(w_far[3], attended)))
    pieces = [Came(piece) for piece in w_far + w_other]
    sent, w_laid = output_send(table, group_at, Came(gone), near_sum, pieces)
    received = flipped(sent, "tp", 1)
    kept = output_keep(Came(gone), near_sum, w_laid)
    return output(Came(received), kept, hidden, post_gain)


def any_count(hidden, pre_gain, post_gain, wq, wk, wv, w_out, block_of):
    rows = hidden.shape[0]
    lines = lax.axis_size("seq")
    line = (lax.axis_index("seq") - jnp.arange(lines, dtype=jnp.int32)) % lines
    block = (2 * line[:, None] + jnp.arange(2, dtype=jnp.int32)).reshape(-1)
    block_rows = rows * lax.axis_size("tp") // 2
    starts = lookup(block_of, block) * block_rows
    table = jnp.concatenate([jnp.zeros(2, jnp.int32), starts])
    normed = norm(hidden, pre_gain, [rows], 1)[0]
    normed = lax.all_gather(normed, "tp", axis=0, tiled=True)
    place = jnp.arange(block_rows, dtype=jnp.int32)
    trig = rotary_table((starts[:2, None] + place).reshape(-1))
    qs, keys_values, weights = [], [], (wq, wk, wv)
    for at in range(2):
        first = at * block_rows
        q, kv, *held = qkv([normed[first : first + block_rows]], weights, trig, first)
        weights = held[0] if held else weights
        qs.append(q)
        keys_values.append(kv)
    kv = lax.all_gather(jnp.stack(keys_values), "seq")[line].reshape(-1, block_rows, 2 * HD)
    rest = list(range(2, 2 * lines))
    runs = [(0, 0, block_rows)]
    attended = attention(
        [Step(0, 0, [1], same=0), Step(1, 0, [0], same=1), Step(0, 0, rest), Step(1, 0, rest)],
        table,
        qs,
        [Chunk(2, runs, 0), Chunk(3, runs, 0)],
        [[kv]],
        [Chunk(2, runs, 0)],
        [None, None],
        final=[[(0, 0, block_rows), (1, 0, block_rows)]],
    )[0]
    partial = jnp.dot(attended, w_out, preferred_element_type=jnp.float32)
    summed = lax.psum_scatter(
        partial.astype(jnp.bfloat16), "tp", scatter_dimension=0, tiled=True
    ).astype(jnp.float32)
    mean = jnp.mean(summed * summed, axis=-1, keepdims=True)
    projected = summed * lax.rsqrt(mean + EPS) * post_gain
    return (hidden.astype(jnp.float32) + projected).astype(jnp.bfloat16)


def solution(mesh):
    return jax.shard_map(
        two_chips if mesh.shape["tp"] == 4 else any_count,
        mesh=mesh,
        in_specs=(
            P(("groups", "seq", "tp"), None),
            P(),
            P(),
            P(None, "tp"),
            P(None, "tp"),
            P(None, "tp"),
            P("tp", None),
            P(),
        ),
        out_specs=P(("groups", "seq", "tp"), None),
        check_vma=False,
    )
```

```python
import functools
import math

import jax
import jax.numpy as jnp
from jax import lax
from jax.experimental import pallas as pl
from jax.experimental.pallas import tpu as pltpu
from jax.sharding import PartitionSpec as P

HD = 128
ATT_SCALAR = 144
EPS = 1e-6
MIB = 1024 * 1024
HIDDEN = -1e30
NEVER = 1 << 30
COST = pl.CostEstimate(flops=1, bytes_accessed=1, transcendentals=0)

ANY = pl.BlockSpec(memory_space=pl.ANY)
HBM = pl.BlockSpec(memory_space=pltpu.HBM)
VMEM = pl.BlockSpec(memory_space=pltpu.VMEM)
SMEM = pl.BlockSpec(memory_space=pltpu.SMEM)


class Came:
    def __init__(self, array):
        self.array, self.shape = array, array.shape


def call(kernel, name, mib, in_specs, outs, scratch, *args, aliases=None):
    in_specs, pinned = list(in_specs), []
    for at, arg in enumerate(args):
        if isinstance(arg, Came):
            arg, in_specs[at] = arg.array, ANY
        elif in_specs[at] is not SMEM:
            arg = pltpu.with_memory_space_constraint(arg, in_specs[at].memory_space)
        pinned.append(arg)
    return pl.pallas_call(
        kernel,
        in_specs=in_specs,
        out_specs=[spec for _, _, spec in outs],
        out_shape=[spec.memory_space(shape, dtype) for shape, dtype, spec in outs],
        scratch_shapes=scratch,
        input_output_aliases=aliases or {},
        compiler_params=pltpu.CompilerParams(vmem_limit_bytes=mib * MIB),
        cost_estimate=COST,
        name=name,
    )(*pinned)


class Copies:
    def __init__(self, semaphores):
        self.semaphores, self.used = semaphores, 0

    def start(self, source, target):
        copy = pltpu.make_async_copy(source, target, self.semaphores.at[self.used])
        self.used += 1
        copy.start()
        return copy


def norm_kernel(cuts, pieces, hidden, gain, *refs):
    parts, (gains, rows, staged, semaphores) = refs[: len(cuts)], refs[len(cuts) :]
    copies = Copies(semaphores)
    count, width = hidden.shape
    step = count // pieces
    spans = [pl.ds(at * step, step) for at in range(pieces)]
    ins = [copies.start(hidden.at[span], rows.at[span]) for span in spans]
    copies.start(gain, gains).wait()
    scale = gains[...].reshape(1, width)
    outs = []
    for at, span in enumerate(spans):
        ins[at].wait()
        x = rows[span, :].astype(jnp.float32)
        square = x * x
        folded = square[:, :128]
        for lane in range(128, width, 128):
            folded = folded + square[:, lane : lane + 128]
        mean = jnp.sum(folded, axis=1, keepdims=True) / width
        staged[span, :] = (x * lax.rsqrt(mean + EPS) * scale).astype(jnp.bfloat16)
        begin = 0
        for cut, part in zip(cuts, parts):
            if begin <= at * step < begin + cut:
                inside = pl.ds(at * step - begin, step)
                outs.append(copies.start(staged.at[span], part.at[inside]))
            begin += cut
    for copy in outs:
        copy.wait()


def norm(hidden, gain, cuts, pieces=3):
    rows, width = hidden.shape
    bf16 = jnp.bfloat16
    return call(
        functools.partial(norm_kernel, cuts, pieces),
        "norm_rows",
        8,
        [HBM, HBM],
        [((cut, width), bf16, HBM) for cut in cuts],
        [
            pltpu.VMEM((width,), jnp.float32),
            pltpu.VMEM((rows, width), bf16),
            pltpu.VMEM((rows, width), bf16),
            pltpu.SemaphoreType.DMA((1 + 2 * pieces,)),
        ],
        hidden,
        gain,
    )


def rotate_into(product, angles, q, kv):
    cos, sin = angles[:, :HD], angles[:, HD:]
    queries = product.shape[1] - 2 * HD

    def rotated(at):
        y = product[:, at : at + HD]
        return y * cos + pltpu.roll(y, HD // 2, 1) * sin

    factor = ATT_SCALAR ** (-0.5) * math.log2(math.e)
    kv[:, :HD] = rotated(queries).astype(jnp.bfloat16)
    kv[:, HD:] = product[:, queries + HD :].astype(jnp.bfloat16)
    for head in range(queries // HD):
        q[head] = (rotated(head * HD) * factor).astype(jnp.bfloat16)


def qkv_kernel(count, first, chunks, trig, wq, wk, wv, *refs):
    parts = refs[:count]
    q, kv, weights, rows, angles, semaphores = refs[count:]
    copies, waits = Copies(semaphores), []
    depth = weights.shape[0] // chunks
    for chunk in range(chunks):
        span, put, column, here = pl.ds(chunk * depth, depth), 0, 0, []
        for part in parts:
            target = rows.at[pl.ds(put, part.shape[0]), span]
            here.append(copies.start(part.at[:, span], target))
            put += part.shape[0]
        for weight in (wq, wk, wv):
            target = weights.at[span, pl.ds(column, weight.shape[1])]
            here.append(copies.start(weight.at[span], target))
            column += weight.shape[1]
        waits.append(here)
    late = copies.start(trig.at[pl.ds(first, put)], angles)
    product = None
    for chunk, here in enumerate(waits):
        for copy in here:
            copy.wait()
        span = pl.ds(chunk * depth, depth)
        term = jnp.dot(rows[:, span], weights[span, :], preferred_element_type=jnp.float32)
        product = term if product is None else product + term
    late.wait()
    rotate_into(product, angles, q, kv)


def qkv(parts, weights, trig, first, chunks=6):
    total, width = sum(part.shape[0] for part in parts), parts[0].shape[1]
    columns = sum(weight.shape[1] for weight in weights)
    heads, bf16 = columns // HD - 2, jnp.bfloat16
    return call(
        functools.partial(qkv_kernel, len(parts), first, chunks),
        "qkv",
        14,
        [HBM] * (4 + len(parts)),
        [((heads, total, HD), bf16, VMEM), ((total, 2 * HD), bf16, VMEM)],
        [
            pltpu.VMEM((width, columns), bf16),
            pltpu.VMEM((total, width), bf16),
            pltpu.VMEM((total, 2 * HD), jnp.float32),
            pltpu.SemaphoreType.DMA((1 + (len(parts) + 3) * chunks,)),
        ],
        trig,
        *weights,
        *parts,
    )


class Step:
    def __init__(self, q, group, slots, same=None, merged=False):
        self.q, self.group, self.slots = q, group, slots
        self.same, self.merged = same, merged


class Chunk:
    def __init__(self, at, runs, share):
        self.at, self.runs, self.share = at, runs, share

    def places(self, core, axis, first, size):
        shape = (size, 1) if axis == 0 else (1, size)
        index = first + lax.broadcasted_iota(jnp.int32, shape, axis)
        result, begin = index, 0
        for which, offset, rows in self.runs:
            base = (core if which == 0 else 1 - core) * self.share + offset - begin
            inside = (index >= begin) & (index < begin + rows)
            result = jnp.where(inside, index + base, result)
            begin += rows
        return result


def attention_kernel(plan, q_chunks, k_chunks, group_parts, fresh, final, table, *refs):
    refs = list(refs)
    take = lambda n: [refs.pop(0) for _ in range(n)]
    count = len(q_chunks)
    qs = take(count)
    kv_parts = [take(n) for n in group_parts]
    take(2 * (count - len(fresh)))
    outs = take(len(final))
    states = [take(2) for _ in range(count)]
    kvs, staged = take(len(group_parts)), take(len(final))
    (semaphores,) = refs
    copies = Copies(semaphores)
    core = table[0]
    waits = {}
    for group, (parts, kv) in enumerate(zip(kv_parts, kvs)):
        each = kv.shape[0] // len(parts)
        waits[group] = [
            copies.start(part, kv.at[pl.ds(slot * each, each)])
            for slot, part in enumerate(parts)
        ]

    def ready(group):
        for copy in waits.pop(group, []):
            copy.wait()

    def attend(q, keys_values, begin, visible=None, bias=None):
        q_ref, (peak, acc) = qs[q], states[q]
        heads, rows, _ = q_ref.shape
        keys, values = keys_values[:, :HD], keys_values[:, HD:]
        values = jnp.concatenate([values, jnp.ones_like(values)], axis=1)
        count = keys.shape[0]
        tile = min(rows, 128)
        for first in range(0, rows, tile):
            q_tile = q_ref[:, first : first + tile, :].reshape(heads * tile, HD)
            scores = lax.dot_general(
                q_tile, keys, (((1,), (1,)), ((), ())), preferred_element_type=jnp.float32
            )
            if visible is not None:
                seen = jnp.concatenate([visible(first, tile)] * heads, axis=0)
                scores = jnp.where(seen, scores, HIDDEN)
            if bias is not None:
                scores = scores + bias
            top = jnp.max(scores, axis=1, keepdims=True)
            top = jnp.broadcast_to(top, (heads * tile, HD))
            span = pl.ds(first * heads, heads * tile)
            if not begin:
                before = peak[span, :]
                top = jnp.maximum(before, top)
            wide = jnp.concatenate([top] * (count // HD), axis=1)
            weights = jnp.exp2(scores - wide).astype(jnp.bfloat16)
            summed = jnp.dot(weights, values, preferred_element_type=jnp.float32)
            if not begin:
                fade = jnp.exp2(before - top)
                summed = summed + acc[span, :] * jnp.concatenate([fade, fade], axis=1)
            acc[span, :] = summed
            peak[span, :] = top

    begun = set(range(count)) - set(fresh)
    for step in plan:
        q, group, kv = step.q, step.group, kvs[step.group]
        q_chunk, k_chunk = q_chunks[q], k_chunks[group]
        if step.same is not None:
            keys_at = k_chunk.places(core, 1, 0, kv.shape[1])
            visible = lambda first, tile: keys_at <= q_chunk.places(core, 0, first, tile)
            own = kv_parts[group][0]
            attend(q, own[step.same], q not in begun, visible=visible)
            begun.add(q)
        start = table[q_chunk.at]
        slots = step.slots
        if not slots:
            continue
        ready(group)
        if step.merged:
            shown = [table[k_chunk.at + slot] < start for slot in slots]

            @pl.when(functools.reduce(jnp.logical_or, shown))
            def _():
                rows = kv.shape[1]
                bias = [
                    jnp.where(see, 0.0, HIDDEN) * jnp.ones((1, rows), jnp.float32)
                    for see in shown
                ]
                keys_values = kv[slots[0] : slots[-1] + 1].reshape(len(slots) * rows, 2 * HD)
                attend(q, keys_values, False, bias=jnp.concatenate(bias, axis=1))

        else:

            def one(slot, carry):
                @pl.when(table[k_chunk.at + slot] < start)
                def _():
                    attend(q, kv[slot], False)

                return carry

            lax.fori_loop(slots[0], slots[-1] + 1, one, 0)

    for group in list(waits):
        ready(group)
    stores = []
    for out, stage, spans in zip(outs, staged, final):
        put = 0
        for q, first, rows in spans:
            acc = states[q][1]
            heads, q_rows, _ = qs[q].shape
            tile = min(q_rows, 128)
            size = min(tile, rows)
            for head in range(heads):
                for at in range(first, first + rows, size):
                    begin = at // tile * tile * heads + head * tile + at % tile
                    part = acc[begin : begin + size, :]
                    to = put + at - first
                    stage[to : to + size, head * HD : (head + 1) * HD] = (
                        part[:, :HD] / part[:, HD:]
                    ).astype(jnp.bfloat16)
            put += rows
        stores.append(copies.start(stage, out))
    for copy in stores:
        copy.wait()


def attention(plan, table, qs, q_chunks, groups, k_chunks, state, final=()):
    fresh = [at for at, held in enumerate(state) if held is None]
    shapes = []
    for q in qs:
        heads, rows, _ = q.shape
        shapes += [(heads * rows, HD), (heads * rows, 2 * HD)]
    width = qs[0].shape[0] * HD
    sums = [sum(rows for _, _, rows in spans) for spans in final]
    outs = [((rows, width), jnp.bfloat16, HBM) for rows in sums]
    scratch = []
    for parts in groups:
        slots = sum(part.shape[0] for part in parts)
        scratch.append(pltpu.VMEM((slots,) + parts[0].shape[1:], jnp.bfloat16))
    scratch += [pltpu.VMEM((rows, width), jnp.bfloat16) for rows in sums]
    parts = [part for parts in groups for part in parts]
    sizes = [len(parts) for parts in groups]
    inputs, aliases = [table, *qs, *parts], {}
    for at, pair in enumerate(state):
        for half, array in enumerate(pair or ()):
            aliases[len(inputs)] = len(outs) + 2 * at + half
            inputs.append(array)
    results = call(
        functools.partial(attention_kernel, plan, q_chunks, k_chunks, sizes, fresh, final),
        "attention",
        10,
        [SMEM] + [VMEM] * (len(inputs) - 1),
        outs + [(shape, jnp.float32, VMEM) for shape in shapes],
        scratch + [pltpu.SemaphoreType.DMA((len(parts) + len(outs),))],
        *inputs,
        aliases=aliases,
    )
    if final:
        return results[: len(final)]
    return [tuple(results[2 * at : 2 * at + 2]) for at in range(len(qs))]


def cut_kernel(pieces, at, table, weights, *refs):
    outs, (held, semaphores) = refs[:pieces], refs[pieces:]
    copies = Copies(semaphores)
    size = outs[0].shape[0]
    half = size * pieces
    first = pl.multiple_of(table[at] * half, half)
    ins = [
        copies.start(
            weights.at[pl.ds(first + piece * size, size)], held.at[pl.ds(piece * size, size)]
        )
        for piece in range(pieces)
    ]
    stores = []
    for piece in range(pieces):
        ins[piece].wait()
        stores.append(copies.start(held.at[pl.ds(piece * size, size)], outs[piece]))
    for copy in stores:
        copy.wait()


def cut(table, at, weights, pieces):
    depth, width = weights.shape
    size = depth // 2 // pieces
    return call(
        functools.partial(cut_kernel, pieces, at),
        "cut_weights",
        4,
        [SMEM, HBM],
        [((size, width), weights.dtype, HBM)] * pieces,
        [
            pltpu.VMEM((depth // 2, width), weights.dtype),
            pltpu.SemaphoreType.DMA((2 * pieces,)),
        ],
        table,
        weights,
    )


def near_kernel(chunks, left_hbm, weights_hbm, out, left, weights, semaphores):
    copies = Copies(semaphores)
    step = out.shape[1] // chunks
    first = copies.start(left_hbm, left)
    lanes = [pl.ds(chunk * step, step) for chunk in range(chunks)]
    waits = [copies.start(weights_hbm.at[:, at], weights.at[:, at]) for at in lanes]
    first.wait()
    for at, copy in zip(lanes, waits):
        copy.wait()
        out[:, at] = jnp.dot(left[...], weights[:, at], preferred_element_type=jnp.float32)


def output_near(left, weights, chunks=6):
    (rows, columns), width = left.shape, weights.shape[1]
    return call(
        functools.partial(near_kernel, chunks),
        "output_near",
        8,
        [HBM] * 2,
        [((rows, width), jnp.float32, VMEM)],
        [
            pltpu.VMEM(left.shape, left.dtype),
            pltpu.VMEM(weights.shape, weights.dtype),
            pltpu.SemaphoreType.DMA((1 + chunks,)),
        ],
        left,
        weights,
    )[0]


def send_kernel(at, chunks, table, left_hbm, near, *refs):
    count = len(refs) - 5
    pieces, (out, weights, left, staged, semaphores) = refs[:count], refs[count:]
    copies = Copies(semaphores)
    depth, width = weights.shape
    size = pieces[0].shape[0]
    step = width // chunks
    first = copies.start(left_hbm, left)
    waits = []
    for index, piece in enumerate(pieces):
        half = table[at] if index < count // 2 else 1 - table[at]
        row = half * (depth // 2) + index % (count // 2) * size
        target = weights.at[pl.ds(pl.multiple_of(row, size), size)]
        waits.append(copies.start(piece, target))
    for copy in waits:
        copy.wait()
    first.wait()
    half = left.shape[0] // 2
    stores = []
    for chunk in range(chunks):
        span = pl.ds(chunk * step, step)
        staged[:, span] = (
            near[half:, span]
            + jnp.dot(left[half:, :], weights[:, span], preferred_element_type=jnp.float32)
        ).astype(jnp.bfloat16)
        stores.append(copies.start(staged.at[:, span], out.at[:, span]))
    for copy in stores:
        copy.wait()


def output_send(table, at, left, near, pieces, chunks=6):
    (rows, width), columns = near.shape, left.shape[1]
    half, bf16 = (rows // 2, width), jnp.bfloat16
    return call(
        functools.partial(send_kernel, at, chunks),
        "output_send",
        8,
        [SMEM, HBM, VMEM] + [HBM] * len(pieces),
        [(half, bf16, HBM), ((columns, width), bf16, VMEM)],
        [
            pltpu.VMEM(left.shape, bf16),
            pltpu.VMEM(half, bf16),
            pltpu.SemaphoreType.DMA((1 + len(pieces) + chunks,)),
        ],
        table,
        left,
        near,
        *pieces,
    )


def keep_kernel(chunks, left_hbm, hidden, near, weights, out, held, left, semaphores):
    copies = Copies(semaphores)
    first, late = copies.start(left_hbm, left), copies.start(hidden, held)
    first.wait()
    half, step = left.shape[0] // 2, out.shape[1] // chunks
    for chunk in range(chunks):
        span = pl.ds(chunk * step, step)
        out[:, span] = near[:half, span] + jnp.dot(
            left[:half, :], weights[:, span], preferred_element_type=jnp.float32
        )
    late.wait()


def output_keep(left, hidden, near, weights, chunks=6):
    rows, width = near.shape
    return call(
        functools.partial(keep_kernel, chunks),
        "output_keep",
        4,
        [HBM, HBM, VMEM, VMEM],
        [((rows // 2, width), jnp.float32, VMEM), (hidden.shape, hidden.dtype, VMEM)],
        [pltpu.VMEM(left.shape, jnp.bfloat16), pltpu.SemaphoreType.DMA((2,))],
        left,
        hidden,
        near,
        weights,
    )


def final_kernel(chunks, received, hidden, kept, gain, out, other, staged, gains, semaphores):
    copies = Copies(semaphores)
    width = hidden.shape[1]
    step = width // chunks
    lanes = [pl.ds(chunk * step, step) for chunk in range(chunks)]
    waits = [copies.start(received.at[:, span], other.at[:, span]) for span in lanes]
    late = copies.start(gain, gains)
    square = jnp.zeros((hidden.shape[0], 128), jnp.float32)
    for span, copy in zip(lanes, waits):
        copy.wait()
        total = kept[:, span] + other[:, span].astype(jnp.float32)
        for lane in range(0, step, 128):
            part = total[:, lane : lane + 128]
            square = square + part * part
    mean = jnp.sum(square, axis=1, keepdims=True) / width
    scale = lax.rsqrt(mean + EPS)
    late.wait()
    row = gains[...].reshape(1, width)
    stores = []
    for chunk, span in enumerate(lanes):
        total = kept[:, span] + other[:, span].astype(jnp.float32)
        normed = total * scale * row[:, chunk * step : (chunk + 1) * step]
        staged[:, span] = (hidden[:, span].astype(jnp.float32) + normed).astype(jnp.bfloat16)
        stores.append(copies.start(staged.at[:, span], out.at[:, span]))
    for store in stores:
        store.wait()


def output(received, hidden, kept, gain, chunks=6):
    rows, width = hidden.shape
    bf16 = jnp.bfloat16
    return call(
        functools.partial(final_kernel, chunks),
        "output_norm",
        8,
        [HBM, VMEM, VMEM, HBM],
        [((rows, width), bf16, HBM)],
        [
            pltpu.VMEM((rows, width), bf16),
            pltpu.VMEM((rows, width), bf16),
            pltpu.VMEM((width,), jnp.float32),
            pltpu.SemaphoreType.DMA((1 + 2 * chunks,)),
        ],
        received,
        hidden,
        kept,
        gain,
    )[0]


def rotary_table(positions):
    half = HD // 2
    frequency = jnp.power(
        jnp.float32(10000.0), -jnp.arange(half, dtype=jnp.float32) * (2.0 / HD)
    )
    angles = positions.astype(jnp.float32)[:, None] * frequency[None, :]
    cos, sin = jnp.cos(angles), jnp.sin(angles)
    return jnp.concatenate([cos, cos, -sin, sin], axis=1)


def lookup(block_of, index):
    ids = jnp.arange(block_of.shape[0], dtype=jnp.int32)
    return jnp.sum(jnp.where(index[..., None] == ids, block_of, 0), axis=-1)


def flipped(array, axis, bit):
    size = lax.axis_size(axis)
    return lax.ppermute(array, axis, [(i, i ^ bit) for i in range(size)])


def along_line(array):
    size = lax.axis_size("seq")
    parts = [array[None]]
    for by in range(1, size):
        part = lax.ppermute(array, "seq", [(i, (i + by) % size) for i in range(size)])
        parts.append(Came(part[None]))
    return parts


def along_four(array):
    move = lambda array, pairs: lax.ppermute(array, "seq", pairs)
    across = move(array, [(0, 2), (1, 3), (2, 0), (3, 1)])
    up, down = move(array, [(0, 1), (1, 2), (2, 3)]), move(array, [(1, 0), (2, 1), (3, 2)])
    passed = move(across, [(1, 0), (2, 3)])
    return [array[None]] + [Came(part[None]) for part in (up, down, across, passed)]


def came(parts):
    return [part.array for part in parts if isinstance(part, Came)]


def after(array, *others):
    return lax.optimization_barrier((array, *others))[0]


def two_chips(hidden, pre_gain, post_gain, wq, wk, wv, w_out, block_of):
    rows = hidden.shape[0]
    block_rows = 2 * rows
    lines, tp = lax.axis_size("seq"), lax.axis_index("tp")
    seq, group = lax.axis_index("seq"), lax.axis_index("groups")
    chip, core = tp // 2, tp % 2

    line = (seq - jnp.arange(lines, dtype=jnp.int32)) % lines
    near_starts = lookup(block_of, 2 * line + chip) * block_rows
    inner = (seq == 1) | (seq == 2)
    four = jnp.stack([seq, seq - 1, seq + 1, (seq + 2) % 4, 3 - seq])
    there = jnp.stack([seq >= 0, seq > 0, seq < 3, seq >= 0, ~inner])
    far_starts = lookup(block_of, 2 * four + 1 - chip) * block_rows
    far_starts = jnp.where(there, far_starts, NEVER)
    table = jnp.concatenate([jnp.stack([core, group]).astype(jnp.int32), near_starts, far_starts])
    group_at, near_at, far_at = 1, 2, 2 + lines
    run = jnp.arange(rows, dtype=jnp.int32)
    place = jnp.concatenate([core * rows + run, (1 - core) * rows + run])
    trig = rotary_table(jnp.concatenate([near_starts[0] + place, far_starts[0] + place]))
    runs = [(0, 0, rows), (1, 0, rows)]
    near_chunk, far_chunk = Chunk(near_at, runs, rows), Chunk(far_at, runs, rows)
    others, everyone = list(range(1, lines)), list(range(lines))

    own = norm(hidden, pre_gain, [rows])[0]
    away = flipped(own, "tp", 2)
    partner = flipped(own, "tp", 1)

    weights = (wq, wk, wv)
    q_near, kv_near = qkv([own, Came(partner)], weights, trig, 0)
    near = along_line(kv_near)
    w_cut = cut(table, group_at, after(w_out, kv_near), 4)
    q_near = after(q_near, *w_cut)
    (near_state,) = attention(
        [Step(0, 0, others, same=0)], table, [q_near], [near_chunk], [near], [near_chunk], [None]
    )

    away = after(away, *near_state)
    q_far, kv_far = qkv([Came(away), Came(flipped(away, "tp", 1))], weights, trig, block_rows)
    far = along_four(kv_far)

    fetched = lambda piece, *others: flipped(after(piece, *others), "tp", 2)
    swap = lambda array: flipped(array, "groups", 1)
    w_far = [fetched(piece, away) for piece in w_cut[:2]]
    w_far[0] = after(w_far[0], kv_far)
    w_far.append(fetched(w_cut[2], w_far[0]))
    w_other = [swap(w_far[0])]

    near_state, far_state = attention(
        [Step(1, 1, [], same=0), Step(1, 0, everyone), Step(0, 1, [0])],
        table,
        [q_near, after(q_far, w_other[0])],
        [near_chunk, far_chunk],
        [near, far[:1]],
        [near_chunk, far_chunk],
        [near_state, None],
    )
    w_far[1:] = [after(piece, came(far)[0]) for piece in w_far[1:]]
    w_far.append(after(fetched(w_cut[3], w_far[1]), *far_state))
    w_other += [swap(piece) for piece in w_far[1:3]]
    attended, gone = attention(
        [Step(1, 0, list(range(1, 5))), Step(0, 0, list(range(1, 5)))],
        table,
        [q_near, q_far],
        [near_chunk, far_chunk],
        [far],
        [far_chunk],
        [near_state, far_state],
        final=[[(0, 0, block_rows)], [(1, 0, block_rows)]],
    )
    gone = flipped(gone, "tp", 2)
    near_sum = output_near(attended, w_out)
    w_other.append(swap(w_far[3]))
    pieces = [Came(piece) for piece in w_far + w_other]
    sent, w_laid = output_send(table, group_at, Came(gone), near_sum, pieces)
    received = flipped(sent, "tp", 1)
    kept, held = output_keep(Came(gone), hidden, near_sum, w_laid)
    return output(Came(received), held, kept, post_gain)


def any_count(hidden, pre_gain, post_gain, wq, wk, wv, w_out, block_of):
    rows = hidden.shape[0]
    lines = lax.axis_size("seq")
    line = (lax.axis_index("seq") - jnp.arange(lines, dtype=jnp.int32)) % lines
    block = (2 * line[:, None] + jnp.arange(2, dtype=jnp.int32)).reshape(-1)
    block_rows = rows * lax.axis_size("tp") // 2
    starts = lookup(block_of, block) * block_rows
    table = jnp.concatenate([jnp.zeros(2, jnp.int32), starts])
    normed = norm(hidden, pre_gain, [rows], 1)[0]
    normed = lax.all_gather(normed, "tp", axis=0, tiled=True)
    place = jnp.arange(block_rows, dtype=jnp.int32)
    trig = rotary_table((starts[:2, None] + place).reshape(-1))
    qs, keys_values, weights = [], [], (wq, wk, wv)
    for at in range(2):
        first = at * block_rows
        q, kv = qkv([normed[first : first + block_rows]], weights, trig, first)
        qs.append(q)
        keys_values.append(kv)
    kv = lax.all_gather(jnp.stack(keys_values), "seq")[line].reshape(-1, block_rows, 2 * HD)
    rest = list(range(2, 2 * lines))
    runs = [(0, 0, block_rows)]
    attended = attention(
        [Step(0, 0, [1], same=0), Step(1, 0, [0], same=1), Step(0, 0, rest), Step(1, 0, rest)],
        table,
        qs,
        [Chunk(2, runs, 0), Chunk(3, runs, 0)],
        [[kv]],
        [Chunk(2, runs, 0)],
        [None, None],
        final=[[(0, 0, block_rows), (1, 0, block_rows)]],
    )[0]
    partial = jnp.dot(attended, w_out, preferred_element_type=jnp.float32)
    summed = lax.psum_scatter(
        partial.astype(jnp.bfloat16), "tp", scatter_dimension=0, tiled=True
    ).astype(jnp.float32)
    mean = jnp.mean(summed * summed, axis=-1, keepdims=True)
    projected = summed * lax.rsqrt(mean + EPS) * post_gain
    return (hidden.astype(jnp.float32) + projected).astype(jnp.bfloat16)


def solution(mesh):
    return jax.shard_map(
        two_chips if mesh.shape["tp"] == mesh.shape["seq"] == 4 else any_count,
        mesh=mesh,
        in_specs=(
            P(("groups", "seq", "tp"), None),
            P(),
            P(),
            P(None, "tp"),
            P(None, "tp"),
            P(None, "tp"),
            P("tp", None),
            P(),
        ),
        out_specs=P(("groups", "seq", "tp"), None),
        check_vma=False,
    )
```

```python
import functools
import math

import jax
import jax.numpy as jnp
from jax import lax
from jax.experimental import pallas as pl
from jax.experimental.pallas import tpu as pltpu
from jax.sharding import PartitionSpec as P

HD = 128
ATT_SCALAR = 144
EPS = 1e-6
MIB = 1024 * 1024
HIDDEN = -1e30
NEVER = 1 << 30
ONES = 16
COST = pl.CostEstimate(flops=1, bytes_accessed=1, transcendentals=0)

ANY = pl.BlockSpec(memory_space=pl.ANY)
HBM = pl.BlockSpec(memory_space=pltpu.HBM)
VMEM = pl.BlockSpec(memory_space=pltpu.VMEM)
SMEM = pl.BlockSpec(memory_space=pltpu.SMEM)


class Came:
    def __init__(self, array):
        self.array, self.shape = array, array.shape


def call(kernel, name, mib, in_specs, outs, scratch, *args, aliases=None):
    in_specs, pinned = list(in_specs), []
    for at, arg in enumerate(args):
        if isinstance(arg, Came):
            arg, in_specs[at] = arg.array, ANY
        elif in_specs[at] is not SMEM:
            arg = pltpu.with_memory_space_constraint(arg, in_specs[at].memory_space)
        pinned.append(arg)
    return pl.pallas_call(
        kernel,
        in_specs=in_specs,
        out_specs=[spec for _, _, spec in outs],
        out_shape=[spec.memory_space(shape, dtype) for shape, dtype, spec in outs],
        scratch_shapes=scratch,
        input_output_aliases=aliases or {},
        compiler_params=pltpu.CompilerParams(vmem_limit_bytes=mib * MIB),
        cost_estimate=COST,
        name=name,
    )(*pinned)


class Copies:
    def __init__(self, semaphores):
        self.semaphores, self.used = semaphores, 0

    def start(self, source, target):
        copy = pltpu.make_async_copy(source, target, self.semaphores.at[self.used])
        self.used += 1
        copy.start()
        return copy


def norm_kernel(cuts, pieces, hidden, gain, *refs):
    parts, (gains, rows, staged, semaphores) = refs[: len(cuts)], refs[len(cuts) :]
    copies = Copies(semaphores)
    count, width = hidden.shape
    step = count // pieces
    spans = [pl.ds(at * step, step) for at in range(pieces)]
    ins = [copies.start(hidden.at[span], rows.at[span]) for span in spans]
    copies.start(gain, gains).wait()
    scale = gains[...].reshape(1, width)
    outs = []
    for at, span in enumerate(spans):
        ins[at].wait()
        x = rows[span, :].astype(jnp.float32)
        square = x * x
        folded = square[:, :128]
        for lane in range(128, width, 128):
            folded = folded + square[:, lane : lane + 128]
        mean = jnp.sum(folded, axis=1, keepdims=True) / width
        staged[span, :] = (x * lax.rsqrt(mean + EPS) * scale).astype(jnp.bfloat16)
        begin = 0
        for cut, part in zip(cuts, parts):
            if begin <= at * step < begin + cut:
                inside = pl.ds(at * step - begin, step)
                outs.append(copies.start(staged.at[span], part.at[inside]))
            begin += cut
    for copy in outs:
        copy.wait()


def norm(hidden, gain, cuts, pieces=3):
    rows, width = hidden.shape
    bf16 = jnp.bfloat16
    return call(
        functools.partial(norm_kernel, cuts, pieces),
        "norm_rows",
        8,
        [HBM, HBM],
        [((cut, width), bf16, HBM) for cut in cuts],
        [
            pltpu.VMEM((width,), jnp.float32),
            pltpu.VMEM((rows, width), bf16),
            pltpu.VMEM((rows, width), bf16),
            pltpu.SemaphoreType.DMA((1 + 2 * pieces,)),
        ],
        hidden,
        gain,
    )


def rotate_into(product, angles, q, kv):
    cos, sin = angles[:, :HD], angles[:, HD:]
    queries = product.shape[1] - 2 * HD

    def rotated(at):
        y = product[:, at : at + HD]
        return y * cos + pltpu.roll(y, HD // 2, 1) * sin

    factor = ATT_SCALAR ** (-0.5) * math.log2(math.e)
    kv[:, :HD] = rotated(queries).astype(jnp.bfloat16)
    kv[:, HD:] = product[:, queries + HD :].astype(jnp.bfloat16)
    for head in range(queries // HD):
        q[head] = (rotated(head * HD) * factor).astype(jnp.bfloat16)


def qkv_kernel(count, first, chunks, trig, wq, wk, wv, *refs):
    parts = refs[:count]
    q, kv, weights, rows, angles, semaphores = refs[count:]
    copies, waits = Copies(semaphores), []
    depth = weights.shape[0] // chunks
    for chunk in range(chunks):
        span, put, column, here = pl.ds(chunk * depth, depth), 0, 0, []
        for part in parts:
            target = rows.at[pl.ds(put, part.shape[0]), span]
            here.append(copies.start(part.at[:, span], target))
            put += part.shape[0]
        for weight in (wq, wk, wv):
            target = weights.at[span, pl.ds(column, weight.shape[1])]
            here.append(copies.start(weight.at[span], target))
            column += weight.shape[1]
        waits.append(here)
    late = copies.start(trig.at[pl.ds(first, put)], angles)
    product = None
    for chunk, here in enumerate(waits):
        for copy in here:
            copy.wait()
        span = pl.ds(chunk * depth, depth)
        term = jnp.dot(rows[:, span], weights[span, :], preferred_element_type=jnp.float32)
        product = term if product is None else product + term
    late.wait()
    rotate_into(product, angles, q, kv)


def qkv(parts, weights, trig, first, chunks=6):
    total, width = sum(part.shape[0] for part in parts), parts[0].shape[1]
    columns = sum(weight.shape[1] for weight in weights)
    heads, bf16 = columns // HD - 2, jnp.bfloat16
    return call(
        functools.partial(qkv_kernel, len(parts), first, chunks),
        "qkv",
        14,
        [HBM] * (4 + len(parts)),
        [((heads, total, HD), bf16, VMEM), ((total, 2 * HD), bf16, VMEM)],
        [
            pltpu.VMEM((width, columns), bf16),
            pltpu.VMEM((total, width), bf16),
            pltpu.VMEM((total, 2 * HD), jnp.float32),
            pltpu.SemaphoreType.DMA((1 + (len(parts) + 3) * chunks,)),
        ],
        trig,
        *weights,
        *parts,
    )


class Step:
    def __init__(self, q, group, slots, same=None, merged=False):
        self.q, self.group, self.slots = q, group, slots
        self.same, self.merged = same, merged


class Chunk:
    def __init__(self, at, runs, share):
        self.at, self.runs, self.share = at, runs, share

    def places(self, core, axis, first, size):
        shape = (size, 1) if axis == 0 else (1, size)
        index = first + lax.broadcasted_iota(jnp.int32, shape, axis)
        result, begin = index, 0
        for which, offset, rows in self.runs:
            base = (core if which == 0 else 1 - core) * self.share + offset - begin
            inside = (index >= begin) & (index < begin + rows)
            result = jnp.where(inside, index + base, result)
            begin += rows
        return result


def attention_kernel(plan, q_chunks, k_chunks, group_parts, fresh, final, table, *refs):
    refs = list(refs)
    take = lambda n: [refs.pop(0) for _ in range(n)]
    count = len(q_chunks)
    qs = take(count)
    kv_parts = [take(n) for n in group_parts]
    take(2 * (count - len(fresh)))
    outs = take(len(final))
    states = [take(2) for _ in range(count)]
    kvs, staged = take(len(group_parts)), take(len(final))
    (semaphores,) = refs
    copies = Copies(semaphores)
    core = table[0]
    waits = {}
    for group, (parts, kv) in enumerate(zip(kv_parts, kvs)):
        each = kv.shape[0] // len(parts)
        waits[group] = [
            copies.start(part, kv.at[pl.ds(slot * each, each)])
            for slot, part in enumerate(parts)
        ]

    def ready(group):
        for copy in waits.pop(group, []):
            copy.wait()

    def attend(q, keys_values, begin, visible=None, bias=None):
        q_ref, (peak, acc) = qs[q], states[q]
        heads = q_ref.shape[0]
        keys = keys_values[:, :HD]
        values = keys_values[:, HD:].T
        values = jnp.concatenate([values, jnp.ones((ONES, keys.shape[0]), values.dtype)], axis=0)
        for at in range(acc.shape[0]):
            tile = acc.shape[2] // heads
            q_tile = q_ref[:, at * tile : (at + 1) * tile, :].reshape(heads * tile, HD)
            scores = lax.dot_general(
                keys, q_tile, (((1,), (1,)), ((), ())), preferred_element_type=jnp.float32
            )
            if visible is not None:
                seen = jnp.concatenate([visible(at * tile, tile)] * heads, axis=1)
                scores = jnp.where(seen, scores, HIDDEN)
            if bias is not None:
                scores = scores + bias
            top = jnp.max(scores, axis=0, keepdims=True)
            if not begin:
                before = peak[at, 0:1, :]
                top = jnp.maximum(before, top)
            weights = jnp.exp2(scores - top).astype(jnp.bfloat16)
            summed = jnp.dot(values, weights, preferred_element_type=jnp.float32)
            if not begin:
                summed = summed + acc[at] * jnp.exp2(before - top)
            acc[at] = summed
            peak[at] = jnp.broadcast_to(top, peak.shape[1:])

    begun = set(range(count)) - set(fresh)
    for step in plan:
        q, group, kv = step.q, step.group, kvs[step.group]
        q_chunk, k_chunk = q_chunks[q], k_chunks[group]
        if step.same is not None:
            keys_at = k_chunk.places(core, 0, 0, kv.shape[1])
            visible = lambda first, tile: keys_at <= q_chunk.places(core, 1, first, tile)
            own = kv_parts[group][0]
            attend(q, own[step.same], q not in begun, visible=visible)
            begun.add(q)
        start = table[q_chunk.at]
        slots = step.slots
        if not slots:
            continue
        ready(group)
        if step.merged:
            shown = [table[k_chunk.at + slot] < start for slot in slots]

            @pl.when(functools.reduce(jnp.logical_or, shown))
            def _():
                rows = kv.shape[1]
                bias = [
                    jnp.where(see, 0.0, HIDDEN) * jnp.ones((rows, 1), jnp.float32)
                    for see in shown
                ]
                keys_values = kv[slots[0] : slots[-1] + 1].reshape(len(slots) * rows, 2 * HD)
                attend(q, keys_values, False, bias=jnp.concatenate(bias, axis=0))

        else:

            def one(slot, carry):
                @pl.when(table[k_chunk.at + slot] < start)
                def _():
                    attend(q, kv[slot], False)

                return carry

            lax.fori_loop(slots[0], slots[-1] + 1, one, 0)

    for group in list(waits):
        ready(group)
    stores = []
    for out, stage, order in zip(outs, staged, final):
        put = 0
        for q in order:
            acc, heads = states[q][1], qs[q].shape[0]
            tile = acc.shape[2] // heads
            for at in range(acc.shape[0]):
                rows = acc[at, :HD, :] / acc[at, HD : HD + 1, :]
                rows = rows.T.astype(jnp.bfloat16)
                for head in range(heads):
                    stage[put : put + tile, head * HD : (head + 1) * HD] = rows[
                        head * tile : (head + 1) * tile
                    ]
                put += tile
        stores.append(copies.start(stage, out))
    for copy in stores:
        copy.wait()


def attention(plan, table, qs, q_chunks, groups, k_chunks, state, final=()):
    fresh = [at for at, held in enumerate(state) if held is None]
    shapes = []
    for q in qs:
        heads, rows, _ = q.shape
        tile = min(rows, 128)
        shapes += [(rows // tile, deep, heads * tile) for deep in (8, HD + ONES)]
    width = qs[0].shape[0] * HD
    sums = [sum(qs[q].shape[1] for q in order) for order in final]
    outs = [((rows, width), jnp.bfloat16, HBM) for rows in sums]
    scratch = []
    for parts in groups:
        slots = sum(part.shape[0] for part in parts)
        scratch.append(pltpu.VMEM((slots,) + parts[0].shape[1:], jnp.bfloat16))
    scratch += [pltpu.VMEM((rows, width), jnp.bfloat16) for rows in sums]
    parts = [part for parts in groups for part in parts]
    sizes = [len(parts) for parts in groups]
    inputs, aliases = [table, *qs, *parts], {}
    for at, pair in enumerate(state):
        for half, array in enumerate(pair or ()):
            aliases[len(inputs)] = len(outs) + 2 * at + half
            inputs.append(array)
    results = call(
        functools.partial(attention_kernel, plan, q_chunks, k_chunks, sizes, fresh, final),
        "attention",
        10,
        [SMEM] + [VMEM] * (len(inputs) - 1),
        outs + [(shape, jnp.float32, VMEM) for shape in shapes],
        scratch + [pltpu.SemaphoreType.DMA((len(parts) + len(outs),))],
        *inputs,
        aliases=aliases,
    )
    if final:
        return results[: len(final)]
    return [tuple(results[2 * at : 2 * at + 2]) for at in range(len(qs))]


def cut_kernel(pieces, at, table, weights, *refs):
    outs, (held, semaphores) = refs[:pieces], refs[pieces:]
    copies = Copies(semaphores)
    size = outs[0].shape[0]
    half = size * pieces
    first = pl.multiple_of(table[at] * half, half)
    ins = [
        copies.start(
            weights.at[pl.ds(first + piece * size, size)], held.at[pl.ds(piece * size, size)]
        )
        for piece in range(pieces)
    ]
    stores = []
    for piece in range(pieces):
        ins[piece].wait()
        stores.append(copies.start(held.at[pl.ds(piece * size, size)], outs[piece]))
    for copy in stores:
        copy.wait()


def cut(table, at, weights, pieces):
    depth, width = weights.shape
    size = depth // 2 // pieces
    return call(
        functools.partial(cut_kernel, pieces, at),
        "cut_weights",
        4,
        [SMEM, HBM],
        [((size, width), weights.dtype, HBM)] * pieces,
        [
            pltpu.VMEM((depth // 2, width), weights.dtype),
            pltpu.SemaphoreType.DMA((2 * pieces,)),
        ],
        table,
        weights,
    )


def near_kernel(chunks, left_hbm, weights_hbm, out, left, weights, semaphores):
    copies = Copies(semaphores)
    step = out.shape[1] // chunks
    first = copies.start(left_hbm, left)
    lanes = [pl.ds(chunk * step, step) for chunk in range(chunks)]
    waits = [copies.start(weights_hbm.at[:, at], weights.at[:, at]) for at in lanes]
    first.wait()
    for at, copy in zip(lanes, waits):
        copy.wait()
        out[:, at] = jnp.dot(left[...], weights[:, at], preferred_element_type=jnp.float32)


def output_near(left, weights, chunks=6):
    (rows, columns), width = left.shape, weights.shape[1]
    return call(
        functools.partial(near_kernel, chunks),
        "output_near",
        8,
        [HBM] * 2,
        [((rows, width), jnp.float32, VMEM)],
        [
            pltpu.VMEM(left.shape, left.dtype),
            pltpu.VMEM(weights.shape, weights.dtype),
            pltpu.SemaphoreType.DMA((1 + chunks,)),
        ],
        left,
        weights,
    )[0]


def send_kernel(at, chunks, table, left_hbm, near, *refs):
    count = len(refs) - 5
    pieces, (out, weights, left, staged, semaphores) = refs[:count], refs[count:]
    copies = Copies(semaphores)
    depth, width = weights.shape
    size = pieces[0].shape[0]
    step = width // chunks
    first = copies.start(left_hbm, left)
    waits = []
    for index, piece in enumerate(pieces):
        half = table[at] if index < count // 2 else 1 - table[at]
        row = half * (depth // 2) + index % (count // 2) * size
        target = weights.at[pl.ds(pl.multiple_of(row, size), size)]
        waits.append(copies.start(piece, target))
    for copy in waits:
        copy.wait()
    first.wait()
    half = left.shape[0] // 2
    stores = []
    for chunk in range(chunks):
        span = pl.ds(chunk * step, step)
        staged[:, span] = (
            near[half:, span]
            + jnp.dot(left[half:, :], weights[:, span], preferred_element_type=jnp.float32)
        ).astype(jnp.bfloat16)
        stores.append(copies.start(staged.at[:, span], out.at[:, span]))
    for copy in stores:
        copy.wait()


def output_send(table, at, left, near, pieces, chunks=6):
    (rows, width), columns = near.shape, left.shape[1]
    half, bf16 = (rows // 2, width), jnp.bfloat16
    return call(
        functools.partial(send_kernel, at, chunks),
        "output_send",
        8,
        [SMEM, HBM, VMEM] + [HBM] * len(pieces),
        [(half, bf16, HBM), ((columns, width), bf16, VMEM)],
        [
            pltpu.VMEM(left.shape, bf16),
            pltpu.VMEM(half, bf16),
            pltpu.SemaphoreType.DMA((1 + len(pieces) + chunks,)),
        ],
        table,
        left,
        near,
        *pieces,
    )


def keep_kernel(chunks, left_hbm, hidden, near, weights, out, held, left, semaphores):
    copies = Copies(semaphores)
    first, late = copies.start(left_hbm, left), copies.start(hidden, held)
    first.wait()
    half, step = left.shape[0] // 2, out.shape[1] // chunks
    for chunk in range(chunks):
        span = pl.ds(chunk * step, step)
        out[:, span] = near[:half, span] + jnp.dot(
            left[:half, :], weights[:, span], preferred_element_type=jnp.float32
        )
    late.wait()


def output_keep(left, hidden, near, weights, chunks=6):
    rows, width = near.shape
    return call(
        functools.partial(keep_kernel, chunks),
        "output_keep",
        4,
        [HBM, HBM, VMEM, VMEM],
        [((rows // 2, width), jnp.float32, VMEM), (hidden.shape, hidden.dtype, VMEM)],
        [pltpu.VMEM(left.shape, jnp.bfloat16), pltpu.SemaphoreType.DMA((2,))],
        left,
        hidden,
        near,
        weights,
    )


def final_kernel(chunks, received, hidden, kept, gain, out, other, staged, gains, semaphores):
    copies = Copies(semaphores)
    width = hidden.shape[1]
    step = width // chunks
    lanes = [pl.ds(chunk * step, step) for chunk in range(chunks)]
    waits = [copies.start(received.at[:, span], other.at[:, span]) for span in lanes]
    late = copies.start(gain, gains)
    square = jnp.zeros((hidden.shape[0], 128), jnp.float32)
    for span, copy in zip(lanes, waits):
        copy.wait()
        total = kept[:, span] + other[:, span].astype(jnp.float32)
        for lane in range(0, step, 128):
            part = total[:, lane : lane + 128]
            square = square + part * part
    mean = jnp.sum(square, axis=1, keepdims=True) / width
    scale = lax.rsqrt(mean + EPS)
    late.wait()
    row = gains[...].reshape(1, width)
    stores = []
    for chunk, span in enumerate(lanes):
        total = kept[:, span] + other[:, span].astype(jnp.float32)
        normed = total * scale * row[:, chunk * step : (chunk + 1) * step]
        staged[:, span] = (hidden[:, span].astype(jnp.float32) + normed).astype(jnp.bfloat16)
        stores.append(copies.start(staged.at[:, span], out.at[:, span]))
    for store in stores:
        store.wait()


def output(received, hidden, kept, gain, chunks=6):
    rows, width = hidden.shape
    bf16 = jnp.bfloat16
    return call(
        functools.partial(final_kernel, chunks),
        "output_norm",
        8,
        [HBM, VMEM, VMEM, HBM],
        [((rows, width), bf16, HBM)],
        [
            pltpu.VMEM((rows, width), bf16),
            pltpu.VMEM((rows, width), bf16),
            pltpu.VMEM((width,), jnp.float32),
            pltpu.SemaphoreType.DMA((1 + 2 * chunks,)),
        ],
        received,
        hidden,
        kept,
        gain,
    )[0]


def rotary_table(positions):
    half = HD // 2
    frequency = jnp.power(
        jnp.float32(10000.0), -jnp.arange(half, dtype=jnp.float32) * (2.0 / HD)
    )
    angles = positions.astype(jnp.float32)[:, None] * frequency[None, :]
    cos, sin = jnp.cos(angles), jnp.sin(angles)
    return jnp.concatenate([cos, cos, -sin, sin], axis=1)


def lookup(block_of, index):
    ids = jnp.arange(block_of.shape[0], dtype=jnp.int32)
    return jnp.sum(jnp.where(index[..., None] == ids, block_of, 0), axis=-1)


def flipped(array, axis, bit):
    size = lax.axis_size(axis)
    return lax.ppermute(array, axis, [(i, i ^ bit) for i in range(size)])


def along_line(array):
    size = lax.axis_size("seq")
    parts = [array[None]]
    for by in range(1, size):
        part = lax.ppermute(array, "seq", [(i, (i + by) % size) for i in range(size)])
        parts.append(Came(part[None]))
    return parts


def along_four(array):
    move = lambda array, pairs: lax.ppermute(array, "seq", pairs)
    across = move(array, [(0, 2), (1, 3), (2, 0), (3, 1)])
    up, down = move(array, [(0, 1), (1, 2), (2, 3)]), move(array, [(1, 0), (2, 1), (3, 2)])
    passed = move(across, [(1, 0), (2, 3)])
    return [array[None]] + [Came(part[None]) for part in (up, down, across, passed)]


def came(parts):
    return [part.array for part in parts if isinstance(part, Came)]


def after(array, *others):
    return lax.optimization_barrier((array, *others))[0]


def two_chips(hidden, pre_gain, post_gain, wq, wk, wv, w_out, block_of):
    rows = hidden.shape[0]
    block_rows = 2 * rows
    lines, tp = lax.axis_size("seq"), lax.axis_index("tp")
    seq, group = lax.axis_index("seq"), lax.axis_index("groups")
    chip, core = tp // 2, tp % 2

    line = (seq - jnp.arange(lines, dtype=jnp.int32)) % lines
    near_starts = lookup(block_of, 2 * line + chip) * block_rows
    inner = (seq == 1) | (seq == 2)
    four = jnp.stack([seq, seq - 1, seq + 1, (seq + 2) % 4, 3 - seq])
    there = jnp.stack([seq >= 0, seq > 0, seq < 3, seq >= 0, ~inner])
    far_starts = lookup(block_of, 2 * four + 1 - chip) * block_rows
    far_starts = jnp.where(there, far_starts, NEVER)
    table = jnp.concatenate([jnp.stack([core, group]).astype(jnp.int32), near_starts, far_starts])
    group_at, near_at, far_at = 1, 2, 2 + lines
    run = jnp.arange(rows, dtype=jnp.int32)
    place = jnp.concatenate([core * rows + run, (1 - core) * rows + run])
    trig = rotary_table(jnp.concatenate([near_starts[0] + place, far_starts[0] + place]))
    runs = [(0, 0, rows), (1, 0, rows)]
    near_chunk, far_chunk = Chunk(near_at, runs, rows), Chunk(far_at, runs, rows)
    others, everyone = list(range(1, lines)), list(range(lines))

    own = norm(hidden, pre_gain, [rows])[0]
    away = flipped(own, "tp", 2)
    partner = flipped(own, "tp", 1)

    weights = (wq, wk, wv)
    q_near, kv_near = qkv([own, Came(partner)], weights, trig, 0)
    near = along_line(kv_near)
    w_cut = cut(table, group_at, after(w_out, kv_near), 4)
    q_near = after(q_near, *w_cut)
    (near_state,) = attention(
        [Step(0, 0, others, same=0)], table, [q_near], [near_chunk], [near], [near_chunk], [None]
    )

    away = after(away, *near_state)
    q_far, kv_far = qkv([Came(away), Came(flipped(away, "tp", 1))], weights, trig, block_rows)
    far = along_four(kv_far)

    fetched = lambda piece, *others: flipped(after(piece, *others), "tp", 2)
    swap = lambda array: flipped(array, "groups", 1)
    w_far = [fetched(piece, away) for piece in w_cut[:2]]
    w_far[0] = after(w_far[0], kv_far)
    w_far.append(fetched(w_cut[2], w_far[0]))
    w_other = [swap(w_far[0])]

    near_state, far_state = attention(
        [Step(1, 1, [], same=0), Step(1, 0, everyone), Step(0, 1, [0])],
        table,
        [q_near, after(q_far, w_other[0])],
        [near_chunk, far_chunk],
        [near, far[:1]],
        [near_chunk, far_chunk],
        [near_state, None],
    )
    w_far[1:] = [after(piece, came(far)[0]) for piece in w_far[1:]]
    w_far.append(after(fetched(w_cut[3], w_far[1]), *far_state))
    w_other += [swap(piece) for piece in w_far[1:3]]
    attended, gone = attention(
        [Step(1, 0, list(range(1, 5))), Step(0, 0, list(range(1, 5)))],
        table,
        [q_near, q_far],
        [near_chunk, far_chunk],
        [far],
        [far_chunk],
        [near_state, far_state],
        final=[[0], [1]],
    )
    gone = flipped(gone, "tp", 2)
    near_sum = output_near(attended, w_out)
    w_other.append(swap(w_far[3]))
    pieces = [Came(piece) for piece in w_far + w_other]
    sent, w_laid = output_send(table, group_at, Came(gone), near_sum, pieces)
    received = flipped(sent, "tp", 1)
    kept, held = output_keep(Came(gone), hidden, near_sum, w_laid)
    return output(Came(received), held, kept, post_gain)


def any_count(hidden, pre_gain, post_gain, wq, wk, wv, w_out, block_of):
    rows = hidden.shape[0]
    lines = lax.axis_size("seq")
    line = (lax.axis_index("seq") - jnp.arange(lines, dtype=jnp.int32)) % lines
    block = (2 * line[:, None] + jnp.arange(2, dtype=jnp.int32)).reshape(-1)
    block_rows = rows * lax.axis_size("tp") // 2
    starts = lookup(block_of, block) * block_rows
    table = jnp.concatenate([jnp.zeros(2, jnp.int32), starts])
    normed = norm(hidden, pre_gain, [rows], 1)[0]
    normed = lax.all_gather(normed, "tp", axis=0, tiled=True)
    place = jnp.arange(block_rows, dtype=jnp.int32)
    trig = rotary_table((starts[:2, None] + place).reshape(-1))
    qs, keys_values, weights = [], [], (wq, wk, wv)
    for at in range(2):
        first = at * block_rows
        q, kv = qkv([normed[first : first + block_rows]], weights, trig, first)
        qs.append(q)
        keys_values.append(kv)
    kv = lax.all_gather(jnp.stack(keys_values), "seq")[line].reshape(-1, block_rows, 2 * HD)
    rest = list(range(2, 2 * lines))
    runs = [(0, 0, block_rows)]
    attended = attention(
        [Step(0, 0, [1], same=0), Step(1, 0, [0], same=1), Step(0, 0, rest), Step(1, 0, rest)],
        table,
        qs,
        [Chunk(2, runs, 0), Chunk(3, runs, 0)],
        [[kv]],
        [Chunk(2, runs, 0)],
        [None, None],
        final=[[0, 1]],
    )[0]
    partial = jnp.dot(attended, w_out, preferred_element_type=jnp.float32)
    summed = lax.psum_scatter(
        partial.astype(jnp.bfloat16), "tp", scatter_dimension=0, tiled=True
    ).astype(jnp.float32)
    mean = jnp.mean(summed * summed, axis=-1, keepdims=True)
    projected = summed * lax.rsqrt(mean + EPS) * post_gain
    return (hidden.astype(jnp.float32) + projected).astype(jnp.bfloat16)


def solution(mesh):
    return jax.shard_map(
        two_chips if mesh.shape["tp"] == mesh.shape["seq"] == 4 else any_count,
        mesh=mesh,
        in_specs=(
            P(("groups", "seq", "tp"), None),
            P(),
            P(),
            P(None, "tp"),
            P(None, "tp"),
            P(None, "tp"),
            P("tp", None),
            P(),
        ),
        out_specs=P(("groups", "seq", "tp"), None),
        check_vma=False,
    )
```

```python
import functools
import math

import jax
import jax.numpy as jnp
from jax import lax
from jax.experimental import pallas as pl
from jax.experimental.pallas import tpu as pltpu
from jax.sharding import PartitionSpec as P

HD = 128
ATT_SCALAR = 144
EPS = 1e-6
MIB = 1024 * 1024
HIDDEN = -1e30
ONES = 16
COST = pl.CostEstimate(flops=1, bytes_accessed=1, transcendentals=0)

ANY = pl.BlockSpec(memory_space=pl.ANY)
HBM = pl.BlockSpec(memory_space=pltpu.HBM)
VMEM = pl.BlockSpec(memory_space=pltpu.VMEM)
SMEM = pl.BlockSpec(memory_space=pltpu.SMEM)


class Came:
    def __init__(self, array):
        self.array, self.shape = array, array.shape


def call(kernel, name, mib, in_specs, outs, scratch, *args, aliases=None):
    in_specs, pinned = list(in_specs), []
    for at, arg in enumerate(args):
        if isinstance(arg, Came):
            arg, in_specs[at] = arg.array, ANY
        elif in_specs[at] is not SMEM:
            arg = pltpu.with_memory_space_constraint(arg, in_specs[at].memory_space)
        pinned.append(arg)
    return pl.pallas_call(
        kernel,
        in_specs=in_specs,
        out_specs=[spec for _, _, spec in outs],
        out_shape=[spec.memory_space(shape, dtype) for shape, dtype, spec in outs],
        scratch_shapes=scratch,
        input_output_aliases=aliases or {},
        compiler_params=pltpu.CompilerParams(vmem_limit_bytes=mib * MIB),
        cost_estimate=COST,
        name=name,
    )(*pinned)


class Copies:
    def __init__(self, semaphores):
        self.semaphores, self.used = semaphores, 0

    def start(self, source, target):
        copy = pltpu.make_async_copy(source, target, self.semaphores.at[self.used])
        self.used += 1
        copy.start()
        return copy


def norm_kernel(cuts, pieces, hidden, gain, *refs):
    parts, (gains, rows, staged, semaphores) = refs[: len(cuts)], refs[len(cuts) :]
    copies = Copies(semaphores)
    count, width = hidden.shape
    step = count // pieces
    spans = [pl.ds(at * step, step) for at in range(pieces)]
    ins = [copies.start(hidden.at[span], rows.at[span]) for span in spans]
    copies.start(gain, gains).wait()
    scale = gains[...].reshape(1, width)
    outs = []
    for at, span in enumerate(spans):
        ins[at].wait()
        x = rows[span, :].astype(jnp.float32)
        square = x * x
        folded = square[:, :128]
        for lane in range(128, width, 128):
            folded = folded + square[:, lane : lane + 128]
        mean = jnp.sum(folded, axis=1, keepdims=True) / width
        staged[span, :] = (x * lax.rsqrt(mean + EPS) * scale).astype(jnp.bfloat16)
        begin = 0
        for cut, part in zip(cuts, parts):
            if begin <= at * step < begin + cut:
                inside = pl.ds(at * step - begin, step)
                outs.append(copies.start(staged.at[span], part.at[inside]))
            begin += cut
    for copy in outs:
        copy.wait()


def norm(hidden, gain, cuts, pieces=3):
    rows, width = hidden.shape
    bf16 = jnp.bfloat16
    return call(
        functools.partial(norm_kernel, cuts, pieces),
        "norm_rows",
        8,
        [HBM, HBM],
        [((cut, width), bf16, HBM) for cut in cuts],
        [
            pltpu.VMEM((width,), jnp.float32),
            pltpu.VMEM((rows, width), bf16),
            pltpu.VMEM((rows, width), bf16),
            pltpu.SemaphoreType.DMA((1 + 2 * pieces,)),
        ],
        hidden,
        gain,
    )


def rotate_into(product, angles, q, kv):
    cos, sin = angles[:, :HD], angles[:, HD:]
    queries = product.shape[1] - 2 * HD

    def rotated(at):
        y = product[:, at : at + HD]
        return y * cos + pltpu.roll(y, HD // 2, 1) * sin

    factor = ATT_SCALAR ** (-0.5) * math.log2(math.e)
    kv[:, :HD] = rotated(queries).astype(jnp.bfloat16)
    kv[:, HD:] = product[:, queries + HD :].astype(jnp.bfloat16)
    for head in range(queries // HD):
        q[head] = (rotated(head * HD) * factor).astype(jnp.bfloat16)


def qkv_kernel(count, first, chunks, trig, wq, wk, wv, *refs):
    parts = refs[:count]
    q, kv, weights, rows, angles, semaphores = refs[count:]
    copies, waits = Copies(semaphores), []
    depth = weights.shape[0] // chunks
    for chunk in range(chunks):
        span, put, column, here = pl.ds(chunk * depth, depth), 0, 0, []
        for part in parts:
            target = rows.at[pl.ds(put, part.shape[0]), span]
            here.append(copies.start(part.at[:, span], target))
            put += part.shape[0]
        for weight in (wq, wk, wv):
            target = weights.at[span, pl.ds(column, weight.shape[1])]
            here.append(copies.start(weight.at[span], target))
            column += weight.shape[1]
        waits.append(here)
    late = copies.start(trig.at[pl.ds(first, put)], angles)
    product = None
    for chunk, here in enumerate(waits):
        for copy in here:
            copy.wait()
        span = pl.ds(chunk * depth, depth)
        term = jnp.dot(rows[:, span], weights[span, :], preferred_element_type=jnp.float32)
        product = term if product is None else product + term
    late.wait()
    rotate_into(product, angles, q, kv)


def qkv(parts, weights, trig, first, chunks=6):
    total, width = sum(part.shape[0] for part in parts), parts[0].shape[1]
    columns = sum(weight.shape[1] for weight in weights)
    heads, bf16 = columns // HD - 2, jnp.bfloat16
    return call(
        functools.partial(qkv_kernel, len(parts), first, chunks),
        "qkv",
        14,
        [HBM] * (4 + len(parts)),
        [((heads, total, HD), bf16, VMEM), ((total, 2 * HD), bf16, VMEM)],
        [
            pltpu.VMEM((width, columns), bf16),
            pltpu.VMEM((total, width), bf16),
            pltpu.VMEM((total, 2 * HD), jnp.float32),
            pltpu.SemaphoreType.DMA((1 + (len(parts) + 3) * chunks,)),
        ],
        trig,
        *weights,
        *parts,
    )


class Step:
    def __init__(self, q, group, slots, same=None, merged=False):
        self.q, self.group, self.slots = q, group, slots
        self.same, self.merged = same, merged


class Chunk:
    def __init__(self, at, runs, share):
        self.at, self.runs, self.share = at, runs, share

    def places(self, core, axis, first, size):
        shape = (size, 1) if axis == 0 else (1, size)
        index = first + lax.broadcasted_iota(jnp.int32, shape, axis)
        result, begin = index, 0
        for which, offset, rows in self.runs:
            base = (core if which == 0 else 1 - core) * self.share + offset - begin
            inside = (index >= begin) & (index < begin + rows)
            result = jnp.where(inside, index + base, result)
            begin += rows
        return result


def attention_kernel(plan, q_chunks, k_chunks, group_parts, fresh, final, table, *refs):
    refs = list(refs)
    take = lambda n: [refs.pop(0) for _ in range(n)]
    count = len(q_chunks)
    qs = take(count)
    kv_parts = [take(n) for n in group_parts]
    take(2 * (count - len(fresh)))
    outs = take(len(final))
    states = [take(2) for _ in range(count)]
    kvs, staged = take(len(group_parts)), take(len(final))
    (semaphores,) = refs
    copies = Copies(semaphores)
    core = table[0]
    waits = {}
    for group, (parts, kv) in enumerate(zip(kv_parts, kvs)):
        each = kv.shape[0] // len(parts)
        waits[group] = [
            copies.start(part, kv.at[pl.ds(slot * each, each)])
            for slot, part in enumerate(parts)
        ]

    def ready(group):
        for copy in waits.pop(group, []):
            copy.wait()

    def attend(q, keys_values, begin, visible=None, bias=None):
        q_ref, (peak, acc) = qs[q], states[q]
        heads = q_ref.shape[0]
        keys = keys_values[:, :HD]
        values = keys_values[:, HD:].T
        values = jnp.concatenate([values, jnp.ones((ONES, keys.shape[0]), values.dtype)], axis=0)
        tiles, tile = acc.shape[0], acc.shape[2] // heads
        scores, tops, weights = [], [], []
        for at in range(tiles):
            q_tile = q_ref[:, at * tile : (at + 1) * tile, :].reshape(heads * tile, HD)
            score = lax.dot_general(
                keys, q_tile, (((1,), (1,)), ((), ())), preferred_element_type=jnp.float32
            )
            if visible is not None:
                seen = jnp.concatenate([visible(at * tile, tile)] * heads, axis=1)
                score = jnp.where(seen, score, HIDDEN)
            if bias is not None:
                score = score + bias
            scores.append(score)
        for at in range(tiles):
            top = jnp.max(scores[at], axis=0, keepdims=True)
            if not begin:
                top = jnp.maximum(peak[at, 0:1, :], top)
            tops.append(top)
            weights.append(jnp.exp2((scores[at] - top).astype(jnp.bfloat16)))
        for at in range(tiles):
            summed = jnp.dot(values, weights[at], preferred_element_type=jnp.float32)
            if not begin:
                summed = summed + acc[at] * jnp.exp2(peak[at, 0:1, :] - tops[at])
            acc[at] = summed
            peak[at] = jnp.broadcast_to(tops[at], peak.shape[1:])

    begun = set(range(count)) - set(fresh)
    for step in plan:
        q, group, kv = step.q, step.group, kvs[step.group]
        q_chunk, k_chunk = q_chunks[q], k_chunks[group]
        if step.same is not None:
            keys_at = k_chunk.places(core, 0, 0, kv.shape[1])
            visible = lambda first, tile: keys_at <= q_chunk.places(core, 1, first, tile)
            own = kv_parts[group][0]
            attend(q, own[step.same], q not in begun, visible=visible)
            begun.add(q)
        start = table[q_chunk.at]
        slots = step.slots
        if not slots:
            continue
        ready(group)
        if step.merged:
            shown = [table[k_chunk.at + slot] < start for slot in slots]

            @pl.when(functools.reduce(jnp.logical_or, shown))
            def _():
                rows = kv.shape[1]
                bias = [
                    jnp.where(see, 0.0, HIDDEN) * jnp.ones((rows, 1), jnp.float32)
                    for see in shown
                ]
                keys_values = kv[slots[0] : slots[-1] + 1].reshape(len(slots) * rows, 2 * HD)
                attend(q, keys_values, False, bias=jnp.concatenate(bias, axis=0))

        else:

            def one(slot, carry):
                @pl.when(table[k_chunk.at + slot] < start)
                def _():
                    attend(q, kv[slot], False)

                return carry

            lax.fori_loop(slots[0], slots[-1] + 1, one, 0)

    for group in list(waits):
        ready(group)
    stores = []
    for out, stage, order in zip(outs, staged, final):
        put = 0
        for q in order:
            acc, heads = states[q][1], qs[q].shape[0]
            tile = acc.shape[2] // heads
            for at in range(acc.shape[0]):
                rows = acc[at, :HD, :] / acc[at, HD : HD + 1, :]
                rows = rows.T.astype(jnp.bfloat16)
                for head in range(heads):
                    stage[put : put + tile, head * HD : (head + 1) * HD] = rows[
                        head * tile : (head + 1) * tile
                    ]
                put += tile
        stores.append(copies.start(stage, out))
    for copy in stores:
        copy.wait()


def attention(plan, table, qs, q_chunks, groups, k_chunks, state, final=()):
    fresh = [at for at, held in enumerate(state) if held is None]
    shapes = []
    for q in qs:
        heads, rows, _ = q.shape
        tile = min(rows, 128)
        shapes += [(rows // tile, deep, heads * tile) for deep in (8, HD + ONES)]
    width = qs[0].shape[0] * HD
    sums = [sum(qs[q].shape[1] for q in order) for order in final]
    outs = [((rows, width), jnp.bfloat16, HBM) for rows in sums]
    scratch = []
    for parts in groups:
        slots = sum(part.shape[0] for part in parts)
        scratch.append(pltpu.VMEM((slots,) + parts[0].shape[1:], jnp.bfloat16))
    scratch += [pltpu.VMEM((rows, width), jnp.bfloat16) for rows in sums]
    parts = [part for parts in groups for part in parts]
    sizes = [len(parts) for parts in groups]
    inputs, aliases = [table, *qs, *parts], {}
    for at, pair in enumerate(state):
        for half, array in enumerate(pair or ()):
            aliases[len(inputs)] = len(outs) + 2 * at + half
            inputs.append(array)
    results = call(
        functools.partial(attention_kernel, plan, q_chunks, k_chunks, sizes, fresh, final),
        "attention",
        10,
        [SMEM] + [VMEM] * (len(inputs) - 1),
        outs + [(shape, jnp.float32, VMEM) for shape in shapes],
        scratch + [pltpu.SemaphoreType.DMA((len(parts) + len(outs),))],
        *inputs,
        aliases=aliases,
    )
    if final:
        return results[: len(final)]
    return [tuple(results[2 * at : 2 * at + 2]) for at in range(len(qs))]


def cut_kernel(sizes, at, table, weights, *refs):
    outs, (held, semaphores) = refs[: len(sizes)], refs[len(sizes) :]
    copies = Copies(semaphores)
    half = sum(sizes)
    first = pl.multiple_of(table[at] * half, half)
    ins, put = [], 0
    for size in sizes:
        target = held.at[pl.ds(put, size)]
        ins.append((copies.start(weights.at[pl.ds(first + put, size)], target), target))
        put += size
    stores = []
    for (copy, piece), out in zip(ins, outs):
        copy.wait()
        stores.append(copies.start(piece, out))
    for copy in stores:
        copy.wait()


def cut(table, at, weights, sizes):
    depth, width = weights.shape
    return call(
        functools.partial(cut_kernel, sizes, at),
        "cut_weights",
        4,
        [SMEM, HBM],
        [((size, width), weights.dtype, HBM) for size in sizes],
        [
            pltpu.VMEM((depth // 2, width), weights.dtype),
            pltpu.SemaphoreType.DMA((2 * len(sizes),)),
        ],
        table,
        weights,
    )


def near_kernel(chunks, left_hbm, weights_hbm, out, left, weights, semaphores):
    copies = Copies(semaphores)
    step = out.shape[1] // chunks
    first = copies.start(left_hbm, left)
    lanes = [pl.ds(chunk * step, step) for chunk in range(chunks)]
    waits = [copies.start(weights_hbm.at[:, at], weights.at[:, at]) for at in lanes]
    first.wait()
    for at, copy in zip(lanes, waits):
        copy.wait()
        out[:, at] = jnp.dot(left[...], weights[:, at], preferred_element_type=jnp.float32)


def output_near(left, weights, chunks=6):
    (rows, columns), width = left.shape, weights.shape[1]
    return call(
        functools.partial(near_kernel, chunks),
        "output_near",
        8,
        [HBM] * 2,
        [((rows, width), jnp.float32, VMEM)],
        [
            pltpu.VMEM(left.shape, left.dtype),
            pltpu.VMEM(weights.shape, weights.dtype),
            pltpu.SemaphoreType.DMA((1 + chunks,)),
        ],
        left,
        weights,
    )[0]


def send_kernel(at, chunks, table, left_hbm, near, *refs):
    count = len(refs) - 5
    pieces, (out, weights, left, staged, semaphores) = refs[:count], refs[count:]
    copies = Copies(semaphores)
    depth, width = weights.shape
    step = width // chunks
    first = copies.start(left_hbm, left)
    waits, put = [], 0
    for index, piece in enumerate(pieces):
        half = table[at] if index < count // 2 else 1 - table[at]
        row = pl.multiple_of(half * (depth // 2) + put % (depth // 2), 16)
        waits.append(copies.start(piece, weights.at[pl.ds(row, piece.shape[0])]))
        put += piece.shape[0]
    for copy in waits:
        copy.wait()
    first.wait()
    half = left.shape[0] // 2
    stores = []
    for chunk in range(chunks):
        span = pl.ds(chunk * step, step)
        staged[:, span] = (
            near[half:, span]
            + jnp.dot(left[half:, :], weights[:, span], preferred_element_type=jnp.float32)
        ).astype(jnp.bfloat16)
        stores.append(copies.start(staged.at[:, span], out.at[:, span]))
    for copy in stores:
        copy.wait()


def output_send(table, at, left, near, pieces, chunks=6):
    (rows, width), columns = near.shape, left.shape[1]
    half, bf16 = (rows // 2, width), jnp.bfloat16
    return call(
        functools.partial(send_kernel, at, chunks),
        "output_send",
        8,
        [SMEM, HBM, VMEM] + [HBM] * len(pieces),
        [(half, bf16, HBM), ((columns, width), bf16, VMEM)],
        [
            pltpu.VMEM(left.shape, bf16),
            pltpu.VMEM(half, bf16),
            pltpu.SemaphoreType.DMA((1 + len(pieces) + chunks,)),
        ],
        table,
        left,
        near,
        *pieces,
    )


def keep_kernel(chunks, left_hbm, hidden, near, weights, out, held, left, semaphores):
    copies = Copies(semaphores)
    first, late = copies.start(left_hbm, left), copies.start(hidden, held)
    first.wait()
    half, step = left.shape[0] // 2, out.shape[1] // chunks
    for chunk in range(chunks):
        span = pl.ds(chunk * step, step)
        out[:, span] = near[:half, span] + jnp.dot(
            left[:half, :], weights[:, span], preferred_element_type=jnp.float32
        )
    late.wait()


def output_keep(left, hidden, near, weights, chunks=6):
    rows, width = near.shape
    return call(
        functools.partial(keep_kernel, chunks),
        "output_keep",
        4,
        [HBM, HBM, VMEM, VMEM],
        [((rows // 2, width), jnp.float32, VMEM), (hidden.shape, hidden.dtype, VMEM)],
        [pltpu.VMEM(left.shape, jnp.bfloat16), pltpu.SemaphoreType.DMA((2,))],
        left,
        hidden,
        near,
        weights,
    )


def final_kernel(chunks, received, hidden, kept, gain, out, other, staged, gains, semaphores):
    copies = Copies(semaphores)
    width = hidden.shape[1]
    step = width // chunks
    lanes = [pl.ds(chunk * step, step) for chunk in range(chunks)]
    waits = [copies.start(received.at[:, span], other.at[:, span]) for span in lanes]
    late = copies.start(gain, gains)
    square = jnp.zeros((hidden.shape[0], 128), jnp.float32)
    for span, copy in zip(lanes, waits):
        copy.wait()
        total = kept[:, span] + other[:, span].astype(jnp.float32)
        for lane in range(0, step, 128):
            part = total[:, lane : lane + 128]
            square = square + part * part
    mean = jnp.sum(square, axis=1, keepdims=True) / width
    scale = lax.rsqrt(mean + EPS)
    late.wait()
    row = gains[...].reshape(1, width)
    stores = []
    for chunk, span in enumerate(lanes):
        total = kept[:, span] + other[:, span].astype(jnp.float32)
        normed = total * scale * row[:, chunk * step : (chunk + 1) * step]
        staged[:, span] = (hidden[:, span].astype(jnp.float32) + normed).astype(jnp.bfloat16)
        stores.append(copies.start(staged.at[:, span], out.at[:, span]))
    for store in stores:
        store.wait()


def output(received, hidden, kept, gain, chunks=6):
    rows, width = hidden.shape
    bf16 = jnp.bfloat16
    return call(
        functools.partial(final_kernel, chunks),
        "output_norm",
        8,
        [HBM, VMEM, VMEM, HBM],
        [((rows, width), bf16, HBM)],
        [
            pltpu.VMEM((rows, width), bf16),
            pltpu.VMEM((rows, width), bf16),
            pltpu.VMEM((width,), jnp.float32),
            pltpu.SemaphoreType.DMA((1 + 2 * chunks,)),
        ],
        received,
        hidden,
        kept,
        gain,
    )[0]


def rotary_table(positions):
    half = HD // 2
    frequency = jnp.power(
        jnp.float32(10000.0), -jnp.arange(half, dtype=jnp.float32) * (2.0 / HD)
    )
    angles = positions.astype(jnp.float32)[:, None] * frequency[None, :]
    cos, sin = jnp.cos(angles), jnp.sin(angles)
    return jnp.concatenate([cos, cos, -sin, sin], axis=1)


def lookup(block_of, index):
    ids = jnp.arange(block_of.shape[0], dtype=jnp.int32)
    return jnp.sum(jnp.where(index[..., None] == ids, block_of, 0), axis=-1)


def flipped(array, axis, bit):
    size = lax.axis_size(axis)
    return lax.ppermute(array, axis, [(i, i ^ bit) for i in range(size)])


def along_line(array):
    size = lax.axis_size("seq")
    parts = [array[None]]
    for by in range(1, size):
        part = lax.ppermute(array, "seq", [(i, (i + by) % size) for i in range(size)])
        parts.append(Came(part[None]))
    return parts


def came(parts):
    return [part.array for part in parts if isinstance(part, Came)]


def after(array, *others):
    return lax.optimization_barrier((array, *others))[0]


def two_chips(hidden, pre_gain, post_gain, wq, wk, wv, w_out, block_of):
    rows = hidden.shape[0]
    block_rows = 2 * rows
    lines, tp = lax.axis_size("seq"), lax.axis_index("tp")
    seq, group = lax.axis_index("seq"), lax.axis_index("groups")
    chip, core = tp // 2, tp % 2

    line = (seq - jnp.arange(lines, dtype=jnp.int32)) % lines
    near_starts = lookup(block_of, 2 * line + chip) * block_rows
    far_starts = lookup(block_of, 2 * line + 1 - chip) * block_rows
    table = jnp.concatenate([jnp.stack([core, group]).astype(jnp.int32), near_starts, far_starts])
    group_at, near_at, far_at = 1, 2, 2 + lines
    run = jnp.arange(rows, dtype=jnp.int32)
    place = jnp.concatenate([core * rows + run, (1 - core) * rows + run])
    trig = rotary_table(jnp.concatenate([near_starts[0] + place, far_starts[0] + place]))
    runs = [(0, 0, rows), (1, 0, rows)]
    near_chunk, far_chunk = Chunk(near_at, runs, rows), Chunk(far_at, runs, rows)
    others, everyone = list(range(1, lines)), list(range(lines))

    own = norm(hidden, pre_gain, [rows])[0]
    away = flipped(own, "tp", 2)
    partner = flipped(own, "tp", 1)

    weights = (wq, wk, wv)
    q_near, kv_near = qkv([own, Came(partner)], weights, trig, 0)
    near = along_line(kv_near)
    half = w_out.shape[0] // 2
    w_cut = cut(table, group_at, after(w_out, kv_near), [half // 4, half * 3 // 8, half * 3 // 8])
    q_near = after(q_near, *w_cut)
    (near_state,) = attention(
        [Step(0, 0, others, same=0)], table, [q_near], [near_chunk], [near], [near_chunk], [None]
    )

    away = after(away, *near_state)
    q_far, kv_far = qkv([Came(away), Came(flipped(away, "tp", 1))], weights, trig, block_rows)
    far = along_line(kv_far)

    fetched = lambda piece, *others: flipped(after(piece, *others), "tp", 2)
    swap = lambda array: flipped(array, "groups", 1)
    w_far = [fetched(piece, away) for piece in w_cut[:2]]
    w_far[0] = after(w_far[0], kv_far)
    near_state, far_state = attention(
        [Step(1, 1, [], same=0), Step(1, 0, everyone), Step(0, 1, [0])],
        table,
        [q_near, q_far],
        [near_chunk, far_chunk],
        [near, far[:1]],
        [near_chunk, far_chunk],
        [near_state, None],
    )
    w_other = [swap(w_far[0])]
    w_far[1] = after(w_far[1], *far_state, *came(far)[:2], w_other[0])
    w_far.append(fetched(w_cut[2], w_far[1]))
    attended, gone = attention(
        [Step(1, 0, others), Step(0, 0, others)],
        table,
        [q_near, q_far],
        [near_chunk, far_chunk],
        [far],
        [far_chunk],
        [near_state, far_state],
        final=[[0], [1]],
    )
    gone = flipped(gone, "tp", 2)
    near_sum = output_near(attended, w_out)
    w_far[2] = after(w_far[2], attended)
    w_other += [swap(piece) for piece in w_far[1:]]
    pieces = [Came(piece) for piece in w_far + w_other]
    sent, w_laid = output_send(table, group_at, Came(gone), near_sum, pieces)
    received = flipped(sent, "tp", 1)
    kept, held = output_keep(Came(gone), hidden, near_sum, w_laid)
    return output(Came(received), held, kept, post_gain)


def any_count(hidden, pre_gain, post_gain, wq, wk, wv, w_out, block_of):
    rows = hidden.shape[0]
    lines = lax.axis_size("seq")
    line = (lax.axis_index("seq") - jnp.arange(lines, dtype=jnp.int32)) % lines
    block = (2 * line[:, None] + jnp.arange(2, dtype=jnp.int32)).reshape(-1)
    block_rows = rows * lax.axis_size("tp") // 2
    starts = lookup(block_of, block) * block_rows
    table = jnp.concatenate([jnp.zeros(2, jnp.int32), starts])
    normed = norm(hidden, pre_gain, [rows], 1)[0]
    normed = lax.all_gather(normed, "tp", axis=0, tiled=True)
    place = jnp.arange(block_rows, dtype=jnp.int32)
    trig = rotary_table((starts[:2, None] + place).reshape(-1))
    qs, keys_values, weights = [], [], (wq, wk, wv)
    for at in range(2):
        first = at * block_rows
        q, kv = qkv([normed[first : first + block_rows]], weights, trig, first)
        qs.append(q)
        keys_values.append(kv)
    kv = lax.all_gather(jnp.stack(keys_values), "seq")[line].reshape(-1, block_rows, 2 * HD)
    rest = list(range(2, 2 * lines))
    runs = [(0, 0, block_rows)]
    attended = attention(
        [Step(0, 0, [1], same=0), Step(1, 0, [0], same=1), Step(0, 0, rest), Step(1, 0, rest)],
        table,
        qs,
        [Chunk(2, runs, 0), Chunk(3, runs, 0)],
        [[kv]],
        [Chunk(2, runs, 0)],
        [None, None],
        final=[[0, 1]],
    )[0]
    partial = jnp.dot(attended, w_out, preferred_element_type=jnp.float32)
    summed = lax.psum_scatter(
        partial.astype(jnp.bfloat16), "tp", scatter_dimension=0, tiled=True
    ).astype(jnp.float32)
    mean = jnp.mean(summed * summed, axis=-1, keepdims=True)
    projected = summed * lax.rsqrt(mean + EPS) * post_gain
    return (hidden.astype(jnp.float32) + projected).astype(jnp.bfloat16)


def solution(mesh):
    return jax.shard_map(
        two_chips if mesh.shape["tp"] == 4 else any_count,
        mesh=mesh,
        in_specs=(
            P(("groups", "seq", "tp"), None),
            P(),
            P(),
            P(None, "tp"),
            P(None, "tp"),
            P(None, "tp"),
            P("tp", None),
            P(),
        ),
        out_specs=P(("groups", "seq", "tp"), None),
        check_vma=False,
    )
```

```python
import functools
import math

import jax
import jax.numpy as jnp
from jax import lax
from jax.experimental import pallas as pl
from jax.experimental.pallas import tpu as pltpu
from jax.sharding import PartitionSpec as P

HD = 128
ATT_SCALAR = 144
EPS = 1e-6
MIB = 1024 * 1024
HIDDEN = -1e30
ONES = 16
COST = pl.CostEstimate(flops=1, bytes_accessed=1, transcendentals=0)

ANY = pl.BlockSpec(memory_space=pl.ANY)
HBM = pl.BlockSpec(memory_space=pltpu.HBM)
VMEM = pl.BlockSpec(memory_space=pltpu.VMEM)
SMEM = pl.BlockSpec(memory_space=pltpu.SMEM)


class Came:
    def __init__(self, array):
        self.array, self.shape = array, array.shape


def call(kernel, name, mib, in_specs, outs, scratch, *args, aliases=None):
    in_specs, pinned = list(in_specs), []
    for at, arg in enumerate(args):
        if isinstance(arg, Came):
            arg, in_specs[at] = arg.array, ANY
        elif in_specs[at] is not SMEM:
            arg = pltpu.with_memory_space_constraint(arg, in_specs[at].memory_space)
        pinned.append(arg)
    return pl.pallas_call(
        kernel,
        in_specs=in_specs,
        out_specs=[spec for _, _, spec in outs],
        out_shape=[spec.memory_space(shape, dtype) for shape, dtype, spec in outs],
        scratch_shapes=scratch,
        input_output_aliases=aliases or {},
        compiler_params=pltpu.CompilerParams(vmem_limit_bytes=mib * MIB),
        cost_estimate=COST,
        name=name,
    )(*pinned)


class Copies:
    def __init__(self, semaphores):
        self.semaphores, self.used = semaphores, 0

    def start(self, source, target):
        copy = pltpu.make_async_copy(source, target, self.semaphores.at[self.used])
        self.used += 1
        copy.start()
        return copy


def norm_kernel(cuts, pieces, hidden, gain, *refs):
    parts, (gains, rows, staged, semaphores) = refs[: len(cuts)], refs[len(cuts) :]
    copies = Copies(semaphores)
    count, width = hidden.shape
    step = count // pieces
    spans = [pl.ds(at * step, step) for at in range(pieces)]
    ins = [copies.start(hidden.at[span], rows.at[span]) for span in spans]
    copies.start(gain, gains).wait()
    scale = gains[...].reshape(1, width)
    outs = []
    for at, span in enumerate(spans):
        ins[at].wait()
        x = rows[span, :].astype(jnp.float32)
        square = x * x
        folded = square[:, :128]
        for lane in range(128, width, 128):
            folded = folded + square[:, lane : lane + 128]
        mean = jnp.sum(folded, axis=1, keepdims=True) / width
        staged[span, :] = (x * lax.rsqrt(mean + EPS) * scale).astype(jnp.bfloat16)
        begin = 0
        for cut, part in zip(cuts, parts):
            if begin <= at * step < begin + cut:
                inside = pl.ds(at * step - begin, step)
                outs.append(copies.start(staged.at[span], part.at[inside]))
            begin += cut
    for copy in outs:
        copy.wait()


def norm(hidden, gain, cuts, pieces=3):
    rows, width = hidden.shape
    bf16 = jnp.bfloat16
    return call(
        functools.partial(norm_kernel, cuts, pieces),
        "norm_rows",
        8,
        [HBM, HBM],
        [((cut, width), bf16, HBM) for cut in cuts],
        [
            pltpu.VMEM((width,), jnp.float32),
            pltpu.VMEM((rows, width), bf16),
            pltpu.VMEM((rows, width), bf16),
            pltpu.SemaphoreType.DMA((1 + 2 * pieces,)),
        ],
        hidden,
        gain,
    )


def rotate_into(product, angles, q, kv):
    cos, sin = angles[:, :HD], angles[:, HD:]
    queries = product.shape[1] - 2 * HD

    def rotated(at):
        y = product[:, at : at + HD]
        return y * cos + pltpu.roll(y, HD // 2, 1) * sin

    factor = ATT_SCALAR ** (-0.5) * math.log2(math.e)
    kv[:, :HD] = rotated(queries).astype(jnp.bfloat16)
    kv[:, HD:] = product[:, queries + HD :].astype(jnp.bfloat16)
    for head in range(queries // HD):
        q[head] = (rotated(head * HD) * factor).astype(jnp.bfloat16)


def qkv_kernel(count, first, chunks, trig, wq, wk, wv, *refs):
    parts = refs[:count]
    q, kv, weights, rows, angles, semaphores = refs[count:]
    copies, waits = Copies(semaphores), []
    depth = weights.shape[0] // chunks
    for chunk in range(chunks):
        span, put, column, here = pl.ds(chunk * depth, depth), 0, 0, []
        for part in parts:
            target = rows.at[pl.ds(put, part.shape[0]), span]
            here.append(copies.start(part.at[:, span], target))
            put += part.shape[0]
        for weight in (wq, wk, wv):
            target = weights.at[span, pl.ds(column, weight.shape[1])]
            here.append(copies.start(weight.at[span], target))
            column += weight.shape[1]
        waits.append(here)
    late = copies.start(trig.at[pl.ds(first, put)], angles)
    product = None
    for chunk, here in enumerate(waits):
        for copy in here:
            copy.wait()
        span = pl.ds(chunk * depth, depth)
        term = jnp.dot(rows[:, span], weights[span, :], preferred_element_type=jnp.float32)
        product = term if product is None else product + term
    late.wait()
    rotate_into(product, angles, q, kv)


def qkv(parts, weights, trig, first, chunks=6):
    total, width = sum(part.shape[0] for part in parts), parts[0].shape[1]
    columns = sum(weight.shape[1] for weight in weights)
    heads, bf16 = columns // HD - 2, jnp.bfloat16
    return call(
        functools.partial(qkv_kernel, len(parts), first, chunks),
        "qkv",
        14,
        [HBM] * (4 + len(parts)),
        [((heads, total, HD), bf16, VMEM), ((total, 2 * HD), bf16, VMEM)],
        [
            pltpu.VMEM((width, columns), bf16),
            pltpu.VMEM((total, width), bf16),
            pltpu.VMEM((total, 2 * HD), jnp.float32),
            pltpu.SemaphoreType.DMA((1 + (len(parts) + 3) * chunks,)),
        ],
        trig,
        *weights,
        *parts,
    )


class Step:
    def __init__(self, q, group, slots, same=None, merged=False):
        self.q, self.group, self.slots = q, group, slots
        self.same, self.merged = same, merged


class Chunk:
    def __init__(self, at, runs, share):
        self.at, self.runs, self.share = at, runs, share

    def places(self, core, axis, first, size):
        shape = (size, 1) if axis == 0 else (1, size)
        index = first + lax.broadcasted_iota(jnp.int32, shape, axis)
        result, begin = index, 0
        for which, offset, rows in self.runs:
            base = (core if which == 0 else 1 - core) * self.share + offset - begin
            inside = (index >= begin) & (index < begin + rows)
            result = jnp.where(inside, index + base, result)
            begin += rows
        return result


def attention_kernel(plan, q_chunks, k_chunks, group_parts, fresh, final, table, *refs):
    refs = list(refs)
    take = lambda n: [refs.pop(0) for _ in range(n)]
    count = len(q_chunks)
    qs = take(count)
    kv_parts = [take(n) for n in group_parts]
    take(2 * (count - len(fresh)))
    outs = take(len(final))
    states = [take(2) for _ in range(count)]
    kvs, staged = take(len(group_parts)), take(len(final))
    (semaphores,) = refs
    copies = Copies(semaphores)
    core = table[0]
    waits = {}
    for group, (parts, kv) in enumerate(zip(kv_parts, kvs)):
        each = kv.shape[0] // len(parts)
        waits[group] = [
            copies.start(part, kv.at[pl.ds(slot * each, each)])
            for slot, part in enumerate(parts)
        ]

    def ready(group):
        for copy in waits.pop(group, []):
            copy.wait()

    def attend(q, keys_values, begin, visible=None, bias=None):
        q_ref, (peak, acc) = qs[q], states[q]
        heads = q_ref.shape[0]
        keys = keys_values[:, :HD]
        values = keys_values[:, HD:].T
        values = jnp.concatenate([values, jnp.ones((ONES, keys.shape[0]), values.dtype)], axis=0)
        tiles, tile = acc.shape[0], acc.shape[2] // heads
        scores, tops, weights = [], [], []
        for at in range(tiles):
            q_tile = q_ref[:, at * tile : (at + 1) * tile, :].reshape(heads * tile, HD)
            score = lax.dot_general(
                keys, q_tile, (((1,), (1,)), ((), ())), preferred_element_type=jnp.float32
            )
            if visible is not None:
                seen = jnp.concatenate([visible(at * tile, tile)] * heads, axis=1)
                score = jnp.where(seen, score, HIDDEN)
            if bias is not None:
                score = score + bias
            scores.append(score)
        for at in range(tiles):
            top = jnp.max(scores[at], axis=0, keepdims=True)
            if not begin:
                top = jnp.maximum(peak[at, 0:1, :], top)
            tops.append(top)
            weights.append(jnp.exp2((scores[at] - top).astype(jnp.bfloat16)))
        for at in range(tiles):
            summed = jnp.dot(values, weights[at], preferred_element_type=jnp.float32)
            if not begin:
                summed = summed + acc[at] * jnp.exp2(peak[at, 0:1, :] - tops[at])
            acc[at] = summed
            peak[at] = jnp.broadcast_to(tops[at], peak.shape[1:])

    begun = set(range(count)) - set(fresh)
    for step in plan:
        q, group, kv = step.q, step.group, kvs[step.group]
        q_chunk, k_chunk = q_chunks[q], k_chunks[group]
        if step.same is not None:
            keys_at = k_chunk.places(core, 0, 0, kv.shape[1])
            visible = lambda first, tile: keys_at <= q_chunk.places(core, 1, first, tile)
            own = kv_parts[group][0]
            attend(q, own[step.same], q not in begun, visible=visible)
            begun.add(q)
        start = table[q_chunk.at]
        slots = step.slots
        if not slots:
            continue
        ready(group)
        if step.merged:
            shown = [table[k_chunk.at + slot] < start for slot in slots]

            @pl.when(functools.reduce(jnp.logical_or, shown))
            def _():
                rows = kv.shape[1]
                bias = [
                    jnp.where(see, 0.0, HIDDEN) * jnp.ones((rows, 1), jnp.float32)
                    for see in shown
                ]
                keys_values = kv[slots[0] : slots[-1] + 1].reshape(len(slots) * rows, 2 * HD)
                attend(q, keys_values, False, bias=jnp.concatenate(bias, axis=0))

        else:

            def one(slot, carry):
                @pl.when(table[k_chunk.at + slot] < start)
                def _():
                    attend(q, kv[slot], False)

                return carry

            lax.fori_loop(slots[0], slots[-1] + 1, one, 0)

    for group in list(waits):
        ready(group)
    stores = []
    for out, stage, order in zip(outs, staged, final):
        put = 0
        for q in order:
            acc, heads = states[q][1], qs[q].shape[0]
            tile = acc.shape[2] // heads
            for at in range(acc.shape[0]):
                rows = acc[at, :HD, :] / acc[at, HD : HD + 1, :]
                rows = rows.T.astype(jnp.bfloat16)
                for head in range(heads):
                    stage[put : put + tile, head * HD : (head + 1) * HD] = rows[
                        head * tile : (head + 1) * tile
                    ]
                put += tile
        stores.append(copies.start(stage, out))
    for copy in stores:
        copy.wait()


def attention(plan, table, qs, q_chunks, groups, k_chunks, state, final=()):
    fresh = [at for at, held in enumerate(state) if held is None]
    shapes = []
    for q in qs:
        heads, rows, _ = q.shape
        tile = min(rows, 128)
        shapes += [(rows // tile, deep, heads * tile) for deep in (8, HD + ONES)]
    width = qs[0].shape[0] * HD
    sums = [sum(qs[q].shape[1] for q in order) for order in final]
    outs = [((rows, width), jnp.bfloat16, HBM) for rows in sums]
    scratch = []
    for parts in groups:
        slots = sum(part.shape[0] for part in parts)
        scratch.append(pltpu.VMEM((slots,) + parts[0].shape[1:], jnp.bfloat16))
    scratch += [pltpu.VMEM((rows, width), jnp.bfloat16) for rows in sums]
    parts = [part for parts in groups for part in parts]
    sizes = [len(parts) for parts in groups]
    inputs, aliases = [table, *qs, *parts], {}
    for at, pair in enumerate(state):
        for half, array in enumerate(pair or ()):
            aliases[len(inputs)] = len(outs) + 2 * at + half
            inputs.append(array)
    results = call(
        functools.partial(attention_kernel, plan, q_chunks, k_chunks, sizes, fresh, final),
        "attention",
        10,
        [SMEM] + [VMEM] * (len(inputs) - 1),
        outs + [(shape, jnp.float32, VMEM) for shape in shapes],
        scratch + [pltpu.SemaphoreType.DMA((len(parts) + len(outs),))],
        *inputs,
        aliases=aliases,
    )
    if final:
        return results[: len(final)]
    return [tuple(results[2 * at : 2 * at + 2]) for at in range(len(qs))]


def cut_kernel(sizes, at, table, weights, *refs):
    outs, (held, semaphores) = refs[: len(sizes)], refs[len(sizes) :]
    copies = Copies(semaphores)
    half = sum(sizes)
    first = pl.multiple_of(table[at] * half, half)
    ins, put = [], 0
    for size in sizes:
        target = held.at[pl.ds(put, size)]
        ins.append((copies.start(weights.at[pl.ds(first + put, size)], target), target))
        put += size
    stores = []
    for (copy, piece), out in zip(ins, outs):
        copy.wait()
        stores.append(copies.start(piece, out))
    for copy in stores:
        copy.wait()


def cut(table, at, weights, sizes):
    depth, width = weights.shape
    return call(
        functools.partial(cut_kernel, sizes, at),
        "cut_weights",
        4,
        [SMEM, HBM],
        [((size, width), weights.dtype, HBM) for size in sizes],
        [
            pltpu.VMEM((depth // 2, width), weights.dtype),
            pltpu.SemaphoreType.DMA((2 * len(sizes),)),
        ],
        table,
        weights,
    )


def near_kernel(chunks, left_hbm, weights_hbm, out, left, weights, semaphores):
    copies = Copies(semaphores)
    step = out.shape[1] // chunks
    first = copies.start(left_hbm, left)
    lanes = [pl.ds(chunk * step, step) for chunk in range(chunks)]
    waits = [copies.start(weights_hbm.at[:, at], weights.at[:, at]) for at in lanes]
    first.wait()
    for at, copy in zip(lanes, waits):
        copy.wait()
        out[:, at] = jnp.dot(left[...], weights[:, at], preferred_element_type=jnp.float32)


def output_near(left, weights, chunks=6):
    (rows, columns), width = left.shape, weights.shape[1]
    return call(
        functools.partial(near_kernel, chunks),
        "output_near",
        8,
        [HBM] * 2,
        [((rows, width), jnp.float32, VMEM)],
        [
            pltpu.VMEM(left.shape, left.dtype),
            pltpu.VMEM(weights.shape, weights.dtype),
            pltpu.SemaphoreType.DMA((1 + chunks,)),
        ],
        left,
        weights,
    )[0]


def send_kernel(at, chunks, table, left_hbm, near, *refs):
    count = len(refs) - 5
    pieces, (out, weights, left, staged, semaphores) = refs[:count], refs[count:]
    copies = Copies(semaphores)
    depth, width = weights.shape
    step = width // chunks
    first = copies.start(left_hbm, left)
    waits, put = [], 0
    for index, piece in enumerate(pieces):
        half = table[at] if index < count // 2 else 1 - table[at]
        row = pl.multiple_of(half * (depth // 2) + put % (depth // 2), 16)
        waits.append(copies.start(piece, weights.at[pl.ds(row, piece.shape[0])]))
        put += piece.shape[0]
    for copy in waits:
        copy.wait()
    first.wait()
    half = left.shape[0] // 2
    stores = []
    for chunk in range(chunks):
        span = pl.ds(chunk * step, step)
        staged[:, span] = (
            near[half:, span]
            + jnp.dot(left[half:, :], weights[:, span], preferred_element_type=jnp.float32)
        ).astype(jnp.bfloat16)
        stores.append(copies.start(staged.at[:, span], out.at[:, span]))
    for copy in stores:
        copy.wait()


def output_send(table, at, left, near, pieces, chunks=6):
    (rows, width), columns = near.shape, left.shape[1]
    half, bf16 = (rows // 2, width), jnp.bfloat16
    return call(
        functools.partial(send_kernel, at, chunks),
        "output_send",
        8,
        [SMEM, HBM, VMEM] + [HBM] * len(pieces),
        [(half, bf16, HBM), ((columns, width), bf16, VMEM)],
        [
            pltpu.VMEM(left.shape, bf16),
            pltpu.VMEM(half, bf16),
            pltpu.SemaphoreType.DMA((1 + len(pieces) + chunks,)),
        ],
        table,
        left,
        near,
        *pieces,
    )


def keep_kernel(chunks, left_hbm, hidden, near, weights, out, held, left, semaphores):
    copies = Copies(semaphores)
    first, late = copies.start(left_hbm, left), copies.start(hidden, held)
    first.wait()
    half, step = left.shape[0] // 2, out.shape[1] // chunks
    for chunk in range(chunks):
        span = pl.ds(chunk * step, step)
        out[:, span] = near[:half, span] + jnp.dot(
            left[:half, :], weights[:, span], preferred_element_type=jnp.float32
        )
    late.wait()


def output_keep(left, hidden, near, weights, chunks=6):
    rows, width = near.shape
    return call(
        functools.partial(keep_kernel, chunks),
        "output_keep",
        4,
        [HBM, HBM, VMEM, VMEM],
        [((rows // 2, width), jnp.float32, VMEM), (hidden.shape, hidden.dtype, VMEM)],
        [pltpu.VMEM(left.shape, jnp.bfloat16), pltpu.SemaphoreType.DMA((2,))],
        left,
        hidden,
        near,
        weights,
    )


def final_kernel(chunks, received, hidden, kept, gain, out, other, staged, gains, semaphores):
    copies = Copies(semaphores)
    width = hidden.shape[1]
    step = width // chunks
    lanes = [pl.ds(chunk * step, step) for chunk in range(chunks)]
    waits = [copies.start(received.at[:, span], other.at[:, span]) for span in lanes]
    late = copies.start(gain, gains)
    square = jnp.zeros((hidden.shape[0], 128), jnp.float32)
    for span, copy in zip(lanes, waits):
        copy.wait()
        total = kept[:, span] + other[:, span].astype(jnp.float32)
        for lane in range(0, step, 128):
            part = total[:, lane : lane + 128]
            square = square + part * part
    mean = jnp.sum(square, axis=1, keepdims=True) / width
    scale = lax.rsqrt(mean + EPS)
    late.wait()
    row = gains[...].reshape(1, width)
    stores = []
    for chunk, span in enumerate(lanes):
        total = kept[:, span] + other[:, span].astype(jnp.float32)
        normed = total * scale * row[:, chunk * step : (chunk + 1) * step]
        staged[:, span] = (hidden[:, span].astype(jnp.float32) + normed).astype(jnp.bfloat16)
        stores.append(copies.start(staged.at[:, span], out.at[:, span]))
    for store in stores:
        store.wait()


def output(received, hidden, kept, gain, chunks=6):
    rows, width = hidden.shape
    bf16 = jnp.bfloat16
    return call(
        functools.partial(final_kernel, chunks),
        "output_norm",
        8,
        [HBM, VMEM, VMEM, HBM],
        [((rows, width), bf16, HBM)],
        [
            pltpu.VMEM((rows, width), bf16),
            pltpu.VMEM((rows, width), bf16),
            pltpu.VMEM((width,), jnp.float32),
            pltpu.SemaphoreType.DMA((1 + 2 * chunks,)),
        ],
        received,
        hidden,
        kept,
        gain,
    )[0]


def rotary_table(positions):
    half = HD // 2
    frequency = jnp.power(
        jnp.float32(10000.0), -jnp.arange(half, dtype=jnp.float32) * (2.0 / HD)
    )
    angles = positions.astype(jnp.float32)[:, None] * frequency[None, :]
    cos, sin = jnp.cos(angles), jnp.sin(angles)
    return jnp.concatenate([cos, cos, -sin, sin], axis=1)


def lookup(block_of, index):
    ids = jnp.arange(block_of.shape[0], dtype=jnp.int32)
    return jnp.sum(jnp.where(index[..., None] == ids, block_of, 0), axis=-1)


def flipped(array, axis, bit):
    size = lax.axis_size(axis)
    return lax.ppermute(array, axis, [(i, i ^ bit) for i in range(size)])


def along_line(array):
    size = lax.axis_size("seq")
    parts = [array[None]]
    for by in range(1, size):
        part = lax.ppermute(array, "seq", [(i, (i + by) % size) for i in range(size)])
        parts.append(Came(part[None]))
    return parts


def along_ring(array):
    size = lax.axis_size("seq")
    parts, part = [array[None]], array
    for _ in range(1, size):
        part = lax.ppermute(part, "seq", [(i, (i + 1) % size) for i in range(size)])
        parts.append(Came(part[None]))
    return parts


def came(parts):
    return [part.array for part in parts if isinstance(part, Came)]


def after(array, *others):
    return lax.optimization_barrier((array, *others))[0]


def two_chips(hidden, pre_gain, post_gain, wq, wk, wv, w_out, block_of):
    rows = hidden.shape[0]
    block_rows = 2 * rows
    lines, tp = lax.axis_size("seq"), lax.axis_index("tp")
    seq, group = lax.axis_index("seq"), lax.axis_index("groups")
    chip, core = tp // 2, tp % 2

    line = (seq - jnp.arange(lines, dtype=jnp.int32)) % lines
    near_starts = lookup(block_of, 2 * line + chip) * block_rows
    far_starts = lookup(block_of, 2 * line + 1 - chip) * block_rows
    table = jnp.concatenate([jnp.stack([core, group]).astype(jnp.int32), near_starts, far_starts])
    group_at, near_at, far_at = 1, 2, 2 + lines
    run = jnp.arange(rows, dtype=jnp.int32)
    place = jnp.concatenate([core * rows + run, (1 - core) * rows + run])
    trig = rotary_table(jnp.concatenate([near_starts[0] + place, far_starts[0] + place]))
    runs = [(0, 0, rows), (1, 0, rows)]
    near_chunk, far_chunk = Chunk(near_at, runs, rows), Chunk(far_at, runs, rows)
    others, everyone = list(range(1, lines)), list(range(lines))

    own = norm(hidden, pre_gain, [rows])[0]
    away = flipped(own, "tp", 2)
    partner = flipped(own, "tp", 1)

    weights = (wq, wk, wv)
    q_near, kv_near = qkv([own, Came(partner)], weights, trig, 0)
    near = along_line(kv_near)
    half = w_out.shape[0] // 2
    w_cut = cut(table, group_at, after(w_out, kv_near), [half // 4] * 4)
    q_near = after(q_near, *w_cut)
    (near_state,) = attention(
        [Step(0, 0, others, same=0)], table, [q_near], [near_chunk], [near], [near_chunk], [None]
    )

    away = after(away, *near_state)
    q_far, kv_far = qkv([Came(away), Came(flipped(away, "tp", 1))], weights, trig, block_rows)
    far = along_ring(kv_far)

    fetched = lambda piece, *others: flipped(after(piece, *others), "tp", 2)
    swap = lambda array: flipped(array, "groups", 1)
    w_far = [fetched(piece, away) for piece in w_cut[:2]]
    w_far[0] = after(w_far[0], kv_far)
    w_far.append(fetched(w_cut[2], w_far[0]))
    w_other = [swap(w_far[0])]
    w_far[1] = after(w_far[1], came(far)[0], w_other[0])
    w_far.append(fetched(w_cut[3], w_far[1]))
    w_other.append(swap(w_far[1]))

    near_state, far_state = attention(
        [Step(1, 1, [], same=0), Step(1, 0, everyone), Step(0, 1, [0])],
        table,
        [q_near, q_far],
        [near_chunk, far_chunk],
        [near, far[:1]],
        [near_chunk, far_chunk],
        [near_state, None],
    )
    w_far[2] = after(w_far[2], *far_state, w_other[1])
    w_other.append(swap(w_far[2]))
    attended, gone = attention(
        [Step(1, 0, others), Step(0, 0, others)],
        table,
        [q_near, q_far],
        [near_chunk, far_chunk],
        [far],
        [far_chunk],
        [near_state, far_state],
        final=[[0], [1]],
    )
    gone = flipped(gone, "tp", 2)
    near_sum = output_near(attended, w_out)
    w_other.append(swap(after(w_far[3], attended)))
    pieces = [Came(piece) for piece in w_far + w_other]
    sent, w_laid = output_send(table, group_at, Came(gone), near_sum, pieces)
    received = flipped(sent, "tp", 1)
    kept, held = output_keep(Came(gone), hidden, near_sum, w_laid)
    return output(Came(received), held, kept, post_gain)


def any_count(hidden, pre_gain, post_gain, wq, wk, wv, w_out, block_of):
    rows = hidden.shape[0]
    lines = lax.axis_size("seq")
    line = (lax.axis_index("seq") - jnp.arange(lines, dtype=jnp.int32)) % lines
    block = (2 * line[:, None] + jnp.arange(2, dtype=jnp.int32)).reshape(-1)
    block_rows = rows * lax.axis_size("tp") // 2
    starts = lookup(block_of, block) * block_rows
    table = jnp.concatenate([jnp.zeros(2, jnp.int32), starts])
    normed = norm(hidden, pre_gain, [rows], 1)[0]
    normed = lax.all_gather(normed, "tp", axis=0, tiled=True)
    place = jnp.arange(block_rows, dtype=jnp.int32)
    trig = rotary_table((starts[:2, None] + place).reshape(-1))
    qs, keys_values, weights = [], [], (wq, wk, wv)
    for at in range(2):
        first = at * block_rows
        q, kv = qkv([normed[first : first + block_rows]], weights, trig, first)
        qs.append(q)
        keys_values.append(kv)
    kv = lax.all_gather(jnp.stack(keys_values), "seq")[line].reshape(-1, block_rows, 2 * HD)
    rest = list(range(2, 2 * lines))
    runs = [(0, 0, block_rows)]
    attended = attention(
        [Step(0, 0, [1], same=0), Step(1, 0, [0], same=1), Step(0, 0, rest), Step(1, 0, rest)],
        table,
        qs,
        [Chunk(2, runs, 0), Chunk(3, runs, 0)],
        [[kv]],
        [Chunk(2, runs, 0)],
        [None, None],
        final=[[0, 1]],
    )[0]
    partial = jnp.dot(attended, w_out, preferred_element_type=jnp.float32)
    summed = lax.psum_scatter(
        partial.astype(jnp.bfloat16), "tp", scatter_dimension=0, tiled=True
    ).astype(jnp.float32)
    mean = jnp.mean(summed * summed, axis=-1, keepdims=True)
    projected = summed * lax.rsqrt(mean + EPS) * post_gain
    return (hidden.astype(jnp.float32) + projected).astype(jnp.bfloat16)


def solution(mesh):
    return jax.shard_map(
        two_chips if mesh.shape["tp"] == 4 else any_count,
        mesh=mesh,
        in_specs=(
            P(("groups", "seq", "tp"), None),
            P(),
            P(),
            P(None, "tp"),
            P(None, "tp"),
            P(None, "tp"),
            P("tp", None),
            P(),
        ),
        out_specs=P(("groups", "seq", "tp"), None),
        check_vma=False,
    )
```

```python
import functools
import math

import jax
import jax.numpy as jnp
from jax import lax
from jax.experimental import pallas as pl
from jax.experimental.pallas import tpu as pltpu
from jax.sharding import PartitionSpec as P

HD = 128
ATT_SCALAR = 144
EPS = 1e-6
MIB = 1024 * 1024
HIDDEN = -1e30
ONES = 16
COST = pl.CostEstimate(flops=1, bytes_accessed=1, transcendentals=0)

ANY = pl.BlockSpec(memory_space=pl.ANY)
HBM = pl.BlockSpec(memory_space=pltpu.HBM)
VMEM = pl.BlockSpec(memory_space=pltpu.VMEM)
SMEM = pl.BlockSpec(memory_space=pltpu.SMEM)


class Came:
    def __init__(self, array):
        self.array, self.shape = array, array.shape


def call(kernel, name, mib, in_specs, outs, scratch, *args, aliases=None):
    in_specs, pinned = list(in_specs), []
    for at, arg in enumerate(args):
        if isinstance(arg, Came):
            arg, in_specs[at] = arg.array, ANY
        elif in_specs[at] is not SMEM:
            arg = pltpu.with_memory_space_constraint(arg, in_specs[at].memory_space)
        pinned.append(arg)
    return pl.pallas_call(
        kernel,
        in_specs=in_specs,
        out_specs=[spec for _, _, spec in outs],
        out_shape=[spec.memory_space(shape, dtype) for shape, dtype, spec in outs],
        scratch_shapes=scratch,
        input_output_aliases=aliases or {},
        compiler_params=pltpu.CompilerParams(vmem_limit_bytes=mib * MIB),
        cost_estimate=COST,
        name=name,
    )(*pinned)


class Copies:
    def __init__(self, semaphores):
        self.semaphores, self.used = semaphores, 0

    def start(self, source, target):
        copy = pltpu.make_async_copy(source, target, self.semaphores.at[self.used])
        self.used += 1
        copy.start()
        return copy


def norm_kernel(cuts, pieces, hidden, gain, *refs):
    parts, (gains, rows, staged, semaphores) = refs[: len(cuts)], refs[len(cuts) :]
    copies = Copies(semaphores)
    count, width = hidden.shape
    step = count // pieces
    spans = [pl.ds(at * step, step) for at in range(pieces)]
    ins = [copies.start(hidden.at[span], rows.at[span]) for span in spans]
    copies.start(gain, gains).wait()
    scale = gains[...].reshape(1, width)
    outs = []
    for at, span in enumerate(spans):
        ins[at].wait()
        x = rows[span, :].astype(jnp.float32)
        square = x * x
        folded = square[:, :128]
        for lane in range(128, width, 128):
            folded = folded + square[:, lane : lane + 128]
        mean = jnp.sum(folded, axis=1, keepdims=True) / width
        staged[span, :] = (x * lax.rsqrt(mean + EPS) * scale).astype(jnp.bfloat16)
        begin = 0
        for cut, part in zip(cuts, parts):
            if begin <= at * step < begin + cut:
                inside = pl.ds(at * step - begin, step)
                outs.append(copies.start(staged.at[span], part.at[inside]))
            begin += cut
    for copy in outs:
        copy.wait()


def norm(hidden, gain, cuts, pieces=3):
    rows, width = hidden.shape
    bf16 = jnp.bfloat16
    return call(
        functools.partial(norm_kernel, cuts, pieces),
        "norm_rows",
        8,
        [HBM, HBM],
        [((cut, width), bf16, HBM) for cut in cuts],
        [
            pltpu.VMEM((width,), jnp.float32),
            pltpu.VMEM((rows, width), bf16),
            pltpu.VMEM((rows, width), bf16),
            pltpu.SemaphoreType.DMA((1 + 2 * pieces,)),
        ],
        hidden,
        gain,
    )


def qkv_kernel(count, kinds, first, chunks, trig, *refs):
    refs = list(refs)
    take = lambda n: [refs.pop(0) for _ in range(n)]
    given, parts = take(len(kinds)), take(count)
    q, kv = take(1)[0] if "q" in kinds else None, take(1)[0] if "k" in kinds else None
    weights, rows, angles, semaphores = refs
    copies, waits = Copies(semaphores), []
    depth = weights.shape[0] // chunks
    for chunk in range(chunks):
        span, put, column, here = pl.ds(chunk * depth, depth), 0, 0, []
        for part in parts:
            target = rows.at[pl.ds(put, part.shape[0]), span]
            here.append(copies.start(part.at[:, span], target))
            put += part.shape[0]
        for weight in given:
            target = weights.at[span, pl.ds(column, weight.shape[1])]
            here.append(copies.start(weight.at[span], target))
            column += weight.shape[1]
        waits.append(here)
    late = copies.start(trig.at[pl.ds(first, put)], angles)
    product = None
    for chunk, here in enumerate(waits):
        for copy in here:
            copy.wait()
        span = pl.ds(chunk * depth, depth)
        term = jnp.dot(rows[:, span], weights[span, :], preferred_element_type=jnp.float32)
        product = term if product is None else product + term
    late.wait()
    cos, sin = angles[:, :HD], angles[:, HD:]

    def rotated(at):
        y = product[:, at : at + HD]
        return y * cos + pltpu.roll(y, HD // 2, 1) * sin

    factor = ATT_SCALAR ** (-0.5) * math.log2(math.e)
    if kv is not None:
        begin = product.shape[1] - 2 * HD
        kv[:, :HD] = rotated(begin).astype(jnp.bfloat16)
        kv[:, HD:] = product[:, begin + HD :].astype(jnp.bfloat16)
    if q is not None:
        for head in range(q.shape[0]):
            q[head] = (rotated(head * HD) * factor).astype(jnp.bfloat16)


def qkv(parts, weights, kinds, trig, first, chunks=6):
    given = [weights["qkv".index(kind)] for kind in kinds]
    total, width = sum(part.shape[0] for part in parts), parts[0].shape[1]
    columns = sum(weight.shape[1] for weight in given)
    heads, bf16 = weights[0].shape[1] // HD, jnp.bfloat16
    outs = [((heads, total, HD), bf16, VMEM)] * ("q" in kinds)
    outs += [((total, 2 * HD), bf16, VMEM)] * ("k" in kinds)
    return call(
        functools.partial(qkv_kernel, len(parts), kinds, first, chunks),
        "project_" + kinds,
        14,
        [HBM] * (1 + len(given) + len(parts)),
        outs,
        [
            pltpu.VMEM((width, columns), bf16),
            pltpu.VMEM((total, width), bf16),
            pltpu.VMEM((total, 2 * HD), jnp.float32),
            pltpu.SemaphoreType.DMA((1 + (len(parts) + len(given)) * chunks,)),
        ],
        trig,
        *given,
        *parts,
    )


class Step:
    def __init__(self, q, group, slots, same=None, merged=False):
        self.q, self.group, self.slots = q, group, slots
        self.same, self.merged = same, merged


class Chunk:
    def __init__(self, at, runs, share):
        self.at, self.runs, self.share = at, runs, share

    def places(self, core, axis, first, size):
        shape = (size, 1) if axis == 0 else (1, size)
        index = first + lax.broadcasted_iota(jnp.int32, shape, axis)
        result, begin = index, 0
        for which, offset, rows in self.runs:
            base = (core if which == 0 else 1 - core) * self.share + offset - begin
            inside = (index >= begin) & (index < begin + rows)
            result = jnp.where(inside, index + base, result)
            begin += rows
        return result


def attention_kernel(plan, q_chunks, k_chunks, group_parts, fresh, final, table, *refs):
    refs = list(refs)
    take = lambda n: [refs.pop(0) for _ in range(n)]
    count = len(q_chunks)
    qs = take(count)
    kv_parts = [take(n) for n in group_parts]
    take(2 * (count - len(fresh)))
    outs = take(len(final))
    states = [take(2) for _ in range(count)]
    kvs, staged = take(len(group_parts)), take(len(final))
    (semaphores,) = refs
    copies = Copies(semaphores)
    core = table[0]
    waits = {}
    for group, (parts, kv) in enumerate(zip(kv_parts, kvs)):
        each = kv.shape[0] // len(parts)
        waits[group] = [
            copies.start(part, kv.at[pl.ds(slot * each, each)])
            for slot, part in enumerate(parts)
        ]

    def ready(group):
        for copy in waits.pop(group, []):
            copy.wait()

    def attend(q, keys_values, begin, visible=None, bias=None):
        q_ref, (peak, acc) = qs[q], states[q]
        heads = q_ref.shape[0]
        keys = keys_values[:, :HD]
        values = keys_values[:, HD:].T
        values = jnp.concatenate([values, jnp.ones((ONES, keys.shape[0]), values.dtype)], axis=0)
        tiles, tile = acc.shape[0], acc.shape[2] // heads
        scores, tops, weights = [], [], []
        for at in range(tiles):
            q_tile = q_ref[:, at * tile : (at + 1) * tile, :].reshape(heads * tile, HD)
            score = lax.dot_general(
                keys, q_tile, (((1,), (1,)), ((), ())), preferred_element_type=jnp.float32
            )
            if visible is not None:
                seen = jnp.concatenate([visible(at * tile, tile)] * heads, axis=1)
                score = jnp.where(seen, score, HIDDEN)
            if bias is not None:
                score = score + bias
            scores.append(score)
        for at in range(tiles):
            top = jnp.max(scores[at], axis=0, keepdims=True)
            if not begin:
                top = jnp.maximum(peak[at, 0:1, :], top)
            tops.append(top)
            weights.append(jnp.exp2((scores[at] - top).astype(jnp.bfloat16)))
        for at in range(tiles):
            summed = jnp.dot(values, weights[at], preferred_element_type=jnp.float32)
            if not begin:
                summed = summed + acc[at] * jnp.exp2(peak[at, 0:1, :] - tops[at])
            acc[at] = summed
            peak[at] = jnp.broadcast_to(tops[at], peak.shape[1:])

    begun = set(range(count)) - set(fresh)
    for step in plan:
        q, group, kv = step.q, step.group, kvs[step.group]
        q_chunk, k_chunk = q_chunks[q], k_chunks[group]
        if step.same is not None:
            keys_at = k_chunk.places(core, 0, 0, kv.shape[1])
            visible = lambda first, tile: keys_at <= q_chunk.places(core, 1, first, tile)
            own = kv_parts[group][0]
            attend(q, own[step.same], q not in begun, visible=visible)
            begun.add(q)
        start = table[q_chunk.at]
        slots = step.slots
        if not slots:
            continue
        ready(group)
        if step.merged:
            shown = [table[k_chunk.at + slot] < start for slot in slots]

            @pl.when(functools.reduce(jnp.logical_or, shown))
            def _():
                rows = kv.shape[1]
                bias = [
                    jnp.where(see, 0.0, HIDDEN) * jnp.ones((rows, 1), jnp.float32)
                    for see in shown
                ]
                keys_values = kv[slots[0] : slots[-1] + 1].reshape(len(slots) * rows, 2 * HD)
                attend(q, keys_values, False, bias=jnp.concatenate(bias, axis=0))

        else:

            def one(slot, carry):
                @pl.when(table[k_chunk.at + slot] < start)
                def _():
                    attend(q, kv[slot], False)

                return carry

            lax.fori_loop(slots[0], slots[-1] + 1, one, 0)

    for group in list(waits):
        ready(group)
    stores = []
    for out, stage, order in zip(outs, staged, final):
        put = 0
        for q in order:
            acc, heads = states[q][1], qs[q].shape[0]
            tile = acc.shape[2] // heads
            for at in range(acc.shape[0]):
                rows = acc[at, :HD, :] / acc[at, HD : HD + 1, :]
                rows = rows.T.astype(jnp.bfloat16)
                for head in range(heads):
                    stage[put : put + tile, head * HD : (head + 1) * HD] = rows[
                        head * tile : (head + 1) * tile
                    ]
                put += tile
        stores.append(copies.start(stage, out))
    for copy in stores:
        copy.wait()


def attention(plan, table, qs, q_chunks, groups, k_chunks, state, final=()):
    fresh = [at for at, held in enumerate(state) if held is None]
    shapes = []
    for q in qs:
        heads, rows, _ = q.shape
        tile = min(rows, 128)
        shapes += [(rows // tile, deep, heads * tile) for deep in (8, HD + ONES)]
    width = qs[0].shape[0] * HD
    sums = [sum(qs[q].shape[1] for q in order) for order in final]
    outs = [((rows, width), jnp.bfloat16, HBM) for rows in sums]
    scratch = []
    for parts in groups:
        slots = sum(part.shape[0] for part in parts)
        scratch.append(pltpu.VMEM((slots,) + parts[0].shape[1:], jnp.bfloat16))
    scratch += [pltpu.VMEM((rows, width), jnp.bfloat16) for rows in sums]
    parts = [part for parts in groups for part in parts]
    sizes = [len(parts) for parts in groups]
    inputs, aliases = [table, *qs, *parts], {}
    for at, pair in enumerate(state):
        for half, array in enumerate(pair or ()):
            aliases[len(inputs)] = len(outs) + 2 * at + half
            inputs.append(array)
    results = call(
        functools.partial(attention_kernel, plan, q_chunks, k_chunks, sizes, fresh, final),
        "attention",
        10,
        [SMEM] + [VMEM] * (len(inputs) - 1),
        outs + [(shape, jnp.float32, VMEM) for shape in shapes],
        scratch + [pltpu.SemaphoreType.DMA((len(parts) + len(outs),))],
        *inputs,
        aliases=aliases,
    )
    if final:
        return results[: len(final)]
    return [tuple(results[2 * at : 2 * at + 2]) for at in range(len(qs))]


def cut_kernel(sizes, at, table, weights, *refs):
    outs, (held, semaphores) = refs[: len(sizes)], refs[len(sizes) :]
    copies = Copies(semaphores)
    half = sum(sizes)
    first = pl.multiple_of(table[at] * half, half)
    ins, put = [], 0
    for size in sizes:
        target = held.at[pl.ds(put, size)]
        ins.append((copies.start(weights.at[pl.ds(first + put, size)], target), target))
        put += size
    stores = []
    for (copy, piece), out in zip(ins, outs):
        copy.wait()
        stores.append(copies.start(piece, out))
    for copy in stores:
        copy.wait()


def cut(table, at, weights, sizes):
    depth, width = weights.shape
    return call(
        functools.partial(cut_kernel, sizes, at),
        "cut_weights",
        4,
        [SMEM, HBM],
        [((size, width), weights.dtype, HBM) for size in sizes],
        [
            pltpu.VMEM((depth // 2, width), weights.dtype),
            pltpu.SemaphoreType.DMA((2 * len(sizes),)),
        ],
        table,
        weights,
    )


def near_kernel(chunks, left_hbm, weights_hbm, out, left, weights, semaphores):
    copies = Copies(semaphores)
    step = out.shape[1] // chunks
    first = copies.start(left_hbm, left)
    lanes = [pl.ds(chunk * step, step) for chunk in range(chunks)]
    waits = [copies.start(weights_hbm.at[:, at], weights.at[:, at]) for at in lanes]
    first.wait()
    for at, copy in zip(lanes, waits):
        copy.wait()
        out[:, at] = jnp.dot(left[...], weights[:, at], preferred_element_type=jnp.float32)


def output_near(left, weights, chunks=6):
    (rows, columns), width = left.shape, weights.shape[1]
    return call(
        functools.partial(near_kernel, chunks),
        "output_near",
        8,
        [HBM] * 2,
        [((rows, width), jnp.float32, VMEM)],
        [
            pltpu.VMEM(left.shape, left.dtype),
            pltpu.VMEM(weights.shape, weights.dtype),
            pltpu.SemaphoreType.DMA((1 + chunks,)),
        ],
        left,
        weights,
    )[0]


def send_kernel(at, chunks, table, left_hbm, near, *refs):
    count = len(refs) - 5
    pieces, (out, weights, left, staged, semaphores) = refs[:count], refs[count:]
    copies = Copies(semaphores)
    depth, width = weights.shape
    step = width // chunks
    first = copies.start(left_hbm, left)
    waits, put = [], 0
    for index, piece in enumerate(pieces):
        half = table[at] if index < count // 2 else 1 - table[at]
        row = pl.multiple_of(half * (depth // 2) + put % (depth // 2), 16)
        waits.append(copies.start(piece, weights.at[pl.ds(row, piece.shape[0])]))
        put += piece.shape[0]
    for copy in waits:
        copy.wait()
    first.wait()
    half = left.shape[0] // 2
    stores = []
    for chunk in range(chunks):
        span = pl.ds(chunk * step, step)
        staged[:, span] = (
            near[half:, span]
            + jnp.dot(left[half:, :], weights[:, span], preferred_element_type=jnp.float32)
        ).astype(jnp.bfloat16)
        stores.append(copies.start(staged.at[:, span], out.at[:, span]))
    for copy in stores:
        copy.wait()


def output_send(table, at, left, near, pieces, chunks=6):
    (rows, width), columns = near.shape, left.shape[1]
    half, bf16 = (rows // 2, width), jnp.bfloat16
    return call(
        functools.partial(send_kernel, at, chunks),
        "output_send",
        8,
        [SMEM, HBM, VMEM] + [HBM] * len(pieces),
        [(half, bf16, HBM), ((columns, width), bf16, VMEM)],
        [
            pltpu.VMEM(left.shape, bf16),
            pltpu.VMEM(half, bf16),
            pltpu.SemaphoreType.DMA((1 + len(pieces) + chunks,)),
        ],
        table,
        left,
        near,
        *pieces,
    )


def keep_kernel(chunks, left_hbm, hidden, near, weights, out, held, left, semaphores):
    copies = Copies(semaphores)
    first, late = copies.start(left_hbm, left), copies.start(hidden, held)
    first.wait()
    half, step = left.shape[0] // 2, out.shape[1] // chunks
    for chunk in range(chunks):
        span = pl.ds(chunk * step, step)
        out[:, span] = near[:half, span] + jnp.dot(
            left[:half, :], weights[:, span], preferred_element_type=jnp.float32
        )
    late.wait()


def output_keep(left, hidden, near, weights, chunks=6):
    rows, width = near.shape
    return call(
        functools.partial(keep_kernel, chunks),
        "output_keep",
        4,
        [HBM, HBM, VMEM, VMEM],
        [((rows // 2, width), jnp.float32, VMEM), (hidden.shape, hidden.dtype, VMEM)],
        [pltpu.VMEM(left.shape, jnp.bfloat16), pltpu.SemaphoreType.DMA((2,))],
        left,
        hidden,
        near,
        weights,
    )


def final_kernel(chunks, received, hidden, kept, gain, out, other, staged, gains, semaphores):
    copies = Copies(semaphores)
    width = hidden.shape[1]
    step = width // chunks
    lanes = [pl.ds(chunk * step, step) for chunk in range(chunks)]
    waits = [copies.start(received.at[:, span], other.at[:, span]) for span in lanes]
    late = copies.start(gain, gains)
    square = jnp.zeros((hidden.shape[0], 128), jnp.float32)
    for span, copy in zip(lanes, waits):
        copy.wait()
        total = kept[:, span] + other[:, span].astype(jnp.float32)
        for lane in range(0, step, 128):
            part = total[:, lane : lane + 128]
            square = square + part * part
    mean = jnp.sum(square, axis=1, keepdims=True) / width
    scale = lax.rsqrt(mean + EPS)
    late.wait()
    row = gains[...].reshape(1, width)
    stores = []
    for chunk, span in enumerate(lanes):
        total = kept[:, span] + other[:, span].astype(jnp.float32)
        normed = total * scale * row[:, chunk * step : (chunk + 1) * step]
        staged[:, span] = (hidden[:, span].astype(jnp.float32) + normed).astype(jnp.bfloat16)
        stores.append(copies.start(staged.at[:, span], out.at[:, span]))
    for store in stores:
        store.wait()


def output(received, hidden, kept, gain, chunks=6):
    rows, width = hidden.shape
    bf16 = jnp.bfloat16
    return call(
        functools.partial(final_kernel, chunks),
        "output_norm",
        8,
        [HBM, VMEM, VMEM, HBM],
        [((rows, width), bf16, HBM)],
        [
            pltpu.VMEM((rows, width), bf16),
            pltpu.VMEM((rows, width), bf16),
            pltpu.VMEM((width,), jnp.float32),
            pltpu.SemaphoreType.DMA((1 + 2 * chunks,)),
        ],
        received,
        hidden,
        kept,
        gain,
    )[0]


def rotary_table(positions):
    half = HD // 2
    frequency = jnp.power(
        jnp.float32(10000.0), -jnp.arange(half, dtype=jnp.float32) * (2.0 / HD)
    )
    angles = positions.astype(jnp.float32)[:, None] * frequency[None, :]
    cos, sin = jnp.cos(angles), jnp.sin(angles)
    return jnp.concatenate([cos, cos, -sin, sin], axis=1)


def lookup(block_of, index):
    ids = jnp.arange(block_of.shape[0], dtype=jnp.int32)
    return jnp.sum(jnp.where(index[..., None] == ids, block_of, 0), axis=-1)


def flipped(array, axis, bit):
    size = lax.axis_size(axis)
    return lax.ppermute(array, axis, [(i, i ^ bit) for i in range(size)])


def along_line(array):
    size = lax.axis_size("seq")
    parts = [array[None]]
    for by in range(1, size):
        part = lax.ppermute(array, "seq", [(i, (i + by) % size) for i in range(size)])
        parts.append(Came(part[None]))
    return parts


def along_ring(array):
    size = lax.axis_size("seq")
    parts, part = [array[None]], array
    for _ in range(1, size):
        part = lax.ppermute(part, "seq", [(i, (i + 1) % size) for i in range(size)])
        parts.append(Came(part[None]))
    return parts


def came(parts):
    return [part.array for part in parts if isinstance(part, Came)]


def after(array, *others):
    return lax.optimization_barrier((array, *others))[0]


def two_chips(hidden, pre_gain, post_gain, wq, wk, wv, w_out, block_of):
    rows = hidden.shape[0]
    block_rows = 2 * rows
    lines, tp = lax.axis_size("seq"), lax.axis_index("tp")
    seq, group = lax.axis_index("seq"), lax.axis_index("groups")
    chip, core = tp // 2, tp % 2

    line = (seq - jnp.arange(lines, dtype=jnp.int32)) % lines
    near_starts = lookup(block_of, 2 * line + chip) * block_rows
    far_starts = lookup(block_of, 2 * line + 1 - chip) * block_rows
    table = jnp.concatenate([jnp.stack([core, group]).astype(jnp.int32), near_starts, far_starts])
    group_at, near_at, far_at = 1, 2, 2 + lines
    run = jnp.arange(rows, dtype=jnp.int32)
    place = jnp.concatenate([core * rows + run, (1 - core) * rows + run])
    trig = rotary_table(jnp.concatenate([near_starts[0] + place, far_starts[0] + place]))
    runs = [(0, 0, rows), (1, 0, rows)]
    near_chunk, far_chunk = Chunk(near_at, runs, rows), Chunk(far_at, runs, rows)
    others, everyone = list(range(1, lines)), list(range(lines))

    own = norm(hidden, pre_gain, [rows])[0]
    away = flipped(own, "tp", 2)
    partner = flipped(own, "tp", 1)

    weights = (wq, wk, wv)
    q_near, kv_near = qkv([own, Came(partner)], weights, "qkv", trig, 0)
    near = along_line(kv_near)
    half = w_out.shape[0] // 2
    w_cut = cut(table, group_at, after(w_out, kv_near), [half // 4, half // 4, half * 3 // 8, half // 8])
    q_near = after(q_near, *w_cut)
    (near_state,) = attention(
        [Step(0, 0, others, same=0)], table, [q_near], [near_chunk], [near], [near_chunk], [None]
    )

    away = after(away, *near_state)
    rows_far = [Came(away), Came(flipped(away, "tp", 1))]
    (kv_far,) = qkv(rows_far, weights, "kv", trig, block_rows)
    rows_far[1] = Came(after(rows_far[1].array, kv_far))
    (q_far,) = qkv(rows_far, weights, "q", trig, block_rows)
    far = along_ring(kv_far)

    fetched = lambda piece, *others: flipped(after(piece, *others), "tp", 2)
    swap = lambda array: flipped(array, "groups", 1)
    w_far = [fetched(piece, away) for piece in w_cut[:3]]
    w_other = [swap(after(w_far[0], q_far))]
    w_far[1] = after(w_far[1], w_other[0], came(far)[1])
    w_far.append(fetched(w_cut[3], w_far[1]))
    w_other.append(swap(w_far[1]))

    near_state, far_state = attention(
        [Step(1, 1, [], same=0), Step(1, 0, everyone), Step(0, 1, [0])],
        table,
        [q_near, q_far],
        [near_chunk, far_chunk],
        [near, far[:1]],
        [near_chunk, far_chunk],
        [near_state, None],
    )
    w_far[2] = after(w_far[2], w_other[1], *far_state, came(far)[-1])
    w_other.append(swap(w_far[2]))
    attended, gone = attention(
        [Step(1, 0, others), Step(0, 0, others)],
        table,
        [q_near, q_far],
        [near_chunk, far_chunk],
        [far],
        [far_chunk],
        [near_state, far_state],
        final=[[0], [1]],
    )
    gone = flipped(gone, "tp", 2)
    near_sum = output_near(attended, w_out)
    w_other.append(swap(after(w_far[3], attended)))
    pieces = [Came(piece) for piece in w_far + w_other]
    sent, w_laid = output_send(table, group_at, Came(gone), near_sum, pieces)
    received = flipped(sent, "tp", 1)
    kept, held = output_keep(Came(gone), hidden, near_sum, w_laid)
    return output(Came(received), held, kept, post_gain)


def any_count(hidden, pre_gain, post_gain, wq, wk, wv, w_out, block_of):
    rows = hidden.shape[0]
    lines = lax.axis_size("seq")
    line = (lax.axis_index("seq") - jnp.arange(lines, dtype=jnp.int32)) % lines
    block = (2 * line[:, None] + jnp.arange(2, dtype=jnp.int32)).reshape(-1)
    block_rows = rows * lax.axis_size("tp") // 2
    starts = lookup(block_of, block) * block_rows
    table = jnp.concatenate([jnp.zeros(2, jnp.int32), starts])
    normed = norm(hidden, pre_gain, [rows], 1)[0]
    normed = lax.all_gather(normed, "tp", axis=0, tiled=True)
    place = jnp.arange(block_rows, dtype=jnp.int32)
    trig = rotary_table((starts[:2, None] + place).reshape(-1))
    qs, keys_values, weights = [], [], (wq, wk, wv)
    for at in range(2):
        first = at * block_rows
        q, kv = qkv([normed[first : first + block_rows]], weights, "qkv", trig, first)
        qs.append(q)
        keys_values.append(kv)
    kv = lax.all_gather(jnp.stack(keys_values), "seq")[line].reshape(-1, block_rows, 2 * HD)
    rest = list(range(2, 2 * lines))
    runs = [(0, 0, block_rows)]
    attended = attention(
        [Step(0, 0, [1], same=0), Step(1, 0, [0], same=1), Step(0, 0, rest), Step(1, 0, rest)],
        table,
        qs,
        [Chunk(2, runs, 0), Chunk(3, runs, 0)],
        [[kv]],
        [Chunk(2, runs, 0)],
        [None, None],
        final=[[0, 1]],
    )[0]
    partial = jnp.dot(attended, w_out, preferred_element_type=jnp.float32)
    summed = lax.psum_scatter(
        partial.astype(jnp.bfloat16), "tp", scatter_dimension=0, tiled=True
    ).astype(jnp.float32)
    mean = jnp.mean(summed * summed, axis=-1, keepdims=True)
    projected = summed * lax.rsqrt(mean + EPS) * post_gain
    return (hidden.astype(jnp.float32) + projected).astype(jnp.bfloat16)


def solution(mesh):
    return jax.shard_map(
        two_chips if mesh.shape["tp"] == 4 else any_count,
        mesh=mesh,
        in_specs=(
            P(("groups", "seq", "tp"), None),
            P(),
            P(),
            P(None, "tp"),
            P(None, "tp"),
            P(None, "tp"),
            P("tp", None),
            P(),
        ),
        out_specs=P(("groups", "seq", "tp"), None),
        check_vma=False,
    )
```

```python
import functools
import math

import jax
import jax.numpy as jnp
from jax import lax
from jax.experimental import pallas as pl
from jax.experimental.pallas import tpu as pltpu
from jax.sharding import PartitionSpec as P

HD = 128
ATT_SCALAR = 144
EPS = 1e-6
MIB = 1024 * 1024
HIDDEN = -1e30
ONES = 16
COST = pl.CostEstimate(flops=1, bytes_accessed=1, transcendentals=0)

ANY = pl.BlockSpec(memory_space=pl.ANY)
HBM = pl.BlockSpec(memory_space=pltpu.HBM)
VMEM = pl.BlockSpec(memory_space=pltpu.VMEM)
SMEM = pl.BlockSpec(memory_space=pltpu.SMEM)


class Came:
    def __init__(self, array):
        self.array, self.shape = array, array.shape


def call(kernel, name, mib, in_specs, outs, scratch, *args, aliases=None):
    in_specs, pinned = list(in_specs), []
    for at, arg in enumerate(args):
        if isinstance(arg, Came):
            arg, in_specs[at] = arg.array, ANY
        elif in_specs[at] is not SMEM:
            arg = pltpu.with_memory_space_constraint(arg, in_specs[at].memory_space)
        pinned.append(arg)
    return pl.pallas_call(
        kernel,
        in_specs=in_specs,
        out_specs=[spec for _, _, spec in outs],
        out_shape=[spec.memory_space(shape, dtype) for shape, dtype, spec in outs],
        scratch_shapes=scratch,
        input_output_aliases=aliases or {},
        compiler_params=pltpu.CompilerParams(vmem_limit_bytes=mib * MIB),
        cost_estimate=COST,
        name=name,
    )(*pinned)


class Copies:
    def __init__(self, semaphores):
        self.semaphores, self.used = semaphores, 0

    def start(self, source, target):
        copy = pltpu.make_async_copy(source, target, self.semaphores.at[self.used])
        self.used += 1
        copy.start()
        return copy


def norm_kernel(cuts, pieces, hidden, gain, *refs):
    parts, (gains, rows, staged, semaphores) = refs[: len(cuts)], refs[len(cuts) :]
    copies = Copies(semaphores)
    count, width = hidden.shape
    step = count // pieces
    spans = [pl.ds(at * step, step) for at in range(pieces)]
    ins = [copies.start(hidden.at[span], rows.at[span]) for span in spans]
    copies.start(gain, gains).wait()
    scale = gains[...].reshape(1, width)
    outs = []
    for at, span in enumerate(spans):
        ins[at].wait()
        x = rows[span, :].astype(jnp.float32)
        square = x * x
        folded = square[:, :128]
        for lane in range(128, width, 128):
            folded = folded + square[:, lane : lane + 128]
        mean = jnp.sum(folded, axis=1, keepdims=True) / width
        staged[span, :] = (x * lax.rsqrt(mean + EPS) * scale).astype(jnp.bfloat16)
        begin = 0
        for cut, part in zip(cuts, parts):
            if begin <= at * step < begin + cut:
                inside = pl.ds(at * step - begin, step)
                outs.append(copies.start(staged.at[span], part.at[inside]))
            begin += cut
    for copy in outs:
        copy.wait()


def norm(hidden, gain, cuts, pieces=3):
    rows, width = hidden.shape
    bf16 = jnp.bfloat16
    return call(
        functools.partial(norm_kernel, cuts, pieces),
        "norm_rows",
        8,
        [HBM, HBM],
        [((cut, width), bf16, HBM) for cut in cuts],
        [
            pltpu.VMEM((width,), jnp.float32),
            pltpu.VMEM((rows, width), bf16),
            pltpu.VMEM((rows, width), bf16),
            pltpu.SemaphoreType.DMA((1 + 2 * pieces,)),
        ],
        hidden,
        gain,
    )


def qkv_kernel(count, kinds, first, chunks, trig, *refs):
    refs = list(refs)
    take = lambda n: [refs.pop(0) for _ in range(n)]
    given, parts = take(len(kinds)), take(count)
    q, kv = take(1)[0] if "q" in kinds else None, take(1)[0] if "k" in kinds else None
    weights, rows, angles, semaphores = refs
    copies, waits = Copies(semaphores), []
    depth = weights.shape[0] // chunks
    for chunk in range(chunks):
        span, put, column, here = pl.ds(chunk * depth, depth), 0, 0, []
        for part in parts:
            target = rows.at[pl.ds(put, part.shape[0]), span]
            here.append(copies.start(part.at[:, span], target))
            put += part.shape[0]
        for weight in given:
            target = weights.at[span, pl.ds(column, weight.shape[1])]
            here.append(copies.start(weight.at[span], target))
            column += weight.shape[1]
        waits.append(here)
    late = copies.start(trig.at[pl.ds(first, put)], angles)
    product = None
    for chunk, here in enumerate(waits):
        for copy in here:
            copy.wait()
        span = pl.ds(chunk * depth, depth)
        term = jnp.dot(rows[:, span], weights[span, :], preferred_element_type=jnp.float32)
        product = term if product is None else product + term
    late.wait()
    cos, sin = angles[:, :HD], angles[:, HD:]

    def rotated(at):
        y = product[:, at : at + HD]
        return y * cos + pltpu.roll(y, HD // 2, 1) * sin

    factor = ATT_SCALAR ** (-0.5) * math.log2(math.e)
    if kv is not None:
        begin = product.shape[1] - 2 * HD
        kv[:, :HD] = rotated(begin).astype(jnp.bfloat16)
        kv[:, HD:] = product[:, begin + HD :].astype(jnp.bfloat16)
    if q is not None:
        for head in range(q.shape[0]):
            q[head] = (rotated(head * HD) * factor).astype(jnp.bfloat16)


def qkv(parts, weights, kinds, trig, first, chunks=3):
    given = [weights["qkv".index(kind)] for kind in kinds]
    total, width = sum(part.shape[0] for part in parts), parts[0].shape[1]
    columns = sum(weight.shape[1] for weight in given)
    heads, bf16 = weights[0].shape[1] // HD, jnp.bfloat16
    outs = [((heads, total, HD), bf16, VMEM)] * ("q" in kinds)
    outs += [((total, 2 * HD), bf16, VMEM)] * ("k" in kinds)
    return call(
        functools.partial(qkv_kernel, len(parts), kinds, first, chunks),
        "project_" + kinds,
        14,
        [HBM] * (1 + len(given) + len(parts)),
        outs,
        [
            pltpu.VMEM((width, columns), bf16),
            pltpu.VMEM((total, width), bf16),
            pltpu.VMEM((total, 2 * HD), jnp.float32),
            pltpu.SemaphoreType.DMA((1 + (len(parts) + len(given)) * chunks,)),
        ],
        trig,
        *given,
        *parts,
    )


class Step:
    def __init__(self, q, group, slots, same=None, merged=False):
        self.q, self.group, self.slots = q, group, slots
        self.same, self.merged = same, merged


class Chunk:
    def __init__(self, at, runs, share):
        self.at, self.runs, self.share = at, runs, share

    def places(self, core, axis, first, size):
        shape = (size, 1) if axis == 0 else (1, size)
        index = first + lax.broadcasted_iota(jnp.int32, shape, axis)
        result, begin = index, 0
        for which, offset, rows in self.runs:
            base = (core if which == 0 else 1 - core) * self.share + offset - begin
            inside = (index >= begin) & (index < begin + rows)
            result = jnp.where(inside, index + base, result)
            begin += rows
        return result


def attention_kernel(plan, q_chunks, k_chunks, group_parts, fresh, final, table, *refs):
    refs = list(refs)
    take = lambda n: [refs.pop(0) for _ in range(n)]
    count = len(q_chunks)
    qs = take(count)
    kv_parts = [take(n) for n in group_parts]
    take(2 * (count - len(fresh)))
    outs = take(len(final))
    states = [take(2) for _ in range(count)]
    kvs, staged = take(len(group_parts)), take(len(final))
    (semaphores,) = refs
    copies = Copies(semaphores)
    core = table[0]
    waits = {}
    for group, (parts, kv) in enumerate(zip(kv_parts, kvs)):
        each = kv.shape[0] // len(parts)
        waits[group] = [
            copies.start(part, kv.at[pl.ds(slot * each, each)])
            for slot, part in enumerate(parts)
        ]

    def ready(group):
        for copy in waits.pop(group, []):
            copy.wait()

    def attend(q, keys_values, begin, visible=None, bias=None):
        q_ref, (peak, acc) = qs[q], states[q]
        heads = q_ref.shape[0]
        keys = keys_values[:, :HD]
        values = keys_values[:, HD:].T
        values = jnp.concatenate([values, jnp.ones((ONES, keys.shape[0]), values.dtype)], axis=0)
        tiles, tile = acc.shape[0], acc.shape[2] // heads
        scores, tops, weights = [], [], []
        for at in range(tiles):
            q_tile = q_ref[:, at * tile : (at + 1) * tile, :].reshape(heads * tile, HD)
            score = lax.dot_general(
                keys, q_tile, (((1,), (1,)), ((), ())), preferred_element_type=jnp.float32
            )
            if visible is not None:
                seen = jnp.concatenate([visible(at * tile, tile)] * heads, axis=1)
                score = jnp.where(seen, score, HIDDEN)
            if bias is not None:
                score = score + bias
            scores.append(score)
        for at in range(tiles):
            top = jnp.max(scores[at], axis=0, keepdims=True)
            if not begin:
                top = jnp.maximum(peak[at, 0:1, :], top)
            tops.append(top)
            weights.append(jnp.exp2((scores[at] - top).astype(jnp.bfloat16)))
        for at in range(tiles):
            summed = jnp.dot(values, weights[at], preferred_element_type=jnp.float32)
            if not begin:
                summed = summed + acc[at] * jnp.exp2(peak[at, 0:1, :] - tops[at])
            acc[at] = summed
            peak[at] = jnp.broadcast_to(tops[at], peak.shape[1:])

    begun = set(range(count)) - set(fresh)
    for step in plan:
        q, group, kv = step.q, step.group, kvs[step.group]
        q_chunk, k_chunk = q_chunks[q], k_chunks[group]
        if step.same is not None:
            keys_at = k_chunk.places(core, 0, 0, kv.shape[1])
            visible = lambda first, tile: keys_at <= q_chunk.places(core, 1, first, tile)
            own = kv_parts[group][0]
            attend(q, own[step.same], q not in begun, visible=visible)
            begun.add(q)
        start = table[q_chunk.at]
        slots = step.slots
        if not slots:
            continue
        ready(group)
        if step.merged:
            shown = [table[k_chunk.at + slot] < start for slot in slots]

            @pl.when(functools.reduce(jnp.logical_or, shown))
            def _():
                rows = kv.shape[1]
                bias = [
                    jnp.where(see, 0.0, HIDDEN) * jnp.ones((rows, 1), jnp.float32)
                    for see in shown
                ]
                keys_values = kv[slots[0] : slots[-1] + 1].reshape(len(slots) * rows, 2 * HD)
                attend(q, keys_values, False, bias=jnp.concatenate(bias, axis=0))

        else:

            def one(slot, carry):
                @pl.when(table[k_chunk.at + slot] < start)
                def _():
                    attend(q, kv[slot], False)

                return carry

            lax.fori_loop(slots[0], slots[-1] + 1, one, 0)

    for group in list(waits):
        ready(group)
    stores = []
    for out, stage, order in zip(outs, staged, final):
        put = 0
        for q in order:
            acc, heads = states[q][1], qs[q].shape[0]
            tile = acc.shape[2] // heads
            for at in range(acc.shape[0]):
                rows = acc[at, :HD, :] / acc[at, HD : HD + 1, :]
                rows = rows.T.astype(jnp.bfloat16)
                for head in range(heads):
                    stage[put : put + tile, head * HD : (head + 1) * HD] = rows[
                        head * tile : (head + 1) * tile
                    ]
                put += tile
        stores.append(copies.start(stage, out))
    for copy in stores:
        copy.wait()


def attention(plan, table, qs, q_chunks, groups, k_chunks, state, final=()):
    fresh = [at for at, held in enumerate(state) if held is None]
    shapes = []
    for q in qs:
        heads, rows, _ = q.shape
        tile = min(rows, 128)
        shapes += [(rows // tile, deep, heads * tile) for deep in (8, HD + ONES)]
    width = qs[0].shape[0] * HD
    sums = [sum(qs[q].shape[1] for q in order) for order in final]
    outs = [((rows, width), jnp.bfloat16, HBM) for rows in sums]
    scratch = []
    for parts in groups:
        slots = sum(part.shape[0] for part in parts)
        scratch.append(pltpu.VMEM((slots,) + parts[0].shape[1:], jnp.bfloat16))
    scratch += [pltpu.VMEM((rows, width), jnp.bfloat16) for rows in sums]
    parts = [part for parts in groups for part in parts]
    sizes = [len(parts) for parts in groups]
    inputs, aliases = [table, *qs, *parts], {}
    for at, pair in enumerate(state):
        for half, array in enumerate(pair or ()):
            aliases[len(inputs)] = len(outs) + 2 * at + half
            inputs.append(array)
    results = call(
        functools.partial(attention_kernel, plan, q_chunks, k_chunks, sizes, fresh, final),
        "attention",
        10,
        [SMEM] + [VMEM] * (len(inputs) - 1),
        outs + [(shape, jnp.float32, VMEM) for shape in shapes],
        scratch + [pltpu.SemaphoreType.DMA((len(parts) + len(outs),))],
        *inputs,
        aliases=aliases,
    )
    if final:
        return results[: len(final)]
    return [tuple(results[2 * at : 2 * at + 2]) for at in range(len(qs))]


def cut_kernel(sizes, at, table, weights, *refs):
    outs, (held, semaphores) = refs[: len(sizes)], refs[len(sizes) :]
    copies = Copies(semaphores)
    half = sum(sizes)
    first = pl.multiple_of(table[at] * half, half)
    ins, put = [], 0
    for size in sizes:
        target = held.at[pl.ds(put, size)]
        ins.append((copies.start(weights.at[pl.ds(first + put, size)], target), target))
        put += size
    stores = []
    for (copy, piece), out in zip(ins, outs):
        copy.wait()
        stores.append(copies.start(piece, out))
    for copy in stores:
        copy.wait()


def cut(table, at, weights, sizes):
    depth, width = weights.shape
    return call(
        functools.partial(cut_kernel, sizes, at),
        "cut_weights",
        4,
        [SMEM, HBM],
        [((size, width), weights.dtype, HBM) for size in sizes],
        [
            pltpu.VMEM((depth // 2, width), weights.dtype),
            pltpu.SemaphoreType.DMA((2 * len(sizes),)),
        ],
        table,
        weights,
    )


def near_kernel(chunks, left_hbm, weights_hbm, out, left, weights, semaphores):
    copies = Copies(semaphores)
    step = out.shape[1] // chunks
    first = copies.start(left_hbm, left)
    lanes = [pl.ds(chunk * step, step) for chunk in range(chunks)]
    waits = [copies.start(weights_hbm.at[:, at], weights.at[:, at]) for at in lanes]
    first.wait()
    for at, copy in zip(lanes, waits):
        copy.wait()
        out[:, at] = jnp.dot(left[...], weights[:, at], preferred_element_type=jnp.float32)


def output_near(left, weights, chunks=6):
    (rows, columns), width = left.shape, weights.shape[1]
    return call(
        functools.partial(near_kernel, chunks),
        "output_near",
        8,
        [HBM] * 2,
        [((rows, width), jnp.float32, VMEM)],
        [
            pltpu.VMEM(left.shape, left.dtype),
            pltpu.VMEM(weights.shape, weights.dtype),
            pltpu.SemaphoreType.DMA((1 + chunks,)),
        ],
        left,
        weights,
    )[0]


def send_kernel(at, chunks, table, left_hbm, near, *refs):
    count = len(refs) - 5
    pieces, (out, weights, left, staged, semaphores) = refs[:count], refs[count:]
    copies = Copies(semaphores)
    depth, width = weights.shape
    step = width // chunks
    first = copies.start(left_hbm, left)
    waits, put = [], 0
    for index, piece in enumerate(pieces):
        half = table[at] if index < count // 2 else 1 - table[at]
        row = pl.multiple_of(half * (depth // 2) + put % (depth // 2), 16)
        waits.append(copies.start(piece, weights.at[pl.ds(row, piece.shape[0])]))
        put += piece.shape[0]
    for copy in waits:
        copy.wait()
    first.wait()
    half = left.shape[0] // 2
    stores = []
    for chunk in range(chunks):
        span = pl.ds(chunk * step, step)
        staged[:, span] = (
            near[half:, span]
            + jnp.dot(left[half:, :], weights[:, span], preferred_element_type=jnp.float32)
        ).astype(jnp.bfloat16)
        stores.append(copies.start(staged.at[:, span], out.at[:, span]))
    for copy in stores:
        copy.wait()


def output_send(table, at, left, near, pieces, chunks=6):
    (rows, width), columns = near.shape, left.shape[1]
    half, bf16 = (rows // 2, width), jnp.bfloat16
    return call(
        functools.partial(send_kernel, at, chunks),
        "output_send",
        8,
        [SMEM, HBM, VMEM] + [HBM] * len(pieces),
        [(half, bf16, HBM), ((columns, width), bf16, VMEM)],
        [
            pltpu.VMEM(left.shape, bf16),
            pltpu.VMEM(half, bf16),
            pltpu.SemaphoreType.DMA((1 + len(pieces) + chunks,)),
        ],
        table,
        left,
        near,
        *pieces,
    )


def keep_kernel(chunks, left_hbm, hidden, near, weights, out, held, left, semaphores):
    copies = Copies(semaphores)
    first, late = copies.start(left_hbm, left), copies.start(hidden, held)
    first.wait()
    half, step = left.shape[0] // 2, out.shape[1] // chunks
    for chunk in range(chunks):
        span = pl.ds(chunk * step, step)
        out[:, span] = near[:half, span] + jnp.dot(
            left[:half, :], weights[:, span], preferred_element_type=jnp.float32
        )
    late.wait()


def output_keep(left, hidden, near, weights, chunks=6):
    rows, width = near.shape
    return call(
        functools.partial(keep_kernel, chunks),
        "output_keep",
        4,
        [HBM, HBM, VMEM, VMEM],
        [((rows // 2, width), jnp.float32, VMEM), (hidden.shape, hidden.dtype, VMEM)],
        [pltpu.VMEM(left.shape, jnp.bfloat16), pltpu.SemaphoreType.DMA((2,))],
        left,
        hidden,
        near,
        weights,
    )


def final_kernel(chunks, received, hidden, kept, gain, out, other, staged, gains, semaphores):
    copies = Copies(semaphores)
    width = hidden.shape[1]
    step = width // chunks
    lanes = [pl.ds(chunk * step, step) for chunk in range(chunks)]
    waits = [copies.start(received.at[:, span], other.at[:, span]) for span in lanes]
    late = copies.start(gain, gains)
    square = jnp.zeros((hidden.shape[0], 128), jnp.float32)
    for span, copy in zip(lanes, waits):
        copy.wait()
        total = kept[:, span] + other[:, span].astype(jnp.float32)
        for lane in range(0, step, 128):
            part = total[:, lane : lane + 128]
            square = square + part * part
    mean = jnp.sum(square, axis=1, keepdims=True) / width
    scale = lax.rsqrt(mean + EPS)
    late.wait()
    row = gains[...].reshape(1, width)
    stores = []
    for chunk, span in enumerate(lanes):
        total = kept[:, span] + other[:, span].astype(jnp.float32)
        normed = total * scale * row[:, chunk * step : (chunk + 1) * step]
        staged[:, span] = (hidden[:, span].astype(jnp.float32) + normed).astype(jnp.bfloat16)
        stores.append(copies.start(staged.at[:, span], out.at[:, span]))
    for store in stores:
        store.wait()


def output(received, hidden, kept, gain, chunks=6):
    rows, width = hidden.shape
    bf16 = jnp.bfloat16
    return call(
        functools.partial(final_kernel, chunks),
        "output_norm",
        8,
        [HBM, VMEM, VMEM, HBM],
        [((rows, width), bf16, HBM)],
        [
            pltpu.VMEM((rows, width), bf16),
            pltpu.VMEM((rows, width), bf16),
            pltpu.VMEM((width,), jnp.float32),
            pltpu.SemaphoreType.DMA((1 + 2 * chunks,)),
        ],
        received,
        hidden,
        kept,
        gain,
    )[0]


def rotary_table(positions):
    half = HD // 2
    frequency = jnp.power(
        jnp.float32(10000.0), -jnp.arange(half, dtype=jnp.float32) * (2.0 / HD)
    )
    angles = positions.astype(jnp.float32)[:, None] * frequency[None, :]
    cos, sin = jnp.cos(angles), jnp.sin(angles)
    return jnp.concatenate([cos, cos, -sin, sin], axis=1)


def lookup(block_of, index):
    ids = jnp.arange(block_of.shape[0], dtype=jnp.int32)
    return jnp.sum(jnp.where(index[..., None] == ids, block_of, 0), axis=-1)


def flipped(array, axis, bit):
    size = lax.axis_size(axis)
    return lax.ppermute(array, axis, [(i, i ^ bit) for i in range(size)])


def along_line(array):
    size = lax.axis_size("seq")
    parts = [array[None]]
    for by in range(1, size):
        part = lax.ppermute(array, "seq", [(i, (i + by) % size) for i in range(size)])
        parts.append(Came(part[None]))
    return parts


def along_ring(array):
    size = lax.axis_size("seq")
    parts, part = [array[None]], array
    for _ in range(1, size):
        part = lax.ppermute(part, "seq", [(i, (i + 1) % size) for i in range(size)])
        parts.append(Came(part[None]))
    return parts


def came(parts):
    return [part.array for part in parts if isinstance(part, Came)]


def after(array, *others):
    return lax.optimization_barrier((array, *others))[0]


def two_chips(hidden, pre_gain, post_gain, wq, wk, wv, w_out, block_of):
    rows = hidden.shape[0]
    block_rows = 2 * rows
    lines, tp = lax.axis_size("seq"), lax.axis_index("tp")
    seq, group = lax.axis_index("seq"), lax.axis_index("groups")
    chip, core = tp // 2, tp % 2

    line = (seq - jnp.arange(lines, dtype=jnp.int32)) % lines
    near_starts = lookup(block_of, 2 * line + chip) * block_rows
    far_starts = lookup(block_of, 2 * line + 1 - chip) * block_rows
    table = jnp.concatenate([jnp.stack([core, group]).astype(jnp.int32), near_starts, far_starts])
    group_at, near_at, far_at = 1, 2, 2 + lines
    run = jnp.arange(rows, dtype=jnp.int32)
    place = jnp.concatenate([core * rows + run, (1 - core) * rows + run])
    trig = rotary_table(jnp.concatenate([near_starts[0] + place, far_starts[0] + place]))
    runs = [(0, 0, rows), (1, 0, rows)]
    near_chunk, far_chunk = Chunk(near_at, runs, rows), Chunk(far_at, runs, rows)
    others, everyone = list(range(1, lines)), list(range(lines))

    own = norm(hidden, pre_gain, [rows])[0]
    away = flipped(own, "tp", 2)
    partner = flipped(own, "tp", 1)

    weights = (wq, wk, wv)
    q_near, kv_near = qkv([own, Came(partner)], weights, "qkv", trig, 0)
    near = along_line(kv_near)
    half = w_out.shape[0] // 2
    w_cut = cut(table, group_at, after(w_out, kv_near), [half // 4, half * 3 // 8, half // 4, half // 8])
    q_near = after(q_near, *w_cut)
    (near_state,) = attention(
        [Step(0, 0, others, same=0)], table, [q_near], [near_chunk], [near], [near_chunk], [None]
    )

    away = after(away, *near_state)
    q_far, kv_far = qkv(
        [Came(away), Came(flipped(away, "tp", 1))], weights, "qkv", trig, block_rows
    )
    far = along_ring(kv_far)

    fetched = lambda piece, *others: flipped(after(piece, *others), "tp", 2)
    swap = lambda array: flipped(array, "groups", 1)
    w_far = [fetched(piece, away) for piece in w_cut[:3]]
    w_other = [swap(after(w_far[0], q_far))]
    w_far[1] = after(w_far[1], w_other[0], came(far)[1])
    w_far.append(fetched(w_cut[3], w_far[1]))
    w_other.append(swap(w_far[1]))

    near_state, far_state = attention(
        [Step(1, 1, [], same=0), Step(1, 0, everyone), Step(0, 1, [0])],
        table,
        [q_near, q_far],
        [near_chunk, far_chunk],
        [near, far[:1]],
        [near_chunk, far_chunk],
        [near_state, None],
    )
    w_far[2] = after(w_far[2], w_other[1], *far_state, came(far)[-1])
    w_other.append(swap(w_far[2]))
    attended, gone = attention(
        [Step(1, 0, others), Step(0, 0, others)],
        table,
        [q_near, q_far],
        [near_chunk, far_chunk],
        [far],
        [far_chunk],
        [near_state, far_state],
        final=[[0], [1]],
    )
    gone = flipped(gone, "tp", 2)
    near_sum = output_near(attended, w_out)
    w_other.append(swap(after(w_far[3], attended)))
    pieces = [Came(piece) for piece in w_far + w_other]
    sent, w_laid = output_send(table, group_at, Came(gone), near_sum, pieces)
    received = flipped(sent, "tp", 1)
    kept, held = output_keep(Came(gone), hidden, near_sum, w_laid)
    return output(Came(received), held, kept, post_gain)


def any_count(hidden, pre_gain, post_gain, wq, wk, wv, w_out, block_of):
    rows = hidden.shape[0]
    lines = lax.axis_size("seq")
    line = (lax.axis_index("seq") - jnp.arange(lines, dtype=jnp.int32)) % lines
    block = (2 * line[:, None] + jnp.arange(2, dtype=jnp.int32)).reshape(-1)
    block_rows = rows * lax.axis_size("tp") // 2
    starts = lookup(block_of, block) * block_rows
    table = jnp.concatenate([jnp.zeros(2, jnp.int32), starts])
    normed = norm(hidden, pre_gain, [rows], 1)[0]
    normed = lax.all_gather(normed, "tp", axis=0, tiled=True)
    place = jnp.arange(block_rows, dtype=jnp.int32)
    trig = rotary_table((starts[:2, None] + place).reshape(-1))
    qs, keys_values, weights = [], [], (wq, wk, wv)
    for at in range(2):
        first = at * block_rows
        q, kv = qkv([normed[first : first + block_rows]], weights, "qkv", trig, first)
        qs.append(q)
        keys_values.append(kv)
    kv = lax.all_gather(jnp.stack(keys_values), "seq")[line].reshape(-1, block_rows, 2 * HD)
    rest = list(range(2, 2 * lines))
    runs = [(0, 0, block_rows)]
    attended = attention(
        [Step(0, 0, [1], same=0), Step(1, 0, [0], same=1), Step(0, 0, rest), Step(1, 0, rest)],
        table,
        qs,
        [Chunk(2, runs, 0), Chunk(3, runs, 0)],
        [[kv]],
        [Chunk(2, runs, 0)],
        [None, None],
        final=[[0, 1]],
    )[0]
    partial = jnp.dot(attended, w_out, preferred_element_type=jnp.float32)
    summed = lax.psum_scatter(
        partial.astype(jnp.bfloat16), "tp", scatter_dimension=0, tiled=True
    ).astype(jnp.float32)
    mean = jnp.mean(summed * summed, axis=-1, keepdims=True)
    projected = summed * lax.rsqrt(mean + EPS) * post_gain
    return (hidden.astype(jnp.float32) + projected).astype(jnp.bfloat16)


def solution(mesh):
    return jax.shard_map(
        two_chips if mesh.shape["tp"] == 4 else any_count,
        mesh=mesh,
        in_specs=(
            P(("groups", "seq", "tp"), None),
            P(),
            P(),
            P(None, "tp"),
            P(None, "tp"),
            P(None, "tp"),
            P("tp", None),
            P(),
        ),
        out_specs=P(("groups", "seq", "tp"), None),
        check_vma=False,
    )
```

```python
import functools
import math

import jax
import jax.numpy as jnp
from jax import lax
from jax.experimental import pallas as pl
from jax.experimental.pallas import tpu as pltpu
from jax.sharding import PartitionSpec as P

HD = 128
ATT_SCALAR = 144
EPS = 1e-6
MIB = 1024 * 1024
HIDDEN = -1e30
ONES = 16
COST = pl.CostEstimate(flops=1, bytes_accessed=1, transcendentals=0)

ANY = pl.BlockSpec(memory_space=pl.ANY)
HBM = pl.BlockSpec(memory_space=pltpu.HBM)
VMEM = pl.BlockSpec(memory_space=pltpu.VMEM)
SMEM = pl.BlockSpec(memory_space=pltpu.SMEM)


class Came:
    def __init__(self, array):
        self.array, self.shape = array, array.shape


def call(kernel, name, mib, in_specs, outs, scratch, *args, aliases=None):
    in_specs, pinned = list(in_specs), []
    for at, arg in enumerate(args):
        if isinstance(arg, Came):
            arg, in_specs[at] = arg.array, ANY
        elif in_specs[at] is not SMEM:
            arg = pltpu.with_memory_space_constraint(arg, in_specs[at].memory_space)
        pinned.append(arg)
    return pl.pallas_call(
        kernel,
        in_specs=in_specs,
        out_specs=[spec for _, _, spec in outs],
        out_shape=[spec.memory_space(shape, dtype) for shape, dtype, spec in outs],
        scratch_shapes=scratch,
        input_output_aliases=aliases or {},
        compiler_params=pltpu.CompilerParams(vmem_limit_bytes=mib * MIB),
        cost_estimate=COST,
        name=name,
    )(*pinned)


class Copies:
    def __init__(self, semaphores):
        self.semaphores, self.used = semaphores, 0

    def start(self, source, target):
        copy = pltpu.make_async_copy(source, target, self.semaphores.at[self.used])
        self.used += 1
        copy.start()
        return copy


def norm_kernel(cuts, pieces, first, hidden, gain, *refs):
    parts, (gains, rows, staged, semaphores) = refs[: len(cuts)], refs[len(cuts) :]
    copies = Copies(semaphores)
    count, width = rows.shape
    step = count // pieces
    spans = [pl.ds(at * step, step) for at in range(pieces)]
    ins = [
        copies.start(hidden.at[pl.ds(first + at * step, step)], rows.at[span])
        for at, span in enumerate(spans)
    ]
    copies.start(gain, gains).wait()
    scale = gains[...].reshape(1, width)
    outs = []
    for at, span in enumerate(spans):
        ins[at].wait()
        x = rows[span, :].astype(jnp.float32)
        square = x * x
        folded = square[:, :128]
        for lane in range(128, width, 128):
            folded = folded + square[:, lane : lane + 128]
        mean = jnp.sum(folded, axis=1, keepdims=True) / width
        staged[span, :] = (x * lax.rsqrt(mean + EPS) * scale).astype(jnp.bfloat16)
        begin = 0
        for cut, part in zip(cuts, parts):
            if begin <= at * step < begin + cut:
                inside = pl.ds(at * step - begin, step)
                outs.append(copies.start(staged.at[span], part.at[inside]))
            begin += cut
    for copy in outs:
        copy.wait()


def norm(hidden, gain, first, cuts, pieces=3):
    rows, width = sum(cuts), hidden.shape[1]
    bf16 = jnp.bfloat16
    return call(
        functools.partial(norm_kernel, cuts, pieces, first),
        "norm_rows",
        8,
        [HBM, HBM],
        [((cut, width), bf16, HBM) for cut in cuts],
        [
            pltpu.VMEM((width,), jnp.float32),
            pltpu.VMEM((rows, width), bf16),
            pltpu.VMEM((rows, width), bf16),
            pltpu.SemaphoreType.DMA((1 + 2 * pieces,)),
        ],
        hidden,
        gain,
    )


def qkv_kernel(places, first, chunks, held, trig, wq, wk, wv, *refs):
    parts, refs = refs[: len(places)], refs[len(places) + 2 * held :]
    q, kv, weights, rows, angles, semaphores = refs
    copies, waits = Copies(semaphores), []
    depth = weights.shape[0] // chunks
    for chunk in range(chunks):
        span, put, column, here = pl.ds(chunk * depth, depth), 0, 0, []
        for part in parts:
            target = rows.at[pl.ds(put, part.shape[0]), span]
            here.append(copies.start(part.at[:, span], target))
            put += part.shape[0]
        for weight in (wq, wk, wv):
            target = weights.at[span, pl.ds(column, weight.shape[1])]
            here.append(copies.start(weight.at[span], target))
            column += weight.shape[1]
        waits.append(here)
    late, put = [], 0
    for part, place in zip(parts, places):
        count = part.shape[0]
        source = trig.at[pl.ds(first + place, count)]
        late.append(copies.start(source, angles.at[pl.ds(put, count)]))
        put += count
    product = None
    for chunk, here in enumerate(waits):
        for copy in here:
            copy.wait()
        span = pl.ds(chunk * depth, depth)
        term = jnp.dot(rows[:, span], weights[span, :], preferred_element_type=jnp.float32)
        product = term if product is None else product + term
    for copy in late:
        copy.wait()
    cos, sin = angles[:, :HD], angles[:, HD:]
    queries = product.shape[1] - 2 * HD

    def rotated(at):
        y = product[:, at : at + HD]
        return y * cos + pltpu.roll(y, HD // 2, 1) * sin

    factor = ATT_SCALAR ** (-0.5) * math.log2(math.e)
    keys = rotated(queries).astype(jnp.bfloat16)
    values = product[:, queries + HD :].astype(jnp.bfloat16)
    heads = [(rotated(at) * factor).astype(jnp.bfloat16) for at in range(0, queries, HD)]
    put = 0
    for part, place in zip(parts, places):
        count = part.shape[0]
        kv[place : place + count, :HD] = keys[put : put + count]
        kv[place : place + count, HD:] = values[put : put + count]
        for head, rotated_head in enumerate(heads):
            q[head, place : place + count, :] = rotated_head[put : put + count]
        put += count


def qkv(parts, places, total, weights, trig, first, held=(), chunks=4):
    rows, width = sum(part.shape[0] for part in parts), parts[0].shape[1]
    columns = sum(weight.shape[1] for weight in weights)
    heads, bf16 = weights[0].shape[1] // HD, jnp.bfloat16
    given = 4 + len(parts)
    return call(
        functools.partial(qkv_kernel, places, first, chunks, bool(held)),
        "qkv",
        14,
        [HBM] * given + [VMEM] * len(held),
        [((heads, total, HD), bf16, VMEM), ((total, 2 * HD), bf16, VMEM)],
        [
            pltpu.VMEM((width, columns), bf16),
            pltpu.VMEM((rows, width), bf16),
            pltpu.VMEM((rows, 2 * HD), jnp.float32),
            pltpu.SemaphoreType.DMA((len(parts) + (len(parts) + 3) * chunks,)),
        ],
        trig,
        *weights,
        *parts,
        *held,
        aliases={given + at: at for at in range(len(held))},
    )


class Step:
    def __init__(self, q, group, slots, same=None, merged=False):
        self.q, self.group, self.slots = q, group, slots
        self.same, self.merged = same, merged


class Chunk:
    def __init__(self, at, runs, share):
        self.at, self.runs, self.share = at, runs, share

    def places(self, core, axis, first, size):
        shape = (size, 1) if axis == 0 else (1, size)
        index = first + lax.broadcasted_iota(jnp.int32, shape, axis)
        result, begin = index, 0
        for which, offset, rows in self.runs:
            base = (core if which == 0 else 1 - core) * self.share + offset - begin
            inside = (index >= begin) & (index < begin + rows)
            result = jnp.where(inside, index + base, result)
            begin += rows
        return result


def attention_kernel(plan, q_chunks, k_chunks, group_parts, fresh, final, table, *refs):
    refs = list(refs)
    take = lambda n: [refs.pop(0) for _ in range(n)]
    count = len(q_chunks)
    qs = take(count)
    kv_parts = [take(n) for n in group_parts]
    take(2 * (count - len(fresh)))
    outs = take(len(final))
    states = [take(2) for _ in range(count)]
    kvs, staged = take(len(group_parts)), take(len(final))
    (semaphores,) = refs
    copies = Copies(semaphores)
    core = table[0]
    waits = {}
    for group, (parts, kv) in enumerate(zip(kv_parts, kvs)):
        each = kv.shape[0] // len(parts)
        waits[group] = [
            copies.start(part, kv.at[pl.ds(slot * each, each)])
            for slot, part in enumerate(parts)
        ]

    def ready(group):
        for copy in waits.pop(group, []):
            copy.wait()

    def attend(q, keys_values, begin, visible=None, bias=None):
        q_ref, (peak, acc) = qs[q], states[q]
        heads = q_ref.shape[0]
        keys = keys_values[:, :HD]
        values = keys_values[:, HD:].T
        values = jnp.concatenate([values, jnp.ones((ONES, keys.shape[0]), values.dtype)], axis=0)
        tiles, tile = acc.shape[0], acc.shape[2] // heads
        scores, tops, weights = [], [], []
        for at in range(tiles):
            q_tile = q_ref[:, at * tile : (at + 1) * tile, :].reshape(heads * tile, HD)
            score = lax.dot_general(
                keys, q_tile, (((1,), (1,)), ((), ())), preferred_element_type=jnp.float32
            )
            if visible is not None:
                seen = jnp.concatenate([visible(at * tile, tile)] * heads, axis=1)
                score = jnp.where(seen, score, HIDDEN)
            if bias is not None:
                score = score + bias
            scores.append(score)
        for at in range(tiles):
            top = jnp.max(scores[at], axis=0, keepdims=True)
            if not begin:
                top = jnp.maximum(peak[at, 0:1, :], top)
            tops.append(top)
            weights.append(jnp.exp2((scores[at] - top).astype(jnp.bfloat16)))
        for at in range(tiles):
            summed = jnp.dot(values, weights[at], preferred_element_type=jnp.float32)
            if not begin:
                summed = summed + acc[at] * jnp.exp2(peak[at, 0:1, :] - tops[at])
            acc[at] = summed
            peak[at] = jnp.broadcast_to(tops[at], peak.shape[1:])

    begun = set(range(count)) - set(fresh)
    for step in plan:
        q, group, kv = step.q, step.group, kvs[step.group]
        q_chunk, k_chunk = q_chunks[q], k_chunks[group]
        if step.same is not None:
            keys_at = k_chunk.places(core, 0, 0, kv.shape[1])
            visible = lambda first, tile: keys_at <= q_chunk.places(core, 1, first, tile)
            own = kv_parts[group][0]
            attend(q, own[step.same], q not in begun, visible=visible)
            begun.add(q)
        start = table[q_chunk.at]
        slots = step.slots
        if not slots:
            continue
        ready(group)
        if step.merged:
            shown = [table[k_chunk.at + slot] < start for slot in slots]

            @pl.when(functools.reduce(jnp.logical_or, shown))
            def _():
                rows = kv.shape[1]
                bias = [
                    jnp.where(see, 0.0, HIDDEN) * jnp.ones((rows, 1), jnp.float32)
                    for see in shown
                ]
                keys_values = kv[slots[0] : slots[-1] + 1].reshape(len(slots) * rows, 2 * HD)
                attend(q, keys_values, False, bias=jnp.concatenate(bias, axis=0))

        else:

            def one(slot, carry):
                @pl.when(table[k_chunk.at + slot] < start)
                def _():
                    attend(q, kv[slot], False)

                return carry

            lax.fori_loop(slots[0], slots[-1] + 1, one, 0)

    for group in list(waits):
        ready(group)
    stores = []
    for out, stage, order in zip(outs, staged, final):
        put = 0
        for q in order:
            acc, heads = states[q][1], qs[q].shape[0]
            tile = acc.shape[2] // heads
            for at in range(acc.shape[0]):
                rows = acc[at, :HD, :] / acc[at, HD : HD + 1, :]
                rows = rows.T.astype(jnp.bfloat16)
                for head in range(heads):
                    stage[put : put + tile, head * HD : (head + 1) * HD] = rows[
                        head * tile : (head + 1) * tile
                    ]
                put += tile
        stores.append(copies.start(stage, out))
    for copy in stores:
        copy.wait()


def attention(plan, table, qs, q_chunks, groups, k_chunks, state, final=()):
    fresh = [at for at, held in enumerate(state) if held is None]
    shapes = []
    for q in qs:
        heads, rows, _ = q.shape
        tile = min(rows, 128)
        shapes += [(rows // tile, deep, heads * tile) for deep in (8, HD + ONES)]
    width = qs[0].shape[0] * HD
    sums = [sum(qs[q].shape[1] for q in order) for order in final]
    outs = [((rows, width), jnp.bfloat16, HBM) for rows in sums]
    scratch = []
    for parts in groups:
        slots = sum(part.shape[0] for part in parts)
        scratch.append(pltpu.VMEM((slots,) + parts[0].shape[1:], jnp.bfloat16))
    scratch += [pltpu.VMEM((rows, width), jnp.bfloat16) for rows in sums]
    parts = [part for parts in groups for part in parts]
    sizes = [len(parts) for parts in groups]
    inputs, aliases = [table, *qs, *parts], {}
    for at, pair in enumerate(state):
        for half, array in enumerate(pair or ()):
            aliases[len(inputs)] = len(outs) + 2 * at + half
            inputs.append(array)
    results = call(
        functools.partial(attention_kernel, plan, q_chunks, k_chunks, sizes, fresh, final),
        "attention",
        10,
        [SMEM] + [VMEM] * (len(inputs) - 1),
        outs + [(shape, jnp.float32, VMEM) for shape in shapes],
        scratch + [pltpu.SemaphoreType.DMA((len(parts) + len(outs),))],
        *inputs,
        aliases=aliases,
    )
    if final:
        return results[: len(final)]
    return [tuple(results[2 * at : 2 * at + 2]) for at in range(len(qs))]


def cut_kernel(sizes, at, table, weights, *refs):
    outs, (held, semaphores) = refs[: len(sizes)], refs[len(sizes) :]
    copies = Copies(semaphores)
    half = sum(sizes)
    first = pl.multiple_of(table[at] * half, half)
    ins, put = [], 0
    for size in sizes:
        target = held.at[pl.ds(put, size)]
        ins.append((copies.start(weights.at[pl.ds(first + put, size)], target), target))
        put += size
    stores = []
    for (copy, piece), out in zip(ins, outs):
        copy.wait()
        stores.append(copies.start(piece, out))
    for copy in stores:
        copy.wait()


def cut(table, at, weights, sizes):
    depth, width = weights.shape
    return call(
        functools.partial(cut_kernel, sizes, at),
        "cut_weights",
        4,
        [SMEM, HBM],
        [((size, width), weights.dtype, HBM) for size in sizes],
        [
            pltpu.VMEM((depth // 2, width), weights.dtype),
            pltpu.SemaphoreType.DMA((2 * len(sizes),)),
        ],
        table,
        weights,
    )


def near_kernel(chunks, left_hbm, weights_hbm, out, left, weights, semaphores):
    copies = Copies(semaphores)
    step = out.shape[1] // chunks
    first = copies.start(left_hbm, left)
    lanes = [pl.ds(chunk * step, step) for chunk in range(chunks)]
    waits = [copies.start(weights_hbm.at[:, at], weights.at[:, at]) for at in lanes]
    first.wait()
    for at, copy in zip(lanes, waits):
        copy.wait()
        out[:, at] = jnp.dot(left[...], weights[:, at], preferred_element_type=jnp.float32)


def output_near(left, weights, chunks=6):
    (rows, columns), width = left.shape, weights.shape[1]
    return call(
        functools.partial(near_kernel, chunks),
        "output_near",
        8,
        [HBM] * 2,
        [((rows, width), jnp.float32, VMEM)],
        [
            pltpu.VMEM(left.shape, left.dtype),
            pltpu.VMEM(weights.shape, weights.dtype),
            pltpu.SemaphoreType.DMA((1 + chunks,)),
        ],
        left,
        weights,
    )[0]


def send_kernel(at, chunks, table, left_hbm, near, *refs):
    count = len(refs) - 5
    pieces, (out, weights, left, staged, semaphores) = refs[:count], refs[count:]
    copies = Copies(semaphores)
    depth, width = weights.shape
    step = width // chunks
    first = copies.start(left_hbm, left)
    waits, put = [], 0
    for index, piece in enumerate(pieces):
        half = table[at] if index < count // 2 else 1 - table[at]
        row = pl.multiple_of(half * (depth // 2) + put % (depth // 2), 16)
        waits.append(copies.start(piece, weights.at[pl.ds(row, piece.shape[0])]))
        put += piece.shape[0]
    for copy in waits:
        copy.wait()
    first.wait()
    half = left.shape[0] // 2
    stores = []
    for chunk in range(chunks):
        span = pl.ds(chunk * step, step)
        staged[:, span] = (
            near[half:, span]
            + jnp.dot(left[half:, :], weights[:, span], preferred_element_type=jnp.float32)
        ).astype(jnp.bfloat16)
        stores.append(copies.start(staged.at[:, span], out.at[:, span]))
    for copy in stores:
        copy.wait()


def output_send(table, at, left, near, pieces, chunks=6):
    (rows, width), columns = near.shape, left.shape[1]
    half, bf16 = (rows // 2, width), jnp.bfloat16
    return call(
        functools.partial(send_kernel, at, chunks),
        "output_send",
        8,
        [SMEM, HBM, VMEM] + [HBM] * len(pieces),
        [(half, bf16, HBM), ((columns, width), bf16, VMEM)],
        [
            pltpu.VMEM(left.shape, bf16),
            pltpu.VMEM(half, bf16),
            pltpu.SemaphoreType.DMA((1 + len(pieces) + chunks,)),
        ],
        table,
        left,
        near,
        *pieces,
    )


def keep_kernel(chunks, left_hbm, hidden, near, weights, out, held, left, semaphores):
    copies = Copies(semaphores)
    first, late = copies.start(left_hbm, left), copies.start(hidden, held)
    first.wait()
    half, step = left.shape[0] // 2, out.shape[1] // chunks
    for chunk in range(chunks):
        span = pl.ds(chunk * step, step)
        out[:, span] = near[:half, span] + jnp.dot(
            left[:half, :], weights[:, span], preferred_element_type=jnp.float32
        )
    late.wait()


def output_keep(left, hidden, near, weights, chunks=6):
    rows, width = near.shape
    return call(
        functools.partial(keep_kernel, chunks),
        "output_keep",
        4,
        [HBM, HBM, VMEM, VMEM],
        [((rows // 2, width), jnp.float32, VMEM), (hidden.shape, hidden.dtype, VMEM)],
        [pltpu.VMEM(left.shape, jnp.bfloat16), pltpu.SemaphoreType.DMA((2,))],
        left,
        hidden,
        near,
        weights,
    )


def final_kernel(chunks, received, hidden, kept, gain, out, other, staged, gains, semaphores):
    copies = Copies(semaphores)
    width = hidden.shape[1]
    step = width // chunks
    lanes = [pl.ds(chunk * step, step) for chunk in range(chunks)]
    waits = [copies.start(received.at[:, span], other.at[:, span]) for span in lanes]
    late = copies.start(gain, gains)
    square = jnp.zeros((hidden.shape[0], 128), jnp.float32)
    for span, copy in zip(lanes, waits):
        copy.wait()
        total = kept[:, span] + other[:, span].astype(jnp.float32)
        for lane in range(0, step, 128):
            part = total[:, lane : lane + 128]
            square = square + part * part
    mean = jnp.sum(square, axis=1, keepdims=True) / width
    scale = lax.rsqrt(mean + EPS)
    late.wait()
    row = gains[...].reshape(1, width)
    stores = []
    for chunk, span in enumerate(lanes):
        total = kept[:, span] + other[:, span].astype(jnp.float32)
        normed = total * scale * row[:, chunk * step : (chunk + 1) * step]
        staged[:, span] = (hidden[:, span].astype(jnp.float32) + normed).astype(jnp.bfloat16)
        stores.append(copies.start(staged.at[:, span], out.at[:, span]))
    for store in stores:
        store.wait()


def output(received, hidden, kept, gain, chunks=6):
    rows, width = hidden.shape
    bf16 = jnp.bfloat16
    return call(
        functools.partial(final_kernel, chunks),
        "output_norm",
        8,
        [HBM, VMEM, VMEM, HBM],
        [((rows, width), bf16, HBM)],
        [
            pltpu.VMEM((rows, width), bf16),
            pltpu.VMEM((rows, width), bf16),
            pltpu.VMEM((width,), jnp.float32),
            pltpu.SemaphoreType.DMA((1 + 2 * chunks,)),
        ],
        received,
        hidden,
        kept,
        gain,
    )[0]


def rotary_table(positions):
    half = HD // 2
    frequency = jnp.power(
        jnp.float32(10000.0), -jnp.arange(half, dtype=jnp.float32) * (2.0 / HD)
    )
    angles = positions.astype(jnp.float32)[:, None] * frequency[None, :]
    cos, sin = jnp.cos(angles), jnp.sin(angles)
    return jnp.concatenate([cos, cos, -sin, sin], axis=1)


def lookup(block_of, index):
    ids = jnp.arange(block_of.shape[0], dtype=jnp.int32)
    return jnp.sum(jnp.where(index[..., None] == ids, block_of, 0), axis=-1)


def flipped(array, axis, bit):
    size = lax.axis_size(axis)
    return lax.ppermute(array, axis, [(i, i ^ bit) for i in range(size)])


def along_line(array):
    size = lax.axis_size("seq")
    parts = [array[None]]
    for by in range(1, size):
        part = lax.ppermute(array, "seq", [(i, (i + by) % size) for i in range(size)])
        parts.append(Came(part[None]))
    return parts


def along_ring(array):
    size = lax.axis_size("seq")
    parts, part = [array[None]], array
    for _ in range(1, size):
        part = lax.ppermute(part, "seq", [(i, (i + 1) % size) for i in range(size)])
        parts.append(Came(part[None]))
    return parts


def came(parts):
    return [part.array for part in parts if isinstance(part, Came)]


def after(array, *others):
    return lax.optimization_barrier((array, *others))[0]


def two_chips(hidden, pre_gain, post_gain, wq, wk, wv, w_out, block_of):
    rows = hidden.shape[0]
    block_rows = 2 * rows
    lines, tp = lax.axis_size("seq"), lax.axis_index("tp")
    seq, group = lax.axis_index("seq"), lax.axis_index("groups")
    chip, core = tp // 2, tp % 2

    line = (seq - jnp.arange(lines, dtype=jnp.int32)) % lines
    near_starts = lookup(block_of, 2 * line + chip) * block_rows
    far_starts = lookup(block_of, 2 * line + 1 - chip) * block_rows
    table = jnp.concatenate([jnp.stack([core, group]).astype(jnp.int32), near_starts, far_starts])
    group_at, near_at, far_at = 1, 2, 2 + lines
    run = jnp.arange(rows, dtype=jnp.int32)
    place = jnp.concatenate([core * rows + run, (1 - core) * rows + run])
    trig = rotary_table(jnp.concatenate([near_starts[0] + place, far_starts[0] + place]))
    runs = [(0, 0, rows), (1, 0, rows)]
    near_chunk, far_chunk = Chunk(near_at, runs, rows), Chunk(far_at, runs, rows)
    others, everyone = list(range(1, lines)), list(range(lines))

    half = rows // 2
    own = [norm(hidden, pre_gain, at * half, [half])[0] for at in range(2)]
    away = [flipped(part, "tp", 2) for part in own]
    partner = [Came(flipped(part, "tp", 1)) for part in own]

    weights = (wq, wk, wv)
    places = [0, half, rows, rows + half]
    q_near, kv_near = qkv([*own, *partner], places, block_rows, weights, trig, 0)
    near = along_line(kv_near)
    w_cut = cut(table, group_at, after(w_out, kv_near), [w_out.shape[0] // 8] * 4)
    q_near = after(q_near, *w_cut)
    (near_state,) = attention(
        [Step(0, 0, others, same=0)], table, [q_near], [near_chunk], [near], [near_chunk], [None]
    )

    away[0] = after(away[0], *near_state)
    quarter = half // 2
    swapped = [flipped(away[0][at : at + quarter], "tp", 1) for at in (0, quarter)]
    held = qkv(
        [Came(away[0]), *[Came(part) for part in swapped]],
        [0, rows, rows + quarter],
        block_rows,
        weights,
        trig,
        block_rows,
    )
    away[1] = after(away[1], *held)
    held = qkv(
        [Came(away[1]), Came(flipped(away[1], "tp", 1))],
        [half, rows + half],
        block_rows,
        weights,
        trig,
        block_rows,
        held,
    )
    q_far, kv_far = held
    far = along_ring(kv_far)

    fetched = lambda piece, *others: flipped(after(piece, *others), "tp", 2)
    swap = lambda array: flipped(array, "groups", 1)
    w_far = [fetched(piece, away[1]) for piece in w_cut[:2]]
    w_far[0] = after(w_far[0], kv_far)
    w_far.append(fetched(w_cut[2], w_far[0]))
    w_other = [swap(w_far[0])]
    w_far[1] = after(w_far[1], came(far)[0], w_other[0])
    w_far.append(fetched(w_cut[3], w_far[1]))
    w_other.append(swap(w_far[1]))

    near_state, far_state = attention(
        [Step(1, 1, [], same=0), Step(1, 0, everyone), Step(0, 1, [0])],
        table,
        [q_near, q_far],
        [near_chunk, far_chunk],
        [near, far[:1]],
        [near_chunk, far_chunk],
        [near_state, None],
    )
    w_far[2] = after(w_far[2], *far_state, w_other[1])
    w_other.append(swap(w_far[2]))
    attended, gone = attention(
        [Step(1, 0, others), Step(0, 0, others)],
        table,
        [q_near, q_far],
        [near_chunk, far_chunk],
        [far],
        [far_chunk],
        [near_state, far_state],
        final=[[0], [1]],
    )
    gone = flipped(gone, "tp", 2)
    near_sum = output_near(attended, w_out)
    w_other.append(swap(after(w_far[3], attended)))
    pieces = [Came(piece) for piece in w_far + w_other]
    sent, w_laid = output_send(table, group_at, Came(gone), near_sum, pieces)
    received = flipped(sent, "tp", 1)
    kept, held = output_keep(Came(gone), hidden, near_sum, w_laid)
    return output(Came(received), held, kept, post_gain)


def any_count(hidden, pre_gain, post_gain, wq, wk, wv, w_out, block_of):
    rows = hidden.shape[0]
    lines = lax.axis_size("seq")
    line = (lax.axis_index("seq") - jnp.arange(lines, dtype=jnp.int32)) % lines
    block = (2 * line[:, None] + jnp.arange(2, dtype=jnp.int32)).reshape(-1)
    block_rows = rows * lax.axis_size("tp") // 2
    starts = lookup(block_of, block) * block_rows
    table = jnp.concatenate([jnp.zeros(2, jnp.int32), starts])
    normed = norm(hidden, pre_gain, 0, [rows], 1)[0]
    normed = lax.all_gather(normed, "tp", axis=0, tiled=True)
    place = jnp.arange(block_rows, dtype=jnp.int32)
    trig = rotary_table((starts[:2, None] + place).reshape(-1))
    qs, keys_values, weights = [], [], (wq, wk, wv)
    for at in range(2):
        first = at * block_rows
        rows_here = [normed[first : first + block_rows]]
        q, kv = qkv(rows_here, [0], block_rows, weights, trig, first)
        qs.append(q)
        keys_values.append(kv)
    kv = lax.all_gather(jnp.stack(keys_values), "seq")[line].reshape(-1, block_rows, 2 * HD)
    rest = list(range(2, 2 * lines))
    runs = [(0, 0, block_rows)]
    attended = attention(
        [Step(0, 0, [1], same=0), Step(1, 0, [0], same=1), Step(0, 0, rest), Step(1, 0, rest)],
        table,
        qs,
        [Chunk(2, runs, 0), Chunk(3, runs, 0)],
        [[kv]],
        [Chunk(2, runs, 0)],
        [None, None],
        final=[[0, 1]],
    )[0]
    partial = jnp.dot(attended, w_out, preferred_element_type=jnp.float32)
    summed = lax.psum_scatter(
        partial.astype(jnp.bfloat16), "tp", scatter_dimension=0, tiled=True
    ).astype(jnp.float32)
    mean = jnp.mean(summed * summed, axis=-1, keepdims=True)
    projected = summed * lax.rsqrt(mean + EPS) * post_gain
    return (hidden.astype(jnp.float32) + projected).astype(jnp.bfloat16)


def solution(mesh):
    return jax.shard_map(
        two_chips if mesh.shape["tp"] == 4 else any_count,
        mesh=mesh,
        in_specs=(
            P(("groups", "seq", "tp"), None),
            P(),
            P(),
            P(None, "tp"),
            P(None, "tp"),
            P(None, "tp"),
            P("tp", None),
            P(),
        ),
        out_specs=P(("groups", "seq", "tp"), None),
        check_vma=False,
    )
```

```python
import functools
import math

import jax
import jax.numpy as jnp
from jax import lax
from jax.experimental import pallas as pl
from jax.experimental.pallas import tpu as pltpu
from jax.sharding import PartitionSpec as P

HD = 128
ATT_SCALAR = 144
EPS = 1e-6
MIB = 1024 * 1024
HIDDEN = -1e30
ONES = 16
COST = pl.CostEstimate(flops=1, bytes_accessed=1, transcendentals=0)

ANY = pl.BlockSpec(memory_space=pl.ANY)
HBM = pl.BlockSpec(memory_space=pltpu.HBM)
VMEM = pl.BlockSpec(memory_space=pltpu.VMEM)
SMEM = pl.BlockSpec(memory_space=pltpu.SMEM)


class Came:
    def __init__(self, array):
        self.array, self.shape = array, array.shape


def call(kernel, name, mib, in_specs, outs, scratch, *args, aliases=None):
    in_specs, pinned = list(in_specs), []
    for at, arg in enumerate(args):
        if isinstance(arg, Came):
            arg, in_specs[at] = arg.array, ANY
        elif in_specs[at] is not SMEM:
            arg = pltpu.with_memory_space_constraint(arg, in_specs[at].memory_space)
        pinned.append(arg)
    return pl.pallas_call(
        kernel,
        in_specs=in_specs,
        out_specs=[spec for _, _, spec in outs],
        out_shape=[spec.memory_space(shape, dtype) for shape, dtype, spec in outs],
        scratch_shapes=scratch,
        input_output_aliases=aliases or {},
        compiler_params=pltpu.CompilerParams(vmem_limit_bytes=mib * MIB),
        cost_estimate=COST,
        name=name,
    )(*pinned)


class Copies:
    def __init__(self, semaphores):
        self.semaphores, self.used = semaphores, 0

    def start(self, source, target):
        copy = pltpu.make_async_copy(source, target, self.semaphores.at[self.used])
        self.used += 1
        copy.start()
        return copy


def norm_kernel(cuts, pieces, first, hidden, gain, *refs):
    parts, (gains, rows, staged, semaphores) = refs[: len(cuts)], refs[len(cuts) :]
    copies = Copies(semaphores)
    count, width = rows.shape
    step = count // pieces
    spans = [pl.ds(at * step, step) for at in range(pieces)]
    ins = [
        copies.start(hidden.at[pl.ds(first + at * step, step)], rows.at[span])
        for at, span in enumerate(spans)
    ]
    copies.start(gain, gains).wait()
    scale = gains[...].reshape(1, width)
    outs = []
    for at, span in enumerate(spans):
        ins[at].wait()
        x = rows[span, :].astype(jnp.float32)
        square = x * x
        folded = square[:, :128]
        for lane in range(128, width, 128):
            folded = folded + square[:, lane : lane + 128]
        mean = jnp.sum(folded, axis=1, keepdims=True) / width
        staged[span, :] = (x * lax.rsqrt(mean + EPS) * scale).astype(jnp.bfloat16)
        begin = 0
        for cut, part in zip(cuts, parts):
            if begin <= at * step < begin + cut:
                inside = pl.ds(at * step - begin, step)
                outs.append(copies.start(staged.at[span], part.at[inside]))
            begin += cut
    for copy in outs:
        copy.wait()


def norm(hidden, gain, first, cuts, pieces=3):
    rows, width = sum(cuts), hidden.shape[1]
    bf16 = jnp.bfloat16
    return call(
        functools.partial(norm_kernel, cuts, pieces, first),
        "norm_rows",
        8,
        [HBM, HBM],
        [((cut, width), bf16, HBM) for cut in cuts],
        [
            pltpu.VMEM((width,), jnp.float32),
            pltpu.VMEM((rows, width), bf16),
            pltpu.VMEM((rows, width), bf16),
            pltpu.SemaphoreType.DMA((1 + 2 * pieces,)),
        ],
        hidden,
        gain,
    )


def qkv_kernel(places, first, chunks, held, trig, wq, wk, wv, *refs):
    parts, refs = refs[: len(places)], refs[len(places) + 2 * held :]
    q, kv, weights, rows, angles, semaphores = refs
    copies, waits = Copies(semaphores), []
    depth = weights.shape[0] // chunks
    for chunk in range(chunks):
        span, put, column, here = pl.ds(chunk * depth, depth), 0, 0, []
        for part in parts:
            target = rows.at[pl.ds(put, part.shape[0]), span]
            here.append(copies.start(part.at[:, span], target))
            put += part.shape[0]
        for weight in (wq, wk, wv):
            target = weights.at[span, pl.ds(column, weight.shape[1])]
            here.append(copies.start(weight.at[span], target))
            column += weight.shape[1]
        waits.append(here)
    late, put = [], 0
    for part, place in zip(parts, places):
        count = part.shape[0]
        source = trig.at[pl.ds(first + place, count)]
        late.append(copies.start(source, angles.at[pl.ds(put, count)]))
        put += count
    product = None
    for chunk, here in enumerate(waits):
        for copy in here:
            copy.wait()
        span = pl.ds(chunk * depth, depth)
        term = jnp.dot(rows[:, span], weights[span, :], preferred_element_type=jnp.float32)
        product = term if product is None else product + term
    for copy in late:
        copy.wait()
    cos, sin = angles[:, :HD], angles[:, HD:]
    queries = product.shape[1] - 2 * HD

    def rotated(at):
        y = product[:, at : at + HD]
        return y * cos + pltpu.roll(y, HD // 2, 1) * sin

    factor = ATT_SCALAR ** (-0.5) * math.log2(math.e)
    keys = rotated(queries).astype(jnp.bfloat16)
    values = product[:, queries + HD :].astype(jnp.bfloat16)
    heads = [(rotated(at) * factor).astype(jnp.bfloat16) for at in range(0, queries, HD)]
    put = 0
    for part, place in zip(parts, places):
        count = part.shape[0]
        kv[place : place + count, :HD] = keys[put : put + count]
        kv[place : place + count, HD:] = values[put : put + count]
        for head, rotated_head in enumerate(heads):
            q[head, place : place + count, :] = rotated_head[put : put + count]
        put += count


def qkv(parts, places, total, weights, trig, first, held=(), chunks=4):
    rows, width = sum(part.shape[0] for part in parts), parts[0].shape[1]
    columns = sum(weight.shape[1] for weight in weights)
    heads, bf16 = weights[0].shape[1] // HD, jnp.bfloat16
    given = 4 + len(parts)
    return call(
        functools.partial(qkv_kernel, places, first, chunks, bool(held)),
        "qkv",
        14,
        [HBM] * given + [VMEM] * len(held),
        [((heads, total, HD), bf16, VMEM), ((total, 2 * HD), bf16, VMEM)],
        [
            pltpu.VMEM((width, columns), bf16),
            pltpu.VMEM((rows, width), bf16),
            pltpu.VMEM((rows, 2 * HD), jnp.float32),
            pltpu.SemaphoreType.DMA((len(parts) + (len(parts) + 3) * chunks,)),
        ],
        trig,
        *weights,
        *parts,
        *held,
        aliases={given + at: at for at in range(len(held))},
    )


class Step:
    def __init__(self, q, group, slots, same=None, merged=False):
        self.q, self.group, self.slots = q, group, slots
        self.same, self.merged = same, merged


class Chunk:
    def __init__(self, at, runs, share):
        self.at, self.runs, self.share = at, runs, share

    def places(self, core, axis, first, size):
        shape = (size, 1) if axis == 0 else (1, size)
        index = first + lax.broadcasted_iota(jnp.int32, shape, axis)
        result, begin = index, 0
        for which, offset, rows in self.runs:
            base = (core if which == 0 else 1 - core) * self.share + offset - begin
            inside = (index >= begin) & (index < begin + rows)
            result = jnp.where(inside, index + base, result)
            begin += rows
        return result


def attention_kernel(plan, q_chunks, k_chunks, group_parts, fresh, final, table, *refs):
    refs = list(refs)
    take = lambda n: [refs.pop(0) for _ in range(n)]
    count = len(q_chunks)
    qs = take(count)
    kv_parts = [take(n) for n in group_parts]
    take(2 * (count - len(fresh)))
    outs = take(len(final))
    states = [take(2) for _ in range(count)]
    kvs, staged = take(len(group_parts)), take(len(final))
    (semaphores,) = refs
    copies = Copies(semaphores)
    core = table[0]
    waits = {}
    for group, (parts, kv) in enumerate(zip(kv_parts, kvs)):
        each = kv.shape[0] // len(parts)
        waits[group] = [
            copies.start(part, kv.at[pl.ds(slot * each, each)])
            for slot, part in enumerate(parts)
        ]

    def ready(group):
        for copy in waits.pop(group, []):
            copy.wait()

    def attend(q, keys_values, begin, visible=None, bias=None):
        q_ref, (peak, acc) = qs[q], states[q]
        heads = q_ref.shape[0]
        keys = keys_values[:, :HD]
        values = keys_values[:, HD:].T
        values = jnp.concatenate([values, jnp.ones((ONES, keys.shape[0]), values.dtype)], axis=0)
        tiles, tile = acc.shape[0], acc.shape[2] // heads
        scores, tops, weights = [], [], []
        for at in range(tiles):
            q_tile = q_ref[:, at * tile : (at + 1) * tile, :].reshape(heads * tile, HD)
            score = lax.dot_general(
                keys, q_tile, (((1,), (1,)), ((), ())), preferred_element_type=jnp.float32
            )
            if visible is not None:
                seen = jnp.concatenate([visible(at * tile, tile)] * heads, axis=1)
                score = jnp.where(seen, score, HIDDEN)
            if bias is not None:
                score = score + bias
            scores.append(score)
        for at in range(tiles):
            top = jnp.max(scores[at], axis=0, keepdims=True)
            if not begin:
                top = jnp.maximum(peak[at, 0:1, :], top)
            tops.append(top)
            weights.append(jnp.exp2((scores[at] - top).astype(jnp.bfloat16)))
        for at in range(tiles):
            summed = jnp.dot(values, weights[at], preferred_element_type=jnp.float32)
            if not begin:
                summed = summed + acc[at] * jnp.exp2(peak[at, 0:1, :] - tops[at])
            acc[at] = summed
            peak[at] = jnp.broadcast_to(tops[at], peak.shape[1:])

    begun = set(range(count)) - set(fresh)
    for step in plan:
        q, group, kv = step.q, step.group, kvs[step.group]
        q_chunk, k_chunk = q_chunks[q], k_chunks[group]
        if step.same is not None:
            keys_at = k_chunk.places(core, 0, 0, kv.shape[1])
            visible = lambda first, tile: keys_at <= q_chunk.places(core, 1, first, tile)
            own = kv_parts[group][0]
            attend(q, own[step.same], q not in begun, visible=visible)
            begun.add(q)
        start = table[q_chunk.at]
        slots = step.slots
        if not slots:
            continue
        ready(group)
        if step.merged:
            shown = [table[k_chunk.at + slot] < start for slot in slots]

            @pl.when(functools.reduce(jnp.logical_or, shown))
            def _():
                rows = kv.shape[1]
                bias = [
                    jnp.where(see, 0.0, HIDDEN) * jnp.ones((rows, 1), jnp.float32)
                    for see in shown
                ]
                keys_values = kv[slots[0] : slots[-1] + 1].reshape(len(slots) * rows, 2 * HD)
                attend(q, keys_values, False, bias=jnp.concatenate(bias, axis=0))

        else:

            def one(slot, carry):
                @pl.when(table[k_chunk.at + slot] < start)
                def _():
                    attend(q, kv[slot], False)

                return carry

            lax.fori_loop(slots[0], slots[-1] + 1, one, 0)

    for group in list(waits):
        ready(group)
    stores = []
    for out, stage, order in zip(outs, staged, final):
        put = 0
        for q in order:
            acc, heads = states[q][1], qs[q].shape[0]
            tile = acc.shape[2] // heads
            for at in range(acc.shape[0]):
                rows = acc[at, :HD, :] / acc[at, HD : HD + 1, :]
                rows = rows.T.astype(jnp.bfloat16)
                for head in range(heads):
                    stage[put : put + tile, head * HD : (head + 1) * HD] = rows[
                        head * tile : (head + 1) * tile
                    ]
                put += tile
        stores.append(copies.start(stage, out))
    for copy in stores:
        copy.wait()


def attention(plan, table, qs, q_chunks, groups, k_chunks, state, final=()):
    fresh = [at for at, held in enumerate(state) if held is None]
    shapes = []
    for q in qs:
        heads, rows, _ = q.shape
        tile = min(rows, 128)
        shapes += [(rows // tile, deep, heads * tile) for deep in (8, HD + ONES)]
    width = qs[0].shape[0] * HD
    sums = [sum(qs[q].shape[1] for q in order) for order in final]
    outs = [((rows, width), jnp.bfloat16, HBM) for rows in sums]
    scratch = []
    for parts in groups:
        slots = sum(part.shape[0] for part in parts)
        scratch.append(pltpu.VMEM((slots,) + parts[0].shape[1:], jnp.bfloat16))
    scratch += [pltpu.VMEM((rows, width), jnp.bfloat16) for rows in sums]
    parts = [part for parts in groups for part in parts]
    sizes = [len(parts) for parts in groups]
    inputs, aliases = [table, *qs, *parts], {}
    for at, pair in enumerate(state):
        for half, array in enumerate(pair or ()):
            aliases[len(inputs)] = len(outs) + 2 * at + half
            inputs.append(array)
    results = call(
        functools.partial(attention_kernel, plan, q_chunks, k_chunks, sizes, fresh, final),
        "attention",
        10,
        [SMEM] + [VMEM] * (len(inputs) - 1),
        outs + [(shape, jnp.float32, VMEM) for shape in shapes],
        scratch + [pltpu.SemaphoreType.DMA((len(parts) + len(outs),))],
        *inputs,
        aliases=aliases,
    )
    if final:
        return results[: len(final)]
    return [tuple(results[2 * at : 2 * at + 2]) for at in range(len(qs))]


def cut_kernel(sizes, at, table, weights, *refs):
    outs, (held, semaphores) = refs[: len(sizes)], refs[len(sizes) :]
    copies = Copies(semaphores)
    half = sum(sizes)
    first = pl.multiple_of(table[at] * half, half)
    ins, put = [], 0
    for size in sizes:
        target = held.at[pl.ds(put, size)]
        ins.append((copies.start(weights.at[pl.ds(first + put, size)], target), target))
        put += size
    stores = []
    for (copy, piece), out in zip(ins, outs):
        copy.wait()
        stores.append(copies.start(piece, out))
    for copy in stores:
        copy.wait()


def cut(table, at, weights, sizes):
    depth, width = weights.shape
    return call(
        functools.partial(cut_kernel, sizes, at),
        "cut_weights",
        4,
        [SMEM, HBM],
        [((size, width), weights.dtype, HBM) for size in sizes],
        [
            pltpu.VMEM((depth // 2, width), weights.dtype),
            pltpu.SemaphoreType.DMA((2 * len(sizes),)),
        ],
        table,
        weights,
    )


def near_kernel(chunks, left_hbm, weights_hbm, out, left, weights, semaphores):
    copies = Copies(semaphores)
    step = out.shape[1] // chunks
    first = copies.start(left_hbm, left)
    lanes = [pl.ds(chunk * step, step) for chunk in range(chunks)]
    waits = [copies.start(weights_hbm.at[:, at], weights.at[:, at]) for at in lanes]
    first.wait()
    for at, copy in zip(lanes, waits):
        copy.wait()
        out[:, at] = jnp.dot(left[...], weights[:, at], preferred_element_type=jnp.float32)


def output_near(left, weights, chunks=6):
    (rows, columns), width = left.shape, weights.shape[1]
    return call(
        functools.partial(near_kernel, chunks),
        "output_near",
        8,
        [HBM] * 2,
        [((rows, width), jnp.float32, VMEM)],
        [
            pltpu.VMEM(left.shape, left.dtype),
            pltpu.VMEM(weights.shape, weights.dtype),
            pltpu.SemaphoreType.DMA((1 + chunks,)),
        ],
        left,
        weights,
    )[0]


def send_kernel(at, chunks, table, left_hbm, near, *refs):
    count = len(refs) - 5
    pieces, (out, weights, left, staged, semaphores) = refs[:count], refs[count:]
    copies = Copies(semaphores)
    depth, width = weights.shape
    step = width // chunks
    first = copies.start(left_hbm, left)
    waits, put = [], 0
    for index, piece in enumerate(pieces):
        half = table[at] if index < count // 2 else 1 - table[at]
        row = pl.multiple_of(half * (depth // 2) + put % (depth // 2), 16)
        waits.append(copies.start(piece, weights.at[pl.ds(row, piece.shape[0])]))
        put += piece.shape[0]
    for copy in waits:
        copy.wait()
    first.wait()
    half = left.shape[0] // 2
    stores = []
    for chunk in range(chunks):
        span = pl.ds(chunk * step, step)
        staged[:, span] = (
            near[half:, span]
            + jnp.dot(left[half:, :], weights[:, span], preferred_element_type=jnp.float32)
        ).astype(jnp.bfloat16)
        stores.append(copies.start(staged.at[:, span], out.at[:, span]))
    for copy in stores:
        copy.wait()


def output_send(table, at, left, near, pieces, chunks=6):
    (rows, width), columns = near.shape, left.shape[1]
    half, bf16 = (rows // 2, width), jnp.bfloat16
    return call(
        functools.partial(send_kernel, at, chunks),
        "output_send",
        8,
        [SMEM, HBM, VMEM] + [HBM] * len(pieces),
        [(half, bf16, HBM), ((columns, width), bf16, VMEM)],
        [
            pltpu.VMEM(left.shape, bf16),
            pltpu.VMEM(half, bf16),
            pltpu.SemaphoreType.DMA((1 + len(pieces) + chunks,)),
        ],
        table,
        left,
        near,
        *pieces,
    )


def keep_kernel(chunks, left_hbm, hidden, near, weights, out, held, left, semaphores):
    copies = Copies(semaphores)
    first, late = copies.start(left_hbm, left), copies.start(hidden, held)
    first.wait()
    half, step = left.shape[0] // 2, out.shape[1] // chunks
    for chunk in range(chunks):
        span = pl.ds(chunk * step, step)
        out[:, span] = near[:half, span] + jnp.dot(
            left[:half, :], weights[:, span], preferred_element_type=jnp.float32
        )
    late.wait()


def output_keep(left, hidden, near, weights, chunks=6):
    rows, width = near.shape
    return call(
        functools.partial(keep_kernel, chunks),
        "output_keep",
        4,
        [HBM, HBM, VMEM, VMEM],
        [((rows // 2, width), jnp.float32, VMEM), (hidden.shape, hidden.dtype, VMEM)],
        [pltpu.VMEM(left.shape, jnp.bfloat16), pltpu.SemaphoreType.DMA((2,))],
        left,
        hidden,
        near,
        weights,
    )


def final_kernel(chunks, received, hidden, kept, gain, out, other, staged, gains, semaphores):
    copies = Copies(semaphores)
    width = hidden.shape[1]
    step = width // chunks
    lanes = [pl.ds(chunk * step, step) for chunk in range(chunks)]
    waits = [copies.start(received.at[:, span], other.at[:, span]) for span in lanes]
    late = copies.start(gain, gains)
    square = jnp.zeros((hidden.shape[0], 128), jnp.float32)
    for span, copy in zip(lanes, waits):
        copy.wait()
        total = kept[:, span] + other[:, span].astype(jnp.float32)
        for lane in range(0, step, 128):
            part = total[:, lane : lane + 128]
            square = square + part * part
    mean = jnp.sum(square, axis=1, keepdims=True) / width
    scale = lax.rsqrt(mean + EPS)
    late.wait()
    row = gains[...].reshape(1, width)
    stores = []
    for chunk, span in enumerate(lanes):
        total = kept[:, span] + other[:, span].astype(jnp.float32)
        normed = total * scale * row[:, chunk * step : (chunk + 1) * step]
        staged[:, span] = (hidden[:, span].astype(jnp.float32) + normed).astype(jnp.bfloat16)
        stores.append(copies.start(staged.at[:, span], out.at[:, span]))
    for store in stores:
        store.wait()


def output(received, hidden, kept, gain, chunks=6):
    rows, width = hidden.shape
    bf16 = jnp.bfloat16
    return call(
        functools.partial(final_kernel, chunks),
        "output_norm",
        8,
        [HBM, VMEM, VMEM, HBM],
        [((rows, width), bf16, HBM)],
        [
            pltpu.VMEM((rows, width), bf16),
            pltpu.VMEM((rows, width), bf16),
            pltpu.VMEM((width,), jnp.float32),
            pltpu.SemaphoreType.DMA((1 + 2 * chunks,)),
        ],
        received,
        hidden,
        kept,
        gain,
    )[0]


def rotary_table(positions):
    half = HD // 2
    frequency = jnp.power(
        jnp.float32(10000.0), -jnp.arange(half, dtype=jnp.float32) * (2.0 / HD)
    )
    angles = positions.astype(jnp.float32)[:, None] * frequency[None, :]
    cos, sin = jnp.cos(angles), jnp.sin(angles)
    return jnp.concatenate([cos, cos, -sin, sin], axis=1)


def lookup(block_of, index):
    ids = jnp.arange(block_of.shape[0], dtype=jnp.int32)
    return jnp.sum(jnp.where(index[..., None] == ids, block_of, 0), axis=-1)


def flipped(array, axis, bit):
    size = lax.axis_size(axis)
    return lax.ppermute(array, axis, [(i, i ^ bit) for i in range(size)])


def along_line(array):
    size = lax.axis_size("seq")
    parts = [array[None]]
    for by in range(1, size):
        part = lax.ppermute(array, "seq", [(i, (i + by) % size) for i in range(size)])
        parts.append(Came(part[None]))
    return parts


def along_ring(array):
    size = lax.axis_size("seq")
    parts, part = [array[None]], array
    for _ in range(1, size):
        part = lax.ppermute(part, "seq", [(i, (i + 1) % size) for i in range(size)])
        parts.append(Came(part[None]))
    return parts


def came(parts):
    return [part.array for part in parts if isinstance(part, Came)]


def after(array, *others):
    return lax.optimization_barrier((array, *others))[0]


def two_chips(hidden, pre_gain, post_gain, wq, wk, wv, w_out, block_of):
    rows = hidden.shape[0]
    block_rows = 2 * rows
    lines, tp = lax.axis_size("seq"), lax.axis_index("tp")
    seq, group = lax.axis_index("seq"), lax.axis_index("groups")
    chip, core = tp // 2, tp % 2

    line = (seq - jnp.arange(lines, dtype=jnp.int32)) % lines
    near_starts = lookup(block_of, 2 * line + chip) * block_rows
    far_starts = lookup(block_of, 2 * line + 1 - chip) * block_rows
    table = jnp.concatenate([jnp.stack([core, group]).astype(jnp.int32), near_starts, far_starts])
    group_at, near_at, far_at = 1, 2, 2 + lines
    run = jnp.arange(rows, dtype=jnp.int32)
    place = jnp.concatenate([core * rows + run, (1 - core) * rows + run])
    trig = rotary_table(jnp.concatenate([near_starts[0] + place, far_starts[0] + place]))
    runs = [(0, 0, rows), (1, 0, rows)]
    near_chunk, far_chunk = Chunk(near_at, runs, rows), Chunk(far_at, runs, rows)
    others, everyone = list(range(1, lines)), list(range(lines))

    half = rows // 2
    own = [norm(hidden, pre_gain, at * half, [half])[0] for at in range(2)]
    away = [flipped(part, "tp", 2) for part in own]
    partner = [Came(flipped(part, "tp", 1)) for part in own]

    weights = (wq, wk, wv)
    places = [0, half, rows, rows + half]
    q_near, kv_near = qkv([*own, *partner], places, block_rows, weights, trig, 0)
    near = along_line(kv_near)
    w_cut = cut(table, group_at, after(w_out, kv_near), [w_out.shape[0] // 8] * 4)
    q_near = after(q_near, *w_cut)
    (near_state,) = attention(
        [Step(0, 0, others, same=0)], table, [q_near], [near_chunk], [near], [near_chunk], [None]
    )

    away[0] = after(away[0], *near_state)
    quarter = half // 2
    swapped = [flipped(away[0][at : at + quarter], "tp", 1) for at in (0, quarter)]
    held = qkv(
        [Came(away[0]), *[Came(part) for part in swapped]],
        [0, rows, rows + quarter],
        block_rows,
        weights,
        trig,
        block_rows,
    )
    away[1] = after(away[1], *held)
    held = qkv(
        [Came(away[1]), Came(flipped(away[1], "tp", 1))],
        [half, rows + half],
        block_rows,
        weights,
        trig,
        block_rows,
        held,
    )
    q_far, kv_far = held
    far = along_ring(kv_far)

    fetched = lambda piece, *others: flipped(after(piece, *others), "tp", 2)
    swap = lambda array: flipped(array, "groups", 1)
    w_far = [fetched(piece, away[1]) for piece in w_cut[:2]]
    w_far[:2] = [after(piece, came(far)[0]) for piece in w_far]
    w_far += [fetched(piece, before) for piece, before in zip(w_cut[2:], w_far[:2])]
    w_other = [swap(piece) for piece in w_far[:2]]

    near_state, far_state = attention(
        [Step(1, 1, [], same=0), Step(1, 0, everyone), Step(0, 1, [0])],
        table,
        [q_near, q_far],
        [near_chunk, far_chunk],
        [near, far[:1]],
        [near_chunk, far_chunk],
        [near_state, None],
    )
    w_far[2] = after(w_far[2], *far_state, *w_other)
    w_other.append(swap(w_far[2]))
    attended, gone = attention(
        [Step(1, 0, others), Step(0, 0, others)],
        table,
        [q_near, q_far],
        [near_chunk, far_chunk],
        [far],
        [far_chunk],
        [near_state, far_state],
        final=[[0], [1]],
    )
    gone = flipped(gone, "tp", 2)
    near_sum = output_near(attended, w_out)
    w_other.append(swap(after(w_far[3], attended)))
    pieces = [Came(piece) for piece in w_far + w_other]
    sent, w_laid = output_send(table, group_at, Came(gone), near_sum, pieces)
    received = flipped(sent, "tp", 1)
    kept, held = output_keep(Came(gone), hidden, near_sum, w_laid)
    return output(Came(received), held, kept, post_gain)


def any_count(hidden, pre_gain, post_gain, wq, wk, wv, w_out, block_of):
    rows = hidden.shape[0]
    lines = lax.axis_size("seq")
    line = (lax.axis_index("seq") - jnp.arange(lines, dtype=jnp.int32)) % lines
    block = (2 * line[:, None] + jnp.arange(2, dtype=jnp.int32)).reshape(-1)
    block_rows = rows * lax.axis_size("tp") // 2
    starts = lookup(block_of, block) * block_rows
    table = jnp.concatenate([jnp.zeros(2, jnp.int32), starts])
    normed = norm(hidden, pre_gain, 0, [rows], 1)[0]
    normed = lax.all_gather(normed, "tp", axis=0, tiled=True)
    place = jnp.arange(block_rows, dtype=jnp.int32)
    trig = rotary_table((starts[:2, None] + place).reshape(-1))
    qs, keys_values, weights = [], [], (wq, wk, wv)
    for at in range(2):
        first = at * block_rows
        rows_here = [normed[first : first + block_rows]]
        q, kv = qkv(rows_here, [0], block_rows, weights, trig, first)
        qs.append(q)
        keys_values.append(kv)
    kv = lax.all_gather(jnp.stack(keys_values), "seq")[line].reshape(-1, block_rows, 2 * HD)
    rest = list(range(2, 2 * lines))
    runs = [(0, 0, block_rows)]
    attended = attention(
        [Step(0, 0, [1], same=0), Step(1, 0, [0], same=1), Step(0, 0, rest), Step(1, 0, rest)],
        table,
        qs,
        [Chunk(2, runs, 0), Chunk(3, runs, 0)],
        [[kv]],
        [Chunk(2, runs, 0)],
        [None, None],
        final=[[0, 1]],
    )[0]
    partial = jnp.dot(attended, w_out, preferred_element_type=jnp.float32)
    summed = lax.psum_scatter(
        partial.astype(jnp.bfloat16), "tp", scatter_dimension=0, tiled=True
    ).astype(jnp.float32)
    mean = jnp.mean(summed * summed, axis=-1, keepdims=True)
    projected = summed * lax.rsqrt(mean + EPS) * post_gain
    return (hidden.astype(jnp.float32) + projected).astype(jnp.bfloat16)


def solution(mesh):
    return jax.shard_map(
        two_chips if mesh.shape["tp"] == 4 else any_count,
        mesh=mesh,
        in_specs=(
            P(("groups", "seq", "tp"), None),
            P(),
            P(),
            P(None, "tp"),
            P(None, "tp"),
            P(None, "tp"),
            P("tp", None),
            P(),
        ),
        out_specs=P(("groups", "seq", "tp"), None),
        check_vma=False,
    )
```

```python
import functools
import math

import jax
import jax.numpy as jnp
from jax import lax
from jax.experimental import pallas as pl
from jax.experimental.pallas import tpu as pltpu
from jax.sharding import PartitionSpec as P

HD = 128
ATT_SCALAR = 144
EPS = 1e-6
MIB = 1024 * 1024
HIDDEN = -1e30
ONES = 16
COST = pl.CostEstimate(flops=1, bytes_accessed=1, transcendentals=0)

ANY = pl.BlockSpec(memory_space=pl.ANY)
HBM = pl.BlockSpec(memory_space=pltpu.HBM)
VMEM = pl.BlockSpec(memory_space=pltpu.VMEM)
SMEM = pl.BlockSpec(memory_space=pltpu.SMEM)


class Came:
    def __init__(self, array):
        self.array, self.shape = array, array.shape


def call(kernel, name, mib, in_specs, outs, scratch, *args, aliases=None):
    in_specs, pinned = list(in_specs), []
    for at, arg in enumerate(args):
        if isinstance(arg, Came):
            arg, in_specs[at] = arg.array, ANY
        elif in_specs[at] is not SMEM:
            arg = pltpu.with_memory_space_constraint(arg, in_specs[at].memory_space)
        pinned.append(arg)
    return pl.pallas_call(
        kernel,
        in_specs=in_specs,
        out_specs=[spec for _, _, spec in outs],
        out_shape=[spec.memory_space(shape, dtype) for shape, dtype, spec in outs],
        scratch_shapes=scratch,
        input_output_aliases=aliases or {},
        compiler_params=pltpu.CompilerParams(vmem_limit_bytes=mib * MIB),
        cost_estimate=COST,
        name=name,
    )(*pinned)


class Copies:
    def __init__(self, semaphores):
        self.semaphores, self.used = semaphores, 0

    def start(self, source, target):
        copy = pltpu.make_async_copy(source, target, self.semaphores.at[self.used])
        self.used += 1
        copy.start()
        return copy


def norm_kernel(cuts, pieces, first, hidden, gain, *refs):
    parts, (gains, rows, staged, semaphores) = refs[: len(cuts)], refs[len(cuts) :]
    copies = Copies(semaphores)
    count, width = rows.shape
    step = count // pieces
    spans = [pl.ds(at * step, step) for at in range(pieces)]
    ins = [
        copies.start(hidden.at[pl.ds(first + at * step, step)], rows.at[span])
        for at, span in enumerate(spans)
    ]
    copies.start(gain, gains).wait()
    scale = gains[...].reshape(1, width)
    outs = []
    for at, span in enumerate(spans):
        ins[at].wait()
        x = rows[span, :].astype(jnp.float32)
        square = x * x
        folded = square[:, :128]
        for lane in range(128, width, 128):
            folded = folded + square[:, lane : lane + 128]
        mean = jnp.sum(folded, axis=1, keepdims=True) / width
        staged[span, :] = (x * lax.rsqrt(mean + EPS) * scale).astype(jnp.bfloat16)
        begin = 0
        for cut, part in zip(cuts, parts):
            if begin <= at * step < begin + cut:
                inside = pl.ds(at * step - begin, step)
                outs.append(copies.start(staged.at[span], part.at[inside]))
            begin += cut
    for copy in outs:
        copy.wait()


def norm(hidden, gain, first, cuts, pieces=3):
    rows, width = sum(cuts), hidden.shape[1]
    bf16 = jnp.bfloat16
    return call(
        functools.partial(norm_kernel, cuts, pieces, first),
        "norm_rows",
        8,
        [HBM, HBM],
        [((cut, width), bf16, HBM) for cut in cuts],
        [
            pltpu.VMEM((width,), jnp.float32),
            pltpu.VMEM((rows, width), bf16),
            pltpu.VMEM((rows, width), bf16),
            pltpu.SemaphoreType.DMA((1 + 2 * pieces,)),
        ],
        hidden,
        gain,
    )


def qkv_kernel(places, first, chunks, held, trig, wq, wk, wv, *refs):
    parts, refs = refs[: len(places)], refs[len(places) + 2 * held :]
    q, kv, weights, rows, angles, semaphores = refs
    copies, waits = Copies(semaphores), []
    depth = weights.shape[0] // chunks
    for chunk in range(chunks):
        span, put, column, here = pl.ds(chunk * depth, depth), 0, 0, []
        for part in parts:
            target = rows.at[pl.ds(put, part.shape[0]), span]
            here.append(copies.start(part.at[:, span], target))
            put += part.shape[0]
        for weight in (wq, wk, wv):
            target = weights.at[span, pl.ds(column, weight.shape[1])]
            here.append(copies.start(weight.at[span], target))
            column += weight.shape[1]
        waits.append(here)
    late, put = [], 0
    for part, place in zip(parts, places):
        count = part.shape[0]
        source = trig.at[pl.ds(first + place, count)]
        late.append(copies.start(source, angles.at[pl.ds(put, count)]))
        put += count
    product = None
    for chunk, here in enumerate(waits):
        for copy in here:
            copy.wait()
        span = pl.ds(chunk * depth, depth)
        term = jnp.dot(rows[:, span], weights[span, :], preferred_element_type=jnp.float32)
        product = term if product is None else product + term
    for copy in late:
        copy.wait()
    cos, sin = angles[:, :HD], angles[:, HD:]
    queries = product.shape[1] - 2 * HD

    def rotated(at):
        y = product[:, at : at + HD]
        return y * cos + pltpu.roll(y, HD // 2, 1) * sin

    factor = ATT_SCALAR ** (-0.5) * math.log2(math.e)
    keys = rotated(queries).astype(jnp.bfloat16)
    values = product[:, queries + HD :].astype(jnp.bfloat16)
    heads = [(rotated(at) * factor).astype(jnp.bfloat16) for at in range(0, queries, HD)]
    put = 0
    for part, place in zip(parts, places):
        count = part.shape[0]
        kv[place : place + count, :HD] = keys[put : put + count]
        kv[place : place + count, HD:] = values[put : put + count]
        for head, rotated_head in enumerate(heads):
            q[head, place : place + count, :] = rotated_head[put : put + count]
        put += count


def qkv(parts, places, total, weights, trig, first, held=(), chunks=4):
    rows, width = sum(part.shape[0] for part in parts), parts[0].shape[1]
    columns = sum(weight.shape[1] for weight in weights)
    heads, bf16 = weights[0].shape[1] // HD, jnp.bfloat16
    given = 4 + len(parts)
    return call(
        functools.partial(qkv_kernel, places, first, chunks, bool(held)),
        "qkv",
        14,
        [HBM] * given + [VMEM] * len(held),
        [((heads, total, HD), bf16, VMEM), ((total, 2 * HD), bf16, VMEM)],
        [
            pltpu.VMEM((width, columns), bf16),
            pltpu.VMEM((rows, width), bf16),
            pltpu.VMEM((rows, 2 * HD), jnp.float32),
            pltpu.SemaphoreType.DMA((len(parts) + (len(parts) + 3) * chunks,)),
        ],
        trig,
        *weights,
        *parts,
        *held,
        aliases={given + at: at for at in range(len(held))},
    )


class Step:
    def __init__(self, q, group, slots, same=None, merged=False):
        self.q, self.group, self.slots = q, group, slots
        self.same, self.merged = same, merged


class Chunk:
    def __init__(self, at, runs, share):
        self.at, self.runs, self.share = at, runs, share

    def places(self, core, axis, first, size):
        shape = (size, 1) if axis == 0 else (1, size)
        index = first + lax.broadcasted_iota(jnp.int32, shape, axis)
        result, begin = index, 0
        for which, offset, rows in self.runs:
            base = (core if which == 0 else 1 - core) * self.share + offset - begin
            inside = (index >= begin) & (index < begin + rows)
            result = jnp.where(inside, index + base, result)
            begin += rows
        return result


def attention_kernel(plan, q_chunks, k_chunks, group_parts, fresh, final, table, *refs):
    refs = list(refs)
    take = lambda n: [refs.pop(0) for _ in range(n)]
    count = len(q_chunks)
    qs = take(count)
    kv_parts = [take(n) for n in group_parts]
    take(2 * (count - len(fresh)))
    outs = take(len(final))
    states = [take(2) for _ in range(count)]
    kvs, staged = take(len(group_parts)), take(len(final))
    (semaphores,) = refs
    copies = Copies(semaphores)
    core = table[0]
    waits = {}
    for group, (parts, kv) in enumerate(zip(kv_parts, kvs)):
        each = kv.shape[0] // len(parts)
        waits[group] = [
            copies.start(part, kv.at[pl.ds(slot * each, each)])
            for slot, part in enumerate(parts)
        ]

    def ready(group):
        for copy in waits.pop(group, []):
            copy.wait()

    def attend(q, keys_values, begin, visible=None, bias=None):
        q_ref, (peak, acc) = qs[q], states[q]
        heads = q_ref.shape[0]
        keys = keys_values[:, :HD]
        values = keys_values[:, HD:].T
        values = jnp.concatenate([values, jnp.ones((ONES, keys.shape[0]), values.dtype)], axis=0)
        tiles, tile = acc.shape[0], acc.shape[2] // heads
        scores, tops, weights = [], [], []
        for at in range(tiles):
            q_tile = q_ref[:, at * tile : (at + 1) * tile, :].reshape(heads * tile, HD)
            score = lax.dot_general(
                keys, q_tile, (((1,), (1,)), ((), ())), preferred_element_type=jnp.float32
            )
            if visible is not None:
                seen = jnp.concatenate([visible(at * tile, tile)] * heads, axis=1)
                score = jnp.where(seen, score, HIDDEN)
            if bias is not None:
                score = score + bias
            scores.append(score)
        for at in range(tiles):
            top = jnp.max(scores[at], axis=0, keepdims=True)
            if not begin:
                top = jnp.maximum(peak[at, 0:1, :], top)
            tops.append(top)
            weights.append(jnp.exp2((scores[at] - top).astype(jnp.bfloat16)))
        for at in range(tiles):
            summed = jnp.dot(values, weights[at], preferred_element_type=jnp.float32)
            if not begin:
                summed = summed + acc[at] * jnp.exp2(peak[at, 0:1, :] - tops[at])
            acc[at] = summed
            peak[at] = jnp.broadcast_to(tops[at], peak.shape[1:])

    begun = set(range(count)) - set(fresh)
    for step in plan:
        q, group, kv = step.q, step.group, kvs[step.group]
        q_chunk, k_chunk = q_chunks[q], k_chunks[group]
        if step.same is not None:
            keys_at = k_chunk.places(core, 0, 0, kv.shape[1])
            visible = lambda first, tile: keys_at <= q_chunk.places(core, 1, first, tile)
            own = kv_parts[group][0]
            attend(q, own[step.same], q not in begun, visible=visible)
            begun.add(q)
        start = table[q_chunk.at]
        slots = step.slots
        if not slots:
            continue
        ready(group)
        if step.merged:
            shown = [table[k_chunk.at + slot] < start for slot in slots]

            @pl.when(functools.reduce(jnp.logical_or, shown))
            def _():
                rows = kv.shape[1]
                bias = [
                    jnp.where(see, 0.0, HIDDEN) * jnp.ones((rows, 1), jnp.float32)
                    for see in shown
                ]
                keys_values = kv[slots[0] : slots[-1] + 1].reshape(len(slots) * rows, 2 * HD)
                attend(q, keys_values, False, bias=jnp.concatenate(bias, axis=0))

        else:

            def one(slot, carry):
                @pl.when(table[k_chunk.at + slot] < start)
                def _():
                    attend(q, kv[slot], False)

                return carry

            lax.fori_loop(slots[0], slots[-1] + 1, one, 0)

    for group in list(waits):
        ready(group)
    stores = []
    for out, stage, order in zip(outs, staged, final):
        put = 0
        for q in order:
            acc, heads = states[q][1], qs[q].shape[0]
            tile = acc.shape[2] // heads
            for at in range(acc.shape[0]):
                rows = acc[at, :HD, :] / acc[at, HD : HD + 1, :]
                rows = rows.T.astype(jnp.bfloat16)
                for head in range(heads):
                    stage[put : put + tile, head * HD : (head + 1) * HD] = rows[
                        head * tile : (head + 1) * tile
                    ]
                put += tile
        stores.append(copies.start(stage, out))
    for copy in stores:
        copy.wait()


def attention(plan, table, qs, q_chunks, groups, k_chunks, state, final=()):
    fresh = [at for at, held in enumerate(state) if held is None]
    shapes = []
    for q in qs:
        heads, rows, _ = q.shape
        tile = min(rows, 128)
        shapes += [(rows // tile, deep, heads * tile) for deep in (8, HD + ONES)]
    width = qs[0].shape[0] * HD
    sums = [sum(qs[q].shape[1] for q in order) for order in final]
    outs = [((rows, width), jnp.bfloat16, HBM) for rows in sums]
    scratch = []
    for parts in groups:
        slots = sum(part.shape[0] for part in parts)
        scratch.append(pltpu.VMEM((slots,) + parts[0].shape[1:], jnp.bfloat16))
    scratch += [pltpu.VMEM((rows, width), jnp.bfloat16) for rows in sums]
    parts = [part for parts in groups for part in parts]
    sizes = [len(parts) for parts in groups]
    inputs, aliases = [table, *qs, *parts], {}
    for at, pair in enumerate(state):
        for half, array in enumerate(pair or ()):
            aliases[len(inputs)] = len(outs) + 2 * at + half
            inputs.append(array)
    results = call(
        functools.partial(attention_kernel, plan, q_chunks, k_chunks, sizes, fresh, final),
        "attention",
        10,
        [SMEM] + [VMEM] * (len(inputs) - 1),
        outs + [(shape, jnp.float32, VMEM) for shape in shapes],
        scratch + [pltpu.SemaphoreType.DMA((len(parts) + len(outs),))],
        *inputs,
        aliases=aliases,
    )
    if final:
        return results[: len(final)]
    return [tuple(results[2 * at : 2 * at + 2]) for at in range(len(qs))]


def cut_kernel(sizes, at, table, weights, *refs):
    outs, (held, semaphores) = refs[: len(sizes)], refs[len(sizes) :]
    copies = Copies(semaphores)
    half = sum(sizes)
    first = pl.multiple_of(table[at] * half, half)
    ins, put = [], 0
    for size in sizes:
        target = held.at[pl.ds(put, size)]
        ins.append((copies.start(weights.at[pl.ds(first + put, size)], target), target))
        put += size
    stores = []
    for (copy, piece), out in zip(ins, outs):
        copy.wait()
        stores.append(copies.start(piece, out))
    for copy in stores:
        copy.wait()


def cut(table, at, weights, sizes):
    depth, width = weights.shape
    return call(
        functools.partial(cut_kernel, sizes, at),
        "cut_weights",
        4,
        [SMEM, HBM],
        [((size, width), weights.dtype, HBM) for size in sizes],
        [
            pltpu.VMEM((depth // 2, width), weights.dtype),
            pltpu.SemaphoreType.DMA((2 * len(sizes),)),
        ],
        table,
        weights,
    )


def near_kernel(chunks, left_hbm, weights_hbm, out, left, weights, semaphores):
    copies = Copies(semaphores)
    step = out.shape[1] // chunks
    first = copies.start(left_hbm, left)
    lanes = [pl.ds(chunk * step, step) for chunk in range(chunks)]
    waits = [copies.start(weights_hbm.at[:, at], weights.at[:, at]) for at in lanes]
    first.wait()
    for at, copy in zip(lanes, waits):
        copy.wait()
        out[:, at] = jnp.dot(left[...], weights[:, at], preferred_element_type=jnp.float32)


def output_near(left, weights, chunks=6):
    (rows, columns), width = left.shape, weights.shape[1]
    return call(
        functools.partial(near_kernel, chunks),
        "output_near",
        8,
        [HBM] * 2,
        [((rows, width), jnp.float32, VMEM)],
        [
            pltpu.VMEM(left.shape, left.dtype),
            pltpu.VMEM(weights.shape, weights.dtype),
            pltpu.SemaphoreType.DMA((1 + chunks,)),
        ],
        left,
        weights,
    )[0]


def send_kernel(at, chunks, table, left_hbm, near, *refs):
    count = len(refs) - 5
    pieces, (out, weights, left, staged, semaphores) = refs[:count], refs[count:]
    copies = Copies(semaphores)
    depth, width = weights.shape
    step = width // chunks
    first = copies.start(left_hbm, left)
    waits, put = [], 0
    for index, piece in enumerate(pieces):
        half = table[at] if index < count // 2 else 1 - table[at]
        row = pl.multiple_of(half * (depth // 2) + put % (depth // 2), 16)
        waits.append(copies.start(piece, weights.at[pl.ds(row, piece.shape[0])]))
        put += piece.shape[0]
    for copy in waits:
        copy.wait()
    first.wait()
    half = left.shape[0] // 2
    stores = []
    for chunk in range(chunks):
        span = pl.ds(chunk * step, step)
        staged[:, span] = (
            near[half:, span]
            + jnp.dot(left[half:, :], weights[:, span], preferred_element_type=jnp.float32)
        ).astype(jnp.bfloat16)
        stores.append(copies.start(staged.at[:, span], out.at[:, span]))
    for copy in stores:
        copy.wait()


def output_send(table, at, left, near, pieces, chunks=6):
    (rows, width), columns = near.shape, left.shape[1]
    half, bf16 = (rows // 2, width), jnp.bfloat16
    return call(
        functools.partial(send_kernel, at, chunks),
        "output_send",
        8,
        [SMEM, HBM, VMEM] + [HBM] * len(pieces),
        [(half, bf16, HBM), ((columns, width), bf16, VMEM)],
        [
            pltpu.VMEM(left.shape, bf16),
            pltpu.VMEM(half, bf16),
            pltpu.SemaphoreType.DMA((1 + len(pieces) + chunks,)),
        ],
        table,
        left,
        near,
        *pieces,
    )


def keep_kernel(chunks, left_hbm, hidden, near, weights, out, held, left, semaphores):
    copies = Copies(semaphores)
    first, late = copies.start(left_hbm, left), copies.start(hidden, held)
    first.wait()
    half, step = left.shape[0] // 2, out.shape[1] // chunks
    for chunk in range(chunks):
        span = pl.ds(chunk * step, step)
        out[:, span] = near[:half, span] + jnp.dot(
            left[:half, :], weights[:, span], preferred_element_type=jnp.float32
        )
    late.wait()


def output_keep(left, hidden, near, weights, chunks=6):
    rows, width = near.shape
    return call(
        functools.partial(keep_kernel, chunks),
        "output_keep",
        4,
        [HBM, HBM, VMEM, VMEM],
        [((rows // 2, width), jnp.float32, VMEM), (hidden.shape, hidden.dtype, VMEM)],
        [pltpu.VMEM(left.shape, jnp.bfloat16), pltpu.SemaphoreType.DMA((2,))],
        left,
        hidden,
        near,
        weights,
    )


def final_kernel(chunks, received, hidden, kept, gain, out, other, staged, gains, semaphores):
    copies = Copies(semaphores)
    width = hidden.shape[1]
    step = width // chunks
    lanes = [pl.ds(chunk * step, step) for chunk in range(chunks)]
    waits = [copies.start(received.at[:, span], other.at[:, span]) for span in lanes]
    late = copies.start(gain, gains)
    square = jnp.zeros((hidden.shape[0], 128), jnp.float32)
    for span, copy in zip(lanes, waits):
        copy.wait()
        total = kept[:, span] + other[:, span].astype(jnp.float32)
        for lane in range(0, step, 128):
            part = total[:, lane : lane + 128]
            square = square + part * part
    mean = jnp.sum(square, axis=1, keepdims=True) / width
    scale = lax.rsqrt(mean + EPS)
    late.wait()
    row = gains[...].reshape(1, width)
    stores = []
    for chunk, span in enumerate(lanes):
        total = kept[:, span] + other[:, span].astype(jnp.float32)
        normed = total * scale * row[:, chunk * step : (chunk + 1) * step]
        staged[:, span] = (hidden[:, span].astype(jnp.float32) + normed).astype(jnp.bfloat16)
        stores.append(copies.start(staged.at[:, span], out.at[:, span]))
    for store in stores:
        store.wait()


def output(received, hidden, kept, gain, chunks=6):
    rows, width = hidden.shape
    bf16 = jnp.bfloat16
    return call(
        functools.partial(final_kernel, chunks),
        "output_norm",
        8,
        [HBM, VMEM, VMEM, HBM],
        [((rows, width), bf16, HBM)],
        [
            pltpu.VMEM((rows, width), bf16),
            pltpu.VMEM((rows, width), bf16),
            pltpu.VMEM((width,), jnp.float32),
            pltpu.SemaphoreType.DMA((1 + 2 * chunks,)),
        ],
        received,
        hidden,
        kept,
        gain,
    )[0]


def rotary_table(positions):
    half = HD // 2
    frequency = jnp.power(
        jnp.float32(10000.0), -jnp.arange(half, dtype=jnp.float32) * (2.0 / HD)
    )
    angles = positions.astype(jnp.float32)[:, None] * frequency[None, :]
    cos, sin = jnp.cos(angles), jnp.sin(angles)
    return jnp.concatenate([cos, cos, -sin, sin], axis=1)


def lookup(block_of, index):
    ids = jnp.arange(block_of.shape[0], dtype=jnp.int32)
    return jnp.sum(jnp.where(index[..., None] == ids, block_of, 0), axis=-1)


def flipped(array, axis, bit):
    size = lax.axis_size(axis)
    return lax.ppermute(array, axis, [(i, i ^ bit) for i in range(size)])


def along_line(array):
    size = lax.axis_size("seq")
    parts = [array[None]]
    for by in range(1, size):
        part = lax.ppermute(array, "seq", [(i, (i + by) % size) for i in range(size)])
        parts.append(Came(part[None]))
    return parts


def along_ring(array, beside):
    size = lax.axis_size("seq")
    parts, part = [array[None]], array
    for step in range(1, size):
        if step == size - 1:
            part = after(part, beside)
        part = lax.ppermute(part, "seq", [(i, (i + 1) % size) for i in range(size)])
        parts.append(Came(part[None]))
    return parts


def came(parts):
    return [part.array for part in parts if isinstance(part, Came)]


def after(array, *others):
    return lax.optimization_barrier((array, *others))[0]


def two_chips(hidden, pre_gain, post_gain, wq, wk, wv, w_out, block_of):
    rows = hidden.shape[0]
    block_rows = 2 * rows
    lines, tp = lax.axis_size("seq"), lax.axis_index("tp")
    seq, group = lax.axis_index("seq"), lax.axis_index("groups")
    chip, core = tp // 2, tp % 2

    line = (seq - jnp.arange(lines, dtype=jnp.int32)) % lines
    near_starts = lookup(block_of, 2 * line + chip) * block_rows
    far_starts = lookup(block_of, 2 * line + 1 - chip) * block_rows
    table = jnp.concatenate([jnp.stack([core, group]).astype(jnp.int32), near_starts, far_starts])
    group_at, near_at, far_at = 1, 2, 2 + lines
    run = jnp.arange(rows, dtype=jnp.int32)
    place = jnp.concatenate([core * rows + run, (1 - core) * rows + run])
    trig = rotary_table(jnp.concatenate([near_starts[0] + place, far_starts[0] + place]))
    runs = [(0, 0, rows), (1, 0, rows)]
    near_chunk, far_chunk = Chunk(near_at, runs, rows), Chunk(far_at, runs, rows)
    others, everyone = list(range(1, lines)), list(range(lines))

    half = rows // 2
    own = [norm(hidden, pre_gain, at * half, [half])[0] for at in range(2)]
    away = [flipped(part, "tp", 2) for part in own]
    partner = [Came(flipped(part, "tp", 1)) for part in own]

    weights = (wq, wk, wv)
    places = [0, half, rows, rows + half]
    q_near, kv_near = qkv([*own, *partner], places, block_rows, weights, trig, 0)
    near = along_line(kv_near)
    w_cut = cut(table, group_at, after(w_out, kv_near), [w_out.shape[0] // 8] * 4)
    q_near = after(q_near, *w_cut)
    (near_state,) = attention(
        [Step(0, 0, others, same=0)], table, [q_near], [near_chunk], [near], [near_chunk], [None]
    )

    away[0] = after(away[0], *near_state)
    quarter = half // 2
    swapped = [flipped(away[0][at : at + quarter], "tp", 1) for at in (0, quarter)]
    held = qkv(
        [Came(away[0]), *[Came(part) for part in swapped]],
        [0, rows, rows + quarter],
        block_rows,
        weights,
        trig,
        block_rows,
    )
    away[1] = after(away[1], *held)
    held = qkv(
        [Came(away[1]), Came(flipped(away[1], "tp", 1))],
        [half, rows + half],
        block_rows,
        weights,
        trig,
        block_rows,
        held,
    )
    q_far, kv_far = held

    fetched = lambda piece, *others: flipped(after(piece, *others), "tp", 2)
    swap = lambda array: flipped(array, "groups", 1)
    w_far = [fetched(piece, away[1]) for piece in w_cut[:2]]
    w_far[0] = after(w_far[0], kv_far)
    w_other = [swap(w_far[0])]
    far = along_ring(kv_far, w_other[0])
    w_far[1] = after(w_far[1], came(far)[0])
    w_far += [fetched(piece, before) for piece, before in zip(w_cut[2:], w_far[:2])]
    w_other.append(swap(w_far[1]))

    near_state, far_state = attention(
        [Step(1, 1, [], same=0), Step(1, 0, everyone), Step(0, 1, [0])],
        table,
        [q_near, q_far],
        [near_chunk, far_chunk],
        [near, far[:1]],
        [near_chunk, far_chunk],
        [near_state, None],
    )
    w_far[2] = after(w_far[2], *far_state)
    w_other.append(swap(w_far[2]))
    attended, gone = attention(
        [Step(1, 0, others), Step(0, 0, others)],
        table,
        [q_near, q_far],
        [near_chunk, far_chunk],
        [far],
        [far_chunk],
        [near_state, far_state],
        final=[[0], [1]],
    )
    gone = flipped(gone, "tp", 2)
    near_sum = output_near(attended, w_out)
    w_other.append(swap(after(w_far[3], attended, w_other[1])))
    pieces = [Came(piece) for piece in w_far + w_other]
    sent, w_laid = output_send(table, group_at, Came(gone), near_sum, pieces)
    received = flipped(sent, "tp", 1)
    kept, held = output_keep(Came(gone), hidden, near_sum, w_laid)
    return output(Came(received), held, kept, post_gain)


def any_count(hidden, pre_gain, post_gain, wq, wk, wv, w_out, block_of):
    rows = hidden.shape[0]
    lines = lax.axis_size("seq")
    line = (lax.axis_index("seq") - jnp.arange(lines, dtype=jnp.int32)) % lines
    block = (2 * line[:, None] + jnp.arange(2, dtype=jnp.int32)).reshape(-1)
    block_rows = rows * lax.axis_size("tp") // 2
    starts = lookup(block_of, block) * block_rows
    table = jnp.concatenate([jnp.zeros(2, jnp.int32), starts])
    normed = norm(hidden, pre_gain, 0, [rows], 1)[0]
    normed = lax.all_gather(normed, "tp", axis=0, tiled=True)
    place = jnp.arange(block_rows, dtype=jnp.int32)
    trig = rotary_table((starts[:2, None] + place).reshape(-1))
    qs, keys_values, weights = [], [], (wq, wk, wv)
    for at in range(2):
        first = at * block_rows
        rows_here = [normed[first : first + block_rows]]
        q, kv = qkv(rows_here, [0], block_rows, weights, trig, first)
        qs.append(q)
        keys_values.append(kv)
    kv = lax.all_gather(jnp.stack(keys_values), "seq")[line].reshape(-1, block_rows, 2 * HD)
    rest = list(range(2, 2 * lines))
    runs = [(0, 0, block_rows)]
    attended = attention(
        [Step(0, 0, [1], same=0), Step(1, 0, [0], same=1), Step(0, 0, rest), Step(1, 0, rest)],
        table,
        qs,
        [Chunk(2, runs, 0), Chunk(3, runs, 0)],
        [[kv]],
        [Chunk(2, runs, 0)],
        [None, None],
        final=[[0, 1]],
    )[0]
    partial = jnp.dot(attended, w_out, preferred_element_type=jnp.float32)
    summed = lax.psum_scatter(
        partial.astype(jnp.bfloat16), "tp", scatter_dimension=0, tiled=True
    ).astype(jnp.float32)
    mean = jnp.mean(summed * summed, axis=-1, keepdims=True)
    projected = summed * lax.rsqrt(mean + EPS) * post_gain
    return (hidden.astype(jnp.float32) + projected).astype(jnp.bfloat16)


def solution(mesh):
    return jax.shard_map(
        two_chips if mesh.shape["tp"] == 4 else any_count,
        mesh=mesh,
        in_specs=(
            P(("groups", "seq", "tp"), None),
            P(),
            P(),
            P(None, "tp"),
            P(None, "tp"),
            P(None, "tp"),
            P("tp", None),
            P(),
        ),
        out_specs=P(("groups", "seq", "tp"), None),
        check_vma=False,
    )
```

```python
import functools
import math

import jax
import jax.numpy as jnp
from jax import lax
from jax.experimental import pallas as pl
from jax.experimental.pallas import tpu as pltpu
from jax.sharding import PartitionSpec as P

HD = 128
ATT_SCALAR = 144
EPS = 1e-6
MIB = 1024 * 1024
HIDDEN = -1e30
ONES = 16
COST = pl.CostEstimate(flops=1, bytes_accessed=1, transcendentals=0)

ANY = pl.BlockSpec(memory_space=pl.ANY)
HBM = pl.BlockSpec(memory_space=pltpu.HBM)
VMEM = pl.BlockSpec(memory_space=pltpu.VMEM)
SMEM = pl.BlockSpec(memory_space=pltpu.SMEM)


class Came:
    def __init__(self, array):
        self.array, self.shape = array, array.shape


def call(kernel, name, mib, in_specs, outs, scratch, *args, aliases=None):
    in_specs, pinned = list(in_specs), []
    for at, arg in enumerate(args):
        if isinstance(arg, Came):
            arg, in_specs[at] = arg.array, ANY
        elif in_specs[at] is not SMEM:
            arg = pltpu.with_memory_space_constraint(arg, in_specs[at].memory_space)
        pinned.append(arg)
    return pl.pallas_call(
        kernel,
        in_specs=in_specs,
        out_specs=[spec for _, _, spec in outs],
        out_shape=[spec.memory_space(shape, dtype) for shape, dtype, spec in outs],
        scratch_shapes=scratch,
        input_output_aliases=aliases or {},
        compiler_params=pltpu.CompilerParams(vmem_limit_bytes=mib * MIB),
        cost_estimate=COST,
        name=name,
    )(*pinned)


class Copies:
    def __init__(self, semaphores):
        self.semaphores, self.used = semaphores, 0

    def start(self, source, target):
        copy = pltpu.make_async_copy(source, target, self.semaphores.at[self.used])
        self.used += 1
        copy.start()
        return copy


def norm_kernel(cuts, pieces, first, hidden, gain, *refs):
    parts, (gains, rows, staged, semaphores) = refs[: len(cuts)], refs[len(cuts) :]
    copies = Copies(semaphores)
    count, width = rows.shape
    step = count // pieces
    spans = [pl.ds(at * step, step) for at in range(pieces)]
    ins = [
        copies.start(hidden.at[pl.ds(first + at * step, step)], rows.at[span])
        for at, span in enumerate(spans)
    ]
    copies.start(gain, gains).wait()
    scale = gains[...].reshape(1, width)
    outs = []
    for at, span in enumerate(spans):
        ins[at].wait()
        x = rows[span, :].astype(jnp.float32)
        square = x * x
        folded = square[:, :128]
        for lane in range(128, width, 128):
            folded = folded + square[:, lane : lane + 128]
        mean = jnp.sum(folded, axis=1, keepdims=True) / width
        staged[span, :] = (x * lax.rsqrt(mean + EPS) * scale).astype(jnp.bfloat16)
        begin = 0
        for cut, part in zip(cuts, parts):
            if begin <= at * step < begin + cut:
                inside = pl.ds(at * step - begin, step)
                outs.append(copies.start(staged.at[span], part.at[inside]))
            begin += cut
    for copy in outs:
        copy.wait()


def norm(hidden, gain, first, cuts, pieces=3):
    rows, width = sum(cuts), hidden.shape[1]
    bf16 = jnp.bfloat16
    return call(
        functools.partial(norm_kernel, cuts, pieces, first),
        "norm_rows",
        8,
        [HBM, HBM],
        [((cut, width), bf16, HBM) for cut in cuts],
        [
            pltpu.VMEM((width,), jnp.float32),
            pltpu.VMEM((rows, width), bf16),
            pltpu.VMEM((rows, width), bf16),
            pltpu.SemaphoreType.DMA((1 + 2 * pieces,)),
        ],
        hidden,
        gain,
    )


def qkv_kernel(places, first, chunks, held, trig, wq, wk, wv, *refs):
    parts, refs = refs[: len(places)], refs[len(places) + 2 * held :]
    q, kv, weights, rows, angles, semaphores = refs
    copies, waits = Copies(semaphores), []
    depth = weights.shape[0] // chunks
    for chunk in range(chunks):
        span, put, column, here = pl.ds(chunk * depth, depth), 0, 0, []
        for part in parts:
            target = rows.at[pl.ds(put, part.shape[0]), span]
            here.append(copies.start(part.at[:, span], target))
            put += part.shape[0]
        for weight in (wq, wk, wv):
            target = weights.at[span, pl.ds(column, weight.shape[1])]
            here.append(copies.start(weight.at[span], target))
            column += weight.shape[1]
        waits.append(here)
    late, put = [], 0
    for part, place in zip(parts, places):
        count = part.shape[0]
        source = trig.at[pl.ds(first + place, count)]
        late.append(copies.start(source, angles.at[pl.ds(put, count)]))
        put += count
    product = None
    for chunk, here in enumerate(waits):
        for copy in here:
            copy.wait()
        span = pl.ds(chunk * depth, depth)
        term = jnp.dot(rows[:, span], weights[span, :], preferred_element_type=jnp.float32)
        product = term if product is None else product + term
    for copy in late:
        copy.wait()
    cos, sin = angles[:, :HD], angles[:, HD:]
    queries = product.shape[1] - 2 * HD

    def rotated(at):
        y = product[:, at : at + HD]
        return y * cos + pltpu.roll(y, HD // 2, 1) * sin

    factor = ATT_SCALAR ** (-0.5) * math.log2(math.e)
    keys = rotated(queries).astype(jnp.bfloat16)
    values = product[:, queries + HD :].astype(jnp.bfloat16)
    heads = [(rotated(at) * factor).astype(jnp.bfloat16) for at in range(0, queries, HD)]
    put = 0
    for part, place in zip(parts, places):
        count = part.shape[0]
        kv[place : place + count, :HD] = keys[put : put + count]
        kv[place : place + count, HD:] = values[put : put + count]
        for head, rotated_head in enumerate(heads):
            q[head, place : place + count, :] = rotated_head[put : put + count]
        put += count


def qkv(parts, places, total, weights, trig, first, held=(), chunks=4):
    rows, width = sum(part.shape[0] for part in parts), parts[0].shape[1]
    columns = sum(weight.shape[1] for weight in weights)
    heads, bf16 = weights[0].shape[1] // HD, jnp.bfloat16
    given = 4 + len(parts)
    return call(
        functools.partial(qkv_kernel, places, first, chunks, bool(held)),
        "qkv",
        14,
        [HBM] * given + [VMEM] * len(held),
        [((heads, total, HD), bf16, VMEM), ((total, 2 * HD), bf16, VMEM)],
        [
            pltpu.VMEM((width, columns), bf16),
            pltpu.VMEM((rows, width), bf16),
            pltpu.VMEM((rows, 2 * HD), jnp.float32),
            pltpu.SemaphoreType.DMA((len(parts) + (len(parts) + 3) * chunks,)),
        ],
        trig,
        *weights,
        *parts,
        *held,
        aliases={given + at: at for at in range(len(held))},
    )


class Step:
    def __init__(self, q, group, slots, same=None, merged=False):
        self.q, self.group, self.slots = q, group, slots
        self.same, self.merged = same, merged


class Chunk:
    def __init__(self, at, runs, share):
        self.at, self.runs, self.share = at, runs, share

    def places(self, core, axis, first, size):
        shape = (size, 1) if axis == 0 else (1, size)
        index = first + lax.broadcasted_iota(jnp.int32, shape, axis)
        result, begin = index, 0
        for which, offset, rows in self.runs:
            base = (core if which == 0 else 1 - core) * self.share + offset - begin
            inside = (index >= begin) & (index < begin + rows)
            result = jnp.where(inside, index + base, result)
            begin += rows
        return result


def attention_kernel(plan, q_chunks, k_chunks, group_parts, fresh, final, table, *refs):
    refs = list(refs)
    take = lambda n: [refs.pop(0) for _ in range(n)]
    count = len(q_chunks)
    qs = take(count)
    kv_parts = [take(n) for n in group_parts]
    take(2 * (count - len(fresh)))
    outs = take(len(final))
    states = [take(2) for _ in range(count)]
    kvs, staged = take(len(group_parts)), take(len(final))
    (semaphores,) = refs
    copies = Copies(semaphores)
    core = table[0]
    waits = {}
    for group, (parts, kv) in enumerate(zip(kv_parts, kvs)):
        each = kv.shape[0] // len(parts)
        waits[group] = [
            copies.start(part, kv.at[pl.ds(slot * each, each)])
            for slot, part in enumerate(parts)
        ]

    def ready(group):
        for copy in waits.pop(group, []):
            copy.wait()

    def attend(q, keys_values, begin, visible=None, bias=None):
        q_ref, (peak, acc) = qs[q], states[q]
        heads = q_ref.shape[0]
        keys = keys_values[:, :HD]
        values = keys_values[:, HD:].T
        values = jnp.concatenate([values, jnp.ones((ONES, keys.shape[0]), values.dtype)], axis=0)
        tiles, tile = acc.shape[0], acc.shape[2] // heads
        scores, tops, weights = [], [], []
        for at in range(tiles):
            q_tile = q_ref[:, at * tile : (at + 1) * tile, :].reshape(heads * tile, HD)
            score = lax.dot_general(
                keys, q_tile, (((1,), (1,)), ((), ())), preferred_element_type=jnp.float32
            )
            if visible is not None:
                seen = jnp.concatenate([visible(at * tile, tile)] * heads, axis=1)
                score = jnp.where(seen, score, HIDDEN)
            if bias is not None:
                score = score + bias
            scores.append(score)
        for at in range(tiles):
            top = jnp.max(scores[at], axis=0, keepdims=True)
            if not begin:
                top = jnp.maximum(peak[at, 0:1, :], top)
            tops.append(top)
            weights.append(jnp.exp2((scores[at] - top).astype(jnp.bfloat16)))
        for at in range(tiles):
            summed = jnp.dot(values, weights[at], preferred_element_type=jnp.float32)
            if not begin:
                summed = summed + acc[at] * jnp.exp2(peak[at, 0:1, :] - tops[at])
            acc[at] = summed
            peak[at] = jnp.broadcast_to(tops[at], peak.shape[1:])

    begun = set(range(count)) - set(fresh)
    for step in plan:
        q, group, kv = step.q, step.group, kvs[step.group]
        q_chunk, k_chunk = q_chunks[q], k_chunks[group]
        if step.same is not None:
            keys_at = k_chunk.places(core, 0, 0, kv.shape[1])
            visible = lambda first, tile: keys_at <= q_chunk.places(core, 1, first, tile)
            own = kv_parts[group][0]
            attend(q, own[step.same], q not in begun, visible=visible)
            begun.add(q)
        start = table[q_chunk.at]
        slots = step.slots
        if not slots:
            continue
        ready(group)
        if step.merged:
            shown = [table[k_chunk.at + slot] < start for slot in slots]

            @pl.when(functools.reduce(jnp.logical_or, shown))
            def _():
                rows = kv.shape[1]
                bias = [
                    jnp.where(see, 0.0, HIDDEN) * jnp.ones((rows, 1), jnp.float32)
                    for see in shown
                ]
                keys_values = kv[slots[0] : slots[-1] + 1].reshape(len(slots) * rows, 2 * HD)
                attend(q, keys_values, False, bias=jnp.concatenate(bias, axis=0))

        else:

            def one(slot, carry):
                @pl.when(table[k_chunk.at + slot] < start)
                def _():
                    attend(q, kv[slot], False)

                return carry

            lax.fori_loop(slots[0], slots[-1] + 1, one, 0)

    for group in list(waits):
        ready(group)
    stores = []
    for out, stage, order in zip(outs, staged, final):
        put = 0
        for q in order:
            acc, heads = states[q][1], qs[q].shape[0]
            tile = acc.shape[2] // heads
            for at in range(acc.shape[0]):
                rows = acc[at, :HD, :] / acc[at, HD : HD + 1, :]
                rows = rows.T.astype(jnp.bfloat16)
                for head in range(heads):
                    stage[put : put + tile, head * HD : (head + 1) * HD] = rows[
                        head * tile : (head + 1) * tile
                    ]
                put += tile
        stores.append(copies.start(stage, out))
    for copy in stores:
        copy.wait()


def attention(plan, table, qs, q_chunks, groups, k_chunks, state, final=()):
    fresh = [at for at, held in enumerate(state) if held is None]
    shapes = []
    for q in qs:
        heads, rows, _ = q.shape
        tile = min(rows, 128)
        shapes += [(rows // tile, deep, heads * tile) for deep in (8, HD + ONES)]
    width = qs[0].shape[0] * HD
    sums = [sum(qs[q].shape[1] for q in order) for order in final]
    outs = [((rows, width), jnp.bfloat16, HBM) for rows in sums]
    scratch = []
    for parts in groups:
        slots = sum(part.shape[0] for part in parts)
        scratch.append(pltpu.VMEM((slots,) + parts[0].shape[1:], jnp.bfloat16))
    scratch += [pltpu.VMEM((rows, width), jnp.bfloat16) for rows in sums]
    parts = [part for parts in groups for part in parts]
    sizes = [len(parts) for parts in groups]
    inputs, aliases = [table, *qs, *parts], {}
    for at, pair in enumerate(state):
        for half, array in enumerate(pair or ()):
            aliases[len(inputs)] = len(outs) + 2 * at + half
            inputs.append(array)
    results = call(
        functools.partial(attention_kernel, plan, q_chunks, k_chunks, sizes, fresh, final),
        "attention",
        10,
        [SMEM] + [VMEM] * (len(inputs) - 1),
        outs + [(shape, jnp.float32, VMEM) for shape in shapes],
        scratch + [pltpu.SemaphoreType.DMA((len(parts) + len(outs),))],
        *inputs,
        aliases=aliases,
    )
    if final:
        return results[: len(final)]
    return [tuple(results[2 * at : 2 * at + 2]) for at in range(len(qs))]


def cut_kernel(sizes, at, table, weights, *refs):
    outs, (held, semaphores) = refs[: len(sizes) + 1], refs[len(sizes) + 1 :]
    copies = Copies(semaphores)
    half = weights.shape[0] // 2
    first = pl.multiple_of(table[at] * half, half)
    split = sum(sizes)
    rest = half - split
    ins, put = [], 0
    for size in sizes:
        target = held.at[pl.ds(put, size)]
        ins.append((copies.start(weights.at[pl.ds(first + put, size)], target), target))
        put += size
    both = held.at[pl.ds(split, 2 * rest)]
    for side in range(2):
        source = weights.at[pl.ds(side * half + split, rest)]
        copy = copies.start(source, held.at[pl.ds(split + side * rest, rest)])
        ins.append((copy, both if side else None))
    outs, stores = list(outs), []
    for copy, piece in ins:
        copy.wait()
        if piece is not None:
            stores.append(copies.start(piece, outs.pop(0)))
    for copy in stores:
        copy.wait()


def cut(table, at, weights, sizes):
    depth, width = weights.shape
    rest = depth // 2 - sum(sizes)
    return call(
        functools.partial(cut_kernel, sizes, at),
        "cut_weights",
        4,
        [SMEM, HBM],
        [((size, width), weights.dtype, HBM) for size in [*sizes, 2 * rest]],
        [
            pltpu.VMEM((depth // 2 + rest, width), weights.dtype),
            pltpu.SemaphoreType.DMA((2 * len(sizes) + 3,)),
        ],
        table,
        weights,
    )


def near_kernel(chunks, left_hbm, weights_hbm, out, left, weights, semaphores):
    copies = Copies(semaphores)
    step = out.shape[1] // chunks
    first = copies.start(left_hbm, left)
    lanes = [pl.ds(chunk * step, step) for chunk in range(chunks)]
    waits = [copies.start(weights_hbm.at[:, at], weights.at[:, at]) for at in lanes]
    first.wait()
    for at, copy in zip(lanes, waits):
        copy.wait()
        out[:, at] = jnp.dot(left[...], weights[:, at], preferred_element_type=jnp.float32)


def output_near(left, weights, chunks=6):
    (rows, columns), width = left.shape, weights.shape[1]
    return call(
        functools.partial(near_kernel, chunks),
        "output_near",
        8,
        [HBM] * 2,
        [((rows, width), jnp.float32, VMEM)],
        [
            pltpu.VMEM(left.shape, left.dtype),
            pltpu.VMEM(weights.shape, weights.dtype),
            pltpu.SemaphoreType.DMA((1 + chunks,)),
        ],
        left,
        weights,
    )[0]


def send_kernel(at, splits, chunks, table, left_hbm, near, *refs):
    pieces, refs = refs[: 2 * splits + 1], refs[2 * splits + 1 :]
    out, weights, left, staged, semaphores = refs
    copies = Copies(semaphores)
    depth, width = weights.shape
    half, step = depth // 2, width // chunks
    first = copies.start(left_hbm, left)
    waits, put = [], 0
    for own, other in zip(pieces[:splits], pieces[splits:-1]):
        for piece, side in ((own, table[at]), (other, 1 - table[at])):
            row = pl.multiple_of(side * half + put, 16)
            waits.append(copies.start(piece, weights.at[pl.ds(row, piece.shape[0])]))
        put += own.shape[0]
    for side in range(2):
        source = pieces[-1].at[pl.ds(side * (half - put), half - put)]
        waits.append(copies.start(source, weights.at[pl.ds(side * half + put, half - put)]))
    for copy in waits:
        copy.wait()
    first.wait()
    half = left.shape[0] // 2
    stores = []
    for chunk in range(chunks):
        span = pl.ds(chunk * step, step)
        staged[:, span] = (
            near[half:, span]
            + jnp.dot(left[half:, :], weights[:, span], preferred_element_type=jnp.float32)
        ).astype(jnp.bfloat16)
        stores.append(copies.start(staged.at[:, span], out.at[:, span]))
    for copy in stores:
        copy.wait()


def output_send(table, at, left, near, pieces, chunks=6):
    (rows, width), columns = near.shape, left.shape[1]
    half, bf16 = (rows // 2, width), jnp.bfloat16
    return call(
        functools.partial(send_kernel, at, len(pieces) // 2, chunks),
        "output_send",
        8,
        [SMEM, HBM, VMEM] + [HBM] * len(pieces),
        [(half, bf16, HBM), ((columns, width), bf16, VMEM)],
        [
            pltpu.VMEM(left.shape, bf16),
            pltpu.VMEM(half, bf16),
            pltpu.SemaphoreType.DMA((2 + len(pieces) + chunks,)),
        ],
        table,
        left,
        near,
        *pieces,
    )


def keep_kernel(chunks, left_hbm, hidden, near, weights, out, held, left, semaphores):
    copies = Copies(semaphores)
    first, late = copies.start(left_hbm, left), copies.start(hidden, held)
    first.wait()
    half, step = left.shape[0] // 2, out.shape[1] // chunks
    for chunk in range(chunks):
        span = pl.ds(chunk * step, step)
        out[:, span] = near[:half, span] + jnp.dot(
            left[:half, :], weights[:, span], preferred_element_type=jnp.float32
        )
    late.wait()


def output_keep(left, hidden, near, weights, chunks=6):
    rows, width = near.shape
    return call(
        functools.partial(keep_kernel, chunks),
        "output_keep",
        4,
        [HBM, HBM, VMEM, VMEM],
        [((rows // 2, width), jnp.float32, VMEM), (hidden.shape, hidden.dtype, VMEM)],
        [pltpu.VMEM(left.shape, jnp.bfloat16), pltpu.SemaphoreType.DMA((2,))],
        left,
        hidden,
        near,
        weights,
    )


def final_kernel(chunks, received, hidden, kept, gain, out, other, staged, gains, semaphores):
    copies = Copies(semaphores)
    width = hidden.shape[1]
    step = width // chunks
    lanes = [pl.ds(chunk * step, step) for chunk in range(chunks)]
    waits = [copies.start(received.at[:, span], other.at[:, span]) for span in lanes]
    late = copies.start(gain, gains)
    square = jnp.zeros((hidden.shape[0], 128), jnp.float32)
    for span, copy in zip(lanes, waits):
        copy.wait()
        total = kept[:, span] + other[:, span].astype(jnp.float32)
        for lane in range(0, step, 128):
            part = total[:, lane : lane + 128]
            square = square + part * part
    mean = jnp.sum(square, axis=1, keepdims=True) / width
    scale = lax.rsqrt(mean + EPS)
    late.wait()
    row = gains[...].reshape(1, width)
    stores = []
    for chunk, span in enumerate(lanes):
        total = kept[:, span] + other[:, span].astype(jnp.float32)
        normed = total * scale * row[:, chunk * step : (chunk + 1) * step]
        staged[:, span] = (hidden[:, span].astype(jnp.float32) + normed).astype(jnp.bfloat16)
        stores.append(copies.start(staged.at[:, span], out.at[:, span]))
    for store in stores:
        store.wait()


def output(received, hidden, kept, gain, chunks=6):
    rows, width = hidden.shape
    bf16 = jnp.bfloat16
    return call(
        functools.partial(final_kernel, chunks),
        "output_norm",
        8,
        [HBM, VMEM, VMEM, HBM],
        [((rows, width), bf16, HBM)],
        [
            pltpu.VMEM((rows, width), bf16),
            pltpu.VMEM((rows, width), bf16),
            pltpu.VMEM((width,), jnp.float32),
            pltpu.SemaphoreType.DMA((1 + 2 * chunks,)),
        ],
        received,
        hidden,
        kept,
        gain,
    )[0]


def rotary_table(positions):
    half = HD // 2
    frequency = jnp.power(
        jnp.float32(10000.0), -jnp.arange(half, dtype=jnp.float32) * (2.0 / HD)
    )
    angles = positions.astype(jnp.float32)[:, None] * frequency[None, :]
    cos, sin = jnp.cos(angles), jnp.sin(angles)
    return jnp.concatenate([cos, cos, -sin, sin], axis=1)


def lookup(block_of, index):
    ids = jnp.arange(block_of.shape[0], dtype=jnp.int32)
    return jnp.sum(jnp.where(index[..., None] == ids, block_of, 0), axis=-1)


def flipped(array, axis, bit):
    size = lax.axis_size(axis)
    return lax.ppermute(array, axis, [(i, i ^ bit) for i in range(size)])


def along_line(array):
    size = lax.axis_size("seq")
    parts = [array[None]]
    for by in range(1, size):
        part = lax.ppermute(array, "seq", [(i, (i + by) % size) for i in range(size)])
        parts.append(Came(part[None]))
    return parts


def along_ring(array, beside):
    size = lax.axis_size("seq")
    parts, part = [array[None]], array
    for step in range(1, size):
        if step == size - 1:
            part = after(part, beside)
        part = lax.ppermute(part, "seq", [(i, (i + 1) % size) for i in range(size)])
        parts.append(Came(part[None]))
    return parts


def came(parts):
    return [part.array for part in parts if isinstance(part, Came)]


def after(array, *others):
    return lax.optimization_barrier((array, *others))[0]


def two_chips(hidden, pre_gain, post_gain, wq, wk, wv, w_out, block_of):
    rows = hidden.shape[0]
    block_rows = 2 * rows
    lines, tp = lax.axis_size("seq"), lax.axis_index("tp")
    seq, group = lax.axis_index("seq"), lax.axis_index("groups")
    chip, core = tp // 2, tp % 2

    line = (seq - jnp.arange(lines, dtype=jnp.int32)) % lines
    near_starts = lookup(block_of, 2 * line + chip) * block_rows
    far_starts = lookup(block_of, 2 * line + 1 - chip) * block_rows
    table = jnp.concatenate([jnp.stack([core, group]).astype(jnp.int32), near_starts, far_starts])
    group_at, near_at, far_at = 1, 2, 2 + lines
    run = jnp.arange(rows, dtype=jnp.int32)
    place = jnp.concatenate([core * rows + run, (1 - core) * rows + run])
    trig = rotary_table(jnp.concatenate([near_starts[0] + place, far_starts[0] + place]))
    runs = [(0, 0, rows), (1, 0, rows)]
    near_chunk, far_chunk = Chunk(near_at, runs, rows), Chunk(far_at, runs, rows)
    others, everyone = list(range(1, lines)), list(range(lines))

    half = rows // 2
    own = [norm(hidden, pre_gain, at * half, [half])[0] for at in range(2)]
    away = [flipped(part, "tp", 2) for part in own]
    partner = [Came(flipped(part, "tp", 1)) for part in own]

    weights = (wq, wk, wv)
    places = [0, half, rows, rows + half]
    q_near, kv_near = qkv([*own, *partner], places, block_rows, weights, trig, 0)
    near = along_line(kv_near)
    eighth = w_out.shape[0] // 8
    sizes = [eighth, eighth * 3 // 2, eighth]
    w_cut = cut(table, group_at, after(w_out, kv_near), sizes)
    q_near = after(q_near, *w_cut)
    (near_state,) = attention(
        [Step(0, 0, others, same=0)], table, [q_near], [near_chunk], [near], [near_chunk], [None]
    )

    away[0] = after(away[0], *near_state)
    quarter = half // 2
    swapped = [flipped(away[0][at : at + quarter], "tp", 1) for at in (0, quarter)]
    held = qkv(
        [Came(away[0]), *[Came(part) for part in swapped]],
        [0, rows, rows + quarter],
        block_rows,
        weights,
        trig,
        block_rows,
    )
    away[1] = after(away[1], *held)
    held = qkv(
        [Came(away[1]), Came(flipped(away[1], "tp", 1))],
        [half, rows + half],
        block_rows,
        weights,
        trig,
        block_rows,
        held,
    )
    q_far, kv_far = held

    fetched = lambda piece, *others: flipped(after(piece, *others), "tp", 2)
    swap = lambda array: flipped(array, "groups", 1)
    w_far = [fetched(piece, away[1]) for piece in w_cut[:2]]
    w_far[0] = after(w_far[0], kv_far)
    w_other = [swap(w_far[0])]
    far = along_ring(kv_far, w_other[0])
    w_far[1] = after(w_far[1], came(far)[0])
    w_far += [fetched(piece, before) for piece, before in zip(w_cut[2:], w_far[:2])]
    w_other.append(swap(w_far[1]))

    near_state, far_state = attention(
        [Step(1, 1, [], same=0), Step(1, 0, everyone), Step(0, 1, [0])],
        table,
        [q_near, q_far],
        [near_chunk, far_chunk],
        [near, far[:1]],
        [near_chunk, far_chunk],
        [near_state, None],
    )
    w_far[2] = after(w_far[2], *far_state)
    w_other.append(swap(w_far[2]))
    rest = [Step(0, 0, others)]
    (gone,) = attention(
        rest, table, [q_far], [far_chunk], [far], [far_chunk], [far_state], final=[[0]]
    )
    gone = flipped(gone, "tp", 2)
    (attended,) = attention(
        rest, table, [q_near], [near_chunk], [far], [far_chunk], [near_state], final=[[0]]
    )
    near_sum = output_near(attended, w_out)
    pieces = [Came(piece) for piece in w_far[:3] + w_other + w_far[3:]]
    sent, w_laid = output_send(table, group_at, Came(gone), near_sum, pieces)
    received = flipped(sent, "tp", 1)
    kept, held = output_keep(Came(gone), hidden, near_sum, w_laid)
    return output(Came(received), held, kept, post_gain)


def any_count(hidden, pre_gain, post_gain, wq, wk, wv, w_out, block_of):
    rows = hidden.shape[0]
    lines = lax.axis_size("seq")
    line = (lax.axis_index("seq") - jnp.arange(lines, dtype=jnp.int32)) % lines
    block = (2 * line[:, None] + jnp.arange(2, dtype=jnp.int32)).reshape(-1)
    block_rows = rows * lax.axis_size("tp") // 2
    starts = lookup(block_of, block) * block_rows
    table = jnp.concatenate([jnp.zeros(2, jnp.int32), starts])
    normed = norm(hidden, pre_gain, 0, [rows], 1)[0]
    normed = lax.all_gather(normed, "tp", axis=0, tiled=True)
    place = jnp.arange(block_rows, dtype=jnp.int32)
    trig = rotary_table((starts[:2, None] + place).reshape(-1))
    qs, keys_values, weights = [], [], (wq, wk, wv)
    for at in range(2):
        first = at * block_rows
        rows_here = [normed[first : first + block_rows]]
        q, kv = qkv(rows_here, [0], block_rows, weights, trig, first)
        qs.append(q)
        keys_values.append(kv)
    kv = lax.all_gather(jnp.stack(keys_values), "seq")[line].reshape(-1, block_rows, 2 * HD)
    rest = list(range(2, 2 * lines))
    runs = [(0, 0, block_rows)]
    attended = attention(
        [Step(0, 0, [1], same=0), Step(1, 0, [0], same=1), Step(0, 0, rest), Step(1, 0, rest)],
        table,
        qs,
        [Chunk(2, runs, 0), Chunk(3, runs, 0)],
        [[kv]],
        [Chunk(2, runs, 0)],
        [None, None],
        final=[[0, 1]],
    )[0]
    partial = jnp.dot(attended, w_out, preferred_element_type=jnp.float32)
    summed = lax.psum_scatter(
        partial.astype(jnp.bfloat16), "tp", scatter_dimension=0, tiled=True
    ).astype(jnp.float32)
    mean = jnp.mean(summed * summed, axis=-1, keepdims=True)
    projected = summed * lax.rsqrt(mean + EPS) * post_gain
    return (hidden.astype(jnp.float32) + projected).astype(jnp.bfloat16)


def solution(mesh):
    return jax.shard_map(
        two_chips if mesh.shape["tp"] == 4 else any_count,
        mesh=mesh,
        in_specs=(
            P(("groups", "seq", "tp"), None),
            P(),
            P(),
            P(None, "tp"),
            P(None, "tp"),
            P(None, "tp"),
            P("tp", None),
            P(),
        ),
        out_specs=P(("groups", "seq", "tp"), None),
        check_vma=False,
    )
```

```python
import functools
import math

import jax
import jax.numpy as jnp
from jax import lax
from jax.experimental import pallas as pl
from jax.experimental.pallas import tpu as pltpu
from jax.sharding import PartitionSpec as P

HD = 128
ATT_SCALAR = 144
EPS = 1e-6
MIB = 1024 * 1024
HIDDEN = -1e30
ONES = 16
COST = pl.CostEstimate(flops=1, bytes_accessed=1, transcendentals=0)

ANY = pl.BlockSpec(memory_space=pl.ANY)
HBM = pl.BlockSpec(memory_space=pltpu.HBM)
VMEM = pl.BlockSpec(memory_space=pltpu.VMEM)
SMEM = pl.BlockSpec(memory_space=pltpu.SMEM)


class Came:
    def __init__(self, array):
        self.array, self.shape = array, array.shape


def call(kernel, name, mib, in_specs, outs, scratch, *args, aliases=None):
    in_specs, pinned = list(in_specs), []
    for at, arg in enumerate(args):
        if isinstance(arg, Came):
            arg, in_specs[at] = arg.array, ANY
        elif in_specs[at] is not SMEM:
            arg = pltpu.with_memory_space_constraint(arg, in_specs[at].memory_space)
        pinned.append(arg)
    return pl.pallas_call(
        kernel,
        in_specs=in_specs,
        out_specs=[spec for _, _, spec in outs],
        out_shape=[spec.memory_space(shape, dtype) for shape, dtype, spec in outs],
        scratch_shapes=scratch,
        input_output_aliases=aliases or {},
        compiler_params=pltpu.CompilerParams(vmem_limit_bytes=mib * MIB),
        cost_estimate=COST,
        name=name,
    )(*pinned)


class Copies:
    def __init__(self, semaphores):
        self.semaphores, self.used = semaphores, 0

    def start(self, source, target):
        copy = pltpu.make_async_copy(source, target, self.semaphores.at[self.used])
        self.used += 1
        copy.start()
        return copy


def norm_kernel(cuts, pieces, first, hidden, gain, *refs):
    parts, (gains, rows, staged, semaphores) = refs[: len(cuts)], refs[len(cuts) :]
    copies = Copies(semaphores)
    count, width = rows.shape
    step = count // pieces
    spans = [pl.ds(at * step, step) for at in range(pieces)]
    ins = [
        copies.start(hidden.at[pl.ds(first + at * step, step)], rows.at[span])
        for at, span in enumerate(spans)
    ]
    copies.start(gain, gains).wait()
    scale = gains[...].reshape(1, width)
    outs = []
    for at, span in enumerate(spans):
        ins[at].wait()
        x = rows[span, :].astype(jnp.float32)
        square = x * x
        folded = square[:, :128]
        for lane in range(128, width, 128):
            folded = folded + square[:, lane : lane + 128]
        mean = jnp.sum(folded, axis=1, keepdims=True) / width
        staged[span, :] = (x * lax.rsqrt(mean + EPS) * scale).astype(jnp.bfloat16)
        begin = 0
        for cut, part in zip(cuts, parts):
            if begin <= at * step < begin + cut:
                inside = pl.ds(at * step - begin, step)
                outs.append(copies.start(staged.at[span], part.at[inside]))
            begin += cut
    for copy in outs:
        copy.wait()


def norm(hidden, gain, first, cuts, pieces=3):
    rows, width = sum(cuts), hidden.shape[1]
    bf16 = jnp.bfloat16
    return call(
        functools.partial(norm_kernel, cuts, pieces, first),
        "norm_rows",
        8,
        [HBM, HBM],
        [((cut, width), bf16, HBM) for cut in cuts],
        [
            pltpu.VMEM((width,), jnp.float32),
            pltpu.VMEM((rows, width), bf16),
            pltpu.VMEM((rows, width), bf16),
            pltpu.SemaphoreType.DMA((1 + 2 * pieces,)),
        ],
        hidden,
        gain,
    )


def qkv_kernel(places, first, chunks, held, trig, wq, wk, wv, *refs):
    parts, refs = refs[: len(places)], refs[len(places) + 2 * held :]
    q, kv, weights, rows, angles, semaphores = refs
    copies, waits = Copies(semaphores), []
    depth = weights.shape[0] // chunks
    for chunk in range(chunks):
        span, put, column, here = pl.ds(chunk * depth, depth), 0, 0, []
        for part in parts:
            target = rows.at[pl.ds(put, part.shape[0]), span]
            here.append(copies.start(part.at[:, span], target))
            put += part.shape[0]
        for weight in (wq, wk, wv):
            target = weights.at[span, pl.ds(column, weight.shape[1])]
            here.append(copies.start(weight.at[span], target))
            column += weight.shape[1]
        waits.append(here)
    late, put = [], 0
    for part, place in zip(parts, places):
        count = part.shape[0]
        source = trig.at[pl.ds(first + place, count)]
        late.append(copies.start(source, angles.at[pl.ds(put, count)]))
        put += count
    product = None
    for chunk, here in enumerate(waits):
        for copy in here:
            copy.wait()
        span = pl.ds(chunk * depth, depth)
        term = jnp.dot(rows[:, span], weights[span, :], preferred_element_type=jnp.float32)
        product = term if product is None else product + term
    for copy in late:
        copy.wait()
    cos, sin = angles[:, :HD], angles[:, HD:]
    queries = product.shape[1] - 2 * HD

    def rotated(at):
        y = product[:, at : at + HD]
        return y * cos + pltpu.roll(y, HD // 2, 1) * sin

    factor = ATT_SCALAR ** (-0.5) * math.log2(math.e)
    keys = rotated(queries).astype(jnp.bfloat16)
    values = product[:, queries + HD :].astype(jnp.bfloat16)
    heads = [(rotated(at) * factor).astype(jnp.bfloat16) for at in range(0, queries, HD)]
    put = 0
    for part, place in zip(parts, places):
        count = part.shape[0]
        kv[place : place + count, :HD] = keys[put : put + count]
        kv[place : place + count, HD:] = values[put : put + count]
        for head, rotated_head in enumerate(heads):
            q[head, place : place + count, :] = rotated_head[put : put + count]
        put += count


def qkv(parts, places, total, weights, trig, first, held=(), chunks=4):
    rows, width = sum(part.shape[0] for part in parts), parts[0].shape[1]
    columns = sum(weight.shape[1] for weight in weights)
    heads, bf16 = weights[0].shape[1] // HD, jnp.bfloat16
    given = 4 + len(parts)
    return call(
        functools.partial(qkv_kernel, places, first, chunks, bool(held)),
        "qkv",
        14,
        [HBM] * given + [VMEM] * len(held),
        [((heads, total, HD), bf16, VMEM), ((total, 2 * HD), bf16, VMEM)],
        [
            pltpu.VMEM((width, columns), bf16),
            pltpu.VMEM((rows, width), bf16),
            pltpu.VMEM((rows, 2 * HD), jnp.float32),
            pltpu.SemaphoreType.DMA((len(parts) + (len(parts) + 3) * chunks,)),
        ],
        trig,
        *weights,
        *parts,
        *held,
        aliases={given + at: at for at in range(len(held))},
    )


class Step:
    def __init__(self, q, group, slots, same=None, merged=False):
        self.q, self.group, self.slots = q, group, slots
        self.same, self.merged = same, merged


class Chunk:
    def __init__(self, at, runs, share):
        self.at, self.runs, self.share = at, runs, share

    def places(self, core, axis, first, size):
        shape = (size, 1) if axis == 0 else (1, size)
        index = first + lax.broadcasted_iota(jnp.int32, shape, axis)
        result, begin = index, 0
        for which, offset, rows in self.runs:
            base = (core if which == 0 else 1 - core) * self.share + offset - begin
            inside = (index >= begin) & (index < begin + rows)
            result = jnp.where(inside, index + base, result)
            begin += rows
        return result


def attention_kernel(plan, q_chunks, k_chunks, group_parts, fresh, final, table, *refs):
    refs = list(refs)
    take = lambda n: [refs.pop(0) for _ in range(n)]
    count = len(q_chunks)
    qs = take(count)
    kv_parts = [take(n) for n in group_parts]
    take(2 * (count - len(fresh)))
    outs = take(len(final))
    states = [take(2) for _ in range(count)]
    kvs = take(len(group_parts))
    (semaphores,) = refs
    copies = Copies(semaphores)
    core = table[0]
    waits = {}
    for group, (parts, kv) in enumerate(zip(kv_parts, kvs)):
        each = kv.shape[0] // len(parts)
        waits[group] = [
            copies.start(part, kv.at[pl.ds(slot * each, each)])
            for slot, part in enumerate(parts)
        ]

    def ready(group):
        for copy in waits.pop(group, []):
            copy.wait()

    def attend(q, keys_values, begin, visible=None, bias=None):
        q_ref, (peak, acc) = qs[q], states[q]
        heads = q_ref.shape[0]
        keys = keys_values[:, :HD]
        values = keys_values[:, HD:].T
        values = jnp.concatenate([values, jnp.ones((ONES, keys.shape[0]), values.dtype)], axis=0)
        tiles, tile = acc.shape[0], acc.shape[2] // heads
        scores, tops, weights = [], [], []
        for at in range(tiles):
            q_tile = q_ref[:, at * tile : (at + 1) * tile, :].reshape(heads * tile, HD)
            score = lax.dot_general(
                keys, q_tile, (((1,), (1,)), ((), ())), preferred_element_type=jnp.float32
            )
            if visible is not None:
                seen = jnp.concatenate([visible(at * tile, tile)] * heads, axis=1)
                score = jnp.where(seen, score, HIDDEN)
            if bias is not None:
                score = score + bias
            scores.append(score)
        for at in range(tiles):
            top = jnp.max(scores[at], axis=0, keepdims=True)
            if not begin:
                top = jnp.maximum(peak[at, 0:1, :], top)
            tops.append(top)
            weights.append(jnp.exp2((scores[at] - top).astype(jnp.bfloat16)))
        for at in range(tiles):
            summed = jnp.dot(values, weights[at], preferred_element_type=jnp.float32)
            if not begin:
                summed = summed + acc[at] * jnp.exp2(peak[at, 0:1, :] - tops[at])
            acc[at] = summed
            peak[at] = jnp.broadcast_to(tops[at], peak.shape[1:])

    begun = set(range(count)) - set(fresh)
    for step in plan:
        q, group, kv = step.q, step.group, kvs[step.group]
        q_chunk, k_chunk = q_chunks[q], k_chunks[group]
        if step.same is not None:
            keys_at = k_chunk.places(core, 0, 0, kv.shape[1])
            visible = lambda first, tile: keys_at <= q_chunk.places(core, 1, first, tile)
            own = kv_parts[group][0]
            attend(q, own[step.same], q not in begun, visible=visible)
            begun.add(q)
        start = table[q_chunk.at]
        slots = step.slots
        if not slots:
            continue
        ready(group)
        if step.merged:
            shown = [table[k_chunk.at + slot] < start for slot in slots]

            @pl.when(functools.reduce(jnp.logical_or, shown))
            def _():
                rows = kv.shape[1]
                bias = [
                    jnp.where(see, 0.0, HIDDEN) * jnp.ones((rows, 1), jnp.float32)
                    for see in shown
                ]
                keys_values = kv[slots[0] : slots[-1] + 1].reshape(len(slots) * rows, 2 * HD)
                attend(q, keys_values, False, bias=jnp.concatenate(bias, axis=0))

        else:

            def one(slot, carry):
                @pl.when(table[k_chunk.at + slot] < start)
                def _():
                    attend(q, kv[slot], False)

                return carry

            lax.fori_loop(slots[0], slots[-1] + 1, one, 0)

    for group in list(waits):
        ready(group)
    for out, order in zip(outs, final):
        put = 0
        for q in order:
            acc, heads = states[q][1], qs[q].shape[0]
            tile = acc.shape[2] // heads
            for at in range(acc.shape[0]):
                rows = acc[at, :HD, :] / acc[at, HD : HD + 1, :]
                rows = rows.T.astype(jnp.bfloat16)
                for head in range(heads):
                    out[put : put + tile, head * HD : (head + 1) * HD] = rows[
                        head * tile : (head + 1) * tile
                    ]
                put += tile


def attention(plan, table, qs, q_chunks, groups, k_chunks, state, final=()):
    fresh = [at for at, held in enumerate(state) if held is None]
    shapes = []
    for q in qs:
        heads, rows, _ = q.shape
        tile = min(rows, 128)
        shapes += [(rows // tile, deep, heads * tile) for deep in (8, HD + ONES)]
    width = qs[0].shape[0] * HD
    sums = [sum(qs[q].shape[1] for q in order) for order in final]
    outs = [((rows, width), jnp.bfloat16, VMEM) for rows in sums]
    scratch = []
    for parts in groups:
        slots = sum(part.shape[0] for part in parts)
        scratch.append(pltpu.VMEM((slots,) + parts[0].shape[1:], jnp.bfloat16))
    parts = [part for parts in groups for part in parts]
    sizes = [len(parts) for parts in groups]
    inputs, aliases = [table, *qs, *parts], {}
    for at, pair in enumerate(state):
        for half, array in enumerate(pair or ()):
            aliases[len(inputs)] = len(outs) + 2 * at + half
            inputs.append(array)
    results = call(
        functools.partial(attention_kernel, plan, q_chunks, k_chunks, sizes, fresh, final),
        "attention",
        10,
        [SMEM] + [VMEM] * (len(inputs) - 1),
        outs + [(shape, jnp.float32, VMEM) for shape in shapes],
        scratch + [pltpu.SemaphoreType.DMA((len(parts),))],
        *inputs,
        aliases=aliases,
    )
    if final:
        return results[: len(final)]
    return [tuple(results[2 * at : 2 * at + 2]) for at in range(len(qs))]


def cut_kernel(sizes, at, table, weights, *refs):
    outs, (held, semaphores) = refs[: len(sizes) + 1], refs[len(sizes) + 1 :]
    copies = Copies(semaphores)
    half = weights.shape[0] // 2
    first = pl.multiple_of(table[at] * half, half)
    split = sum(sizes)
    rest = half - split
    ins, put = [], 0
    for size in sizes:
        target = held.at[pl.ds(put, size)]
        ins.append((copies.start(weights.at[pl.ds(first + put, size)], target), target))
        put += size
    both = held.at[pl.ds(split, 2 * rest)]
    for side in range(2):
        source = weights.at[pl.ds(side * half + split, rest)]
        copy = copies.start(source, held.at[pl.ds(split + side * rest, rest)])
        ins.append((copy, both if side else None))
    outs, stores = list(outs), []
    for copy, piece in ins:
        copy.wait()
        if piece is not None:
            stores.append(copies.start(piece, outs.pop(0)))
    for copy in stores:
        copy.wait()


def cut(table, at, weights, sizes):
    depth, width = weights.shape
    rest = depth // 2 - sum(sizes)
    return call(
        functools.partial(cut_kernel, sizes, at),
        "cut_weights",
        4,
        [SMEM, HBM],
        [((size, width), weights.dtype, HBM) for size in [*sizes, 2 * rest]],
        [
            pltpu.VMEM((depth // 2 + rest, width), weights.dtype),
            pltpu.SemaphoreType.DMA((2 * len(sizes) + 3,)),
        ],
        table,
        weights,
    )


def near_kernel(chunks, left, weights_hbm, out, weights, semaphores):
    copies = Copies(semaphores)
    step = out.shape[1] // chunks
    lanes = [pl.ds(chunk * step, step) for chunk in range(chunks)]
    waits = [copies.start(weights_hbm.at[:, at], weights.at[:, at]) for at in lanes]
    for at, copy in zip(lanes, waits):
        copy.wait()
        out[:, at] = jnp.dot(
            left[...], weights[:, at], preferred_element_type=jnp.float32
        ).astype(jnp.bfloat16)


def output_near(left, weights, chunks=6):
    rows, width = left.shape[0], weights.shape[1]
    return call(
        functools.partial(near_kernel, chunks),
        "output_near",
        8,
        [VMEM, HBM],
        [((rows, width), jnp.bfloat16, VMEM)],
        [pltpu.VMEM(weights.shape, weights.dtype), pltpu.SemaphoreType.DMA((chunks,))],
        left,
        weights,
    )[0]


def send_kernel(at, splits, chunks, table, left_hbm, near, *refs):
    pieces, refs = refs[: 2 * splits + 1], refs[2 * splits + 1 :]
    out, weights, left, staged, semaphores = refs
    copies = Copies(semaphores)
    depth, width = weights.shape
    half, step = depth // 2, width // chunks
    first = copies.start(left_hbm, left)
    waits, put = [], 0
    for own, other in zip(pieces[:splits], pieces[splits:-1]):
        for piece, side in ((own, table[at]), (other, 1 - table[at])):
            row = pl.multiple_of(side * half + put, 16)
            waits.append(copies.start(piece, weights.at[pl.ds(row, piece.shape[0])]))
        put += own.shape[0]
    for side in range(2):
        source = pieces[-1].at[pl.ds(side * (half - put), half - put)]
        waits.append(copies.start(source, weights.at[pl.ds(side * half + put, half - put)]))
    for copy in waits:
        copy.wait()
    first.wait()
    half = left.shape[0] // 2
    stores = []
    for chunk in range(chunks):
        span = pl.ds(chunk * step, step)
        staged[:, span] = (
            near[half:, span].astype(jnp.float32)
            + jnp.dot(left[half:, :], weights[:, span], preferred_element_type=jnp.float32)
        ).astype(jnp.bfloat16)
        stores.append(copies.start(staged.at[:, span], out.at[:, span]))
    for copy in stores:
        copy.wait()


def output_send(table, at, left, near, pieces, chunks=6):
    (rows, width), columns = near.shape, left.shape[1]
    half, bf16 = (rows // 2, width), jnp.bfloat16
    return call(
        functools.partial(send_kernel, at, len(pieces) // 2, chunks),
        "output_send",
        8,
        [SMEM, HBM, VMEM] + [HBM] * len(pieces),
        [(half, bf16, HBM), ((columns, width), bf16, VMEM)],
        [
            pltpu.VMEM(left.shape, bf16),
            pltpu.VMEM(half, bf16),
            pltpu.SemaphoreType.DMA((2 + len(pieces) + chunks,)),
        ],
        table,
        left,
        near,
        *pieces,
    )


def keep_kernel(chunks, left_hbm, hidden, near, weights, out, held, left, semaphores):
    copies = Copies(semaphores)
    first, late = copies.start(left_hbm, left), copies.start(hidden, held)
    first.wait()
    half, step = left.shape[0] // 2, out.shape[1] // chunks
    for chunk in range(chunks):
        span = pl.ds(chunk * step, step)
        out[:, span] = near[:half, span].astype(jnp.float32) + jnp.dot(
            left[:half, :], weights[:, span], preferred_element_type=jnp.float32
        )
    late.wait()


def output_keep(left, hidden, near, weights, chunks=6):
    rows, width = near.shape
    return call(
        functools.partial(keep_kernel, chunks),
        "output_keep",
        4,
        [HBM, HBM, VMEM, VMEM],
        [((rows // 2, width), jnp.float32, VMEM), (hidden.shape, hidden.dtype, VMEM)],
        [pltpu.VMEM(left.shape, jnp.bfloat16), pltpu.SemaphoreType.DMA((2,))],
        left,
        hidden,
        near,
        weights,
    )


def final_kernel(chunks, received, hidden, kept, gain, out, other, staged, gains, semaphores):
    copies = Copies(semaphores)
    width = hidden.shape[1]
    step = width // chunks
    lanes = [pl.ds(chunk * step, step) for chunk in range(chunks)]
    waits = [copies.start(received.at[:, span], other.at[:, span]) for span in lanes]
    late = copies.start(gain, gains)
    square = jnp.zeros((hidden.shape[0], 128), jnp.float32)
    for span, copy in zip(lanes, waits):
        copy.wait()
        total = kept[:, span] + other[:, span].astype(jnp.float32)
        for lane in range(0, step, 128):
            part = total[:, lane : lane + 128]
            square = square + part * part
    mean = jnp.sum(square, axis=1, keepdims=True) / width
    scale = lax.rsqrt(mean + EPS)
    late.wait()
    row = gains[...].reshape(1, width)
    stores = []
    for chunk, span in enumerate(lanes):
        total = kept[:, span] + other[:, span].astype(jnp.float32)
        normed = total * scale * row[:, chunk * step : (chunk + 1) * step]
        staged[:, span] = (hidden[:, span].astype(jnp.float32) + normed).astype(jnp.bfloat16)
        stores.append(copies.start(staged.at[:, span], out.at[:, span]))
    for store in stores:
        store.wait()


def output(received, hidden, kept, gain, chunks=6):
    rows, width = hidden.shape
    bf16 = jnp.bfloat16
    return call(
        functools.partial(final_kernel, chunks),
        "output_norm",
        8,
        [HBM, VMEM, VMEM, HBM],
        [((rows, width), bf16, HBM)],
        [
            pltpu.VMEM((rows, width), bf16),
            pltpu.VMEM((rows, width), bf16),
            pltpu.VMEM((width,), jnp.float32),
            pltpu.SemaphoreType.DMA((1 + 2 * chunks,)),
        ],
        received,
        hidden,
        kept,
        gain,
    )[0]


def rotary_table(positions):
    half = HD // 2
    frequency = jnp.power(
        jnp.float32(10000.0), -jnp.arange(half, dtype=jnp.float32) * (2.0 / HD)
    )
    angles = positions.astype(jnp.float32)[:, None] * frequency[None, :]
    cos, sin = jnp.cos(angles), jnp.sin(angles)
    return jnp.concatenate([cos, cos, -sin, sin], axis=1)


def lookup(block_of, index):
    ids = jnp.arange(block_of.shape[0], dtype=jnp.int32)
    return jnp.sum(jnp.where(index[..., None] == ids, block_of, 0), axis=-1)


def flipped(array, axis, bit):
    size = lax.axis_size(axis)
    return lax.ppermute(array, axis, [(i, i ^ bit) for i in range(size)])


def along_line(array):
    size = lax.axis_size("seq")
    parts = [array[None]]
    for by in range(1, size):
        part = lax.ppermute(array, "seq", [(i, (i + by) % size) for i in range(size)])
        parts.append(Came(part[None]))
    return parts


def along_ring(array, beside):
    size = lax.axis_size("seq")
    parts, part = [array[None]], array
    for step in range(1, size):
        if step == size - 1:
            part = after(part, beside)
        part = lax.ppermute(part, "seq", [(i, (i + 1) % size) for i in range(size)])
        parts.append(Came(part[None]))
    return parts


def came(parts):
    return [part.array for part in parts if isinstance(part, Came)]


def after(array, *others):
    return lax.optimization_barrier((array, *others))[0]


def two_chips(hidden, pre_gain, post_gain, wq, wk, wv, w_out, block_of):
    rows = hidden.shape[0]
    block_rows = 2 * rows
    lines, tp = lax.axis_size("seq"), lax.axis_index("tp")
    seq, group = lax.axis_index("seq"), lax.axis_index("groups")
    chip, core = tp // 2, tp % 2

    line = (seq - jnp.arange(lines, dtype=jnp.int32)) % lines
    near_starts = lookup(block_of, 2 * line + chip) * block_rows
    far_starts = lookup(block_of, 2 * line + 1 - chip) * block_rows
    table = jnp.concatenate([jnp.stack([core, group]).astype(jnp.int32), near_starts, far_starts])
    group_at, near_at, far_at = 1, 2, 2 + lines
    run = jnp.arange(rows, dtype=jnp.int32)
    place = jnp.concatenate([core * rows + run, (1 - core) * rows + run])
    trig = rotary_table(jnp.concatenate([near_starts[0] + place, far_starts[0] + place]))
    runs = [(0, 0, rows), (1, 0, rows)]
    near_chunk, far_chunk = Chunk(near_at, runs, rows), Chunk(far_at, runs, rows)
    others, everyone = list(range(1, lines)), list(range(lines))

    half = rows // 2
    own = [norm(hidden, pre_gain, at * half, [half])[0] for at in range(2)]
    away = [flipped(part, "tp", 2) for part in own]
    partner = [Came(flipped(part, "tp", 1)) for part in own]

    weights = (wq, wk, wv)
    places = [0, half, rows, rows + half]
    q_near, kv_near = qkv([*own, *partner], places, block_rows, weights, trig, 0)
    near = along_line(kv_near)
    eighth = w_out.shape[0] // 8
    sizes = [eighth, eighth * 3 // 2, eighth]
    w_cut = cut(table, group_at, after(w_out, kv_near), sizes)
    q_near = after(q_near, *w_cut)
    (near_state,) = attention(
        [Step(0, 0, others, same=0)], table, [q_near], [near_chunk], [near], [near_chunk], [None]
    )

    away[0] = after(away[0], *near_state)
    quarter = half // 2
    swapped = [flipped(away[0][at : at + quarter], "tp", 1) for at in (0, quarter)]
    held = qkv(
        [Came(away[0]), *[Came(part) for part in swapped]],
        [0, rows, rows + quarter],
        block_rows,
        weights,
        trig,
        block_rows,
    )
    away[1] = after(away[1], *held)
    held = qkv(
        [Came(away[1]), Came(flipped(away[1], "tp", 1))],
        [half, rows + half],
        block_rows,
        weights,
        trig,
        block_rows,
        held,
    )
    q_far, kv_far = held

    fetched = lambda piece, *others: flipped(after(piece, *others), "tp", 2)
    swap = lambda array: flipped(array, "groups", 1)
    w_far = [fetched(piece, away[1]) for piece in w_cut[:2]]
    w_far[0] = after(w_far[0], kv_far)
    w_other = [swap(w_far[0])]
    far = along_ring(kv_far, w_other[0])
    w_far[1] = after(w_far[1], came(far)[0])
    w_far += [fetched(piece, before) for piece, before in zip(w_cut[2:], w_far[:2])]
    w_other.append(swap(w_far[1]))

    near_state, far_state = attention(
        [Step(1, 1, [], same=0), Step(1, 0, everyone), Step(0, 1, [0])],
        table,
        [q_near, q_far],
        [near_chunk, far_chunk],
        [near, far[:1]],
        [near_chunk, far_chunk],
        [near_state, None],
    )
    w_far[2] = after(w_far[2], *far_state)
    w_other.append(swap(w_far[2]))
    rest = [Step(0, 0, others)]
    (gone,) = attention(
        rest, table, [q_far], [far_chunk], [far], [far_chunk], [far_state], final=[[0]]
    )
    gone = flipped(gone, "tp", 2)
    (attended,) = attention(
        rest, table, [q_near], [near_chunk], [far], [far_chunk], [near_state], final=[[0]]
    )
    near_sum = output_near(attended, w_out)
    pieces = [Came(piece) for piece in w_far[:3] + w_other + w_far[3:]]
    sent, w_laid = output_send(table, group_at, Came(gone), near_sum, pieces)
    received = flipped(sent, "tp", 1)
    kept, held = output_keep(Came(gone), hidden, near_sum, w_laid)
    return output(Came(received), held, kept, post_gain)


def any_count(hidden, pre_gain, post_gain, wq, wk, wv, w_out, block_of):
    rows = hidden.shape[0]
    lines = lax.axis_size("seq")
    line = (lax.axis_index("seq") - jnp.arange(lines, dtype=jnp.int32)) % lines
    block = (2 * line[:, None] + jnp.arange(2, dtype=jnp.int32)).reshape(-1)
    block_rows = rows * lax.axis_size("tp") // 2
    starts = lookup(block_of, block) * block_rows
    table = jnp.concatenate([jnp.zeros(2, jnp.int32), starts])
    normed = norm(hidden, pre_gain, 0, [rows], 1)[0]
    normed = lax.all_gather(normed, "tp", axis=0, tiled=True)
    place = jnp.arange(block_rows, dtype=jnp.int32)
    trig = rotary_table((starts[:2, None] + place).reshape(-1))
    qs, keys_values, weights = [], [], (wq, wk, wv)
    for at in range(2):
        first = at * block_rows
        rows_here = [normed[first : first + block_rows]]
        q, kv = qkv(rows_here, [0], block_rows, weights, trig, first)
        qs.append(q)
        keys_values.append(kv)
    kv = lax.all_gather(jnp.stack(keys_values), "seq")[line].reshape(-1, block_rows, 2 * HD)
    rest = list(range(2, 2 * lines))
    runs = [(0, 0, block_rows)]
    attended = attention(
        [Step(0, 0, [1], same=0), Step(1, 0, [0], same=1), Step(0, 0, rest), Step(1, 0, rest)],
        table,
        qs,
        [Chunk(2, runs, 0), Chunk(3, runs, 0)],
        [[kv]],
        [Chunk(2, runs, 0)],
        [None, None],
        final=[[0, 1]],
    )[0]
    partial = jnp.dot(attended, w_out, preferred_element_type=jnp.float32)
    summed = lax.psum_scatter(
        partial.astype(jnp.bfloat16), "tp", scatter_dimension=0, tiled=True
    ).astype(jnp.float32)
    mean = jnp.mean(summed * summed, axis=-1, keepdims=True)
    projected = summed * lax.rsqrt(mean + EPS) * post_gain
    return (hidden.astype(jnp.float32) + projected).astype(jnp.bfloat16)


def solution(mesh):
    return jax.shard_map(
        two_chips if mesh.shape["tp"] == 4 else any_count,
        mesh=mesh,
        in_specs=(
            P(("groups", "seq", "tp"), None),
            P(),
            P(),
            P(None, "tp"),
            P(None, "tp"),
            P(None, "tp"),
            P("tp", None),
            P(),
        ),
        out_specs=P(("groups", "seq", "tp"), None),
        check_vma=False,
    )
```

```python
import functools
import math

import jax
import jax.numpy as jnp
from jax import lax
from jax.experimental import pallas as pl
from jax.experimental.pallas import tpu as pltpu
from jax.sharding import PartitionSpec as P

HD = 128
ATT_SCALAR = 144
EPS = 1e-6
MIB = 1024 * 1024
HIDDEN = -1e30
ONES = 16
COST = pl.CostEstimate(flops=1, bytes_accessed=1, transcendentals=0)

ANY = pl.BlockSpec(memory_space=pl.ANY)
HBM = pl.BlockSpec(memory_space=pltpu.HBM)
VMEM = pl.BlockSpec(memory_space=pltpu.VMEM)
SMEM = pl.BlockSpec(memory_space=pltpu.SMEM)


class Came:
    def __init__(self, array):
        self.array, self.shape = array, array.shape


def call(kernel, name, mib, in_specs, outs, scratch, *args, aliases=None):
    in_specs, pinned = list(in_specs), []
    for at, arg in enumerate(args):
        if isinstance(arg, Came):
            arg, in_specs[at] = arg.array, ANY
        elif in_specs[at] is not SMEM:
            arg = pltpu.with_memory_space_constraint(arg, in_specs[at].memory_space)
        pinned.append(arg)
    return pl.pallas_call(
        kernel,
        in_specs=in_specs,
        out_specs=[spec for _, _, spec in outs],
        out_shape=[spec.memory_space(shape, dtype) for shape, dtype, spec in outs],
        scratch_shapes=scratch,
        input_output_aliases=aliases or {},
        compiler_params=pltpu.CompilerParams(vmem_limit_bytes=mib * MIB),
        cost_estimate=COST,
        name=name,
    )(*pinned)


class Copies:
    def __init__(self, semaphores):
        self.semaphores, self.used = semaphores, 0

    def start(self, source, target):
        copy = pltpu.make_async_copy(source, target, self.semaphores.at[self.used])
        self.used += 1
        copy.start()
        return copy


def norm_kernel(cuts, pieces, first, hidden, gain, *refs):
    parts, (gains, rows, staged, semaphores) = refs[: len(cuts)], refs[len(cuts) :]
    copies = Copies(semaphores)
    count, width = rows.shape
    step = count // pieces
    spans = [pl.ds(at * step, step) for at in range(pieces)]
    ins = [
        copies.start(hidden.at[pl.ds(first + at * step, step)], rows.at[span])
        for at, span in enumerate(spans)
    ]
    copies.start(gain, gains).wait()
    scale = gains[...].reshape(1, width)
    outs = []
    for at, span in enumerate(spans):
        ins[at].wait()
        x = rows[span, :].astype(jnp.float32)
        square = x * x
        folded = square[:, :128]
        for lane in range(128, width, 128):
            folded = folded + square[:, lane : lane + 128]
        mean = jnp.sum(folded, axis=1, keepdims=True) / width
        staged[span, :] = (x * lax.rsqrt(mean + EPS) * scale).astype(jnp.bfloat16)
        begin = 0
        for cut, part in zip(cuts, parts):
            if begin <= at * step < begin + cut:
                inside = pl.ds(at * step - begin, step)
                outs.append(copies.start(staged.at[span], part.at[inside]))
            begin += cut
    for copy in outs:
        copy.wait()


def norm(hidden, gain, first, cuts, pieces=3):
    rows, width = sum(cuts), hidden.shape[1]
    bf16 = jnp.bfloat16
    return call(
        functools.partial(norm_kernel, cuts, pieces, first),
        "norm_rows",
        8,
        [HBM, HBM],
        [((cut, width), bf16, HBM) for cut in cuts],
        [
            pltpu.VMEM((width,), jnp.float32),
            pltpu.VMEM((rows, width), bf16),
            pltpu.VMEM((rows, width), bf16),
            pltpu.SemaphoreType.DMA((1 + 2 * pieces,)),
        ],
        hidden,
        gain,
    )


def qkv_kernel(places, first, chunks, held, trig, wq, wk, wv, *refs):
    parts, refs = refs[: len(places)], refs[len(places) + 2 * held :]
    q, kv, weights, rows, angles, semaphores = refs
    copies, waits = Copies(semaphores), []
    depth = weights.shape[0] // chunks
    for chunk in range(chunks):
        span, put, column, here = pl.ds(chunk * depth, depth), 0, 0, []
        for part in parts:
            target = rows.at[pl.ds(put, part.shape[0]), span]
            here.append(copies.start(part.at[:, span], target))
            put += part.shape[0]
        for weight in (wq, wk, wv):
            target = weights.at[span, pl.ds(column, weight.shape[1])]
            here.append(copies.start(weight.at[span], target))
            column += weight.shape[1]
        waits.append(here)
    late, put = [], 0
    for part, place in zip(parts, places):
        count = part.shape[0]
        source = trig.at[pl.ds(first + place, count)]
        late.append(copies.start(source, angles.at[pl.ds(put, count)]))
        put += count
    product = None
    for chunk, here in enumerate(waits):
        for copy in here:
            copy.wait()
        span = pl.ds(chunk * depth, depth)
        term = jnp.dot(rows[:, span], weights[span, :], preferred_element_type=jnp.float32)
        product = term if product is None else product + term
    for copy in late:
        copy.wait()
    cos, sin = angles[:, :HD], angles[:, HD:]
    queries = product.shape[1] - 2 * HD

    def rotated(at):
        y = product[:, at : at + HD]
        return y * cos + pltpu.roll(y, HD // 2, 1) * sin

    factor = ATT_SCALAR ** (-0.5) * math.log2(math.e)
    keys = rotated(queries).astype(jnp.bfloat16)
    values = product[:, queries + HD :].astype(jnp.bfloat16)
    heads = [(rotated(at) * factor).astype(jnp.bfloat16) for at in range(0, queries, HD)]
    put = 0
    for part, place in zip(parts, places):
        count = part.shape[0]
        kv[place : place + count, :HD] = keys[put : put + count]
        kv[place : place + count, HD:] = values[put : put + count]
        for head, rotated_head in enumerate(heads):
            q[head, place : place + count, :] = rotated_head[put : put + count]
        put += count


def qkv(parts, places, total, weights, trig, first, held=(), chunks=4):
    rows, width = sum(part.shape[0] for part in parts), parts[0].shape[1]
    columns = sum(weight.shape[1] for weight in weights)
    heads, bf16 = weights[0].shape[1] // HD, jnp.bfloat16
    given = 4 + len(parts)
    return call(
        functools.partial(qkv_kernel, places, first, chunks, bool(held)),
        "qkv",
        14,
        [HBM] * given + [VMEM] * len(held),
        [((heads, total, HD), bf16, VMEM), ((total, 2 * HD), bf16, VMEM)],
        [
            pltpu.VMEM((width, columns), bf16),
            pltpu.VMEM((rows, width), bf16),
            pltpu.VMEM((rows, 2 * HD), jnp.float32),
            pltpu.SemaphoreType.DMA((len(parts) + (len(parts) + 3) * chunks,)),
        ],
        trig,
        *weights,
        *parts,
        *held,
        aliases={given + at: at for at in range(len(held))},
    )


class Step:
    def __init__(self, q, group, slots, same=None, merged=False):
        self.q, self.group, self.slots = q, group, slots
        self.same, self.merged = same, merged


class Chunk:
    def __init__(self, at, runs, share):
        self.at, self.runs, self.share = at, runs, share

    def places(self, core, axis, first, size):
        shape = (size, 1) if axis == 0 else (1, size)
        index = first + lax.broadcasted_iota(jnp.int32, shape, axis)
        result, begin = index, 0
        for which, offset, rows in self.runs:
            base = (core if which == 0 else 1 - core) * self.share + offset - begin
            inside = (index >= begin) & (index < begin + rows)
            result = jnp.where(inside, index + base, result)
            begin += rows
        return result


def attention_kernel(plan, q_chunks, k_chunks, group_parts, fresh, final, table, *refs):
    refs = list(refs)
    take = lambda n: [refs.pop(0) for _ in range(n)]
    count = len(q_chunks)
    qs = take(count)
    kv_parts = [take(n) for n in group_parts]
    take(2 * (count - len(fresh)))
    outs = take(len(final))
    states = [take(2) for _ in range(count)]
    kvs = take(len(group_parts))
    (semaphores,) = refs
    copies = Copies(semaphores)
    core = table[0]
    waits = {}
    for group, (parts, kv) in enumerate(zip(kv_parts, kvs)):
        each = kv.shape[0] // len(parts)
        waits[group] = [
            copies.start(part, kv.at[pl.ds(slot * each, each)])
            for slot, part in enumerate(parts)
        ]

    def ready(group):
        for copy in waits.pop(group, []):
            copy.wait()

    def attend(q, keys_values, begin, visible=None, bias=None):
        q_ref, (peak, acc) = qs[q], states[q]
        heads = q_ref.shape[0]
        keys = keys_values[:, :HD]
        values = keys_values[:, HD:].T
        values = jnp.concatenate([values, jnp.ones((ONES, keys.shape[0]), values.dtype)], axis=0)
        tiles, tile = acc.shape[0], acc.shape[2] // heads
        scores, tops, weights = [], [], []
        for at in range(tiles):
            q_tile = q_ref[:, at * tile : (at + 1) * tile, :].reshape(heads * tile, HD)
            score = lax.dot_general(
                keys, q_tile, (((1,), (1,)), ((), ())), preferred_element_type=jnp.float32
            )
            if visible is not None:
                seen = jnp.concatenate([visible(at * tile, tile)] * heads, axis=1)
                score = jnp.where(seen, score, HIDDEN)
            if bias is not None:
                score = score + bias
            scores.append(score)
        for at in range(tiles):
            top = jnp.max(scores[at], axis=0, keepdims=True)
            if not begin:
                top = jnp.maximum(peak[at, 0:1, :], top)
            tops.append(top)
            weights.append(jnp.exp2((scores[at] - top).astype(jnp.bfloat16)))
        for at in range(tiles):
            summed = jnp.dot(values, weights[at], preferred_element_type=jnp.float32)
            if not begin:
                summed = summed + acc[at] * jnp.exp2(peak[at, 0:1, :] - tops[at])
            acc[at] = summed
            peak[at] = jnp.broadcast_to(tops[at], peak.shape[1:])

    begun = set(range(count)) - set(fresh)
    for step in plan:
        q, group, kv = step.q, step.group, kvs[step.group]
        q_chunk, k_chunk = q_chunks[q], k_chunks[group]
        if step.same is not None:
            keys_at = k_chunk.places(core, 0, 0, kv.shape[1])
            visible = lambda first, tile: keys_at <= q_chunk.places(core, 1, first, tile)
            own = kv_parts[group][0]
            attend(q, own[step.same], q not in begun, visible=visible)
            begun.add(q)
        start = table[q_chunk.at]
        slots = step.slots
        if not slots:
            continue
        ready(group)
        if step.merged:
            shown = [table[k_chunk.at + slot] < start for slot in slots]

            @pl.when(functools.reduce(jnp.logical_or, shown))
            def _():
                rows = kv.shape[1]
                bias = [
                    jnp.where(see, 0.0, HIDDEN) * jnp.ones((rows, 1), jnp.float32)
                    for see in shown
                ]
                keys_values = kv[slots[0] : slots[-1] + 1].reshape(len(slots) * rows, 2 * HD)
                attend(q, keys_values, False, bias=jnp.concatenate(bias, axis=0))

        else:

            def one(slot, carry):
                @pl.when(table[k_chunk.at + slot] < start)
                def _():
                    attend(q, kv[slot], False)

                return carry

            lax.fori_loop(slots[0], slots[-1] + 1, one, 0)

    for group in list(waits):
        ready(group)
    for out, order in zip(outs, final):
        put = 0
        for q in order:
            acc, heads = states[q][1], qs[q].shape[0]
            tile = acc.shape[2] // heads
            for at in range(acc.shape[0]):
                rows = acc[at, :HD, :] / acc[at, HD : HD + 1, :]
                rows = rows.T.astype(jnp.bfloat16)
                for head in range(heads):
                    out[put : put + tile, head * HD : (head + 1) * HD] = rows[
                        head * tile : (head + 1) * tile
                    ]
                put += tile


def attention(plan, table, qs, q_chunks, groups, k_chunks, state, final=()):
    fresh = [at for at, held in enumerate(state) if held is None]
    shapes = []
    for q in qs:
        heads, rows, _ = q.shape
        tile = min(rows, 128)
        shapes += [(rows // tile, deep, heads * tile) for deep in (8, HD + ONES)]
    width = qs[0].shape[0] * HD
    sums = [sum(qs[q].shape[1] for q in order) for order in final]
    outs = [((rows, width), jnp.bfloat16, VMEM) for rows in sums]
    scratch = []
    for parts in groups:
        slots = sum(part.shape[0] for part in parts)
        scratch.append(pltpu.VMEM((slots,) + parts[0].shape[1:], jnp.bfloat16))
    parts = [part for parts in groups for part in parts]
    sizes = [len(parts) for parts in groups]
    inputs, aliases = [table, *qs, *parts], {}
    for at, pair in enumerate(state):
        for half, array in enumerate(pair or ()):
            aliases[len(inputs)] = len(outs) + 2 * at + half
            inputs.append(array)
    results = call(
        functools.partial(attention_kernel, plan, q_chunks, k_chunks, sizes, fresh, final),
        "attention",
        10,
        [SMEM] + [VMEM] * (len(inputs) - 1),
        outs + [(shape, jnp.float32, VMEM) for shape in shapes],
        scratch + [pltpu.SemaphoreType.DMA((len(parts),))],
        *inputs,
        aliases=aliases,
    )
    if final:
        return results[: len(final)]
    return [tuple(results[2 * at : 2 * at + 2]) for at in range(len(qs))]


def cut_kernel(sizes, at, table, weights, *refs):
    outs, (held, semaphores) = refs[: len(sizes) + 1], refs[len(sizes) + 1 :]
    copies = Copies(semaphores)
    half = weights.shape[0] // 2
    first = pl.multiple_of(table[at] * half, half)
    split = sum(sizes)
    rest = half - split
    ins, put = [], 0
    for size in sizes:
        target = held.at[pl.ds(put, size)]
        ins.append((copies.start(weights.at[pl.ds(first + put, size)], target), target))
        put += size
    both = held.at[pl.ds(split, 2 * rest)]
    for side in range(2):
        source = weights.at[pl.ds(side * half + split, rest)]
        copy = copies.start(source, held.at[pl.ds(split + side * rest, rest)])
        ins.append((copy, both if side else None))
    outs, stores = list(outs), []
    for copy, piece in ins:
        copy.wait()
        if piece is not None:
            stores.append(copies.start(piece, outs.pop(0)))
    for copy in stores:
        copy.wait()


def cut(table, at, weights, sizes):
    depth, width = weights.shape
    rest = depth // 2 - sum(sizes)
    return call(
        functools.partial(cut_kernel, sizes, at),
        "cut_weights",
        4,
        [SMEM, HBM],
        [((size, width), weights.dtype, HBM) for size in [*sizes, 2 * rest]],
        [
            pltpu.VMEM((depth // 2 + rest, width), weights.dtype),
            pltpu.SemaphoreType.DMA((2 * len(sizes) + 3,)),
        ],
        table,
        weights,
    )


def near_kernel(chunks, left, weights_hbm, out, weights, semaphores):
    copies = Copies(semaphores)
    step = out.shape[1] // chunks
    lanes = [pl.ds(chunk * step, step) for chunk in range(chunks)]
    waits = [copies.start(weights_hbm.at[:, at], weights.at[:, at]) for at in lanes]
    for at, copy in zip(lanes, waits):
        copy.wait()
        out[:, at] = jnp.dot(
            left[...], weights[:, at], preferred_element_type=jnp.float32
        ).astype(jnp.bfloat16)


def output_near(left, weights, chunks=6):
    rows, width = left.shape[0], weights.shape[1]
    return call(
        functools.partial(near_kernel, chunks),
        "output_near",
        8,
        [VMEM, HBM],
        [((rows, width), jnp.bfloat16, VMEM)],
        [pltpu.VMEM(weights.shape, weights.dtype), pltpu.SemaphoreType.DMA((chunks,))],
        left,
        weights,
    )[0]


def send_kernel(at, splits, chunks, table, left_hbm, near, *refs):
    pieces, refs = refs[: 2 * splits + 1], refs[2 * splits + 1 :]
    out, weights, left, staged, semaphores = refs
    copies = Copies(semaphores)
    depth, width = weights.shape
    half, step = depth // 2, width // chunks
    first = copies.start(left_hbm, left)
    waits, put = [], 0
    for own, other in zip(pieces[:splits], pieces[splits:-1]):
        for piece, side in ((own, table[at]), (other, 1 - table[at])):
            row = pl.multiple_of(side * half + put, 16)
            waits.append(copies.start(piece, weights.at[pl.ds(row, piece.shape[0])]))
        put += own.shape[0]
    for side in range(2):
        source = pieces[-1].at[pl.ds(side * (half - put), half - put)]
        waits.append(copies.start(source, weights.at[pl.ds(side * half + put, half - put)]))
    for copy in waits:
        copy.wait()
    first.wait()
    half = left.shape[0] // 2
    stores = []
    for chunk in range(chunks):
        span = pl.ds(chunk * step, step)
        staged[:, span] = (
            near[half:, span].astype(jnp.float32)
            + jnp.dot(left[half:, :], weights[:, span], preferred_element_type=jnp.float32)
        ).astype(jnp.bfloat16)
        stores.append(copies.start(staged.at[:, span], out.at[:, span]))
    for copy in stores:
        copy.wait()


def output_send(table, at, left, near, pieces, chunks=6):
    (rows, width), columns = near.shape, left.shape[1]
    half, bf16 = (rows // 2, width), jnp.bfloat16
    return call(
        functools.partial(send_kernel, at, len(pieces) // 2, chunks),
        "output_send",
        8,
        [SMEM, HBM, VMEM] + [HBM] * len(pieces),
        [(half, bf16, HBM), ((columns, width), bf16, VMEM)],
        [
            pltpu.VMEM(left.shape, bf16),
            pltpu.VMEM(half, bf16),
            pltpu.SemaphoreType.DMA((2 + len(pieces) + chunks,)),
        ],
        table,
        left,
        near,
        *pieces,
    )


def keep_kernel(chunks, left_hbm, hidden, near, weights, out, held, left, semaphores):
    copies = Copies(semaphores)
    first, late = copies.start(left_hbm, left), copies.start(hidden, held)
    first.wait()
    half, step = left.shape[0] // 2, out.shape[1] // chunks
    for chunk in range(chunks):
        span = pl.ds(chunk * step, step)
        out[:, span] = near[:half, span].astype(jnp.float32) + jnp.dot(
            left[:half, :], weights[:, span], preferred_element_type=jnp.float32
        )
    late.wait()


def output_keep(left, hidden, near, weights, chunks=6):
    rows, width = near.shape
    return call(
        functools.partial(keep_kernel, chunks),
        "output_keep",
        4,
        [HBM, HBM, VMEM, VMEM],
        [((rows // 2, width), jnp.float32, VMEM), (hidden.shape, hidden.dtype, VMEM)],
        [pltpu.VMEM(left.shape, jnp.bfloat16), pltpu.SemaphoreType.DMA((2,))],
        left,
        hidden,
        near,
        weights,
    )


def final_kernel(chunks, received, hidden, kept, gain, out, other, staged, gains, semaphores):
    copies = Copies(semaphores)
    width = hidden.shape[1]
    step = width // chunks
    lanes = [pl.ds(chunk * step, step) for chunk in range(chunks)]
    waits = [copies.start(received.at[:, span], other.at[:, span]) for span in lanes]
    late = copies.start(gain, gains)
    square = jnp.zeros((hidden.shape[0], 128), jnp.float32)
    for span, copy in zip(lanes, waits):
        copy.wait()
        total = kept[:, span] + other[:, span].astype(jnp.float32)
        for lane in range(0, step, 128):
            part = total[:, lane : lane + 128]
            square = square + part * part
    mean = jnp.sum(square, axis=1, keepdims=True) / width
    scale = lax.rsqrt(mean + EPS)
    late.wait()
    row = gains[...].reshape(1, width)
    stores = []
    for chunk, span in enumerate(lanes):
        total = kept[:, span] + other[:, span].astype(jnp.float32)
        normed = total * scale * row[:, chunk * step : (chunk + 1) * step]
        staged[:, span] = (hidden[:, span].astype(jnp.float32) + normed).astype(jnp.bfloat16)
        stores.append(copies.start(staged.at[:, span], out.at[:, span]))
    for store in stores:
        store.wait()


def output(received, hidden, kept, gain, chunks=6):
    rows, width = hidden.shape
    bf16 = jnp.bfloat16
    return call(
        functools.partial(final_kernel, chunks),
        "output_norm",
        8,
        [HBM, VMEM, VMEM, HBM],
        [((rows, width), bf16, HBM)],
        [
            pltpu.VMEM((rows, width), bf16),
            pltpu.VMEM((rows, width), bf16),
            pltpu.VMEM((width,), jnp.float32),
            pltpu.SemaphoreType.DMA((1 + 2 * chunks,)),
        ],
        received,
        hidden,
        kept,
        gain,
    )[0]


def rotary_table(positions):
    half = HD // 2
    frequency = jnp.power(
        jnp.float32(10000.0), -jnp.arange(half, dtype=jnp.float32) * (2.0 / HD)
    )
    angles = positions.astype(jnp.float32)[:, None] * frequency[None, :]
    cos, sin = jnp.cos(angles), jnp.sin(angles)
    return jnp.concatenate([cos, cos, -sin, sin], axis=1)


def lookup(block_of, index):
    ids = jnp.arange(block_of.shape[0], dtype=jnp.int32)
    return jnp.sum(jnp.where(index[..., None] == ids, block_of, 0), axis=-1)


def flipped(array, axis, bit):
    size = lax.axis_size(axis)
    return lax.ppermute(array, axis, [(i, i ^ bit) for i in range(size)])


def along_line(array):
    size = lax.axis_size("seq")
    parts = [array[None]]
    for by in range(1, size):
        part = lax.ppermute(array, "seq", [(i, (i + by) % size) for i in range(size)])
        parts.append(Came(part[None]))
    return parts


def along_ring(array, beside):
    size = lax.axis_size("seq")
    parts, part = [array[None]], array
    for step in range(1, size):
        if step == size - 1:
            part = after(part, beside)
        part = lax.ppermute(part, "seq", [(i, (i + 1) % size) for i in range(size)])
        parts.append(Came(part[None]))
    return parts


def came(parts):
    return [part.array for part in parts if isinstance(part, Came)]


def after(array, *others):
    return lax.optimization_barrier((array, *others))[0]


def two_chips(hidden, pre_gain, post_gain, wq, wk, wv, w_out, block_of):
    rows = hidden.shape[0]
    block_rows = 2 * rows
    lines, tp = lax.axis_size("seq"), lax.axis_index("tp")
    seq, group = lax.axis_index("seq"), lax.axis_index("groups")
    chip, core = tp // 2, tp % 2

    line = (seq - jnp.arange(lines, dtype=jnp.int32)) % lines
    near_starts = lookup(block_of, 2 * line + chip) * block_rows
    far_starts = lookup(block_of, 2 * line + 1 - chip) * block_rows
    table = jnp.concatenate([jnp.stack([core, group]).astype(jnp.int32), near_starts, far_starts])
    group_at, near_at, far_at = 1, 2, 2 + lines
    run = jnp.arange(rows, dtype=jnp.int32)
    place = jnp.concatenate([core * rows + run, (1 - core) * rows + run])
    trig = rotary_table(jnp.concatenate([near_starts[0] + place, far_starts[0] + place]))
    runs = [(0, 0, rows), (1, 0, rows)]
    near_chunk, far_chunk = Chunk(near_at, runs, rows), Chunk(far_at, runs, rows)
    others, everyone = list(range(1, lines)), list(range(lines))

    half = rows // 2
    own = [norm(hidden, pre_gain, at * half, [half])[0] for at in range(2)]
    away = [flipped(part, "tp", 2) for part in own]
    partner = [Came(flipped(part, "tp", 1)) for part in own]

    weights = (wq, wk, wv)
    places = [0, half, rows, rows + half]
    q_near, kv_near = qkv([*own, *partner], places, block_rows, weights, trig, 0)
    near = along_line(kv_near)
    eighth = w_out.shape[0] // 8
    sizes = [eighth, eighth, eighth * 3 // 2]
    w_cut = cut(table, group_at, after(w_out, kv_near), sizes)
    q_near = after(q_near, *w_cut)
    (near_state,) = attention(
        [Step(0, 0, others, same=0)], table, [q_near], [near_chunk], [near], [near_chunk], [None]
    )

    away[0] = after(away[0], *near_state)
    quarter = half // 2
    swapped = [flipped(away[0][at : at + quarter], "tp", 1) for at in (0, quarter)]
    held = qkv(
        [Came(away[0]), *[Came(part) for part in swapped]],
        [0, rows, rows + quarter],
        block_rows,
        weights,
        trig,
        block_rows,
    )
    away[1] = after(away[1], *held)
    held = qkv(
        [Came(away[1]), Came(flipped(away[1], "tp", 1))],
        [half, rows + half],
        block_rows,
        weights,
        trig,
        block_rows,
        held,
    )
    q_far, kv_far = held

    fetched = lambda piece, *others: flipped(after(piece, *others), "tp", 2)
    swap = lambda array: flipped(array, "groups", 1)
    w_far = [fetched(piece, away[1]) for piece in w_cut[:2]]
    w_far[0] = after(w_far[0], kv_far)
    w_other = [swap(w_far[0])]
    far = along_ring(kv_far, w_other[0])
    w_far[1] = after(w_far[1], came(far)[0])
    w_far += [fetched(piece, before) for piece, before in zip(w_cut[2:], w_far[:2])]
    w_other.append(swap(w_far[1]))

    near_state, far_state = attention(
        [Step(1, 1, [], same=0), Step(1, 0, everyone), Step(0, 1, [0])],
        table,
        [q_near, q_far],
        [near_chunk, far_chunk],
        [near, far[:1]],
        [near_chunk, far_chunk],
        [near_state, None],
    )
    w_far[2] = after(w_far[2], *far_state, w_other[1], came(far)[-1])
    w_other.append(swap(w_far[2]))
    rest = [Step(0, 0, others)]
    (gone,) = attention(
        rest, table, [q_far], [far_chunk], [far], [far_chunk], [far_state], final=[[0]]
    )
    gone = flipped(gone, "tp", 2)
    (attended,) = attention(
        rest, table, [q_near], [near_chunk], [far], [far_chunk], [near_state], final=[[0]]
    )
    near_sum = output_near(attended, w_out)
    pieces = [Came(piece) for piece in w_far[:3] + w_other + w_far[3:]]
    sent, w_laid = output_send(table, group_at, Came(gone), near_sum, pieces)
    received = flipped(sent, "tp", 1)
    kept, held = output_keep(Came(gone), hidden, near_sum, w_laid)
    return output(Came(received), held, kept, post_gain)


def any_count(hidden, pre_gain, post_gain, wq, wk, wv, w_out, block_of):
    rows = hidden.shape[0]
    lines = lax.axis_size("seq")
    line = (lax.axis_index("seq") - jnp.arange(lines, dtype=jnp.int32)) % lines
    block = (2 * line[:, None] + jnp.arange(2, dtype=jnp.int32)).reshape(-1)
    block_rows = rows * lax.axis_size("tp") // 2
    starts = lookup(block_of, block) * block_rows
    table = jnp.concatenate([jnp.zeros(2, jnp.int32), starts])
    normed = norm(hidden, pre_gain, 0, [rows], 1)[0]
    normed = lax.all_gather(normed, "tp", axis=0, tiled=True)
    place = jnp.arange(block_rows, dtype=jnp.int32)
    trig = rotary_table((starts[:2, None] + place).reshape(-1))
    qs, keys_values, weights = [], [], (wq, wk, wv)
    for at in range(2):
        first = at * block_rows
        rows_here = [normed[first : first + block_rows]]
        q, kv = qkv(rows_here, [0], block_rows, weights, trig, first)
        qs.append(q)
        keys_values.append(kv)
    kv = lax.all_gather(jnp.stack(keys_values), "seq")[line].reshape(-1, block_rows, 2 * HD)
    rest = list(range(2, 2 * lines))
    runs = [(0, 0, block_rows)]
    attended = attention(
        [Step(0, 0, [1], same=0), Step(1, 0, [0], same=1), Step(0, 0, rest), Step(1, 0, rest)],
        table,
        qs,
        [Chunk(2, runs, 0), Chunk(3, runs, 0)],
        [[kv]],
        [Chunk(2, runs, 0)],
        [None, None],
        final=[[0, 1]],
    )[0]
    partial = jnp.dot(attended, w_out, preferred_element_type=jnp.float32)
    summed = lax.psum_scatter(
        partial.astype(jnp.bfloat16), "tp", scatter_dimension=0, tiled=True
    ).astype(jnp.float32)
    mean = jnp.mean(summed * summed, axis=-1, keepdims=True)
    projected = summed * lax.rsqrt(mean + EPS) * post_gain
    return (hidden.astype(jnp.float32) + projected).astype(jnp.bfloat16)


def solution(mesh):
    return jax.shard_map(
        two_chips if mesh.shape["tp"] == 4 else any_count,
        mesh=mesh,
        in_specs=(
            P(("groups", "seq", "tp"), None),
            P(),
            P(),
            P(None, "tp"),
            P(None, "tp"),
            P(None, "tp"),
            P("tp", None),
            P(),
        ),
        out_specs=P(("groups", "seq", "tp"), None),
        check_vma=False,
    )
```

```python
import functools
import math

import jax
import jax.numpy as jnp
from jax import lax
from jax.experimental import pallas as pl
from jax.experimental.pallas import tpu as pltpu
from jax.sharding import PartitionSpec as P

HD = 128
ATT_SCALAR = 144
EPS = 1e-6
MIB = 1024 * 1024
HIDDEN = -1e30
ONES = 16
COST = pl.CostEstimate(flops=1, bytes_accessed=1, transcendentals=0)

ANY = pl.BlockSpec(memory_space=pl.ANY)
HBM = pl.BlockSpec(memory_space=pltpu.HBM)
VMEM = pl.BlockSpec(memory_space=pltpu.VMEM)
SMEM = pl.BlockSpec(memory_space=pltpu.SMEM)


class Came:
    def __init__(self, array):
        self.array, self.shape = array, array.shape


def call(kernel, name, mib, in_specs, outs, scratch, *args, aliases=None):
    in_specs, pinned = list(in_specs), []
    for at, arg in enumerate(args):
        if isinstance(arg, Came):
            arg, in_specs[at] = arg.array, ANY
        elif in_specs[at] is not SMEM:
            arg = pltpu.with_memory_space_constraint(arg, in_specs[at].memory_space)
        pinned.append(arg)
    return pl.pallas_call(
        kernel,
        in_specs=in_specs,
        out_specs=[spec for _, _, spec in outs],
        out_shape=[spec.memory_space(shape, dtype) for shape, dtype, spec in outs],
        scratch_shapes=scratch,
        input_output_aliases=aliases or {},
        compiler_params=pltpu.CompilerParams(vmem_limit_bytes=mib * MIB),
        cost_estimate=COST,
        name=name,
    )(*pinned)


class Copies:
    def __init__(self, semaphores):
        self.semaphores, self.used = semaphores, 0

    def start(self, source, target):
        copy = pltpu.make_async_copy(source, target, self.semaphores.at[self.used])
        self.used += 1
        copy.start()
        return copy


def norm_kernel(cuts, pieces, first, hidden, gain, *refs):
    parts, (gains, rows, staged, semaphores) = refs[: len(cuts)], refs[len(cuts) :]
    copies = Copies(semaphores)
    count, width = rows.shape
    step = count // pieces
    spans = [pl.ds(at * step, step) for at in range(pieces)]
    ins = [
        copies.start(hidden.at[pl.ds(first + at * step, step)], rows.at[span])
        for at, span in enumerate(spans)
    ]
    copies.start(gain, gains).wait()
    scale = gains[...].reshape(1, width)
    outs = []
    for at, span in enumerate(spans):
        ins[at].wait()
        x = rows[span, :].astype(jnp.float32)
        square = x * x
        folded = square[:, :128]
        for lane in range(128, width, 128):
            folded = folded + square[:, lane : lane + 128]
        mean = jnp.sum(folded, axis=1, keepdims=True) / width
        staged[span, :] = (x * lax.rsqrt(mean + EPS) * scale).astype(jnp.bfloat16)
        begin = 0
        for cut, part in zip(cuts, parts):
            if begin <= at * step < begin + cut:
                inside = pl.ds(at * step - begin, step)
                outs.append(copies.start(staged.at[span], part.at[inside]))
            begin += cut
    for copy in outs:
        copy.wait()


def norm(hidden, gain, first, cuts, pieces=3):
    rows, width = sum(cuts), hidden.shape[1]
    bf16 = jnp.bfloat16
    return call(
        functools.partial(norm_kernel, cuts, pieces, first),
        "norm_rows",
        8,
        [HBM, HBM],
        [((cut, width), bf16, HBM) for cut in cuts],
        [
            pltpu.VMEM((width,), jnp.float32),
            pltpu.VMEM((rows, width), bf16),
            pltpu.VMEM((rows, width), bf16),
            pltpu.SemaphoreType.DMA((1 + 2 * pieces,)),
        ],
        hidden,
        gain,
    )


def qkv_kernel(places, first, chunks, held, trig, wq, wk, wv, *refs):
    parts, refs = refs[: len(places)], refs[len(places) + 2 * held :]
    q, kv, weights, rows, angles, semaphores = refs
    copies, waits = Copies(semaphores), []
    depth = weights.shape[0] // chunks
    for chunk in range(chunks):
        span, put, column, here = pl.ds(chunk * depth, depth), 0, 0, []
        for part in parts:
            target = rows.at[pl.ds(put, part.shape[0]), span]
            here.append(copies.start(part.at[:, span], target))
            put += part.shape[0]
        for weight in (wq, wk, wv):
            target = weights.at[span, pl.ds(column, weight.shape[1])]
            here.append(copies.start(weight.at[span], target))
            column += weight.shape[1]
        waits.append(here)
    late, put = [], 0
    for part, place in zip(parts, places):
        count = part.shape[0]
        source = trig.at[pl.ds(first + place, count)]
        late.append(copies.start(source, angles.at[pl.ds(put, count)]))
        put += count
    product = None
    for chunk, here in enumerate(waits):
        for copy in here:
            copy.wait()
        span = pl.ds(chunk * depth, depth)
        term = jnp.dot(rows[:, span], weights[span, :], preferred_element_type=jnp.float32)
        product = term if product is None else product + term
    for copy in late:
        copy.wait()
    cos, sin = angles[:, :HD], angles[:, HD:]
    queries = product.shape[1] - 2 * HD

    def rotated(at):
        y = product[:, at : at + HD]
        return y * cos + pltpu.roll(y, HD // 2, 1) * sin

    factor = ATT_SCALAR ** (-0.5) * math.log2(math.e)
    keys = rotated(queries).astype(jnp.bfloat16)
    values = product[:, queries + HD :].astype(jnp.bfloat16)
    heads = [(rotated(at) * factor).astype(jnp.bfloat16) for at in range(0, queries, HD)]
    put = 0
    for part, place in zip(parts, places):
        count = part.shape[0]
        kv[place : place + count, :HD] = keys[put : put + count]
        kv[place : place + count, HD:] = values[put : put + count]
        for head, rotated_head in enumerate(heads):
            q[head, place : place + count, :] = rotated_head[put : put + count]
        put += count


def qkv(parts, places, total, weights, trig, first, held=(), chunks=4):
    rows, width = sum(part.shape[0] for part in parts), parts[0].shape[1]
    columns = sum(weight.shape[1] for weight in weights)
    heads, bf16 = weights[0].shape[1] // HD, jnp.bfloat16
    given = 4 + len(parts)
    return call(
        functools.partial(qkv_kernel, places, first, chunks, bool(held)),
        "qkv",
        14,
        [HBM] * given + [VMEM] * len(held),
        [((heads, total, HD), bf16, VMEM), ((total, 2 * HD), bf16, VMEM)],
        [
            pltpu.VMEM((width, columns), bf16),
            pltpu.VMEM((rows, width), bf16),
            pltpu.VMEM((rows, 2 * HD), jnp.float32),
            pltpu.SemaphoreType.DMA((len(parts) + (len(parts) + 3) * chunks,)),
        ],
        trig,
        *weights,
        *parts,
        *held,
        aliases={given + at: at for at in range(len(held))},
    )


class Step:
    def __init__(self, q, group, slots, same=None, merged=False):
        self.q, self.group, self.slots = q, group, slots
        self.same, self.merged = same, merged


class Chunk:
    def __init__(self, at, runs, share):
        self.at, self.runs, self.share = at, runs, share

    def places(self, core, axis, first, size):
        shape = (size, 1) if axis == 0 else (1, size)
        index = first + lax.broadcasted_iota(jnp.int32, shape, axis)
        result, begin = index, 0
        for which, offset, rows in self.runs:
            base = (core if which == 0 else 1 - core) * self.share + offset - begin
            inside = (index >= begin) & (index < begin + rows)
            result = jnp.where(inside, index + base, result)
            begin += rows
        return result


def attention_kernel(plan, q_chunks, k_chunks, group_parts, fresh, final, table, *refs):
    refs = list(refs)
    take = lambda n: [refs.pop(0) for _ in range(n)]
    count = len(q_chunks)
    qs = take(count)
    kv_parts = [take(n) for n in group_parts]
    take(2 * (count - len(fresh)))
    outs = take(len(final))
    states = [take(2) for _ in range(count)]
    kvs = take(len(group_parts))
    (semaphores,) = refs
    copies = Copies(semaphores)
    core = table[0]
    waits = {}
    for group, (parts, kv) in enumerate(zip(kv_parts, kvs)):
        each = kv.shape[0] // len(parts)
        waits[group] = [
            copies.start(part, kv.at[pl.ds(slot * each, each)])
            for slot, part in enumerate(parts)
        ]

    def ready(group):
        for copy in waits.pop(group, []):
            copy.wait()

    def attend(q, keys_values, begin, visible=None, bias=None):
        q_ref, (peak, acc) = qs[q], states[q]
        heads = q_ref.shape[0]
        keys = keys_values[:, :HD]
        values = keys_values[:, HD:].T
        values = jnp.concatenate([values, jnp.ones((ONES, keys.shape[0]), values.dtype)], axis=0)
        tiles, tile = acc.shape[0], acc.shape[2] // heads
        scores, tops, weights = [], [], []
        for at in range(tiles):
            q_tile = q_ref[:, at * tile : (at + 1) * tile, :].reshape(heads * tile, HD)
            score = lax.dot_general(
                keys, q_tile, (((1,), (1,)), ((), ())), preferred_element_type=jnp.float32
            )
            if visible is not None:
                seen = jnp.concatenate([visible(at * tile, tile)] * heads, axis=1)
                score = jnp.where(seen, score, HIDDEN)
            if bias is not None:
                score = score + bias
            scores.append(score)
        for at in range(tiles):
            top = jnp.max(scores[at], axis=0, keepdims=True)
            if not begin:
                top = jnp.maximum(peak[at, 0:1, :], top)
            tops.append(top)
            weights.append(jnp.exp2((scores[at] - top).astype(jnp.bfloat16)))
        for at in range(tiles):
            summed = jnp.dot(values, weights[at], preferred_element_type=jnp.float32)
            if not begin:
                summed = summed + acc[at] * jnp.exp2(peak[at, 0:1, :] - tops[at])
            acc[at] = summed
            peak[at] = jnp.broadcast_to(tops[at], peak.shape[1:])

    begun = set(range(count)) - set(fresh)
    for step in plan:
        q, group, kv = step.q, step.group, kvs[step.group]
        q_chunk, k_chunk = q_chunks[q], k_chunks[group]
        if step.same is not None:
            keys_at = k_chunk.places(core, 0, 0, kv.shape[1])
            visible = lambda first, tile: keys_at <= q_chunk.places(core, 1, first, tile)
            own = kv_parts[group][0]
            attend(q, own[step.same], q not in begun, visible=visible)
            begun.add(q)
        start = table[q_chunk.at]
        slots = step.slots
        if not slots:
            continue
        ready(group)
        if step.merged:
            shown = [table[k_chunk.at + slot] < start for slot in slots]

            @pl.when(functools.reduce(jnp.logical_or, shown))
            def _():
                rows = kv.shape[1]
                bias = [
                    jnp.where(see, 0.0, HIDDEN) * jnp.ones((rows, 1), jnp.float32)
                    for see in shown
                ]
                keys_values = kv[slots[0] : slots[-1] + 1].reshape(len(slots) * rows, 2 * HD)
                attend(q, keys_values, False, bias=jnp.concatenate(bias, axis=0))

        else:

            def one(slot, carry):
                @pl.when(table[k_chunk.at + slot] < start)
                def _():
                    attend(q, kv[slot], False)

                return carry

            lax.fori_loop(slots[0], slots[-1] + 1, one, 0)

    for group in list(waits):
        ready(group)
    for out, order in zip(outs, final):
        put = 0
        for q in order:
            acc, heads = states[q][1], qs[q].shape[0]
            tile = acc.shape[2] // heads
            for at in range(acc.shape[0]):
                rows = acc[at, :HD, :] / acc[at, HD : HD + 1, :]
                rows = rows.T.astype(jnp.bfloat16)
                for head in range(heads):
                    out[put : put + tile, head * HD : (head + 1) * HD] = rows[
                        head * tile : (head + 1) * tile
                    ]
                put += tile


def attention(plan, table, qs, q_chunks, groups, k_chunks, state, final=()):
    fresh = [at for at, held in enumerate(state) if held is None]
    shapes = []
    for q in qs:
        heads, rows, _ = q.shape
        tile = min(rows, 128)
        shapes += [(rows // tile, deep, heads * tile) for deep in (8, HD + ONES)]
    width = qs[0].shape[0] * HD
    sums = [sum(qs[q].shape[1] for q in order) for order in final]
    outs = [((rows, width), jnp.bfloat16, VMEM) for rows in sums]
    scratch = []
    for parts in groups:
        slots = sum(part.shape[0] for part in parts)
        scratch.append(pltpu.VMEM((slots,) + parts[0].shape[1:], jnp.bfloat16))
    parts = [part for parts in groups for part in parts]
    sizes = [len(parts) for parts in groups]
    inputs, aliases = [table, *qs, *parts], {}
    for at, pair in enumerate(state):
        for half, array in enumerate(pair or ()):
            aliases[len(inputs)] = len(outs) + 2 * at + half
            inputs.append(array)
    results = call(
        functools.partial(attention_kernel, plan, q_chunks, k_chunks, sizes, fresh, final),
        "attention",
        10,
        [SMEM] + [VMEM] * (len(inputs) - 1),
        outs + [(shape, jnp.float32, VMEM) for shape in shapes],
        scratch + [pltpu.SemaphoreType.DMA((len(parts),))],
        *inputs,
        aliases=aliases,
    )
    if final:
        return results[: len(final)]
    return [tuple(results[2 * at : 2 * at + 2]) for at in range(len(qs))]


def cut_kernel(sizes, at, table, weights, *refs):
    outs, (held, semaphores) = refs[: len(sizes) + 1], refs[len(sizes) + 1 :]
    copies = Copies(semaphores)
    half = weights.shape[0] // 2
    first = pl.multiple_of(table[at] * half, half)
    split = sum(sizes)
    rest = half - split
    ins, put = [], 0
    for size in sizes:
        target = held.at[pl.ds(put, size)]
        ins.append((copies.start(weights.at[pl.ds(first + put, size)], target), target))
        put += size
    both = held.at[pl.ds(split, 2 * rest)]
    for side in range(2):
        source = weights.at[pl.ds(side * half + split, rest)]
        copy = copies.start(source, held.at[pl.ds(split + side * rest, rest)])
        ins.append((copy, both if side else None))
    outs, stores = list(outs), []
    for copy, piece in ins:
        copy.wait()
        if piece is not None:
            stores.append(copies.start(piece, outs.pop(0)))
    for copy in stores:
        copy.wait()


def cut(table, at, weights, sizes):
    depth, width = weights.shape
    rest = depth // 2 - sum(sizes)
    return call(
        functools.partial(cut_kernel, sizes, at),
        "cut_weights",
        4,
        [SMEM, HBM],
        [((size, width), weights.dtype, HBM) for size in [*sizes, 2 * rest]],
        [
            pltpu.VMEM((depth // 2 + rest, width), weights.dtype),
            pltpu.SemaphoreType.DMA((2 * len(sizes) + 3,)),
        ],
        table,
        weights,
    )


def near_kernel(at, sizes, chunks, table, left, own_hbm, *refs):
    pieces, (out, laid, weights, semaphores) = refs[:-4], refs[-4:]
    copies = Copies(semaphores)
    step = out.shape[1] // chunks
    lanes = [pl.ds(chunk * step, step) for chunk in range(chunks)]
    waits = [copies.start(own_hbm.at[:, span], weights.at[:, span]) for span in lanes]
    half, put, late = laid.shape[0] // 2, 0, []
    for index, size in enumerate(sizes):
        for piece, side in ((index, table[at]), (len(sizes) + index, 1 - table[at])):
            if piece < len(pieces):
                row = pl.multiple_of(side * half + put, 16)
                late.append(copies.start(pieces[piece], laid.at[pl.ds(row, size)]))
        put += size
    for span, copy in zip(lanes, waits):
        copy.wait()
        out[:, span] = jnp.dot(
            left[...], weights[:, span], preferred_element_type=jnp.float32
        ).astype(jnp.bfloat16)
    for copy in late:
        copy.wait()


def output_near(table, at, left, weights, sizes, pieces, chunks=6):
    rows, width = left.shape[0], weights.shape[1]
    return call(
        functools.partial(near_kernel, at, sizes, chunks),
        "output_near",
        8,
        [SMEM, VMEM, HBM] + [HBM] * len(pieces),
        [((rows, width), jnp.bfloat16, VMEM), (weights.shape, weights.dtype, VMEM)],
        [
            pltpu.VMEM(weights.shape, weights.dtype),
            pltpu.SemaphoreType.DMA((chunks + len(pieces),)),
        ],
        table,
        left,
        weights,
        *pieces,
    )


def send_kernel(at, sizes, chunks, table, left_hbm, near, last, both, held, *refs):
    out, weights, left, staged, semaphores = refs
    copies = Copies(semaphores)
    depth, width = weights.shape
    half, step, put = depth // 2, width // chunks, sum(sizes)
    waits = [copies.start(left_hbm, left)]
    row = pl.multiple_of((1 - table[at]) * half + put - sizes[-1], 16)
    waits.append(copies.start(last, weights.at[pl.ds(row, sizes[-1])]))
    for side in range(2):
        source = both.at[pl.ds(side * (half - put), half - put)]
        waits.append(copies.start(source, weights.at[pl.ds(side * half + put, half - put)]))
    for copy in waits:
        copy.wait()
    begin = left.shape[0] // 2
    stores = []
    for chunk in range(chunks):
        span = pl.ds(chunk * step, step)
        staged[:, span] = (
            near[begin:, span].astype(jnp.float32)
            + jnp.dot(left[begin:, :], weights[:, span], preferred_element_type=jnp.float32)
        ).astype(jnp.bfloat16)
        stores.append(copies.start(staged.at[:, span], out.at[:, span]))
    for copy in stores:
        copy.wait()


def output_send(table, at, left, near, laid, sizes, last, both, chunks=6):
    (rows, width), bf16 = near.shape, jnp.bfloat16
    part = (rows // 2, width)
    return call(
        functools.partial(send_kernel, at, sizes, chunks),
        "output_send",
        8,
        [SMEM, HBM, VMEM, HBM, HBM, VMEM],
        [(part, bf16, HBM), (laid.shape, bf16, VMEM)],
        [
            pltpu.VMEM(left.shape, bf16),
            pltpu.VMEM(part, bf16),
            pltpu.SemaphoreType.DMA((4 + chunks,)),
        ],
        table,
        left,
        near,
        last,
        both,
        laid,
        aliases={5: 1},
    )


def keep_kernel(chunks, left_hbm, hidden, near, weights, out, held, left, semaphores):
    copies = Copies(semaphores)
    first, late = copies.start(left_hbm, left), copies.start(hidden, held)
    first.wait()
    half, step = left.shape[0] // 2, out.shape[1] // chunks
    for chunk in range(chunks):
        span = pl.ds(chunk * step, step)
        out[:, span] = near[:half, span].astype(jnp.float32) + jnp.dot(
            left[:half, :], weights[:, span], preferred_element_type=jnp.float32
        )
    late.wait()


def output_keep(left, hidden, near, weights, chunks=6):
    rows, width = near.shape
    return call(
        functools.partial(keep_kernel, chunks),
        "output_keep",
        4,
        [HBM, HBM, VMEM, VMEM],
        [((rows // 2, width), jnp.float32, VMEM), (hidden.shape, hidden.dtype, VMEM)],
        [pltpu.VMEM(left.shape, jnp.bfloat16), pltpu.SemaphoreType.DMA((2,))],
        left,
        hidden,
        near,
        weights,
    )


def final_kernel(chunks, received, hidden, kept, gain, out, other, staged, gains, semaphores):
    copies = Copies(semaphores)
    width = hidden.shape[1]
    step = width // chunks
    lanes = [pl.ds(chunk * step, step) for chunk in range(chunks)]
    waits = [copies.start(received.at[:, span], other.at[:, span]) for span in lanes]
    late = copies.start(gain, gains)
    square = jnp.zeros((hidden.shape[0], 128), jnp.float32)
    for span, copy in zip(lanes, waits):
        copy.wait()
        total = kept[:, span] + other[:, span].astype(jnp.float32)
        for lane in range(0, step, 128):
            part = total[:, lane : lane + 128]
            square = square + part * part
    mean = jnp.sum(square, axis=1, keepdims=True) / width
    scale = lax.rsqrt(mean + EPS)
    late.wait()
    row = gains[...].reshape(1, width)
    stores = []
    for chunk, span in enumerate(lanes):
        total = kept[:, span] + other[:, span].astype(jnp.float32)
        normed = total * scale * row[:, chunk * step : (chunk + 1) * step]
        staged[:, span] = (hidden[:, span].astype(jnp.float32) + normed).astype(jnp.bfloat16)
        stores.append(copies.start(staged.at[:, span], out.at[:, span]))
    for store in stores:
        store.wait()


def output(received, hidden, kept, gain, chunks=6):
    rows, width = hidden.shape
    bf16 = jnp.bfloat16
    return call(
        functools.partial(final_kernel, chunks),
        "output_norm",
        8,
        [HBM, VMEM, VMEM, HBM],
        [((rows, width), bf16, HBM)],
        [
            pltpu.VMEM((rows, width), bf16),
            pltpu.VMEM((rows, width), bf16),
            pltpu.VMEM((width,), jnp.float32),
            pltpu.SemaphoreType.DMA((1 + 2 * chunks,)),
        ],
        received,
        hidden,
        kept,
        gain,
    )[0]


def rotary_table(positions):
    half = HD // 2
    frequency = jnp.power(
        jnp.float32(10000.0), -jnp.arange(half, dtype=jnp.float32) * (2.0 / HD)
    )
    angles = positions.astype(jnp.float32)[:, None] * frequency[None, :]
    cos, sin = jnp.cos(angles), jnp.sin(angles)
    return jnp.concatenate([cos, cos, -sin, sin], axis=1)


def lookup(block_of, index):
    ids = jnp.arange(block_of.shape[0], dtype=jnp.int32)
    return jnp.sum(jnp.where(index[..., None] == ids, block_of, 0), axis=-1)


def flipped(array, axis, bit):
    size = lax.axis_size(axis)
    return lax.ppermute(array, axis, [(i, i ^ bit) for i in range(size)])


def along_line(array):
    size = lax.axis_size("seq")
    parts = [array[None]]
    for by in range(1, size):
        part = lax.ppermute(array, "seq", [(i, (i + by) % size) for i in range(size)])
        parts.append(Came(part[None]))
    return parts


def along_ring(array, second, last):
    size = lax.axis_size("seq")
    parts, part = [array[None]], array
    for step in range(1, size):
        if step == 2:
            part = after(part, second)
        if step == size - 1:
            part = after(part, last)
        part = lax.ppermute(part, "seq", [(i, (i + 1) % size) for i in range(size)])
        parts.append(Came(part[None]))
    return parts


def came(parts):
    return [part.array for part in parts if isinstance(part, Came)]


def after(array, *others):
    return lax.optimization_barrier((array, *others))[0]


def two_chips(hidden, pre_gain, post_gain, wq, wk, wv, w_out, block_of):
    rows = hidden.shape[0]
    block_rows = 2 * rows
    lines, tp = lax.axis_size("seq"), lax.axis_index("tp")
    seq, group = lax.axis_index("seq"), lax.axis_index("groups")
    chip, core = tp // 2, tp % 2

    line = (seq - jnp.arange(lines, dtype=jnp.int32)) % lines
    near_starts = lookup(block_of, 2 * line + chip) * block_rows
    far_starts = lookup(block_of, 2 * line + 1 - chip) * block_rows
    table = jnp.concatenate([jnp.stack([core, group]).astype(jnp.int32), near_starts, far_starts])
    group_at, near_at, far_at = 1, 2, 2 + lines
    run = jnp.arange(rows, dtype=jnp.int32)
    place = jnp.concatenate([core * rows + run, (1 - core) * rows + run])
    trig = rotary_table(jnp.concatenate([near_starts[0] + place, far_starts[0] + place]))
    runs = [(0, 0, rows), (1, 0, rows)]
    near_chunk, far_chunk = Chunk(near_at, runs, rows), Chunk(far_at, runs, rows)
    others, everyone = list(range(1, lines)), list(range(lines))

    half = rows // 2
    own = [norm(hidden, pre_gain, at * half, [half])[0] for at in range(2)]
    away = [flipped(part, "tp", 2) for part in own]
    partner = [Came(flipped(part, "tp", 1)) for part in own]

    weights = (wq, wk, wv)
    places = [0, half, rows, rows + half]
    q_near, kv_near = qkv([*own, *partner], places, block_rows, weights, trig, 0)
    near = along_line(kv_near)
    eighth = w_out.shape[0] // 8
    sizes = [eighth, eighth, eighth * 3 // 2]
    w_cut = cut(table, group_at, after(w_out, kv_near), sizes)
    q_near = after(q_near, *w_cut)
    (near_state,) = attention(
        [Step(0, 0, others, same=0)], table, [q_near], [near_chunk], [near], [near_chunk], [None]
    )

    away[0] = after(away[0], *near_state)
    quarter = half // 2
    swapped = [flipped(away[0][at : at + quarter], "tp", 1) for at in (0, quarter)]
    held = qkv(
        [Came(away[0]), *[Came(part) for part in swapped]],
        [0, rows, rows + quarter],
        block_rows,
        weights,
        trig,
        block_rows,
    )
    away[1] = after(away[1], *held)
    held = qkv(
        [Came(away[1]), Came(flipped(away[1], "tp", 1))],
        [half, rows + half],
        block_rows,
        weights,
        trig,
        block_rows,
        held,
    )
    q_far, kv_far = held

    fetched = lambda piece, *others: flipped(after(piece, *others), "tp", 2)
    swap = lambda array: flipped(array, "groups", 1)
    w_far = [fetched(piece, away[1]) for piece in w_cut[:2]]
    w_far[0] = after(w_far[0], kv_far)
    w_other = [swap(w_far[0])]
    far = along_ring(kv_far, w_far[1], w_other[0])
    w_far[1] = after(w_far[1], came(far)[0])
    w_far += [fetched(piece, before) for piece, before in zip(w_cut[2:], w_far[:2])]
    w_other.append(swap(w_far[1]))

    near_state, far_state = attention(
        [Step(1, 1, [], same=0), Step(1, 0, everyone), Step(0, 1, [0])],
        table,
        [q_near, q_far],
        [near_chunk, far_chunk],
        [near, far[:1]],
        [near_chunk, far_chunk],
        [near_state, None],
    )
    w_far[2] = after(w_far[2], *far_state, w_other[1], came(far)[-1])
    w_other.append(swap(w_far[2]))
    rest = [Step(0, 0, others)]
    (gone,) = attention(
        rest, table, [q_far], [far_chunk], [far], [far_chunk], [far_state], final=[[0]]
    )
    gone = flipped(gone, "tp", 2)
    (attended,) = attention(
        rest, table, [q_near], [near_chunk], [far], [far_chunk], [near_state], final=[[0]]
    )
    arrived = [Came(piece) for piece in w_far[:3] + w_other[:2]]
    near_sum, w_laid = output_near(table, group_at, attended, w_out, sizes, arrived)
    last, both = Came(w_other[2]), Came(w_far[3])
    sent, w_laid = output_send(
        table, group_at, Came(gone), near_sum, w_laid, sizes, last, both
    )
    received = flipped(sent, "tp", 1)
    kept, held = output_keep(Came(gone), hidden, near_sum, w_laid)
    return output(Came(received), held, kept, post_gain)


def any_count(hidden, pre_gain, post_gain, wq, wk, wv, w_out, block_of):
    rows = hidden.shape[0]
    lines = lax.axis_size("seq")
    line = (lax.axis_index("seq") - jnp.arange(lines, dtype=jnp.int32)) % lines
    block = (2 * line[:, None] + jnp.arange(2, dtype=jnp.int32)).reshape(-1)
    block_rows = rows * lax.axis_size("tp") // 2
    starts = lookup(block_of, block) * block_rows
    table = jnp.concatenate([jnp.zeros(2, jnp.int32), starts])
    normed = norm(hidden, pre_gain, 0, [rows], 1)[0]
    normed = lax.all_gather(normed, "tp", axis=0, tiled=True)
    place = jnp.arange(block_rows, dtype=jnp.int32)
    trig = rotary_table((starts[:2, None] + place).reshape(-1))
    qs, keys_values, weights = [], [], (wq, wk, wv)
    for at in range(2):
        first = at * block_rows
        rows_here = [normed[first : first + block_rows]]
        q, kv = qkv(rows_here, [0], block_rows, weights, trig, first)
        qs.append(q)
        keys_values.append(kv)
    kv = lax.all_gather(jnp.stack(keys_values), "seq")[line].reshape(-1, block_rows, 2 * HD)
    rest = list(range(2, 2 * lines))
    runs = [(0, 0, block_rows)]
    attended = attention(
        [Step(0, 0, [1], same=0), Step(1, 0, [0], same=1), Step(0, 0, rest), Step(1, 0, rest)],
        table,
        qs,
        [Chunk(2, runs, 0), Chunk(3, runs, 0)],
        [[kv]],
        [Chunk(2, runs, 0)],
        [None, None],
        final=[[0, 1]],
    )[0]
    partial = jnp.dot(attended, w_out, preferred_element_type=jnp.float32)
    summed = lax.psum_scatter(
        partial.astype(jnp.bfloat16), "tp", scatter_dimension=0, tiled=True
    ).astype(jnp.float32)
    mean = jnp.mean(summed * summed, axis=-1, keepdims=True)
    projected = summed * lax.rsqrt(mean + EPS) * post_gain
    return (hidden.astype(jnp.float32) + projected).astype(jnp.bfloat16)


def solution(mesh):
    return jax.shard_map(
        two_chips if mesh.shape["tp"] == 4 else any_count,
        mesh=mesh,
        in_specs=(
            P(("groups", "seq", "tp"), None),
            P(),
            P(),
            P(None, "tp"),
            P(None, "tp"),
            P(None, "tp"),
            P("tp", None),
            P(),
        ),
        out_specs=P(("groups", "seq", "tp"), None),
        check_vma=False,
    )
```

```python
import functools
import math

import jax
import jax.numpy as jnp
from jax import lax
from jax.experimental import pallas as pl
from jax.experimental.pallas import tpu as pltpu
from jax.sharding import PartitionSpec as P

HD = 128
ATT_SCALAR = 144
EPS = 1e-6
MIB = 1024 * 1024
HIDDEN = -1e30
ONES = 16
COST = pl.CostEstimate(flops=1, bytes_accessed=1, transcendentals=0)

ANY = pl.BlockSpec(memory_space=pl.ANY)
HBM = pl.BlockSpec(memory_space=pltpu.HBM)
VMEM = pl.BlockSpec(memory_space=pltpu.VMEM)
SMEM = pl.BlockSpec(memory_space=pltpu.SMEM)


class Came:
    def __init__(self, array):
        self.array, self.shape = array, array.shape


def call(kernel, name, mib, in_specs, outs, scratch, *args, aliases=None):
    in_specs, pinned = list(in_specs), []
    for at, arg in enumerate(args):
        if isinstance(arg, Came):
            arg, in_specs[at] = arg.array, ANY
        elif in_specs[at] is not SMEM:
            arg = pltpu.with_memory_space_constraint(arg, in_specs[at].memory_space)
        pinned.append(arg)
    return pl.pallas_call(
        kernel,
        in_specs=in_specs,
        out_specs=[spec for _, _, spec in outs],
        out_shape=[spec.memory_space(shape, dtype) for shape, dtype, spec in outs],
        scratch_shapes=scratch,
        input_output_aliases=aliases or {},
        compiler_params=pltpu.CompilerParams(vmem_limit_bytes=mib * MIB),
        cost_estimate=COST,
        name=name,
    )(*pinned)


class Copies:
    def __init__(self, semaphores):
        self.semaphores, self.used = semaphores, 0

    def start(self, source, target):
        copy = pltpu.make_async_copy(source, target, self.semaphores.at[self.used])
        self.used += 1
        copy.start()
        return copy


def norm_kernel(cuts, pieces, first, hidden, gain, *refs):
    parts, (gains, rows, staged, semaphores) = refs[: len(cuts)], refs[len(cuts) :]
    copies = Copies(semaphores)
    count, width = rows.shape
    step = count // pieces
    spans = [pl.ds(at * step, step) for at in range(pieces)]
    ins = [
        copies.start(hidden.at[pl.ds(first + at * step, step)], rows.at[span])
        for at, span in enumerate(spans)
    ]
    copies.start(gain, gains).wait()
    scale = gains[...].reshape(1, width)
    outs = []
    for at, span in enumerate(spans):
        ins[at].wait()
        x = rows[span, :].astype(jnp.float32)
        square = x * x
        folded = square[:, :128]
        for lane in range(128, width, 128):
            folded = folded + square[:, lane : lane + 128]
        mean = jnp.sum(folded, axis=1, keepdims=True) / width
        staged[span, :] = (x * lax.rsqrt(mean + EPS) * scale).astype(jnp.bfloat16)
        begin = 0
        for cut, part in zip(cuts, parts):
            if begin <= at * step < begin + cut:
                inside = pl.ds(at * step - begin, step)
                outs.append(copies.start(staged.at[span], part.at[inside]))
            begin += cut
    for copy in outs:
        copy.wait()


def norm(hidden, gain, first, cuts, pieces=3):
    rows, width = sum(cuts), hidden.shape[1]
    bf16 = jnp.bfloat16
    return call(
        functools.partial(norm_kernel, cuts, pieces, first),
        "norm_rows",
        8,
        [HBM, HBM],
        [((cut, width), bf16, HBM) for cut in cuts],
        [
            pltpu.VMEM((width,), jnp.float32),
            pltpu.VMEM((rows, width), bf16),
            pltpu.VMEM((rows, width), bf16),
            pltpu.SemaphoreType.DMA((1 + 2 * pieces,)),
        ],
        hidden,
        gain,
    )


def qkv_kernel(places, first, chunks, held, trig, wq, wk, wv, *refs):
    parts, refs = refs[: len(places)], refs[len(places) + 2 * held :]
    q, kv, weights, rows, angles, semaphores = refs
    copies, waits = Copies(semaphores), []
    depth = weights.shape[0] // chunks
    for chunk in range(chunks):
        span, put, column, here = pl.ds(chunk * depth, depth), 0, 0, []
        for part in parts:
            target = rows.at[pl.ds(put, part.shape[0]), span]
            here.append(copies.start(part.at[:, span], target))
            put += part.shape[0]
        for weight in (wq, wk, wv):
            target = weights.at[span, pl.ds(column, weight.shape[1])]
            here.append(copies.start(weight.at[span], target))
            column += weight.shape[1]
        waits.append(here)
    late, put = [], 0
    for part, place in zip(parts, places):
        count = part.shape[0]
        source = trig.at[pl.ds(first + place, count)]
        late.append(copies.start(source, angles.at[pl.ds(put, count)]))
        put += count
    product = None
    for chunk, here in enumerate(waits):
        for copy in here:
            copy.wait()
        span = pl.ds(chunk * depth, depth)
        term = jnp.dot(rows[:, span], weights[span, :], preferred_element_type=jnp.float32)
        product = term if product is None else product + term
    for copy in late:
        copy.wait()
    cos, sin = angles[:, :HD], angles[:, HD:]
    queries = product.shape[1] - 2 * HD

    def rotated(at):
        y = product[:, at : at + HD]
        return y * cos + pltpu.roll(y, HD // 2, 1) * sin

    factor = ATT_SCALAR ** (-0.5) * math.log2(math.e)
    keys = rotated(queries).astype(jnp.bfloat16)
    values = product[:, queries + HD :].astype(jnp.bfloat16)
    heads = [(rotated(at) * factor).astype(jnp.bfloat16) for at in range(0, queries, HD)]
    put = 0
    for part, place in zip(parts, places):
        count = part.shape[0]
        kv[place : place + count, :HD] = keys[put : put + count]
        kv[place : place + count, HD:] = values[put : put + count]
        for head, rotated_head in enumerate(heads):
            q[head, place : place + count, :] = rotated_head[put : put + count]
        put += count


def qkv(parts, places, total, weights, trig, first, held=(), chunks=4):
    rows, width = sum(part.shape[0] for part in parts), parts[0].shape[1]
    columns = sum(weight.shape[1] for weight in weights)
    heads, bf16 = weights[0].shape[1] // HD, jnp.bfloat16
    given = 4 + len(parts)
    return call(
        functools.partial(qkv_kernel, places, first, chunks, bool(held)),
        "qkv",
        14,
        [HBM] * given + [VMEM] * len(held),
        [((heads, total, HD), bf16, VMEM), ((total, 2 * HD), bf16, VMEM)],
        [
            pltpu.VMEM((width, columns), bf16),
            pltpu.VMEM((rows, width), bf16),
            pltpu.VMEM((rows, 2 * HD), jnp.float32),
            pltpu.SemaphoreType.DMA((len(parts) + (len(parts) + 3) * chunks,)),
        ],
        trig,
        *weights,
        *parts,
        *held,
        aliases={given + at: at for at in range(len(held))},
    )


class Step:
    def __init__(self, q, group, slots, same=None, merged=False):
        self.q, self.group, self.slots = q, group, slots
        self.same, self.merged = same, merged


class Chunk:
    def __init__(self, at, runs, share):
        self.at, self.runs, self.share = at, runs, share

    def places(self, core, axis, first, size):
        shape = (size, 1) if axis == 0 else (1, size)
        index = first + lax.broadcasted_iota(jnp.int32, shape, axis)
        result, begin = index, 0
        for which, offset, rows in self.runs:
            base = (core if which == 0 else 1 - core) * self.share + offset - begin
            inside = (index >= begin) & (index < begin + rows)
            result = jnp.where(inside, index + base, result)
            begin += rows
        return result


def attention_kernel(plan, q_chunks, k_chunks, group_parts, fresh, final, table, *refs):
    refs = list(refs)
    take = lambda n: [refs.pop(0) for _ in range(n)]
    count = len(q_chunks)
    qs = take(count)
    kv_parts = [take(n) for n in group_parts]
    take(2 * (count - len(fresh)))
    outs = take(len(final))
    states = [take(2) for _ in range(count)]
    kvs = take(len(group_parts))
    (semaphores,) = refs
    copies = Copies(semaphores)
    core = table[0]
    waits = {}
    for group, (parts, kv) in enumerate(zip(kv_parts, kvs)):
        each = kv.shape[0] // len(parts)
        waits[group] = [
            copies.start(part, kv.at[pl.ds(slot * each, each)])
            for slot, part in enumerate(parts)
        ]

    def ready(group):
        for copy in waits.pop(group, []):
            copy.wait()

    def attend(q, keys_values, begin, visible=None, bias=None):
        q_ref, (peak, acc) = qs[q], states[q]
        heads = q_ref.shape[0]
        keys = keys_values[:, :HD]
        values = keys_values[:, HD:].T
        values = jnp.concatenate([values, jnp.ones((ONES, keys.shape[0]), values.dtype)], axis=0)
        tiles, tile = acc.shape[0], acc.shape[2] // heads
        scores, tops, weights = [], [], []
        for at in range(tiles):
            q_tile = q_ref[:, at * tile : (at + 1) * tile, :].reshape(heads * tile, HD)
            score = lax.dot_general(
                keys, q_tile, (((1,), (1,)), ((), ())), preferred_element_type=jnp.float32
            )
            if visible is not None:
                seen = jnp.concatenate([visible(at * tile, tile)] * heads, axis=1)
                score = jnp.where(seen, score, HIDDEN)
            if bias is not None:
                score = score + bias
            scores.append(score)
        for at in range(tiles):
            top = jnp.max(scores[at], axis=0, keepdims=True)
            if not begin:
                top = jnp.maximum(peak[at, 0:1, :], top)
            tops.append(top)
            weights.append(jnp.exp2((scores[at] - top).astype(jnp.bfloat16)))
        for at in range(tiles):
            summed = jnp.dot(values, weights[at], preferred_element_type=jnp.float32)
            if not begin:
                summed = summed + acc[at] * jnp.exp2(peak[at, 0:1, :] - tops[at])
            acc[at] = summed
            peak[at] = jnp.broadcast_to(tops[at], peak.shape[1:])

    begun = set(range(count)) - set(fresh)
    for step in plan:
        q, group, kv = step.q, step.group, kvs[step.group]
        q_chunk, k_chunk = q_chunks[q], k_chunks[group]
        if step.same is not None:
            keys_at = k_chunk.places(core, 0, 0, kv.shape[1])
            visible = lambda first, tile: keys_at <= q_chunk.places(core, 1, first, tile)
            own = kv_parts[group][0]
            attend(q, own[step.same], q not in begun, visible=visible)
            begun.add(q)
        start = table[q_chunk.at]
        slots = step.slots
        if not slots:
            continue
        ready(group)
        if step.merged:
            shown = [table[k_chunk.at + slot] < start for slot in slots]

            @pl.when(functools.reduce(jnp.logical_or, shown))
            def _():
                rows = kv.shape[1]
                bias = [
                    jnp.where(see, 0.0, HIDDEN) * jnp.ones((rows, 1), jnp.float32)
                    for see in shown
                ]
                keys_values = kv[slots[0] : slots[-1] + 1].reshape(len(slots) * rows, 2 * HD)
                attend(q, keys_values, False, bias=jnp.concatenate(bias, axis=0))

        else:

            def one(slot, carry):
                @pl.when(table[k_chunk.at + slot] < start)
                def _():
                    attend(q, kv[slot], False)

                return carry

            lax.fori_loop(slots[0], slots[-1] + 1, one, 0)

    for group in list(waits):
        ready(group)
    for out, order in zip(outs, final):
        put = 0
        for q in order:
            acc, heads = states[q][1], qs[q].shape[0]
            tile = acc.shape[2] // heads
            for at in range(acc.shape[0]):
                rows = acc[at, :HD, :] / acc[at, HD : HD + 1, :]
                rows = rows.T.astype(jnp.bfloat16)
                for head in range(heads):
                    out[put : put + tile, head * HD : (head + 1) * HD] = rows[
                        head * tile : (head + 1) * tile
                    ]
                put += tile


def attention(plan, table, qs, q_chunks, groups, k_chunks, state, final=()):
    fresh = [at for at, held in enumerate(state) if held is None]
    shapes = []
    for q in qs:
        heads, rows, _ = q.shape
        tile = min(rows, 128)
        shapes += [(rows // tile, deep, heads * tile) for deep in (8, HD + ONES)]
    width = qs[0].shape[0] * HD
    sums = [sum(qs[q].shape[1] for q in order) for order in final]
    outs = [((rows, width), jnp.bfloat16, VMEM) for rows in sums]
    scratch = []
    for parts in groups:
        slots = sum(part.shape[0] for part in parts)
        scratch.append(pltpu.VMEM((slots,) + parts[0].shape[1:], jnp.bfloat16))
    parts = [part for parts in groups for part in parts]
    sizes = [len(parts) for parts in groups]
    inputs, aliases = [table, *qs, *parts], {}
    for at, pair in enumerate(state):
        for half, array in enumerate(pair or ()):
            aliases[len(inputs)] = len(outs) + 2 * at + half
            inputs.append(array)
    results = call(
        functools.partial(attention_kernel, plan, q_chunks, k_chunks, sizes, fresh, final),
        "attention",
        10,
        [SMEM] + [VMEM] * (len(inputs) - 1),
        outs + [(shape, jnp.float32, VMEM) for shape in shapes],
        scratch + [pltpu.SemaphoreType.DMA((len(parts),))],
        *inputs,
        aliases=aliases,
    )
    if final:
        return results[: len(final)]
    return [tuple(results[2 * at : 2 * at + 2]) for at in range(len(qs))]


def cut_kernel(sizes, at, table, weights, *refs):
    outs, (held, semaphores) = refs[: len(sizes) + 1], refs[len(sizes) + 1 :]
    copies = Copies(semaphores)
    half = weights.shape[0] // 2
    first = pl.multiple_of(table[at] * half, half)
    split = sum(sizes)
    rest = half - split
    ins, put = [], 0
    for size in sizes:
        target = held.at[pl.ds(put, size)]
        ins.append((copies.start(weights.at[pl.ds(first + put, size)], target), target))
        put += size
    both = held.at[pl.ds(split, 2 * rest)]
    for side in range(2):
        source = weights.at[pl.ds(side * half + split, rest)]
        copy = copies.start(source, held.at[pl.ds(split + side * rest, rest)])
        ins.append((copy, both if side else None))
    outs, stores = list(outs), []
    for copy, piece in ins:
        copy.wait()
        if piece is not None:
            stores.append(copies.start(piece, outs.pop(0)))
    for copy in stores:
        copy.wait()


def cut(table, at, weights, sizes):
    depth, width = weights.shape
    rest = depth // 2 - sum(sizes)
    return call(
        functools.partial(cut_kernel, sizes, at),
        "cut_weights",
        4,
        [SMEM, HBM],
        [((size, width), weights.dtype, HBM) for size in [*sizes, 2 * rest]],
        [
            pltpu.VMEM((depth // 2 + rest, width), weights.dtype),
            pltpu.SemaphoreType.DMA((2 * len(sizes) + 3,)),
        ],
        table,
        weights,
    )


def near_kernel(chunks, left, weights_hbm, out, weights, semaphores):
    copies = Copies(semaphores)
    step = out.shape[1] // chunks
    lanes = [pl.ds(chunk * step, step) for chunk in range(chunks)]
    waits = [copies.start(weights_hbm.at[:, at], weights.at[:, at]) for at in lanes]
    for at, copy in zip(lanes, waits):
        copy.wait()
        out[:, at] = jnp.dot(
            left[...], weights[:, at], preferred_element_type=jnp.float32
        ).astype(jnp.bfloat16)


def output_near(left, weights, chunks=6):
    rows, width = left.shape[0], weights.shape[1]
    return call(
        functools.partial(near_kernel, chunks),
        "output_near",
        8,
        [VMEM, HBM],
        [((rows, width), jnp.bfloat16, VMEM)],
        [pltpu.VMEM(weights.shape, weights.dtype), pltpu.SemaphoreType.DMA((chunks,))],
        left,
        weights,
    )[0]


def send_kernel(at, splits, chunks, table, left_hbm, near, *refs):
    pieces, refs = refs[: 2 * splits + 1], refs[2 * splits + 1 :]
    out, weights, left, staged, semaphores = refs
    copies = Copies(semaphores)
    depth, width = weights.shape
    half, step = depth // 2, width // chunks
    first = copies.start(left_hbm, left)
    waits, put = [], 0
    for own, other in zip(pieces[:splits], pieces[splits:-1]):
        for piece, side in ((own, table[at]), (other, 1 - table[at])):
            row = pl.multiple_of(side * half + put, 16)
            waits.append(copies.start(piece, weights.at[pl.ds(row, piece.shape[0])]))
        put += own.shape[0]
    for side in range(2):
        source = pieces[-1].at[pl.ds(side * (half - put), half - put)]
        waits.append(copies.start(source, weights.at[pl.ds(side * half + put, half - put)]))
    for copy in waits:
        copy.wait()
    first.wait()
    half = left.shape[0] // 2
    stores = []
    for chunk in range(chunks):
        span = pl.ds(chunk * step, step)
        staged[:, span] = (
            near[half:, span].astype(jnp.float32)
            + jnp.dot(left[half:, :], weights[:, span], preferred_element_type=jnp.float32)
        ).astype(jnp.bfloat16)
        stores.append(copies.start(staged.at[:, span], out.at[:, span]))
    for copy in stores:
        copy.wait()


def output_send(table, at, left, near, pieces, chunks=6):
    (rows, width), columns = near.shape, left.shape[1]
    half, bf16 = (rows // 2, width), jnp.bfloat16
    return call(
        functools.partial(send_kernel, at, len(pieces) // 2, chunks),
        "output_send",
        8,
        [SMEM, HBM, VMEM] + [HBM] * len(pieces),
        [(half, bf16, HBM), ((columns, width), bf16, VMEM)],
        [
            pltpu.VMEM(left.shape, bf16),
            pltpu.VMEM(half, bf16),
            pltpu.SemaphoreType.DMA((2 + len(pieces) + chunks,)),
        ],
        table,
        left,
        near,
        *pieces,
    )


def keep_kernel(chunks, left_hbm, hidden, near, weights, out, held, left, semaphores):
    copies = Copies(semaphores)
    first, late = copies.start(left_hbm, left), copies.start(hidden, held)
    first.wait()
    half, step = left.shape[0] // 2, out.shape[1] // chunks
    for chunk in range(chunks):
        span = pl.ds(chunk * step, step)
        out[:, span] = near[:half, span].astype(jnp.float32) + jnp.dot(
            left[:half, :], weights[:, span], preferred_element_type=jnp.float32
        )
    late.wait()


def output_keep(left, hidden, near, weights, chunks=6):
    rows, width = near.shape
    return call(
        functools.partial(keep_kernel, chunks),
        "output_keep",
        4,
        [HBM, HBM, VMEM, VMEM],
        [((rows // 2, width), jnp.float32, VMEM), (hidden.shape, hidden.dtype, VMEM)],
        [pltpu.VMEM(left.shape, jnp.bfloat16), pltpu.SemaphoreType.DMA((2,))],
        left,
        hidden,
        near,
        weights,
    )


def final_kernel(chunks, received, hidden, kept, gain, out, other, staged, gains, semaphores):
    copies = Copies(semaphores)
    width = hidden.shape[1]
    step = width // chunks
    lanes = [pl.ds(chunk * step, step) for chunk in range(chunks)]
    waits = [copies.start(received.at[:, span], other.at[:, span]) for span in lanes]
    late = copies.start(gain, gains)
    square = jnp.zeros((hidden.shape[0], 128), jnp.float32)
    for span, copy in zip(lanes, waits):
        copy.wait()
        total = kept[:, span] + other[:, span].astype(jnp.float32)
        for lane in range(0, step, 128):
            part = total[:, lane : lane + 128]
            square = square + part * part
    mean = jnp.sum(square, axis=1, keepdims=True) / width
    scale = lax.rsqrt(mean + EPS)
    late.wait()
    row = gains[...].reshape(1, width)
    stores = []
    for chunk, span in enumerate(lanes):
        total = kept[:, span] + other[:, span].astype(jnp.float32)
        normed = total * scale * row[:, chunk * step : (chunk + 1) * step]
        staged[:, span] = (hidden[:, span].astype(jnp.float32) + normed).astype(jnp.bfloat16)
        stores.append(copies.start(staged.at[:, span], out.at[:, span]))
    for store in stores:
        store.wait()


def output(received, hidden, kept, gain, chunks=6):
    rows, width = hidden.shape
    bf16 = jnp.bfloat16
    return call(
        functools.partial(final_kernel, chunks),
        "output_norm",
        8,
        [HBM, VMEM, VMEM, HBM],
        [((rows, width), bf16, HBM)],
        [
            pltpu.VMEM((rows, width), bf16),
            pltpu.VMEM((rows, width), bf16),
            pltpu.VMEM((width,), jnp.float32),
            pltpu.SemaphoreType.DMA((1 + 2 * chunks,)),
        ],
        received,
        hidden,
        kept,
        gain,
    )[0]


def rotary_table(positions):
    half = HD // 2
    frequency = jnp.power(
        jnp.float32(10000.0), -jnp.arange(half, dtype=jnp.float32) * (2.0 / HD)
    )
    angles = positions.astype(jnp.float32)[:, None] * frequency[None, :]
    cos, sin = jnp.cos(angles), jnp.sin(angles)
    return jnp.concatenate([cos, cos, -sin, sin], axis=1)


def lookup(block_of, index):
    ids = jnp.arange(block_of.shape[0], dtype=jnp.int32)
    return jnp.sum(jnp.where(index[..., None] == ids, block_of, 0), axis=-1)


def flipped(array, axis, bit):
    size = lax.axis_size(axis)
    return lax.ppermute(array, axis, [(i, i ^ bit) for i in range(size)])


def along_line(array):
    size = lax.axis_size("seq")
    parts = [array[None]]
    for by in range(1, size):
        part = lax.ppermute(array, "seq", [(i, (i + by) % size) for i in range(size)])
        parts.append(Came(part[None]))
    return parts


def along_ring(array, beside):
    size = lax.axis_size("seq")
    parts, part = [array[None]], array
    for step in range(1, size):
        if step == size - 1:
            part = after(part, beside)
        part = lax.ppermute(part, "seq", [(i, (i + 1) % size) for i in range(size)])
        parts.append(Came(part[None]))
    return parts


def came(parts):
    return [part.array for part in parts if isinstance(part, Came)]


def after(array, *others):
    return lax.optimization_barrier((array, *others))[0]


def two_chips(hidden, pre_gain, post_gain, wq, wk, wv, w_out, block_of):
    rows = hidden.shape[0]
    block_rows = 2 * rows
    lines, tp = lax.axis_size("seq"), lax.axis_index("tp")
    seq, group = lax.axis_index("seq"), lax.axis_index("groups")
    chip, core = tp // 2, tp % 2

    line = (seq - jnp.arange(lines, dtype=jnp.int32)) % lines
    near_starts = lookup(block_of, 2 * line + chip) * block_rows
    far_starts = lookup(block_of, 2 * line + 1 - chip) * block_rows
    table = jnp.concatenate([jnp.stack([core, group]).astype(jnp.int32), near_starts, far_starts])
    group_at, near_at, far_at = 1, 2, 2 + lines
    run = jnp.arange(rows, dtype=jnp.int32)
    place = jnp.concatenate([core * rows + run, (1 - core) * rows + run])
    trig = rotary_table(jnp.concatenate([near_starts[0] + place, far_starts[0] + place]))
    runs = [(0, 0, rows), (1, 0, rows)]
    near_chunk, far_chunk = Chunk(near_at, runs, rows), Chunk(far_at, runs, rows)
    others, everyone = list(range(1, lines)), list(range(lines))

    half = rows // 2
    own = [norm(hidden, pre_gain, at * half, [half])[0] for at in range(2)]
    away = [flipped(part, "tp", 2) for part in own]
    partner = [Came(flipped(part, "tp", 1)) for part in own]

    weights = (wq, wk, wv)
    places = [0, half, rows, rows + half]
    q_near, kv_near = qkv([*own, *partner], places, block_rows, weights, trig, 0)
    near = along_line(kv_near)
    eighth = w_out.shape[0] // 8
    sizes = [eighth * 3 // 2, eighth, eighth]
    w_cut = cut(table, group_at, after(w_out, kv_near), sizes)
    q_near = after(q_near, *w_cut)
    (near_state,) = attention(
        [Step(0, 0, others, same=0)], table, [q_near], [near_chunk], [near], [near_chunk], [None]
    )

    away[0] = after(away[0], *near_state)
    quarter = half // 2
    swapped = [flipped(away[0][at : at + quarter], "tp", 1) for at in (0, quarter)]
    held = qkv(
        [Came(away[0]), *[Came(part) for part in swapped]],
        [0, rows, rows + quarter],
        block_rows,
        weights,
        trig,
        block_rows,
    )
    away[1] = after(away[1], *held)
    held = qkv(
        [Came(away[1]), Came(flipped(away[1], "tp", 1))],
        [half, rows + half],
        block_rows,
        weights,
        trig,
        block_rows,
        held,
    )
    q_far, kv_far = held

    fetched = lambda piece, *others: flipped(after(piece, *others), "tp", 2)
    swap = lambda array: flipped(array, "groups", 1)
    w_far = [fetched(piece, away[1]) for piece in w_cut[:2]]
    w_far[0] = after(w_far[0], kv_far)
    w_other = [swap(w_far[0])]
    far = along_ring(kv_far, kv_far)
    w_far.append(fetched(w_cut[2], w_far[0]))

    near_state, far_state = attention(
        [Step(1, 1, [], same=0), Step(1, 0, everyone), Step(0, 1, [0])],
        table,
        [q_near, q_far],
        [near_chunk, far_chunk],
        [near, far[:1]],
        [near_chunk, far_chunk],
        [near_state, None],
    )
    w_far[1] = after(w_far[1], *far_state, w_other[0])
    w_far.append(fetched(w_cut[3], w_far[1]))
    rest = [Step(0, 0, others)]
    (gone,) = attention(
        rest, table, [q_far], [far_chunk], [far], [far_chunk], [far_state], final=[[0]]
    )
    w_far[2] = after(w_far[2], gone)
    w_other += [swap(piece) for piece in w_far[1:3]]
    gone = flipped(gone, "tp", 2)
    (attended,) = attention(
        rest, table, [q_near], [near_chunk], [far], [far_chunk], [near_state], final=[[0]]
    )
    near_sum = output_near(attended, w_out)
    pieces = [Came(piece) for piece in w_far[:3] + w_other + w_far[3:]]
    sent, w_laid = output_send(table, group_at, Came(gone), near_sum, pieces)
    received = flipped(sent, "tp", 1)
    kept, held = output_keep(Came(gone), hidden, near_sum, w_laid)
    return output(Came(received), held, kept, post_gain)


def any_count(hidden, pre_gain, post_gain, wq, wk, wv, w_out, block_of):
    rows = hidden.shape[0]
    lines = lax.axis_size("seq")
    line = (lax.axis_index("seq") - jnp.arange(lines, dtype=jnp.int32)) % lines
    block = (2 * line[:, None] + jnp.arange(2, dtype=jnp.int32)).reshape(-1)
    block_rows = rows * lax.axis_size("tp") // 2
    starts = lookup(block_of, block) * block_rows
    table = jnp.concatenate([jnp.zeros(2, jnp.int32), starts])
    normed = norm(hidden, pre_gain, 0, [rows], 1)[0]
    normed = lax.all_gather(normed, "tp", axis=0, tiled=True)
    place = jnp.arange(block_rows, dtype=jnp.int32)
    trig = rotary_table((starts[:2, None] + place).reshape(-1))
    qs, keys_values, weights = [], [], (wq, wk, wv)
    for at in range(2):
        first = at * block_rows
        rows_here = [normed[first : first + block_rows]]
        q, kv = qkv(rows_here, [0], block_rows, weights, trig, first)
        qs.append(q)
        keys_values.append(kv)
    kv = lax.all_gather(jnp.stack(keys_values), "seq")[line].reshape(-1, block_rows, 2 * HD)
    rest = list(range(2, 2 * lines))
    runs = [(0, 0, block_rows)]
    attended = attention(
        [Step(0, 0, [1], same=0), Step(1, 0, [0], same=1), Step(0, 0, rest), Step(1, 0, rest)],
        table,
        qs,
        [Chunk(2, runs, 0), Chunk(3, runs, 0)],
        [[kv]],
        [Chunk(2, runs, 0)],
        [None, None],
        final=[[0, 1]],
    )[0]
    partial = jnp.dot(attended, w_out, preferred_element_type=jnp.float32)
    summed = lax.psum_scatter(
        partial.astype(jnp.bfloat16), "tp", scatter_dimension=0, tiled=True
    ).astype(jnp.float32)
    mean = jnp.mean(summed * summed, axis=-1, keepdims=True)
    projected = summed * lax.rsqrt(mean + EPS) * post_gain
    return (hidden.astype(jnp.float32) + projected).astype(jnp.bfloat16)


def solution(mesh):
    return jax.shard_map(
        two_chips if mesh.shape["tp"] == 4 else any_count,
        mesh=mesh,
        in_specs=(
            P(("groups", "seq", "tp"), None),
            P(),
            P(),
            P(None, "tp"),
            P(None, "tp"),
            P(None, "tp"),
            P("tp", None),
            P(),
        ),
        out_specs=P(("groups", "seq", "tp"), None),
        check_vma=False,
    )
```
